32 devices in a mesh: rep: 8 (over z, y), fsdp: 4 (over x, core).
Axes of the slice: x: 2, y: 2, z: 4, core: 2. Of those that a mesh axis runs over, the one named last changes fastest.
Arguments:
- tokens: bfloat16 [16384, 576], P(('rep', 'fsdp')), may hold values from -6 to 6
- segments: int32 [16384], P(('rep', 'fsdp')), may hold values from 0 to 7, as said below
- cotangent: bfloat16 [16384, 576], P(('rep', 'fsdp')), may hold values from -6 to 6
- projection_weight: float32 [576, 960], P('fsdp'), may hold values from -0.25 to 0.25
- out_weight: float32 [576, 576], P('fsdp'), may hold values from -1 to 1
- gate_up_weight: float32 [1536, 1152], P('fsdp'), may hold values from -0.25 to 0.25
- down_weight: float32 [1536, 576], P('fsdp'), may hold values from -0.15625 to 0.15625
- norm_gains: float32 [1152], P('fsdp'), may hold values from 0.5 to 1.5
- projection_bias: float32 [960], P('fsdp'), may hold values from -3 to 3
- projection_first_moment: float32 [576, 960], P('fsdp', 'rep'), may hold values from -160 to 160
- out_first: float32 [576, 576], P('fsdp', 'rep'), may hold values from -32 to 32
- gate_up_first: float32 [1536, 1152], P('fsdp', 'rep'), may hold values from -28 to 28
- down_first: float32 [1536, 576], P('fsdp', 'rep'), may hold values from -48 to 48
- gains_first: float32 [1152], P('fsdp'), may hold values from -128 to 128
- bias_first_moment: float32 [960], P('fsdp'), may hold values from -160 to 160
- projection_second_moment: float32 [576, 960], P('fsdp', 'rep'), may hold values from 3449 to 13797
- out_second: float32 [576, 576], P('fsdp', 'rep'), may hold values from 137 to 546
- gate_up_second: float32 [1536, 1152], P('fsdp', 'rep'), may hold values from 97 to 384
- down_second: float32 [1536, 576], P('fsdp', 'rep'), may hold values from 309 to 1260
- gains_second: float32 [1152], P('fsdp'), may hold values from 1638 to 6553
- bias_second_moment: float32 [960], P('fsdp'), may hold values from 3449 to 13797
Outputs:
- output: bfloat16 [16384, 576], P(('rep', 'fsdp'))
- tokens_grad: bfloat16 [16384, 576], P(('rep', 'fsdp'))
- qkv_first_new: float32 [576, 960], P('fsdp', 'rep')
- qkv_second_new: float32 [576, 960], P('fsdp', 'rep')
- qkv_weight_new: float32 [576, 960], P('fsdp', 'rep')
- out_first_new: float32 [576, 576], P('fsdp', 'rep')
- out_second_new: float32 [576, 576], P('fsdp', 'rep')
- out_weight_new: float32 [576, 576], P('fsdp', 'rep')
- gate_up_first_new: float32 [1536, 1152], P('fsdp', 'rep')
- gate_up_second_new: float32 [1536, 1152], P('fsdp', 'rep')
- gate_up_weight_new: float32 [1536, 1152], P('fsdp', 'rep')
- down_first_new: float32 [1536, 576], P('fsdp', 'rep')
- down_second_new: float32 [1536, 576], P('fsdp', 'rep')
- down_weight_new: float32 [1536, 576], P('fsdp', 'rep')
- gains_first_new: float32 [1152], P('fsdp')
- gains_second_new: float32 [1152], P('fsdp')
- gains_new: float32 [1152], P('fsdp')
- biases_first_new: float32 [960], P('fsdp')
- biases_second_new: float32 [960], P('fsdp')
- biases_new: float32 [960], P('fsdp')
The draws below stay inside these ranges and needn't reach their ends.
Inputs may be any that keep to these rules, and one draw needn't show every extreme that they name: `segments`: on each device its 512 tokens hold whole sequences in order: segment numbers start at 0 and rise by one where a new sequence begins, which happens only at multiples of 64 tokens; one device holds a single sequence and another holds eight of 64 tokens each.
All inputs are finite; a program needn't handle non-finite values.
Results may differ from the reference program's by a relative error of at most 0.018.
Values may be sent and summed in bfloat16 or wider, within the bound.
No kernel may reach another device: no remote copies, remote signals or barrier semaphores. Data moves between devices by JAX's collectives and lax.ppermute only.
A program may use at most 128 MiB of HBM per device.

```python
import math
import jax
import jax.numpy as jnp
from jax import lax

MODEL_WIDTH = 576
QUERY_HEADS = 9
KEY_VALUE_HEADS = 3
HEAD_SIZE = 64
FF = 1536
STEP = 10
TOK_DEV = 512
TOKENS_IN_ALL = 16384


def draw_segments(key, part):
    key = jax.random.fold_in(key, 7)
    blocks = TOKENS_IN_ALL // TOK_DEV
    cut_key, pick_key, other_key = jax.random.split(key, 3)
    cuts = jax.random.randint(cut_key, (blocks, 7), 0, 2)
    single = jax.random.randint(pick_key, (), 0, blocks)
    crowded = (single + 1 + jax.random.randint(other_key, (), 0, blocks - 1)) % blocks
    device_ids = jnp.arange(blocks, dtype=jnp.int32)[:, None]
    cuts = jnp.where(device_ids == single, 0, cuts)
    cuts = jnp.where(device_ids == crowded, 1, cuts)
    starts = jnp.zeros((blocks, 1), jnp.int32)
    grains = jnp.concatenate([starts, jnp.cumsum(cuts, axis=1).astype(jnp.int32)], axis=1)
    spread = jnp.repeat(grains, TOK_DEV // 8, axis=1, total_repeat_length=TOK_DEV)
    return spread.reshape(TOKENS_IN_ALL).astype(jnp.int32)


def block_levels(key, dims, shards, smallest, largest):
    factor_of = 1.0
    for axis_at, shards_of in shards:
        steps = jax.random.uniform(jax.random.fold_in(jax.random.fold_in(key, 6), axis_at), (shards_of,), jnp.float32, smallest / len(shards), largest / len(shards))
        factor_of = factor_of * jnp.repeat(jnp.exp(steps), dims[axis_at] // shards_of).reshape((-1,) + (1,) * (len(dims) - 1 - axis_at))
    return factor_of


def scatter_about(rng, shape, scale, bound, cuts=(), held_as=jnp.bfloat16):
    array = scale * jax.random.normal(rng, shape, jnp.float32)
    if cuts:
        array = array * block_levels(rng, shape, cuts, -0.22, 0.18)
    return jnp.clip(array, -bound, bound).astype(held_as)


def setup_inputs(seed: int = 0) -> dict:
    keys = jax.random.split(jax.random.key(seed), 22)
    tokens = scatter_about(keys[0], (TOKENS_IN_ALL, MODEL_WIDTH), 1.0, 6.0, ((0, 32),))
    segments = draw_segments(jax.random.fold_in(keys[21], 71), 0)
    cotangent = scatter_about(keys[2], (TOKENS_IN_ALL, MODEL_WIDTH), 1.0, 6.0, ((0, 32),))
    projection_weight = scatter_about(keys[3], (MODEL_WIDTH, (QUERY_HEADS + 2 * KEY_VALUE_HEADS) * HEAD_SIZE), MODEL_WIDTH ** -0.5, 0.25, ((0, 4),), jnp.float32)
    out_weight = scatter_about(keys[4], (QUERY_HEADS * HEAD_SIZE, MODEL_WIDTH), (max(QUERY_HEADS * HEAD_SIZE // 16, 1)) ** -0.5, 1.0, ((0, 4),), jnp.float32)
    gate_up_weight = scatter_about(keys[5], (FF, 2 * MODEL_WIDTH), MODEL_WIDTH ** -0.5, 0.25, ((0, 4),), jnp.float32)
    down_weight = scatter_about(keys[6], (FF, MODEL_WIDTH), FF ** -0.5, 0.15625, ((0, 4),), jnp.float32)
    norm_gains = jnp.clip(1.0 + 0.1 * jax.random.normal(keys[7], (2 * MODEL_WIDTH,), jnp.float32), 0.5, 1.5)
    projection_bias = scatter_about(keys[8], ((QUERY_HEADS + 2 * KEY_VALUE_HEADS) * HEAD_SIZE,), 0.5, 3.0, ((0, 4),), jnp.float32)
    projection_first_moment = scatter_about(keys[9], (MODEL_WIDTH, (QUERY_HEADS + 2 * KEY_VALUE_HEADS) * HEAD_SIZE), (0.0556 * (TOKENS_IN_ALL * MODEL_WIDTH // max(QUERY_HEADS * HEAD_SIZE // 16, 1)) ** 0.5), 160.0, ((0, 4), (1, 8)), jnp.float32)
    out_first = scatter_about(keys[10], (QUERY_HEADS * HEAD_SIZE, MODEL_WIDTH), (0.0444 * TOKENS_IN_ALL ** 0.5), 32.0, ((0, 4), (1, 8)), jnp.float32)
    gate_up_first = scatter_about(keys[11], (FF, 2 * MODEL_WIDTH), (0.061 * (TOKENS_IN_ALL * MODEL_WIDTH // FF) ** 0.5), 28.0, ((0, 4), (1, 8)), jnp.float32)
    down_first = scatter_about(keys[12], (FF, MODEL_WIDTH), (0.0667 * TOKENS_IN_ALL ** 0.5), 48.0, ((0, 4), (1, 8)), jnp.float32)
    gains_first = scatter_about(keys[13], (2 * MODEL_WIDTH,), (0.157 * TOKENS_IN_ALL ** 0.5), 128.0, ((0, 4),), jnp.float32)
    bias_first_moment = scatter_about(keys[14], ((QUERY_HEADS + 2 * KEY_VALUE_HEADS) * HEAD_SIZE,), (0.0556 * (TOKENS_IN_ALL * MODEL_WIDTH // max(QUERY_HEADS * HEAD_SIZE // 16, 1)) ** 0.5), 160.0, ((0, 4),), jnp.float32)
    projection_second_moment = jnp.clip(jnp.exp(math.log(13797.0) - 1.3863668 * jax.random.uniform(keys[15], (MODEL_WIDTH, (QUERY_HEADS + 2 * KEY_VALUE_HEADS) * HEAD_SIZE), jnp.float32) ** block_levels(keys[15], (MODEL_WIDTH, (QUERY_HEADS + 2 * KEY_VALUE_HEADS) * HEAD_SIZE), ((0, 4), (1, 8)), -0.2, 0.2)), 3449.0, 13797.0)
    out_second = jnp.clip(jnp.exp(math.log(546.0) - 1.38263805 * jax.random.uniform(keys[16], (QUERY_HEADS * HEAD_SIZE, MODEL_WIDTH), jnp.float32) ** block_levels(keys[16], (QUERY_HEADS * HEAD_SIZE, MODEL_WIDTH), ((0, 4), (1, 8)), -0.2, 0.2)), 137.0, 546.0)
    gate_up_second = jnp.clip(jnp.exp(math.log(384.0) - 1.3759316 * jax.random.uniform(keys[17], (FF, 2 * MODEL_WIDTH), jnp.float32) ** block_levels(keys[17], (FF, 2 * MODEL_WIDTH), ((0, 4), (1, 8)), -0.2, 0.2)), 97.0, 384.0)
    down_second = jnp.clip(jnp.exp(math.log(1260.0) - 1.4055257 * jax.random.uniform(keys[18], (FF, MODEL_WIDTH), jnp.float32) ** block_levels(keys[18], (FF, MODEL_WIDTH), ((0, 4), (1, 8)), -0.2, 0.2)), 309.0, 1260.0)
    gains_second = jnp.clip(jnp.exp(math.log(6553.0) - 1.386447 * jax.random.uniform(keys[19], (2 * MODEL_WIDTH,), jnp.float32) ** block_levels(keys[19], (2 * MODEL_WIDTH,), ((0, 4),), -0.2, 0.2)), 1638.0, 6553.0)
    bias_second_moment = jnp.clip(jnp.exp(math.log(13797.0) - 1.3863668 * jax.random.uniform(keys[20], ((QUERY_HEADS + 2 * KEY_VALUE_HEADS) * HEAD_SIZE,), jnp.float32) ** block_levels(keys[20], ((QUERY_HEADS + 2 * KEY_VALUE_HEADS) * HEAD_SIZE,), ((0, 4),), -0.2, 0.2)), 3449.0, 13797.0)
    return dict(tokens=tokens, segments=segments, cotangent=cotangent, projection_weight=projection_weight, out_weight=out_weight, gate_up_weight=gate_up_weight, down_weight=down_weight, norm_gains=norm_gains, projection_bias=projection_bias, projection_first_moment=projection_first_moment, out_first=out_first, gate_up_first=gate_up_first, down_first=down_first, gains_first=gains_first, bias_first_moment=bias_first_moment, projection_second_moment=projection_second_moment, out_second=out_second, gate_up_second=gate_up_second, down_second=down_second, gains_second=gains_second, bias_second_moment=bias_second_moment)


@jax.custom_vjp
def reduced_precision(v):
    return lax.optimization_barrier(v.astype(jnp.bfloat16)).astype(jnp.float32)

@jax.custom_vjp
def low_back(v):
    return v

def low_keep(v):
    return (reduced_precision(v), None)

def low_pass(kept, grad):
    return (grad,)

def back_keep(v):
    return (v, None)

def back_low(kept, grad):
    return (reduced_precision(grad),)
reduced_precision.defvjp(low_keep, low_pass)
low_back.defvjp(back_keep, back_low)
norm_eps = 1e-05
rope_base = 100000.0
beta_one = 0.9
beta_two = 0.95
adam_eps = 1e-08
decay_rate = 0.1
highest = lax.Precision.HIGHEST

def learn_rates():
    out_fan = max(QUERY_HEADS * HEAD_SIZE // 16, 1)
    return (MODEL_WIDTH ** (-0.5), out_fan ** (-0.5), MODEL_WIDTH ** (-0.5), FF ** (-0.5), 0.5, 0.5)

def adam_update(weight, first_moment, second_moment, gradient, step_rate):
    first_new = beta_one * first_moment + (1.0 - beta_one) * gradient
    second_new = beta_two * second_moment + (1.0 - beta_two) * gradient * gradient
    first_fix = 1.0 - beta_one ** STEP
    second_fix = 1.0 - beta_two ** STEP
    direction = first_new / first_fix / (jnp.sqrt(second_new / second_fix) + adam_eps)
    return (first_new, second_new, weight - step_rate * (direction + decay_rate * weight))

def rms_norm(values, gain_vec):
    return values * lax.rsqrt(lax.optimization_barrier(jnp.mean(values * values, axis=-1, keepdims=True)) + norm_eps) * gain_vec

def rope_tables(segments):
    token_count = segments.shape[0]
    position = jnp.arange(token_count, dtype=jnp.int32)
    same_doc = segments[:, None] == segments[None, :]
    earlier = lax.optimization_barrier(jnp.sum((same_doc & (position[None, :] < position[:, None])).astype(jnp.int32), axis=1))
    frequency = rope_base ** (-(jnp.arange(HEAD_SIZE // 2, dtype=jnp.float32) * 2.0 / HEAD_SIZE))
    angles = earlier.astype(jnp.float32)[:, None] * frequency[None, :]
    allowed = same_doc & (position[None, :] <= position[:, None])
    return (jnp.cos(angles)[:, None, :], jnp.sin(angles)[:, None, :], allowed)

def rotate_pairs(values, cosine_table, sine_values):
    half_width = values.shape[-1] // 2
    first_half = values[..., :half_width]
    second_half = values[..., half_width:]
    return jnp.concatenate([first_half * cosine_table - second_half * sine_values, second_half * cosine_table + first_half * sine_values], axis=-1)

def attend_block(block_pair):
    projected_rows, segments = block_pair
    count_of_rows = projected_rows.shape[0]
    cosine_table, sine_values, allowed = rope_tables(segments)
    query_span_width = QUERY_HEADS * HEAD_SIZE
    key_span_width = KEY_VALUE_HEADS * HEAD_SIZE
    query_reduced = reduced_precision(rotate_pairs(projected_rows[:, :query_span_width].reshape(count_of_rows, QUERY_HEADS, HEAD_SIZE), cosine_table, sine_values))
    key_reduced = reduced_precision(rotate_pairs(projected_rows[:, query_span_width:query_span_width + key_span_width].reshape(count_of_rows, KEY_VALUE_HEADS, HEAD_SIZE), cosine_table, sine_values))
    value_reduced = reduced_precision(projected_rows[:, query_span_width + key_span_width:].reshape(count_of_rows, KEY_VALUE_HEADS, HEAD_SIZE))
    query_reduced = query_reduced.reshape(count_of_rows, KEY_VALUE_HEADS, QUERY_HEADS // KEY_VALUE_HEADS, HEAD_SIZE)
    scores = jnp.einsum('qkgd,skd->kgqs', query_reduced, key_reduced, precision=highest) * HEAD_SIZE ** (-0.5)
    scores = jnp.where(allowed[None, None], low_back(scores), -1e+30)
    row_peak = lax.optimization_barrier(jnp.max(scores, axis=-1, keepdims=True))
    lifted = jnp.exp(scores - row_peak)
    attention = reduced_precision(lifted / lax.optimization_barrier(jnp.sum(lifted, axis=-1, keepdims=True)))
    mixed_all = jnp.einsum('kgqs,skd->qkgd', attention, value_reduced, precision=highest)
    return mixed_all.reshape(count_of_rows, QUERY_HEADS * HEAD_SIZE)

def forward(inputs, segments, projection_weight, out_weight, gate_up_weight, down_weight, norm_gains, projection_bias):
    gain_all = reduced_precision(norm_gains)
    normed = reduced_precision(rms_norm(inputs, gain_all[:MODEL_WIDTH]))
    projected_rows = low_back(jnp.dot(normed, reduced_precision(projection_weight), precision=highest) + reduced_precision(projection_bias))
    mixed_all = jax.checkpoint(attend_block)((projected_rows, segments))
    mixed_low = low_back(reduced_precision(mixed_all))
    branch = low_back(jnp.dot(mixed_low, reduced_precision(out_weight), precision=highest))
    middle = inputs + branch
    normed_two = reduced_precision(rms_norm(middle, gain_all[MODEL_WIDTH:]))
    gate_up = reduced_precision(gate_up_weight)
    gate_pre = low_back(jnp.dot(normed_two, gate_up[:, :MODEL_WIDTH].T, precision=highest))
    up_pre = low_back(jnp.dot(normed_two, gate_up[:, MODEL_WIDTH:].T, precision=highest))
    hidden = reduced_precision(gate_pre * lax.logistic(gate_pre) * up_pre)
    return middle + low_back(jnp.dot(hidden, reduced_precision(down_weight), precision=highest))

def reference(tokens, segments, cotangent, projection_weight, out_weight, gate_up_weight, down_weight, norm_gains, projection_bias, projection_first_moment, out_first, gate_up_first, down_first, gains_first, bias_first_moment, projection_second_moment, out_second, gate_up_second, down_second, gains_second, bias_second_moment):
    blocks = TOKENS_IN_ALL // TOK_DEV
    params = (projection_weight, out_weight, gate_up_weight, down_weight, norm_gains, projection_bias)

    def one_device(totals, block_data):
        block_tokens, block_segments, block_cotangent = block_data

        def device_layer(inputs, qkv_matrix, out_matrix, gate_up_matrix, down_matrix, gain_vector, bias_vector):
            return forward(inputs, block_segments, qkv_matrix, out_matrix, gate_up_matrix, down_matrix, gain_vector, bias_vector)
        block_out, pullback = jax.vjp(device_layer, block_tokens.astype(jnp.float32), *params)
        grads = pullback(block_cotangent.astype(jnp.float32))
        terms = (reduced_precision(grads[1]), reduced_precision(grads[2]), grads[3], grads[4], reduced_precision(grads[5]), reduced_precision(grads[6]))
        new_totals = tuple((total + term for total, term in zip(totals, terms)))
        return (new_totals, (block_out.astype(jnp.bfloat16), grads[0].astype(jnp.bfloat16)))
    start = tuple((jnp.zeros(param.shape, jnp.float32) for param in params))
    gradients, outs = lax.scan(one_device, start, (tokens.reshape(blocks, TOK_DEV, MODEL_WIDTH), segments.reshape(blocks, TOK_DEV), cotangent.reshape(blocks, TOK_DEV, MODEL_WIDTH)))
    output = outs[0].reshape(TOKENS_IN_ALL, MODEL_WIDTH)
    tokens_grad = outs[1].reshape(TOKENS_IN_ALL, MODEL_WIDTH)
    step_rates = learn_rates()
    qkv_new = adam_update(projection_weight, projection_first_moment, projection_second_moment, gradients[0], step_rates[0])
    out_new = adam_update(out_weight, out_first, out_second, gradients[1], step_rates[1])
    gate_up_new = adam_update(gate_up_weight, gate_up_first, gate_up_second, gradients[2], step_rates[2])
    down_new = adam_update(down_weight, down_first, down_second, gradients[3], step_rates[3])
    gains_new = adam_update(norm_gains, gains_first, gains_second, gradients[4], step_rates[4])
    biases_new = adam_update(projection_bias, bias_first_moment, bias_second_moment, gradients[5], step_rates[5])
    return (output, tokens_grad, qkv_new[0], qkv_new[1], qkv_new[2], out_new[0], out_new[1], out_new[2], gate_up_new[0], gate_up_new[1], gate_up_new[2], down_new[0], down_new[1], down_new[2], gains_new[0], gains_new[1], gains_new[2], biases_new[0], biases_new[1], biases_new[2])
```

```python
import jax
import jax.numpy as jnp
from jax import lax
from jax.sharding import PartitionSpec as P

MODEL_WIDTH = 576
QUERY_HEADS = 9
KEY_VALUE_HEADS = 3
HEAD_SIZE = 64
FF = 1536
STEP = 10


norm_eps = 1e-05
rope_base = 100000.0
beta_one = 0.9
beta_two = 0.95
adam_eps = 1e-08
decay_rate = 0.1


def learn_rates():
    out_fan = max(QUERY_HEADS * HEAD_SIZE // 16, 1)
    return (MODEL_WIDTH ** (-0.5), out_fan ** (-0.5), MODEL_WIDTH ** (-0.5), FF ** (-0.5), 0.5, 0.5)


def adam_update(weight, first_moment, second_moment, gradient, step_rate):
    first_new = beta_one * first_moment + (1.0 - beta_one) * gradient
    second_new = beta_two * second_moment + (1.0 - beta_two) * gradient * gradient
    first_fix = 1.0 - beta_one**STEP
    second_fix = 1.0 - beta_two**STEP
    direction = first_new / first_fix / (jnp.sqrt(second_new / second_fix) + adam_eps)
    return (first_new, second_new, weight - step_rate * (direction + decay_rate * weight))


def owned_columns(weight, gradient, replica):
    width = gradient.shape[1]
    return lax.dynamic_slice_in_dim(weight, replica * width, width, 1)


def contract_rows(left_side, right_side):
    return lax.dot_general(
        left_side, right_side, (((0,), (0,)), ((), ())), preferred_element_type=jnp.float32
    )


def contract_last(left_side, right_side):
    return lax.dot_general(
        left_side, right_side, (((1,), (1,)), ((), ())), preferred_element_type=jnp.float32
    )


def rope_tables(segments):
    token_count = segments.shape[0]
    position = jnp.arange(token_count, dtype=jnp.int32)
    same_doc = segments[:, None] == segments[None, :]
    earlier = jnp.sum(
        (same_doc & (position[None, :] < position[:, None])).astype(jnp.int32), axis=1
    )
    frequency = rope_base ** (-(jnp.arange(HEAD_SIZE // 2, dtype=jnp.float32) * 2.0 / HEAD_SIZE))
    angles = earlier.astype(jnp.float32)[:, None] * frequency[None, :]
    allowed = same_doc & (position[None, :] <= position[:, None])
    return (jnp.cos(angles)[:, None, :], jnp.sin(angles)[:, None, :], allowed)


def rotate_pairs(values, cosine_table, sine_values):
    half_width = values.shape[-1] // 2
    first_half = values[..., :half_width]
    second_half = values[..., half_width:]
    return jnp.concatenate(
        [
            first_half * cosine_table - second_half * sine_values,
            second_half * cosine_table + first_half * sine_values,
        ],
        axis=-1,
    )


def rotate_back(values, cosine_table, sine_values):
    half_width = values.shape[-1] // 2
    first_half = values[..., :half_width]
    second_half = values[..., half_width:]
    return jnp.concatenate(
        [
            first_half * cosine_table + second_half * sine_values,
            second_half * cosine_table - first_half * sine_values,
        ],
        axis=-1,
    )


def norm_forward(values, gain_vec):
    inverse = lax.rsqrt(jnp.mean(values * values, axis=-1, keepdims=True) + norm_eps)
    return (values * inverse * gain_vec, inverse)


def norm_backward(values, inverse, gain_vec, grad_normed):
    weighted = grad_normed * gain_vec
    inner_mean = jnp.mean(weighted * values, axis=-1, keepdims=True)
    grad_values = inverse * weighted - values * (inverse * inverse * inverse) * inner_mean
    grad_gain = jnp.sum(grad_normed * values * inverse, axis=0)
    return (grad_values, grad_gain)


def attention_scores(query_reduced, key_reduced, allowed):
    scores = jnp.einsum(
        "qkgd,skd->kgqs", query_reduced, key_reduced, preferred_element_type=jnp.float32
    ) * HEAD_SIZE ** (-0.5)
    return jnp.where(allowed[None, None], scores, -1e30)


def feed_forward(normed_low, gate_up_low, down_low):
    gate_pre = contract_last(normed_low, gate_up_low[:, :MODEL_WIDTH])
    up_pre = contract_last(normed_low, gate_up_low[:, MODEL_WIDTH:])
    hidden_low = (gate_pre * lax.logistic(gate_pre) * up_pre).astype(jnp.bfloat16)
    return (
        gate_pre,
        up_pre,
        hidden_low,
        jnp.dot(hidden_low, down_low, preferred_element_type=jnp.float32),
    )


def feed_back(normed_low, gate_pre, up_pre, hidden_low, grad_low, gate_up_low, down_low):
    grad_down = contract_rows(grad_low, hidden_low)
    grad_hidden = contract_last(grad_low, down_low)
    sigma_gate = lax.logistic(gate_pre)
    grad_gate = (
        grad_hidden * up_pre * (sigma_gate * (1.0 + gate_pre * (1.0 - sigma_gate)))
    ).astype(jnp.bfloat16)
    grad_up = (grad_hidden * gate_pre * sigma_gate).astype(jnp.bfloat16)
    grad_gate_up = jnp.concatenate(
        [contract_rows(normed_low, grad_gate), contract_rows(normed_low, grad_up)], axis=0
    )
    grad_normed = jnp.dot(
        grad_gate, gate_up_low[:, :MODEL_WIDTH], preferred_element_type=jnp.float32
    )
    grad_normed = grad_normed + jnp.dot(
        grad_up, gate_up_low[:, MODEL_WIDTH:], preferred_element_type=jnp.float32
    )
    return (grad_gate_up, grad_down, grad_normed)


def swap(values, axis, bit):
    size = lax.axis_size(axis)
    return lax.ppermute(values, axis, [(i, i ^ bit) for i in range(size)])


def gather_rows(shard):
    here = lax.axis_index("fsdp")
    count = lax.axis_size("fsdp")
    held = [shard]
    bit = count // 2
    while bit:
        held = held + [swap(part, "fsdp", bit) for part in held]
        bit //= 2
    order = [0]
    bit = count // 2
    while bit:
        order = order + [k ^ bit for k in order]
        bit //= 2
    rows = shard.shape[0]
    full = jnp.zeros((rows * count,) + shard.shape[1:], shard.dtype)
    for part, offset in zip(held, order):
        start = ((here ^ offset) * rows,) + (0,) * (shard.ndim - 1)
        full = lax.dynamic_update_slice(full, part, start)
    return full


def column_groups():
    return min(lax.axis_size("rep"), 8)


def gradient_blocks(gradient, row_axis, steps):
    groups = column_groups()
    count = lax.axis_size("fsdp")
    shape = gradient.shape
    if row_axis == 0:
        cut = gradient.reshape(count, shape[0] // count, groups, shape[1] // groups)
        cut = cut.transpose(2, 0, 1, 3)
    else:
        cut = gradient.reshape(groups, shape[0] // groups, count, shape[1] // count)
        cut = cut.transpose(0, 2, 1, 3)
    names = []
    dims = []
    for axis, size in (("rep", groups), ("fsdp", count)):
        bit = size // 2
        while bit:
            names.append((axis, bit))
            dims.append(2)
            bit //= 2
    cut = cut.reshape(tuple(dims) + cut.shape[2:])
    place = [names.index(step) for step in steps]
    return cut.transpose(tuple(place) + (len(dims), len(dims) + 1))


def reduce_blocks(blocks, steps):
    extra = lax.axis_size("rep") // column_groups()
    total = blocks
    for axis, bit in steps:
        stride = bit * extra if axis == "rep" else bit
        mine = (lax.axis_index(axis) // stride) % 2
        low = total.astype(jnp.bfloat16)
        sent = lax.dynamic_index_in_dim(low, 1 - mine, 0, keepdims=False)
        kept = lax.dynamic_index_in_dim(low, mine, 0, keepdims=False)
        total = kept.astype(jnp.float32) + swap(sent, axis, stride).astype(jnp.float32)
    bit = 1
    while bit < extra:
        total = total + swap(total, "rep", bit)
        bit *= 2
    return total


def own_part(block, dim):
    extra = lax.axis_size("rep") // column_groups()
    width = block.shape[dim] // extra
    return lax.dynamic_slice_in_dim(block, (lax.axis_index("rep") % extra) * width, width, dim)


def sum_everywhere(values):
    for axis in ("fsdp", "rep"):
        bit = 1
        while bit < lax.axis_size(axis):
            values = values + swap(values, axis, bit)
            bit *= 2
    return values


def on_device(
    tokens,
    segments,
    cotangent,
    projection_weight,
    out_weight,
    gate_up_weight,
    down_weight,
    norm_gains,
    projection_bias,
    projection_first_moment,
    out_first,
    gate_up_first,
    down_first,
    gains_first,
    bias_first_moment,
    projection_second_moment,
    out_second,
    gate_up_second,
    down_second,
    gains_second,
    bias_second_moment,
):
    count_of_rows = tokens.shape[0]
    query_span_width = QUERY_HEADS * HEAD_SIZE
    key_span_width = KEY_VALUE_HEADS * HEAD_SIZE
    head_cluster = QUERY_HEADS // KEY_VALUE_HEADS
    qkv_full, out_full, gains_full, biases_full = (
        gather_rows(projection_weight.astype(jnp.bfloat16)),
        gather_rows(out_weight.astype(jnp.bfloat16)),
        gather_rows(norm_gains.astype(jnp.bfloat16)),
        gather_rows(projection_bias.astype(jnp.bfloat16)),
    )
    gate_up_full, down_full = (
        gather_rows(gate_up_weight.astype(jnp.bfloat16)),
        gather_rows(down_weight.astype(jnp.bfloat16)),
    )
    order_a = (("fsdp", 1), ("fsdp", 2), ("rep", 1), ("rep", 2), ("rep", 4))
    order_b = (("fsdp", 1), ("rep", 1), ("fsdp", 2), ("rep", 2), ("rep", 4))
    gain_one = gains_full[:MODEL_WIDTH].astype(jnp.float32)
    gain_two = gains_full[MODEL_WIDTH:].astype(jnp.float32)
    cosine_table, sine_values, allowed = rope_tables(segments)
    inputs = tokens.astype(jnp.float32)
    normed, inverse_one = norm_forward(inputs, gain_one)
    normed_low = normed.astype(jnp.bfloat16)
    projected_rows = jnp.dot(
        normed_low, qkv_full, preferred_element_type=jnp.float32
    ) + biases_full.astype(jnp.float32)
    query_reduced = rotate_pairs(
        projected_rows[:, :query_span_width].reshape(count_of_rows, QUERY_HEADS, HEAD_SIZE),
        cosine_table,
        sine_values,
    ).astype(jnp.bfloat16)
    query_reduced = query_reduced.reshape(count_of_rows, KEY_VALUE_HEADS, head_cluster, HEAD_SIZE)
    key_reduced = rotate_pairs(
        projected_rows[:, query_span_width : query_span_width + key_span_width].reshape(
            count_of_rows, KEY_VALUE_HEADS, HEAD_SIZE
        ),
        cosine_table,
        sine_values,
    ).astype(jnp.bfloat16)
    value_reduced = (
        projected_rows[:, query_span_width + key_span_width :]
        .reshape(count_of_rows, KEY_VALUE_HEADS, HEAD_SIZE)
        .astype(jnp.bfloat16)
    )
    scores = attention_scores(query_reduced, key_reduced, allowed)
    row_peak = jnp.max(scores, axis=-1, keepdims=True)
    lifted = jnp.exp(scores - row_peak)
    row_total = jnp.sum(lifted, axis=-1, keepdims=True)
    attention_low = (lifted / row_total).astype(jnp.bfloat16)
    mixed_low = jnp.einsum(
        "kgqs,skd->qkgd", attention_low, value_reduced, preferred_element_type=jnp.float32
    )
    mixed_low = mixed_low.reshape(count_of_rows, query_span_width).astype(jnp.bfloat16)
    middle = inputs + jnp.dot(mixed_low, out_full, preferred_element_type=jnp.float32)
    normed_two, inverse_two = norm_forward(middle, gain_two)
    normed_two_low = normed_two.astype(jnp.bfloat16)
    gate_pre, up_pre, hidden_low, mlp_out = feed_forward(normed_two_low, gate_up_full, down_full)
    grad_gate_up, grad_down, grad_normed_two = feed_back(
        normed_two_low, gate_pre, up_pre, hidden_low, cotangent, gate_up_full, down_full
    )
    grad_gate_up = reduce_blocks(
        gradient_blocks(grad_gate_up.astype(jnp.bfloat16), 1, order_a), order_a
    )
    grad_down = reduce_blocks(gradient_blocks(grad_down.astype(jnp.bfloat16), 1, order_b), order_b)
    grad_gate_up = own_part(grad_gate_up, 0).T
    grad_down = own_part(grad_down, 0).T
    output = (middle + mlp_out).astype(jnp.bfloat16)
    grad_middle_norm, grad_gain_two = norm_backward(middle, inverse_two, gain_two, grad_normed_two)
    grad_middle = cotangent.astype(jnp.float32) + grad_middle_norm
    grad_branch_low = grad_middle.astype(jnp.bfloat16)
    grad_out = contract_rows(mixed_low, grad_branch_low)
    grad_mixed_low = (
        contract_last(grad_branch_low, out_full)
        .astype(jnp.bfloat16)
        .reshape(count_of_rows, KEY_VALUE_HEADS, head_cluster, HEAD_SIZE)
    )
    scores = attention_scores(query_reduced, key_reduced, allowed)
    attention = jnp.exp(scores - row_peak) / row_total
    grad_attention = jnp.einsum(
        "qkgd,skd->kgqs", grad_mixed_low, value_reduced, preferred_element_type=jnp.float32
    )
    grad_scores = (
        attention * (grad_attention - jnp.sum(attention * grad_attention, axis=-1, keepdims=True))
    ).astype(jnp.bfloat16)
    grad_value = jnp.einsum(
        "kgqs,qkgd->skd",
        attention.astype(jnp.bfloat16),
        grad_mixed_low,
        preferred_element_type=jnp.float32,
    )
    grad_query = jnp.einsum(
        "kgqs,skd->qkgd", grad_scores, key_reduced, preferred_element_type=jnp.float32
    ) * HEAD_SIZE ** (-0.5)
    grad_key = jnp.einsum(
        "kgqs,qkgd->skd", grad_scores, query_reduced, preferred_element_type=jnp.float32
    ) * HEAD_SIZE ** (-0.5)
    grad_query = rotate_back(
        grad_query.reshape(count_of_rows, QUERY_HEADS, HEAD_SIZE), cosine_table, sine_values
    ).reshape(count_of_rows, query_span_width)
    grad_key = rotate_back(grad_key, cosine_table, sine_values).reshape(
        count_of_rows, key_span_width
    )
    grad_projected_low = jnp.concatenate(
        [grad_query, grad_key, grad_value.reshape(count_of_rows, key_span_width)], axis=1
    ).astype(jnp.bfloat16)
    grad_qkv = contract_rows(normed_low, grad_projected_low)
    grad_bias = jnp.sum(grad_projected_low.astype(jnp.float32), axis=0)
    grad_normed_one = contract_last(grad_projected_low, qkv_full)
    grad_inputs_norm, grad_gain_one = norm_backward(inputs, inverse_one, gain_one, grad_normed_one)
    tokens_grad = (grad_middle + grad_inputs_norm).astype(jnp.bfloat16)
    grad_gains = jnp.concatenate([grad_gain_one, grad_gain_two])
    grad_out = reduce_blocks(gradient_blocks(grad_out.astype(jnp.bfloat16), 0, order_b), order_b)
    grad_qkv = reduce_blocks(gradient_blocks(grad_qkv.astype(jnp.bfloat16), 0, order_a), order_a)
    grad_out = own_part(grad_out, 1)
    grad_qkv = own_part(grad_qkv, 1)
    small = jnp.concatenate([grad_gains, grad_bias]).astype(jnp.bfloat16).astype(jnp.float32)
    small = sum_everywhere(small)
    group_place = lax.axis_index("fsdp")
    gains_size = norm_gains.shape[0]
    bias_size = projection_bias.shape[0]
    grad_gains = lax.dynamic_slice_in_dim(small, group_place * gains_size, gains_size, 0)
    grad_bias = lax.dynamic_slice_in_dim(
        small, 2 * MODEL_WIDTH + group_place * bias_size, bias_size, 0
    )
    replica = lax.axis_index("rep")
    step_rates = learn_rates()
    qkv_new = adam_update(
        owned_columns(projection_weight, grad_qkv, replica),
        projection_first_moment,
        projection_second_moment,
        grad_qkv,
        step_rates[0],
    )
    out_new = adam_update(
        owned_columns(out_weight, grad_out, replica), out_first, out_second, grad_out, step_rates[1]
    )
    gate_up_new = adam_update(
        owned_columns(gate_up_weight, grad_gate_up, replica),
        gate_up_first,
        gate_up_second,
        grad_gate_up,
        step_rates[2],
    )
    down_new = adam_update(
        owned_columns(down_weight, grad_down, replica),
        down_first,
        down_second,
        grad_down,
        step_rates[3],
    )
    gains_new = adam_update(norm_gains, gains_first, gains_second, grad_gains, step_rates[4])
    biases_new = adam_update(
        projection_bias, bias_first_moment, bias_second_moment, grad_bias, step_rates[5]
    )
    return (
        output,
        tokens_grad,
        qkv_new[0],
        qkv_new[1],
        qkv_new[2],
        out_new[0],
        out_new[1],
        out_new[2],
        gate_up_new[0],
        gate_up_new[1],
        gate_up_new[2],
        down_new[0],
        down_new[1],
        down_new[2],
        gains_new[0],
        gains_new[1],
        gains_new[2],
        biases_new[0],
        biases_new[1],
        biases_new[2],
    )


def solution(mesh):
    in_specs = (
        P(("rep", "fsdp"), None),
        P(("rep", "fsdp")),
        P(("rep", "fsdp"), None),
        P("fsdp", None),
        P("fsdp", None),
        P("fsdp", None),
        P("fsdp", None),
        P("fsdp"),
        P("fsdp"),
        P("fsdp", "rep"),
        P("fsdp", "rep"),
        P("fsdp", "rep"),
        P("fsdp", "rep"),
        P("fsdp"),
        P("fsdp"),
        P("fsdp", "rep"),
        P("fsdp", "rep"),
        P("fsdp", "rep"),
        P("fsdp", "rep"),
        P("fsdp"),
        P("fsdp"),
    )
    out_specs = (
        P(("rep", "fsdp"), None),
        P(("rep", "fsdp"), None),
        P("fsdp", "rep"),
        P("fsdp", "rep"),
        P("fsdp", "rep"),
        P("fsdp", "rep"),
        P("fsdp", "rep"),
        P("fsdp", "rep"),
        P("fsdp", "rep"),
        P("fsdp", "rep"),
        P("fsdp", "rep"),
        P("fsdp", "rep"),
        P("fsdp", "rep"),
        P("fsdp", "rep"),
        P("fsdp"),
        P("fsdp"),
        P("fsdp"),
        P("fsdp"),
        P("fsdp"),
        P("fsdp"),
    )
    return jax.shard_map(
        on_device, mesh=mesh, in_specs=in_specs, out_specs=out_specs, check_vma=False
    )
```

```python
import functools
import math

import jax
import jax.numpy as jnp
from jax import lax
from jax.experimental import pallas as pl
from jax.experimental.pallas import tpu as pltpu
from jax.sharding import PartitionSpec as P

MODEL_WIDTH = 576
QUERY_HEADS = 9
KEY_VALUE_HEADS = 3
HEAD_SIZE = 64
FF = 1536
STEP = 10

norm_eps = 1e-05
rope_base = 100000.0
beta_one = 0.9
beta_two = 0.95
adam_eps = 1e-08
decay_rate = 0.1

LANES = 128
QKV_WIDTH = (QUERY_HEADS + 2 * KEY_VALUE_HEADS) * HEAD_SIZE
CLUSTER = QUERY_HEADS // KEY_VALUE_HEADS
SMALL_ROWS = 32
ROW_BLOCK = 256
bf16 = jnp.bfloat16
f32 = jnp.float32


def learn_rates():
    out_fan = max(QUERY_HEADS * HEAD_SIZE // 16, 1)
    return (MODEL_WIDTH ** (-0.5), out_fan ** (-0.5), MODEL_WIDTH ** (-0.5), FF ** (-0.5), 0.5, 0.5)


def adam_update(weight, first_moment, second_moment, gradient, step_rate):
    first_new = beta_one * first_moment + (1.0 - beta_one) * gradient
    second_new = beta_two * second_moment + (1.0 - beta_two) * gradient * gradient
    first_fix = 1.0 - beta_one**STEP
    second_fix = 1.0 - beta_two**STEP
    direction = first_new / first_fix / (jnp.sqrt(second_new / second_fix) + adam_eps)
    return (first_new, second_new, weight - step_rate * (direction + decay_rate * weight))


def dot_plain(left, right):
    return lax.dot_general(left, right, (((1,), (0,)), ((), ())), preferred_element_type=f32)


def dot_last(left, right):
    return lax.dot_general(left, right, (((1,), (1,)), ((), ())), preferred_element_type=f32)


def dot_first(left, right):
    return lax.dot_general(left, right, (((0,), (0,)), ((), ())), preferred_element_type=f32)


def kernel_call(body, outs, name, flops, scratch=(), vmem=40):
    def call(scalars, *arrays):
        moved = sum(a.size * a.dtype.itemsize for a in arrays)
        moved += sum(o.size * o.dtype.itemsize for o in outs)
        return pl.pallas_call(
            body,
            out_shape=tuple(outs),
            in_specs=[pl.BlockSpec(memory_space=pltpu.SMEM)]
            + [pl.BlockSpec(memory_space=pltpu.VMEM)] * len(arrays),
            out_specs=tuple(pl.BlockSpec(memory_space=pltpu.VMEM) for _ in outs),
            scratch_shapes=list(scratch),
            name=name,
            compiler_params=pltpu.CompilerParams(vmem_limit_bytes=vmem * 2**20),
            cost_estimate=pl.CostEstimate(
                flops=int(flops), bytes_accessed=int(moved), transcendentals=0
            ),
        )(scalars, *arrays)

    return call


def shaped(shape, dtype):
    return jax.ShapeDtypeStruct(tuple(shape), dtype)


def lane_index(shape):
    return lax.broadcasted_iota(jnp.int32, shape, len(shape) - 1)


def lower_half(shape):
    return lane_index(shape) < HEAD_SIZE


def swap_pairs(block):
    first = (lane_index(block.shape) & (HEAD_SIZE // 2)) == 0
    ahead = pltpu.roll(block, LANES - HEAD_SIZE // 2, 1)
    behind = pltpu.roll(block, HEAD_SIZE // 2, 1)
    return jnp.where(first, ahead, behind)


def both_halves(block, upper):
    other = pltpu.roll(block, HEAD_SIZE, 1)
    low = lower_half(block.shape)
    return jnp.where(low, other, block) if upper else jnp.where(low, block, other)


def cut_lanes(blocks, start, width):
    at, offset = divmod(start, LANES)
    lane = lane_index(blocks[0].shape)
    part = blocks[at]
    if offset:
        part = pltpu.roll(part, LANES - offset, 1)
        if offset + width > LANES:
            after = pltpu.roll(blocks[at + 1], LANES - offset, 1)
            part = jnp.where(lane < LANES - offset, part, after)
    if width < LANES:
        part = jnp.where(lane < width, part, 0.0)
    return part


def lane_blocks(values):
    width = values.shape[1]
    full = width // LANES
    blocks = [values[:, i * LANES : (i + 1) * LANES] for i in range(full)]
    if width % LANES:
        rest = values[:, full * LANES :]
        fill = jnp.zeros((values.shape[0], LANES - width % LANES), values.dtype)
        blocks.append(jnp.concatenate([rest, fill], axis=1))
    return blocks


def block_place(block, mine, groups):
    away = mine ^ block
    place = 0
    bit = 1
    while bit < groups:
        place = place * 2 + jnp.where((away & bit) == 0, 0, 1)
        bit *= 2
    return place


def pack_kernel(where_ref, qkv_ref, out_ref, gains_ref, bias_ref, pack_ref, low_out_ref):
    rows = qkv_ref.shape[0]
    pack_ref[:rows, :QKV_WIDTH] = qkv_ref[...].astype(bf16)
    pack_ref[:rows, QKV_WIDTH:] = jnp.zeros((rows, pack_ref.shape[1] - QKV_WIDTH), bf16)
    spare = pack_ref.shape[0] - rows
    extra = jnp.concatenate(lane_blocks(bias_ref[...]) + lane_blocks(gains_ref[...]), axis=1)
    line = jnp.concatenate(
        [extra, jnp.zeros((1, pack_ref.shape[1] - extra.shape[1]), f32)], axis=1
    )
    pack_ref[rows:, :] = jnp.broadcast_to(line, (spare, line.shape[1])).astype(bf16)
    low_out_ref[...] = out_ref[...].astype(bf16)


def tables_kernel(where_ref, column_ref, row_ref, e_ref, cos_ref, sin_ref, mask_ref, e_turned_ref):
    tokens = column_ref.shape[0]
    query = lax.broadcasted_iota(jnp.int32, (tokens, tokens), 0)
    key = lax.broadcasted_iota(jnp.int32, (tokens, tokens), 1)
    same = column_ref[...] == row_ref[...]
    earlier = jnp.sum(jnp.where(same & (key < query), 1.0, 0.0), axis=1, keepdims=True)
    mask_ref[...] = jnp.where(same & (key <= query), 0.0, -1e30)
    lane = lane_index((tokens, LANES))
    exponent = (lane & (HEAD_SIZE // 2 - 1)).astype(f32) * (2.0 / HEAD_SIZE)
    frequency = jnp.exp(exponent * (-math.log(rope_base)))
    angles = earlier * frequency
    cos_ref[...] = jnp.cos(angles)
    sine = jnp.sin(angles)
    sin_ref[...] = jnp.where((lane & (HEAD_SIZE // 2)) == 0, -sine, sine)
    e_turned_ref[...] = e_ref[...].astype(f32).T.astype(bf16)


def forward_kernel(
    where_ref, tokens_ref, cos_ref, sin_ref, mask_ref,
    pack0, pack1, pack2, pack3, out0, out1, out2, out3,
    a_ref, q_ref, k_ref, v_ref, e0_ref, e1_ref, e2_ref, inv_ref, o_ref, h_ref,
    a2_ref, a2_shift_ref, a2_turned_ref, weight_ref, out_weight_ref, gains_ref,
):
    me = where_ref[0]
    tokens = tokens_ref.shape[0]
    shard_rows = out0.shape[0]
    packs = (pack0, pack1, pack2, pack3)
    outs = (out0, out1, out2, out3)
    lines = []
    for j in range(4):
        start = pl.multiple_of((me ^ j) * shard_rows, 16)
        weight_ref[pl.ds(start, shard_rows), :] = packs[j][:shard_rows, :]
        out_weight_ref[pl.ds(start, shard_rows), :] = outs[j][...]
        lines.append(packs[j][shard_rows:, :].astype(f32)[:1, :])
    bias_wide = lane_index((1, LANES)) * 0.0
    ordered = []
    for s in range(4):
        line = jnp.where((me ^ s) == 0, lines[0], 0.0)
        for j in range(1, 4):
            line = jnp.where((me ^ s) == j, lines[j], line)
        ordered.append(line)
    bias_blocks = [bias_wide for _ in range(weight_ref.shape[1] // LANES)]
    gain_blocks = [[bias_wide for _ in range(5)] for _ in range(2)]
    lane = lane_index((1, LANES))

    def put(blocks, source, width, start):
        done = 0
        while done < width:
            at, offset = divmod(start + done, LANES)
            count = min(LANES - offset, width - done)
            from_at, from_offset = divmod(done, LANES)
            count = min(count, LANES - from_offset)
            turn = (offset - from_offset) % LANES
            part = source[from_at]
            if turn:
                part = pltpu.roll(part, turn, 1)
            blocks[at] = jnp.where((lane >= offset) & (lane < offset + count), part, blocks[at])
            done += count

    bias_each = QKV_WIDTH // 4
    gain_each = 2 * MODEL_WIDTH // 4
    bias_lanes = -(-bias_each // LANES) * LANES
    for s in range(4):
        pieces = [ordered[s][:, i * LANES : (i + 1) * LANES] for i in range(8)]
        put(bias_blocks, pieces, bias_each, s * bias_each)
        put(gain_blocks[s // 2], pieces[bias_lanes // LANES :], gain_each, (s % 2) * gain_each)
    gains = [jnp.concatenate(blocks, axis=1) for blocks in gain_blocks]
    for i in range(2):
        gains_ref[i : i + 1, :] = gains[i]
    bias = jnp.concatenate(bias_blocks, axis=1)

    x = tokens_ref[...].astype(f32)
    inverse = lax.rsqrt(jnp.mean(x * x, axis=1, keepdims=True) + norm_eps)
    a = (x * inverse * gains[0][:, :MODEL_WIDTH]).astype(bf16)
    a_ref[...] = a
    p = dot_plain(a, weight_ref[...]) + bias
    cosine, sine = cos_ref[...], sin_ref[...]
    blocks = [p[:, i * LANES : (i + 1) * LANES] for i in range(8)]
    for i in range(6):
        blocks[i] = blocks[i] * cosine + swap_pairs(blocks[i]) * sine
    low = lower_half((tokens, LANES))
    for i in range(5):
        scaled = blocks[i] * HEAD_SIZE ** (-0.5)
        if i == 4:
            scaled = jnp.where(low, scaled, 0.0)
        q_ref[:, i * LANES : (i + 1) * LANES] = scaled.astype(bf16)
    keys = [both_halves(blocks[4], True), both_halves(blocks[5], False), both_halves(blocks[5], True)]
    values = [both_halves(blocks[6], False), both_halves(blocks[6], True), both_halves(blocks[7], False)]
    for g in range(KEY_VALUE_HEADS):
        k_ref[:, g * LANES : (g + 1) * LANES] = keys[g].astype(bf16)
        v_ref[:, g * LANES : (g + 1) * LANES] = values[g].astype(bf16)

    e_refs = (e0_ref, e1_ref, e2_ref)
    step = ROW_BLOCK
    low = lower_half((step, LANES))
    for at in range(tokens // step):
        rows = slice(at * step, (at + 1) * step)
        seen = (at + 1) * step
        mixed = []
        inverses = []
        for g in range(KEY_VALUE_HEADS):
            stack = head_stack(q_ref, rows, g)
            scores = dot_last(stack, k_ref[:seen, g * LANES : (g + 1) * LANES])
            scores = scores.reshape(CLUSTER, step, seen) + mask_ref[rows, :seen][None]
            lifted = jnp.exp(scores - jnp.max(scores, axis=2, keepdims=True))
            total = jnp.sum(lifted, axis=2, keepdims=True)
            kept = lifted.astype(bf16)
            e_refs[g][:, rows, :seen] = kept
            gathered = dot_plain(
                kept.reshape(CLUSTER * step, seen), v_ref[:seen, g * LANES : (g + 1) * LANES]
            ).reshape(CLUSTER, step, LANES)
            inverse_total = jnp.broadcast_to(1.0 / total, gathered.shape)
            gathered = gathered * inverse_total
            for t in range(CLUSTER):
                mixed.append(gathered[t])
                inverses.append(inverse_total[t])
        for i in range(5):
            second = mixed[2 * i + 1] if 2 * i + 1 < QUERY_HEADS else 0.0
            part = jnp.where(low, mixed[2 * i], second)
            o_ref[rows, i * LANES : (i + 1) * LANES] = part.astype(bf16)
            second = inverses[2 * i + 1] if 2 * i + 1 < QUERY_HEADS else 0.0
            inv_ref[rows, i * LANES : (i + 1) * LANES] = jnp.where(low, inverses[2 * i], second)

    h = x + dot_plain(o_ref[:, :MODEL_WIDTH], out_weight_ref[...])
    h_ref[...] = h
    inverse = lax.rsqrt(jnp.mean(h * h, axis=1, keepdims=True) + norm_eps)
    a2 = h * inverse * gains[1][:, :MODEL_WIDTH]
    a2_ref[...] = a2.astype(bf16)
    a2_blocks = lane_blocks(a2)
    low = lower_half((tokens, LANES))
    before = jnp.zeros((tokens, LANES), f32)
    for i in range(5):
        part = jnp.where(low, pltpu.roll(before, HEAD_SIZE, 1), pltpu.roll(a2_blocks[i], HEAD_SIZE, 1))
        a2_shift_ref[:, i * LANES : (i + 1) * LANES] = part.astype(bf16)
        before = a2_blocks[i]
    a2_turned_ref[...] = a2.T.astype(bf16)


def head_stack(ref, rows, g):
    parts = []
    for t in range(CLUSTER):
        head = g * CLUSTER + t
        block = ref[rows, (head // 2) * LANES : (head // 2 + 1) * LANES]
        low = lower_half(block.shape)
        keep = low if head % 2 == 0 else jnp.logical_not(low)
        parts.append(jnp.where(keep, block, jnp.zeros_like(block)))
    return jnp.concatenate(parts, axis=0)


def feed_kernel(groups, chunks, first, last, *refs):
    refs = list(refs)
    where_ref = refs.pop(0)
    a2_ref, a2_shift_ref, a2_turned_ref, e_ref, e_turned_ref, base_ref = refs[:6]
    refs = refs[6:]
    if first:
        gate_in = shift_in = None
    else:
        gate_in, shift_in = refs[:2]
        refs = refs[2:]
    gate_ups = refs[: len(chunks)]
    downs = refs[len(chunks) : 2 * len(chunks)]
    refs = refs[2 * len(chunks) :]
    total_ref, gate_acc, shift_acc = refs[:3]
    refs = refs[3:]
    mine = where_ref[1]
    total = base_ref[...]
    for c in range(len(chunks)):
        gate_up, down = gate_ups[c], downs[c]
        gate_weights = gate_up[:, :MODEL_WIDTH]
        up_weights = gate_up[:, MODEL_WIDTH - HEAD_SIZE :]
        gate = dot_last(a2_ref[...], gate_weights)
        up = dot_last(a2_shift_ref[...], up_weights)
        sigma = 1.0 / (1.0 + jnp.exp(-gate))
        active = gate * sigma
        hidden = (active * up).astype(bf16)
        total = total + dot_plain(hidden, down[...])
        grad_hidden = dot_last(e_ref[...], down[...])
        grad_gate = (grad_hidden * up * (sigma * (1.0 + gate * (1.0 - sigma)))).astype(bf16)
        grad_up = (grad_hidden * active).astype(bf16)
        grad_gate_up_ref, grad_down_ref = refs[2 * c], refs[2 * c + 1]
        width = grad_gate_up_ref.shape[1]
        half = groups // 2
        for turned, offset in ((dot_plain(a2_turned_ref[...], grad_gate), 0),
                               (dot_plain(a2_turned_ref[...], grad_up), half)):
            for b in range(half):
                grad_gate_up_ref[block_place(b + offset, mine, groups)] = turned[
                    b * width : (b + 1) * width
                ].astype(bf16)
        turned = dot_plain(e_turned_ref[...], hidden)
        width = grad_down_ref.shape[1]
        for b in range(groups):
            grad_down_ref[block_place(b, mine, groups)] = turned[
                b * width : (b + 1) * width
            ].astype(bf16)
        gate_part = dot_plain(grad_gate, gate_weights)
        shift_part = dot_plain(grad_up, up_weights)
        if c == 0 and first:
            gate_acc[...] = gate_part
            shift_acc[...] = shift_part
        elif c == 0:
            gate_acc[...] = gate_in[...] + gate_part
            shift_acc[...] = shift_in[...] + shift_part
        else:
            gate_acc[...] = gate_acc[...] + gate_part
            shift_acc[...] = shift_acc[...] + shift_part
    total_ref[...] = total.astype(total_ref.dtype)


def middle_kernel(
    groups, where_ref, gate_acc, shift_acc, h_ref, e_ref, gains_ref, o_ref, inv_ref, out_weight_ref,
    dh_ref, dol_ref, small_ref, grad0, grad1, grad2, grad3, held_ref,
):
    me, mine = where_ref[0], where_ref[1]
    tokens = h_ref.shape[0]
    gain = gains_ref[1:2, :MODEL_WIDTH]
    h = h_ref[...]
    low = lower_half((tokens, LANES))
    shifted = [shift_acc[:, i * LANES : (i + 1) * LANES] for i in range(5)]
    parts = []
    for i in range(5):
        part = pltpu.roll(shifted[i], HEAD_SIZE, 1)
        after = pltpu.roll(shifted[i + 1], HEAD_SIZE, 1) if i < 4 else 0.0
        parts.append(jnp.where(low, part, after))
    da2 = gate_acc[...] + jnp.concatenate(parts, axis=1)[:, :MODEL_WIDTH]
    inverse = lax.rsqrt(jnp.mean(h * h, axis=1, keepdims=True) + norm_eps)
    weighted = da2 * gain
    inner = jnp.mean(weighted * h, axis=1, keepdims=True)
    dh = e_ref[...].astype(f32) + inverse * weighted - h * (inverse * inverse * inverse) * inner
    dh_ref[...] = dh
    small_ref[...] = jnp.sum(da2 * h * inverse, axis=0, keepdims=True)
    dhl = dh.astype(bf16)
    spread = dhl.astype(f32)
    blocks = lane_blocks(spread)
    width = MODEL_WIDTH // groups
    chosen = jnp.concatenate(
        [cut_lanes(blocks, b * width, width).astype(bf16) for b in range(groups)], axis=1
    )
    held_ref[...] = dot_first(o_ref[:, :MODEL_WIDTH], chosen).astype(bf16)
    rows = grad0.shape[1]
    for j, grad in enumerate((grad0, grad1, grad2, grad3)):
        start = pl.multiple_of((me ^ j) * rows, 16)
        for b in range(groups):
            grad[block_place(b, mine, groups)] = held_ref[
                pl.ds(start, rows), b * LANES : (b + 1) * LANES
            ]
    dol = dot_last(dhl, out_weight_ref[...])
    dol_blocks = lane_blocks(dol.astype(bf16).astype(f32))
    for i in range(5):
        lanes = slice(i * LANES, (i + 1) * LANES)
        dol_ref[:, lanes] = (dol_blocks[i] * inv_ref[:, lanes]).astype(bf16)


def attention_back_kernel(g, where_ref, q_ref, k_ref, v_ref, lifted_ref, o_ref, dol_ref, dq_ref, dk_ref, dv_ref):
    tokens = q_ref.shape[0]
    step = ROW_BLOCK
    lanes = slice(g * LANES, (g + 1) * LANES)
    dk = None
    dv = None
    for at in reversed(range(tokens // step)):
        rows = slice(at * step, (at + 1) * step)
        seen = (at + 1) * step
        q_stack = head_stack(q_ref, rows, g)
        o_stack = head_stack(o_ref, rows, g)
        dol_stack = head_stack(dol_ref, rows, g)
        lifted = lifted_ref[:, rows, :seen].reshape(CLUSTER * step, seen)
        inner = jnp.sum(o_stack.astype(f32) * dol_stack.astype(f32), axis=1, keepdims=True)
        grad = dot_last(dol_stack, v_ref[:seen, lanes])
        dsl = (lifted.astype(f32) * (grad - inner)).astype(bf16)
        dq = dot_plain(dsl, k_ref[:seen, lanes]) * HEAD_SIZE ** (-0.5)
        dq_ref[:, rows, :] = dq.reshape(CLUSTER, step, LANES)
        dk_part = dot_first(q_stack, dsl)
        dv_part = dot_first(dol_stack, lifted)
        if dk is None:
            dk, dv = dk_part, dv_part
        else:
            dk = jnp.concatenate([dk[:, :seen] + dk_part, dk[:, seen:]], axis=1)
            dv = jnp.concatenate([dv[:, :seen] + dv_part, dv[:, seen:]], axis=1)
    dk = dk.T
    dv = dv.T
    dk_ref[...] = dk + pltpu.roll(dk, HEAD_SIZE, 1)
    dv_ref[...] = dv + pltpu.roll(dv, HEAD_SIZE, 1)


def last_kernel(
    groups, where_ref, dq0, dq1, dq2, dk0, dk1, dk2, dv0, dv1, dv2, cos_ref, sin_ref,
    a_ref, tokens_ref, dh_ref, weight_ref, gains_ref, gain_two_ref,
    sent_ref, kept_ref, tokens_grad_ref, held_ref,
):
    me, mine = where_ref[0], where_ref[1]
    tokens = tokens_ref.shape[0]
    low = lower_half((tokens, LANES))
    heads = [ref[t] for ref in (dq0, dq1, dq2) for t in range(CLUSTER)]
    blocks = [jnp.where(low, heads[2 * i], heads[2 * i + 1]) for i in range(4)]
    blocks.append(jnp.where(low, heads[8], dk0[...]))
    blocks.append(jnp.where(low, dk1[...], dk2[...]))
    cosine, sine = cos_ref[...], sin_ref[...]
    blocks = [block * cosine - swap_pairs(block) * sine for block in blocks]
    blocks.append(jnp.where(low, dv0[...], dv1[...]))
    blocks.append(jnp.where(low, dv2[...], 0.0))
    low_blocks = [block.astype(bf16) for block in blocks]
    blocks = [block.astype(f32) for block in low_blocks]
    dpl = jnp.concatenate(low_blocks, axis=1)
    width = QKV_WIDTH // groups
    chosen = jnp.concatenate(
        [cut_lanes(blocks, b * width, width).astype(bf16) for b in range(groups)], axis=1
    )
    held_ref[...] = dot_first(a_ref[...], chosen).astype(bf16)
    rows = held_ref.shape[0] // 4
    for j in range(4):
        start = pl.multiple_of((me ^ j) * rows, 16)
        target = sent_ref if j % 2 else kept_ref
        for b in range(groups):
            to = pl.multiple_of((block_place(b, mine, groups) + (j // 2) * groups) * rows, 16)
            target[pl.ds(to, rows), :] = held_ref[pl.ds(start, rows), b * LANES : (b + 1) * LANES]

    bias_blocks = [jnp.sum(block, axis=0, keepdims=True) for block in blocks]
    x = tokens_ref[...].astype(f32)
    inverse = lax.rsqrt(jnp.mean(x * x, axis=1, keepdims=True) + norm_eps)
    da = dot_last(dpl, weight_ref[...])
    gain_one_blocks = lane_blocks(jnp.sum(da * x * inverse, axis=0, keepdims=True))
    gain_two_blocks = lane_blocks(gain_two_ref[...])
    weighted = da * gains_ref[0:1, :MODEL_WIDTH]
    inner = jnp.mean(weighted * x, axis=1, keepdims=True)
    tokens_grad_ref[...] = (
        dh_ref[...] + inverse * weighted - x * (inverse * inverse * inverse) * inner
    ).astype(bf16)

    gain_each = 2 * MODEL_WIDTH // 4
    bias_each = QKV_WIDTH // 4
    lines = []
    for s in range(4):
        source = gain_one_blocks if s < 2 else gain_two_blocks
        count = 0
        for t in range(0, gain_each, LANES):
            lines.append(cut_lanes(source, (s % 2) * gain_each + t, min(LANES, gain_each - t)))
            count += 1
        for t in range(0, bias_each, LANES):
            lines.append(cut_lanes(bias_blocks, s * bias_each + t, min(LANES, bias_each - t)))
            count += 1
        lines += [jnp.zeros((1, LANES), f32)] * (SMALL_ROWS // 4 - count)
    small = jnp.concatenate(lines, axis=0).astype(bf16)
    sent_ref[2 * groups * rows :, :] = small
    kept_ref[2 * groups * rows :, :] = small


def halve_kernel(where_ref, kept_ref, came_ref, sent_ref, left_ref):
    part = left_ref.shape[0] - SMALL_ROWS
    total = kept_ref[...].astype(f32) + came_ref[...].astype(f32)
    total = total.astype(bf16)
    left_ref[:part, :] = total[:part]
    left_ref[part:, :] = total[2 * part :]
    sent_ref[...] = total[part:]


def weight_step_kernel(step_rate, turned, parts, where_ref, *refs):
    gradient = refs[0][...].astype(f32)
    for ref in refs[1:parts]:
        gradient = gradient + ref[...].astype(f32)
    if turned:
        gradient = gradient.T
    weight_ref, first_ref, second_ref = refs[parts : parts + 3]
    gradient = gradient[:, : weight_ref.shape[1]]
    new = adam_update(weight_ref[...], first_ref[...], second_ref[...], gradient, step_rate)
    for ref, value in zip(refs[parts + 3 :], new):
        ref[...] = value


def final_kernel(step_rates, parts, where_ref, *refs):
    total = refs[0][...].astype(f32)
    for ref in refs[1:parts]:
        total = total + ref[...].astype(f32)
    rows = total.shape[0] - SMALL_ROWS
    refs = refs[parts:]
    ins, outs = refs[:9], refs[9:]
    gradient = total[:rows, : ins[0].shape[1]]
    new = adam_update(ins[0][...], ins[1][...], ins[2][...], gradient, step_rates[0])
    for i in range(3):
        outs[i][...] = new[i]
    me = where_ref[0]
    each = SMALL_ROWS // 4
    mine = total[rows : rows + each]
    for s in range(1, 4):
        mine = jnp.where(me == s, total[rows + s * each : rows + (s + 1) * each], mine)
    line = 0
    for k, rate in ((3, step_rates[1]), (6, step_rates[2])):
        width = ins[k].shape[1]
        count = -(-width // LANES)
        wide = jnp.concatenate([mine[line + t : line + t + 1, :] for t in range(count)], axis=1)
        line += count
        new = adam_update(ins[k][...], ins[k + 1][...], ins[k + 2][...], wide[:, :width], rate)
        for i in range(3):
            outs[k + i][...] = new[i]


def swap(values, axis, bit):
    size = lax.axis_size(axis)
    return lax.ppermute(values, axis, [(i, i ^ bit) for i in range(size)])


def gather_held(shard):
    across = swap(shard, "fsdp", 2)
    return [shard, swap(shard, "fsdp", 1), across, swap(across, "fsdp", 1)]


def add_low(left, right):
    return (left.astype(f32) + right.astype(f32)).astype(bf16)


def halves(values):
    half = values.shape[0] // 2
    return values[:half], values[half:]


def fold_replicas(kept, extra, bits):
    came = None
    for bit in bits:
        if came is not None:
            kept = add_low(kept, came)
        kept, sent = halves(kept)
        came = swap(sent, "rep", bit * extra)
    return kept, came


def group_first(chunks, extra, groups):
    zero = add_low(chunks[0], swap(chunks[1], "fsdp", 1))
    two = add_low(chunks[2], swap(chunks[3], "fsdp", 1))
    total = add_low(zero, swap(two, "fsdp", 2))
    return fold_replicas(total, extra, [1 << i for i in range(groups.bit_length() - 1)])


def replica_first(chunks, extra, groups):
    zero = add_low(chunks[0], swap(chunks[1], "fsdp", 1))
    two = add_low(chunks[2], swap(chunks[3], "fsdp", 1))
    two_kept, two_sent = halves(two)
    zero_kept, zero_sent = halves(zero)
    two = add_low(two_kept, swap(two_sent, "rep", extra))
    zero = add_low(zero_kept, swap(zero_sent, "rep", extra))
    total = add_low(zero, swap(two, "fsdp", 2))
    return fold_replicas(total, extra, [1 << i for i in range(1, groups.bit_length() - 1)])


def finish_parts(kept, came, extra):
    if extra == 1:
        return [kept, came]
    total = kept.astype(f32) + came.astype(f32)
    bit = 1
    while bit < extra:
        total = total + swap(total, "rep", bit)
        bit *= 2
    return [total]


def owned_columns(weight, width):
    return lax.dynamic_slice_in_dim(weight, lax.axis_index("rep") * width, width, 1)


def on_device(
    tokens,
    segments,
    cotangent,
    projection_weight,
    out_weight,
    gate_up_weight,
    down_weight,
    norm_gains,
    projection_bias,
    projection_first_moment,
    out_first,
    gate_up_first,
    down_first,
    gains_first,
    bias_first_moment,
    projection_second_moment,
    out_second,
    gate_up_second,
    down_second,
    gains_second,
    bias_second_moment,
):
    count = tokens.shape[0]
    replicas = lax.axis_size("rep")
    groups = min(replicas, 8)
    extra = replicas // groups
    where = jnp.stack([lax.axis_index("fsdp"), lax.axis_index("rep") // extra]).astype(jnp.int32)
    rates = learn_rates()
    wide = 1024
    shard_rows = projection_weight.shape[0]

    pack, low_out = kernel_call(
        pack_kernel,
        [shaped((shard_rows + 16, wide), bf16), shaped(out_weight.shape, bf16)],
        "pack_attention", 1e5,
    )(where, projection_weight, out_weight, norm_gains[None], projection_bias[None])
    packs = gather_held(pack)
    low_outs = gather_held(low_out)
    gate_ups = gather_held(gate_up_weight.astype(bf16))
    downs = gather_held(down_weight.astype(bf16))

    cosine, sine, mask, e_turned = kernel_call(
        tables_kernel,
        [shaped((count, LANES), f32)] * 2
        + [shaped((count, count), f32), shaped((MODEL_WIDTH, count), bf16)],
        "tables", 1e6,
    )(where, segments[:, None], segments[None, :], cotangent)

    q_wide = 5 * LANES
    kv_wide = KEY_VALUE_HEADS * LANES
    score_shape = (CLUSTER, count, count)
    (a, q, k, v, lifted0, lifted1, lifted2, inv, o, h, a2, a2_shift, a2_turned,
     weight_full, out_full, gains) = kernel_call(
        forward_kernel,
        [
            shaped((count, MODEL_WIDTH), bf16),
            shaped((count, q_wide), bf16),
            shaped((count, kv_wide), bf16),
            shaped((count, kv_wide), bf16),
            shaped(score_shape, bf16),
            shaped(score_shape, bf16),
            shaped(score_shape, bf16),
            shaped((count, q_wide), f32),
            shaped((count, q_wide), bf16),
            shaped((count, MODEL_WIDTH), f32),
            shaped((count, MODEL_WIDTH), bf16),
            shaped((count, q_wide), bf16),
            shaped((MODEL_WIDTH, count), bf16),
            shaped((MODEL_WIDTH, wide), bf16),
            shaped((MODEL_WIDTH, MODEL_WIDTH), bf16),
            shaped((2, q_wide), f32),
        ],
        "attention_forward", 4e9,
    )(where, tokens, cosine, sine, mask, *packs, *low_outs)

    ff_rows = gate_up_weight.shape[0]
    gate_up_block = (groups, 2 * MODEL_WIDTH // groups, ff_rows)
    down_block = (groups, MODEL_WIDTH // groups, ff_rows)
    grad_gate_ups = {}
    grad_downs = {}
    total, accumulated = h, []
    for chunks, first, last in (((0, 1), True, False), ((3, 2), False, True)):
        blocks = [shaped(shape, bf16) for _ in chunks for shape in (gate_up_block, down_block)]
        results = kernel_call(
            functools.partial(feed_kernel, groups, chunks, first, last),
            [
                shaped((count, MODEL_WIDTH), bf16 if last else f32),
                shaped((count, MODEL_WIDTH), f32),
                shaped((count, q_wide), f32),
            ] + blocks,
            "feed_" + "".join(str(j) for j in chunks), 4.2e9,
        )(
            where, a2, a2_shift, a2_turned, cotangent, e_turned, total, *accumulated,
            *[gate_ups[j] for j in chunks], *[downs[j] for j in chunks],
        )
        total, accumulated = results[0], results[1:3]
        for c, j in enumerate(chunks):
            grad_gate_ups[j] = results[3 + 2 * c]
            grad_downs[j] = results[4 + 2 * c]
    output = total

    gate_up_parts = group_first(grad_gate_ups, extra, groups)
    down_parts = replica_first(grad_downs, extra, groups)

    out_block = (groups, shard_rows, LANES)
    dh, dol, gain_two, *grad_outs = kernel_call(
        functools.partial(middle_kernel, groups),
        [
            shaped((count, MODEL_WIDTH), f32),
            shaped((count, q_wide), bf16),
            shaped((1, MODEL_WIDTH), f32),
        ] + [shaped(out_block, bf16)] * 4,
        "middle", 1e9,
        scratch=[pltpu.VMEM((MODEL_WIDTH, groups * LANES), bf16)],
    )(where, *accumulated, h, cotangent, gains, o, inv, out_full)
    out_parts = replica_first(grad_outs, extra, groups)

    dqs, dks, dvs = [], [], []
    for g, lifted in enumerate((lifted0, lifted1, lifted2)):
        dq, dk, dv = kernel_call(
            functools.partial(attention_back_kernel, g),
            [shaped((CLUSTER, count, LANES), f32), shaped((count, LANES), f32), shaped((count, LANES), f32)],
            "attention_back_" + str(g), 2e9,
        )(where, q, k, v, lifted, o, dol)
        dqs.append(dq)
        dks.append(dk)
        dvs.append(dv)

    message = 2 * groups * shard_rows + SMALL_ROWS
    sent, kept, tokens_grad = kernel_call(
        functools.partial(last_kernel, groups),
        [
            shaped((message, LANES), bf16),
            shaped((message, LANES), bf16),
            shaped((count, MODEL_WIDTH), bf16),
        ],
        "last", 2e9,
        scratch=[pltpu.VMEM((MODEL_WIDTH, groups * LANES), bf16)],
    )(where, *dqs, *dks, *dvs, cosine, sine, a, tokens, dh, weight_full, gains, gain_two)

    steps = [("fsdp", 1), ("fsdp", 2)]
    steps += [("rep", extra << i) for i in range(groups.bit_length() - 1)]
    for at, (axis, bit) in enumerate(steps):
        if at:
            part = (kept.shape[0] - SMALL_ROWS) // 2 + SMALL_ROWS
            sent, kept = kernel_call(
                halve_kernel, [shaped((part, LANES), bf16)] * 2, "halve_" + str(at), 1e5
            )(where, kept, came)
        came = swap(sent, axis, bit)
    qkv_parts = finish_parts(kept, came, extra)

    def own_weight(weight, moment):
        return owned_columns(weight, moment.shape[1])

    def weight_step(parts, turned, weight, first, second, rate, name):
        if extra > 1:
            (term,) = parts
            dim = 0 if turned else 1
            width = first.shape[1]
            at = (lax.axis_index("rep") % extra) * width
            parts = [lax.dynamic_slice_in_dim(term, at, width, dim)]
        return kernel_call(
            functools.partial(weight_step_kernel, rate, turned, len(parts)),
            [shaped(first.shape, f32)] * 3, name, 1e6,
        )(where, *parts, own_weight(weight, first), first, second)

    gate_up_new = weight_step(
        finish_parts(*[part[0] for part in gate_up_parts], extra), True,
        gate_up_weight, gate_up_first, gate_up_second, rates[2], "gate_up_step",
    )
    down_new = weight_step(
        finish_parts(*[part[0] for part in down_parts], extra), True,
        down_weight, down_first, down_second, rates[3], "down_step",
    )
    out_new = weight_step(
        finish_parts(*[part[0] for part in out_parts], extra), False,
        out_weight, out_first, out_second, rates[1], "out_step",
    )
    if extra > 1:
        (term,) = qkv_parts
        width = projection_first_moment.shape[1]
        at = (lax.axis_index("rep") % extra) * width
        own = lax.dynamic_slice_in_dim(term[:-SMALL_ROWS], at, width, 1)
        own = jnp.pad(own, ((0, 0), (0, LANES - width)))
        qkv_parts = [jnp.concatenate([own, term[-SMALL_ROWS:]])]
    vectors = (norm_gains, gains_first, gains_second, projection_bias, bias_first_moment, bias_second_moment)
    news = kernel_call(
        functools.partial(final_kernel, (rates[0], rates[4], rates[5]), len(qkv_parts)),
        [shaped(projection_first_moment.shape, f32)] * 3
        + [shaped((1,) + vector.shape, f32) for vector in vectors],
        "final_step", 1e6,
    )(
        where, *qkv_parts, own_weight(projection_weight, projection_first_moment),
        projection_first_moment, projection_second_moment, *[vector[None] for vector in vectors],
    )
    return (
        output,
        tokens_grad,
        *news[:3],
        *out_new,
        *gate_up_new,
        *down_new,
        *[new[0] for new in news[3:]],
    )


def solution(mesh):
    rows = P(("rep", "fsdp"), None)
    weight = P("fsdp", None)
    state = P("fsdp", "rep")
    vector = P("fsdp")
    states = (state,) * 4 + (vector,) * 2
    in_specs = (rows, P(("rep", "fsdp")), rows) + (weight,) * 4 + (vector,) * 2 + states + states
    out_specs = (rows, rows) + (state,) * 12 + (vector,) * 6
    return jax.shard_map(
        on_device, mesh=mesh, in_specs=in_specs, out_specs=out_specs, check_vma=False
    )
```

```python
import functools
import math

import jax
import jax.numpy as jnp
from jax import lax
from jax.experimental import pallas as pl
from jax.experimental.pallas import tpu as pltpu
from jax.sharding import PartitionSpec as P

MODEL_WIDTH = 576
QUERY_HEADS = 9
KEY_VALUE_HEADS = 3
HEAD_SIZE = 64
FF = 1536
STEP = 10

norm_eps = 1e-05
rope_base = 100000.0
beta_one = 0.9
beta_two = 0.95
adam_eps = 1e-08
decay_rate = 0.1

LANES = 128
QKV_WIDTH = (QUERY_HEADS + 2 * KEY_VALUE_HEADS) * HEAD_SIZE
CLUSTER = QUERY_HEADS // KEY_VALUE_HEADS
SMALL_ROWS = 32
ROW_BLOCK = 256
bf16 = jnp.bfloat16
f32 = jnp.float32


def learn_rates():
    out_fan = max(QUERY_HEADS * HEAD_SIZE // 16, 1)
    return (MODEL_WIDTH ** (-0.5), out_fan ** (-0.5), MODEL_WIDTH ** (-0.5), FF ** (-0.5), 0.5, 0.5)


def adam_update(weight, first_moment, second_moment, gradient, step_rate):
    first_new = beta_one * first_moment + (1.0 - beta_one) * gradient
    second_new = beta_two * second_moment + (1.0 - beta_two) * gradient * gradient
    first_fix = 1.0 - beta_one**STEP
    second_fix = 1.0 - beta_two**STEP
    direction = first_new / first_fix / (jnp.sqrt(second_new / second_fix) + adam_eps)
    return (first_new, second_new, weight - step_rate * (direction + decay_rate * weight))


def dot_plain(left, right):
    return lax.dot_general(left, right, (((1,), (0,)), ((), ())), preferred_element_type=f32)


def dot_last(left, right):
    return lax.dot_general(left, right, (((1,), (1,)), ((), ())), preferred_element_type=f32)


def dot_first(left, right):
    return lax.dot_general(left, right, (((0,), (0,)), ((), ())), preferred_element_type=f32)


def kernel_call(body, outs, name, flops, scratch=(), vmem=24, after=()):
    def call(scalars, *arrays):
        moved = sum(a.size * a.dtype.itemsize for a in arrays)
        moved += sum(o.size * o.dtype.itemsize for o in outs)
        count = len(after)

        def run(*refs):
            body(refs[0], *refs[1 + count :])

        return pl.pallas_call(
            run,
            out_shape=tuple(outs),
            in_specs=[pl.BlockSpec(memory_space=pltpu.SMEM)]
            + [pl.BlockSpec(memory_space=pl.ANY)] * count
            + [pl.BlockSpec(memory_space=pltpu.VMEM)] * len(arrays),
            out_specs=tuple(pl.BlockSpec(memory_space=pltpu.VMEM) for _ in outs),
            scratch_shapes=list(scratch),
            name=name,
            compiler_params=pltpu.CompilerParams(vmem_limit_bytes=vmem * 2**20),
            cost_estimate=pl.CostEstimate(
                flops=0, bytes_accessed=0, transcendentals=0
            ),
        )(scalars, *after, *arrays)

    return call


def gate(values, after, name):
    def nothing(*refs):
        pass

    result = pl.pallas_call(
        nothing,
        out_shape=tuple(shaped(v.shape, v.dtype) for v in values),
        in_specs=[pl.BlockSpec(memory_space=pl.ANY)] * (len(values) + len(after)),
        out_specs=tuple(pl.BlockSpec(memory_space=pl.ANY) for _ in values),
        input_output_aliases={i: i for i in range(len(values))},
        name=name,
        cost_estimate=pl.CostEstimate(flops=0, bytes_accessed=0, transcendentals=0),
    )(*values, *after)
    return list(result)


def shaped(shape, dtype):
    return jax.ShapeDtypeStruct(tuple(shape), dtype)


def lane_index(shape):
    return lax.broadcasted_iota(jnp.int32, shape, len(shape) - 1)


def lower_half(shape):
    return lane_index(shape) < HEAD_SIZE


def swap_pairs(block):
    first = (lane_index(block.shape) & (HEAD_SIZE // 2)) == 0
    ahead = pltpu.roll(block, LANES - HEAD_SIZE // 2, 1)
    behind = pltpu.roll(block, HEAD_SIZE // 2, 1)
    return jnp.where(first, ahead, behind)


def both_halves(block, upper):
    other = pltpu.roll(block, HEAD_SIZE, 1)
    low = lower_half(block.shape)
    return jnp.where(low, other, block) if upper else jnp.where(low, block, other)


def cut_lanes(blocks, start, width):
    at, offset = divmod(start, LANES)
    lane = lane_index(blocks[0].shape)
    part = blocks[at]
    if offset:
        part = pltpu.roll(part, LANES - offset, 1)
        if offset + width > LANES:
            after = pltpu.roll(blocks[at + 1], LANES - offset, 1)
            part = jnp.where(lane < LANES - offset, part, after)
    if width < LANES:
        part = jnp.where(lane < width, part, 0.0)
    return part


def lane_blocks(values):
    width = values.shape[1]
    full = width // LANES
    blocks = [values[:, i * LANES : (i + 1) * LANES] for i in range(full)]
    if width % LANES:
        rest = values[:, full * LANES :]
        fill = jnp.zeros((values.shape[0], LANES - width % LANES), values.dtype)
        blocks.append(jnp.concatenate([rest, fill], axis=1))
    return blocks


def block_place(block, mine, groups):
    away = mine ^ block
    place = 0
    bit = 1
    while bit < groups:
        place = place * 2 + jnp.where((away & bit) == 0, 0, 1)
        bit *= 2
    return place


def own_rows(ref, replica, width):
    if width % 8 == 0:
        return ref[pl.ds(pl.multiple_of(replica * width, 8), width), :]
    rows = ref.shape[0]
    return pltpu.roll(ref[...], rows - replica * width, 0)[:width]


def pack_kernel(where_ref, qkv_ref, out_ref, gains_ref, bias_ref, pack_ref, low_out_ref):
    rows = qkv_ref.shape[0]
    pack_ref[:rows, :QKV_WIDTH] = qkv_ref[...].astype(bf16)
    pack_ref[:rows, QKV_WIDTH:] = jnp.zeros((rows, pack_ref.shape[1] - QKV_WIDTH), bf16)
    spare = pack_ref.shape[0] - rows
    extra = jnp.concatenate(lane_blocks(bias_ref[...]) + lane_blocks(gains_ref[...]), axis=1)
    line = jnp.concatenate(
        [extra, jnp.zeros((1, pack_ref.shape[1] - extra.shape[1]), f32)], axis=1
    )
    pack_ref[rows:, :] = jnp.broadcast_to(line, (spare, line.shape[1])).astype(bf16)
    low_out_ref[...] = out_ref[...].astype(bf16)


def tables_kernel(
    where_ref, column_ref, row_ref, tokens_turned_ref, e_turned_ref, qkv_ref, out_ref, gate_up_ref, down_ref,
    cos_ref, sin_ref, mask_ref, tokens_ref, e_ref, low_gate_up_ref, half_ref, low_down_ref,
    own_qkv_ref, own_out_ref, own_gate_up_ref, own_down_ref, turned_ref,
):
    tokens = column_ref.shape[0]
    query = lax.broadcasted_iota(jnp.int32, (tokens, tokens), 0)
    key = lax.broadcasted_iota(jnp.int32, (tokens, tokens), 1)
    same = column_ref[...] == row_ref[...]
    earlier = jnp.sum(jnp.where(same & (key < query), 1.0, 0.0), axis=1, keepdims=True)
    mask_ref[...] = jnp.where(same & (key <= query), 0.0, -1e30)
    lane = lane_index((tokens, LANES))
    exponent = (lane & (HEAD_SIZE // 2 - 1)).astype(f32) * (2.0 / HEAD_SIZE)
    frequency = jnp.exp(exponent * (-math.log(rope_base)))
    angles = earlier * frequency
    cos_ref[...] = jnp.cos(angles)
    sine = jnp.sin(angles)
    sin_ref[...] = jnp.where((lane & (HEAD_SIZE // 2)) == 0, -sine, sine)
    tokens_ref[...] = tokens_turned_ref[...].astype(f32).T.astype(bf16)
    e_ref[...] = e_turned_ref[...].astype(f32).T.astype(bf16)

    gate_up = gate_up_ref[...]
    low_gate_up_ref[...] = gate_up.astype(bf16)
    rows = half_ref.shape[0]
    start = pl.multiple_of((where_ref[1] & 1) * rows, 16)
    half_ref[...] = gate_up_ref[pl.ds(start, rows), :].astype(bf16)
    low_down_ref[...] = down_ref[...].astype(bf16)
    replica = where_ref[2]
    turned_ref[...] = gate_up.T
    width = own_gate_up_ref.shape[0]
    own_gate_up_ref[...] = own_rows(turned_ref, replica, width)
    width = own_down_ref.shape[0]
    own_down_ref[...] = own_rows(down_ref, replica, width)
    for ref, own in ((qkv_ref, own_qkv_ref), (out_ref, own_out_ref)):
        width = own.shape[1]
        wide = jnp.concatenate(lane_blocks(ref[...]), axis=1)
        own[...] = pltpu.roll(wide, wide.shape[1] - replica * width, 1)[:, :width]


def forward_kernel(
    where_ref, tokens_ref, cos_ref, sin_ref, mask_ref, pack0, pack1, pack2, pack3,
    a_ref, q_ref, k_ref, v_ref, e0_ref, e1_ref, e2_ref, inv_ref, o_ref, weight_ref, gains_ref,
):
    me = where_ref[0]
    tokens = tokens_ref.shape[0]
    shard_rows = MODEL_WIDTH // 4
    packs = (pack0, pack1, pack2, pack3)
    lines = []
    for j in range(4):
        start = pl.multiple_of((me ^ j) * shard_rows, 16)
        weight_ref[pl.ds(start, shard_rows), :] = packs[j][:shard_rows, :]
        lines.append(packs[j][shard_rows:, :].astype(f32)[:1, :])
    bias_wide = lane_index((1, LANES)) * 0.0
    ordered = []
    for s in range(4):
        line = jnp.where((me ^ s) == 0, lines[0], 0.0)
        for j in range(1, 4):
            line = jnp.where((me ^ s) == j, lines[j], line)
        ordered.append(line)
    bias_blocks = [bias_wide for _ in range(weight_ref.shape[1] // LANES)]
    gain_blocks = [[bias_wide for _ in range(5)] for _ in range(2)]
    lane = lane_index((1, LANES))

    def put(blocks, source, width, start):
        done = 0
        while done < width:
            at, offset = divmod(start + done, LANES)
            count = min(LANES - offset, width - done)
            from_at, from_offset = divmod(done, LANES)
            count = min(count, LANES - from_offset)
            turn = (offset - from_offset) % LANES
            part = source[from_at]
            if turn:
                part = pltpu.roll(part, turn, 1)
            blocks[at] = jnp.where((lane >= offset) & (lane < offset + count), part, blocks[at])
            done += count

    bias_each = QKV_WIDTH // 4
    gain_each = 2 * MODEL_WIDTH // 4
    bias_lanes = -(-bias_each // LANES) * LANES
    for s in range(4):
        pieces = [ordered[s][:, i * LANES : (i + 1) * LANES] for i in range(8)]
        put(bias_blocks, pieces, bias_each, s * bias_each)
        put(gain_blocks[s // 2], pieces[bias_lanes // LANES :], gain_each, (s % 2) * gain_each)
    gains = [jnp.concatenate(blocks, axis=1) for blocks in gain_blocks]
    for i in range(2):
        gains_ref[i : i + 1, :] = gains[i]
    bias = jnp.concatenate(bias_blocks, axis=1)

    x = tokens_ref[...].astype(f32)
    inverse = lax.rsqrt(jnp.mean(x * x, axis=1, keepdims=True) + norm_eps)
    a = (x * inverse * gains[0][:, :MODEL_WIDTH]).astype(bf16)
    a_ref[...] = a
    p = dot_plain(a, weight_ref[...]) + bias
    cosine, sine = cos_ref[...], sin_ref[...]
    blocks = [p[:, i * LANES : (i + 1) * LANES] for i in range(8)]
    for i in range(6):
        blocks[i] = blocks[i] * cosine + swap_pairs(blocks[i]) * sine
    low = lower_half((tokens, LANES))
    for i in range(5):
        scaled = blocks[i] * HEAD_SIZE ** (-0.5)
        if i == 4:
            scaled = jnp.where(low, scaled, 0.0)
        q_ref[:, i * LANES : (i + 1) * LANES] = scaled.astype(bf16)
    keys = [both_halves(blocks[4], True), both_halves(blocks[5], False), both_halves(blocks[5], True)]
    values = [both_halves(blocks[6], False), both_halves(blocks[6], True), both_halves(blocks[7], False)]
    for g in range(KEY_VALUE_HEADS):
        k_ref[:, g * LANES : (g + 1) * LANES] = keys[g].astype(bf16)
        v_ref[:, g * LANES : (g + 1) * LANES] = values[g].astype(bf16)

    e_refs = (e0_ref, e1_ref, e2_ref)
    step = ROW_BLOCK
    low = lower_half((step, LANES))
    for at in range(tokens // step):
        rows = slice(at * step, (at + 1) * step)
        seen = (at + 1) * step
        mixed = []
        inverses = []
        for g in range(KEY_VALUE_HEADS):
            stack = head_stack(q_ref, rows, g)
            scores = dot_last(stack, k_ref[:seen, g * LANES : (g + 1) * LANES])
            scores = scores.reshape(CLUSTER, step, seen) + mask_ref[rows, :seen][None]
            lifted = jnp.exp(scores - jnp.max(scores, axis=2, keepdims=True))
            total = jnp.sum(lifted, axis=2, keepdims=True)
            kept = lifted.astype(bf16)
            e_refs[g][:, rows, :seen] = kept
            gathered = dot_plain(
                kept.reshape(CLUSTER * step, seen), v_ref[:seen, g * LANES : (g + 1) * LANES]
            ).reshape(CLUSTER, step, LANES)
            inverse_total = jnp.broadcast_to(1.0 / total, gathered.shape)
            gathered = gathered * inverse_total
            for t in range(CLUSTER):
                mixed.append(gathered[t])
                inverses.append(inverse_total[t])
        for i in range(5):
            second = mixed[2 * i + 1] if 2 * i + 1 < QUERY_HEADS else 0.0
            part = jnp.where(low, mixed[2 * i], second)
            o_ref[rows, i * LANES : (i + 1) * LANES] = part.astype(bf16)
            second = inverses[2 * i + 1] if 2 * i + 1 < QUERY_HEADS else 0.0
            inv_ref[rows, i * LANES : (i + 1) * LANES] = jnp.where(low, inverses[2 * i], second)


def project_kernel(
    where_ref, tokens_ref, o_ref, gains_ref, out0, out1, out2, out3,
    h_ref, a2_ref, a2_shift_ref, a2_turned_ref, out_weight_ref,
):
    me = where_ref[0]
    tokens = tokens_ref.shape[0]
    shard_rows = out0.shape[0]
    for j, out in enumerate((out0, out1, out2, out3)):
        start = pl.multiple_of((me ^ j) * shard_rows, 16)
        out_weight_ref[pl.ds(start, shard_rows), :] = out[...]
    x = tokens_ref[...].astype(f32)
    h = x + dot_plain(o_ref[:, :MODEL_WIDTH], out_weight_ref[...])
    h_ref[...] = h
    inverse = lax.rsqrt(jnp.mean(h * h, axis=1, keepdims=True) + norm_eps)
    a2 = h * inverse * gains_ref[1:2, :MODEL_WIDTH]
    a2_ref[...] = a2.astype(bf16)
    a2_blocks = lane_blocks(a2)
    low = lower_half((tokens, LANES))
    before = jnp.zeros((tokens, LANES), f32)
    for i in range(5):
        part = jnp.where(low, pltpu.roll(before, HEAD_SIZE, 1), pltpu.roll(a2_blocks[i], HEAD_SIZE, 1))
        a2_shift_ref[:, i * LANES : (i + 1) * LANES] = part.astype(bf16)
        before = a2_blocks[i]
    a2_turned_ref[...] = a2.T.astype(bf16)


def head_stack(ref, rows, g):
    parts = []
    for t in range(CLUSTER):
        head = g * CLUSTER + t
        block = ref[rows, (head // 2) * LANES : (head // 2 + 1) * LANES]
        low = lower_half(block.shape)
        keep = low if head % 2 == 0 else jnp.logical_not(low)
        parts.append(jnp.where(keep, block, jnp.zeros_like(block)))
    return jnp.concatenate(parts, axis=0)


def feed_kernel(groups, chunks, first, last, *refs):
    refs = list(refs)

    def take(count):
        taken = refs[:count]
        del refs[:count]
        return taken

    (where_ref, a2_ref, a2_shift_ref, a2_turned_ref, e_ref, e_turned_ref, base_ref) = take(7)
    gate_in, shift_in = (None, None) if first else take(2)
    gate_ups = [take(1 if first else 2) for _ in chunks]
    downs = take(len(chunks))
    total_ref, gate_acc, shift_acc = take(3)
    mine = where_ref[1]
    total = base_ref[...]
    for c in range(len(chunks)):
        grad_gate_up_ref, grad_down_ref = take(2)
        down = downs[c]
        if first:
            gate_up = gate_ups[c][0]
        else:
            gate_up = refs[-1]
            rows = gate_ups[c][0].shape[0]
            for half in range(2):
                start = pl.multiple_of(((mine & 1) ^ half) * rows, 16)
                gate_up[pl.ds(start, rows), :] = gate_ups[c][half][...]
        gate_weights = gate_up[:, :MODEL_WIDTH]
        up_weights = gate_up[:, MODEL_WIDTH - HEAD_SIZE :]
        gate = dot_last(a2_ref[...], gate_weights)
        up = dot_last(a2_shift_ref[...], up_weights)
        sigma = 1.0 / (1.0 + jnp.exp(-gate))
        active = gate * sigma
        hidden = (active * up).astype(bf16)
        total = total + dot_last(hidden, down[...])
        grad_hidden = dot_plain(e_ref[...], down[...])
        grad_gate = (grad_hidden * up * (sigma * (1.0 + gate * (1.0 - sigma)))).astype(bf16)
        grad_up = (grad_hidden * active).astype(bf16)
        width = grad_gate_up_ref.shape[1]
        half = groups // 2
        for turned, offset in ((dot_plain(a2_turned_ref[...], grad_gate), 0),
                               (dot_plain(a2_turned_ref[...], grad_up), half)):
            for b in range(half):
                grad_gate_up_ref[block_place(b + offset, mine, groups)] = turned[
                    b * width : (b + 1) * width
                ].astype(bf16)
        turned = dot_plain(e_turned_ref[...], hidden)
        width = grad_down_ref.shape[1]
        for b in range(groups):
            grad_down_ref[block_place(b, mine, groups)] = turned[
                b * width : (b + 1) * width
            ].astype(bf16)
        gate_part = dot_plain(grad_gate, gate_weights)
        shift_part = dot_plain(grad_up, up_weights)
        if c == 0 and first:
            gate_acc[...] = gate_part
            shift_acc[...] = shift_part
        elif c == 0:
            gate_acc[...] = gate_in[...] + gate_part
            shift_acc[...] = shift_in[...] + shift_part
        else:
            gate_acc[...] = gate_acc[...] + gate_part
            shift_acc[...] = shift_acc[...] + shift_part
    total_ref[...] = total.T.astype(bf16) if last else total


def middle_kernel(
    groups, where_ref, gate_acc, shift_acc, h_ref, e_ref, gains_ref, o_ref, inv_ref, out_weight_ref,
    dh_ref, dol_ref, small_ref, grad0, grad1, grad2, grad3, held_ref,
):
    me, mine = where_ref[0], where_ref[1]
    tokens = h_ref.shape[0]
    gain = gains_ref[1:2, :MODEL_WIDTH]
    h = h_ref[...]
    low = lower_half((tokens, LANES))
    shifted = [shift_acc[:, i * LANES : (i + 1) * LANES] for i in range(5)]
    parts = []
    for i in range(5):
        part = pltpu.roll(shifted[i], HEAD_SIZE, 1)
        after = pltpu.roll(shifted[i + 1], HEAD_SIZE, 1) if i < 4 else 0.0
        parts.append(jnp.where(low, part, after))
    da2 = gate_acc[...] + jnp.concatenate(parts, axis=1)[:, :MODEL_WIDTH]
    inverse = lax.rsqrt(jnp.mean(h * h, axis=1, keepdims=True) + norm_eps)
    weighted = da2 * gain
    inner = jnp.mean(weighted * h, axis=1, keepdims=True)
    dh = e_ref[...].astype(f32) + inverse * weighted - h * (inverse * inverse * inverse) * inner
    dh_ref[...] = dh
    small_ref[...] = jnp.sum(da2 * h * inverse, axis=0, keepdims=True)
    dhl = dh.astype(bf16)
    spread = dhl.astype(f32)
    blocks = lane_blocks(spread)
    width = MODEL_WIDTH // groups
    chosen = jnp.concatenate(
        [cut_lanes(blocks, b * width, width).astype(bf16) for b in range(groups)], axis=1
    )
    held_ref[...] = dot_first(o_ref[:, :MODEL_WIDTH], chosen).astype(bf16)
    rows = grad0.shape[1]
    for j, grad in enumerate((grad0, grad1, grad2, grad3)):
        start = pl.multiple_of((me ^ j) * rows, 16)
        for b in range(groups):
            grad[block_place(b, mine, groups)] = held_ref[
                pl.ds(start, rows), b * LANES : (b + 1) * LANES
            ]
    dol = dot_last(dhl, out_weight_ref[...])
    dol_blocks = lane_blocks(dol.astype(bf16).astype(f32))
    for i in range(5):
        lanes = slice(i * LANES, (i + 1) * LANES)
        dol_ref[:, lanes] = (dol_blocks[i] * inv_ref[:, lanes]).astype(bf16)


def attention_back_kernel(g, where_ref, q_ref, k_ref, v_ref, lifted_ref, o_ref, dol_ref, dq_ref, dk_ref, dv_ref):
    tokens = q_ref.shape[0]
    step = ROW_BLOCK
    lanes = slice(g * LANES, (g + 1) * LANES)
    dk = None
    dv = None
    for at in reversed(range(tokens // step)):
        rows = slice(at * step, (at + 1) * step)
        seen = (at + 1) * step
        q_stack = head_stack(q_ref, rows, g)
        o_stack = head_stack(o_ref, rows, g)
        dol_stack = head_stack(dol_ref, rows, g)
        lifted = lifted_ref[:, rows, :seen].reshape(CLUSTER * step, seen)
        inner = jnp.sum(o_stack.astype(f32) * dol_stack.astype(f32), axis=1, keepdims=True)
        grad = dot_last(dol_stack, v_ref[:seen, lanes])
        dsl = (lifted.astype(f32) * (grad - inner)).astype(bf16)
        dq = dot_plain(dsl, k_ref[:seen, lanes]) * HEAD_SIZE ** (-0.5)
        dq_ref[:, rows, :] = dq.reshape(CLUSTER, step, LANES)
        dk_part = dot_first(q_stack, dsl)
        dv_part = dot_first(dol_stack, lifted)
        if dk is None:
            dk, dv = dk_part, dv_part
        else:
            dk = jnp.concatenate([dk[:, :seen] + dk_part, dk[:, seen:]], axis=1)
            dv = jnp.concatenate([dv[:, :seen] + dv_part, dv[:, seen:]], axis=1)
    dk = dk.T
    dv = dv.T
    dk_ref[...] = dk + pltpu.roll(dk, HEAD_SIZE, 1)
    dv_ref[...] = dv + pltpu.roll(dv, HEAD_SIZE, 1)


def last_kernel(
    groups, where_ref, dq0, dq1, dq2, dk0, dk1, dk2, dv0, dv1, dv2, cos_ref, sin_ref,
    a_ref, tokens_ref, dh_ref, weight_ref, gains_ref, gain_two_ref,
    sent_ref, kept_ref, tokens_grad_ref, held_ref,
):
    me, mine = where_ref[0], where_ref[1]
    tokens = tokens_ref.shape[0]
    low = lower_half((tokens, LANES))
    heads = [ref[t] for ref in (dq0, dq1, dq2) for t in range(CLUSTER)]
    blocks = [jnp.where(low, heads[2 * i], heads[2 * i + 1]) for i in range(4)]
    blocks.append(jnp.where(low, heads[8], dk0[...]))
    blocks.append(jnp.where(low, dk1[...], dk2[...]))
    cosine, sine = cos_ref[...], sin_ref[...]
    blocks = [block * cosine - swap_pairs(block) * sine for block in blocks]
    blocks.append(jnp.where(low, dv0[...], dv1[...]))
    blocks.append(jnp.where(low, dv2[...], 0.0))
    low_blocks = [block.astype(bf16) for block in blocks]
    blocks = [block.astype(f32) for block in low_blocks]
    dpl = jnp.concatenate(low_blocks, axis=1)
    width = QKV_WIDTH // groups
    chosen = jnp.concatenate(
        [cut_lanes(blocks, b * width, width).astype(bf16) for b in range(groups)], axis=1
    )
    held_ref[...] = dot_first(a_ref[...], chosen).astype(bf16)
    rows = held_ref.shape[0] // 4
    for j in range(4):
        start = pl.multiple_of((me ^ j) * rows, 16)
        target = sent_ref if j % 2 else kept_ref
        for b in range(groups):
            to = pl.multiple_of((block_place(b, mine, groups) + (j // 2) * groups) * rows, 16)
            target[pl.ds(to, rows), :] = held_ref[pl.ds(start, rows), b * LANES : (b + 1) * LANES]

    bias_blocks = [jnp.sum(block, axis=0, keepdims=True) for block in blocks]
    x = tokens_ref[...].astype(f32)
    inverse = lax.rsqrt(jnp.mean(x * x, axis=1, keepdims=True) + norm_eps)
    da = dot_last(dpl, weight_ref[...])
    gain_one_blocks = lane_blocks(jnp.sum(da * x * inverse, axis=0, keepdims=True))
    gain_two_blocks = lane_blocks(gain_two_ref[...])
    weighted = da * gains_ref[0:1, :MODEL_WIDTH]
    inner = jnp.mean(weighted * x, axis=1, keepdims=True)
    tokens_grad = dh_ref[...] + inverse * weighted - x * (inverse * inverse * inverse) * inner
    tokens_grad_ref[...] = tokens_grad.T.astype(bf16)

    gain_each = 2 * MODEL_WIDTH // 4
    bias_each = QKV_WIDTH // 4
    lines = []
    for s in range(4):
        source = gain_one_blocks if s < 2 else gain_two_blocks
        count = 0
        for t in range(0, gain_each, LANES):
            lines.append(cut_lanes(source, (s % 2) * gain_each + t, min(LANES, gain_each - t)))
            count += 1
        for t in range(0, bias_each, LANES):
            lines.append(cut_lanes(bias_blocks, s * bias_each + t, min(LANES, bias_each - t)))
            count += 1
        lines += [jnp.zeros((1, LANES), f32)] * (SMALL_ROWS // 4 - count)
    small = jnp.concatenate(lines, axis=0).astype(bf16)
    sent_ref[2 * groups * rows :, :] = small
    kept_ref[2 * groups * rows :, :] = small


def halve_kernel(where_ref, kept_ref, came_ref, sent_ref, left_ref):
    part = left_ref.shape[0] - SMALL_ROWS
    total = kept_ref[...].astype(f32) + came_ref[...].astype(f32)
    total = total.astype(bf16)
    left_ref[:part, :] = total[:part]
    left_ref[part:, :] = total[2 * part :]
    sent_ref[...] = total[part:]


def weight_step_kernel(step_rate, parts, where_ref, *refs):
    gradient = refs[0][...].astype(f32)
    for ref in refs[1:parts]:
        gradient = gradient + ref[...].astype(f32)
    weight_ref, first_ref, second_ref = refs[parts : parts + 3]
    gradient = gradient[:, : weight_ref.shape[1]]
    new = adam_update(weight_ref[...], first_ref[...], second_ref[...], gradient, step_rate)
    for ref, value in zip(refs[parts + 3 :], new):
        ref[...] = value


def final_kernel(step_rates, parts, where_ref, *refs):
    total = refs[0][...].astype(f32)
    for ref in refs[1:parts]:
        total = total + ref[...].astype(f32)
    rows = total.shape[0] - SMALL_ROWS
    refs = refs[parts:]
    ins, outs = refs[:9], refs[9:]
    gradient = total[:rows, : ins[0].shape[1]]
    new = adam_update(ins[0][...], ins[1][...], ins[2][...], gradient, step_rates[0])
    for i in range(3):
        outs[i][...] = new[i]
    me = where_ref[0]
    each = SMALL_ROWS // 4
    mine = total[rows : rows + each]
    for s in range(1, 4):
        mine = jnp.where(me == s, total[rows + s * each : rows + (s + 1) * each], mine)
    line = 0
    for k, rate in ((3, step_rates[1]), (6, step_rates[2])):
        width = ins[k].shape[0]
        count = -(-width // LANES)
        wide = jnp.concatenate([mine[line + t : line + t + 1, :] for t in range(count)], axis=1)
        line += count
        wide = wide[:, :width].reshape(width)
        new = adam_update(ins[k][...], ins[k + 1][...], ins[k + 2][...], wide, rate)
        for i in range(3):
            outs[k + i][...] = new[i]


def swap(values, axis, bit):
    size = lax.axis_size(axis)
    return lax.ppermute(values, axis, [(i, i ^ bit) for i in range(size)])


def add_low(left, right):
    return (left.astype(f32) + right.astype(f32)).astype(bf16)


def halves(values):
    half = values.shape[0] // 2
    return values[:half], values[half:]


def fold_replicas(kept, extra, bits):
    came = None
    for bit in bits:
        if came is not None:
            kept = add_low(kept, came)
        kept, sent = halves(kept)
        came = swap(sent, "rep", bit * extra)
    return kept, came


def core_sum(chunks, at):
    return add_low(chunks[at], swap(chunks[at + 1], "fsdp", 1))


def group_first(zero, two, extra, groups):
    total = add_low(zero, swap(two, "fsdp", 2))
    return fold_replicas(total, extra, [1 << i for i in range(groups.bit_length() - 1)])


def replica_first(zero, two, extra, groups):
    two_kept, two_sent = halves(two)
    zero_kept, zero_sent = halves(zero)
    two = add_low(two_kept, swap(two_sent, "rep", extra))
    zero = add_low(zero_kept, swap(zero_sent, "rep", extra))
    total = add_low(zero, swap(two, "fsdp", 2))
    return fold_replicas(total, extra, [1 << i for i in range(1, groups.bit_length() - 1)])


def finish_parts(kept, came, extra):
    if extra == 1:
        return [kept, came]
    total = kept.astype(f32) + came.astype(f32)
    bit = 1
    while bit < extra:
        total = total + swap(total, "rep", bit)
        bit *= 2
    return [total]


def on_device(
    tokens,
    segments,
    cotangent,
    projection_weight,
    out_weight,
    gate_up_weight,
    down_weight,
    norm_gains,
    projection_bias,
    projection_first_moment,
    out_first,
    gate_up_first,
    down_first,
    gains_first,
    bias_first_moment,
    projection_second_moment,
    out_second,
    gate_up_second,
    down_second,
    gains_second,
    bias_second_moment,
):
    count = tokens.shape[0]
    replicas = lax.axis_size("rep")
    groups = min(replicas, 8)
    extra = replicas // groups
    replica = lax.axis_index("rep")
    where = jnp.stack([lax.axis_index("fsdp"), replica // extra, replica]).astype(jnp.int32)
    rates = learn_rates()
    wide = 1024
    shard_rows, ff_rows = projection_weight.shape[0], gate_up_weight.shape[0]
    q_wide = 5 * LANES
    kv_wide = KEY_VALUE_HEADS * LANES
    tokens_turned, e_turned, down_turned = tokens.T, cotangent.T, down_weight.T

    pack, low_out = kernel_call(
        pack_kernel,
        [shaped((shard_rows + 16, wide), bf16), shaped(out_weight.shape, bf16)],
        "pack_attention", 1e5,
    )(where, projection_weight, out_weight, norm_gains[None], projection_bias[None])
    pack2 = swap(pack, "fsdp", 2)
    pack1 = swap(pack, "fsdp", 1)

    (cosine, sine, mask, tokens_low, e, low_gate_up, half, low_down,
     own_qkv, own_out, own_gate_up, own_down) = kernel_call(
        tables_kernel,
        [
            shaped((count, LANES), f32),
            shaped((count, LANES), f32),
            shaped((count, count), f32),
            shaped((count, MODEL_WIDTH), bf16),
            shaped((count, MODEL_WIDTH), bf16),
            shaped((ff_rows, 2 * MODEL_WIDTH), bf16),
            shaped((ff_rows // 2, 2 * MODEL_WIDTH), bf16),
            shaped((MODEL_WIDTH, ff_rows), bf16),
            shaped(projection_first_moment.shape, f32),
            shaped(out_first.shape, f32),
            shaped(gate_up_first.shape[::-1], f32),
            shaped(down_first.shape[::-1], f32),
        ],
        "tables", 1e6,
        scratch=[pltpu.VMEM((2 * MODEL_WIDTH, ff_rows), f32)], after=(pack,),
    )(
        where, segments[:, None], segments[None, :], tokens_turned, e_turned,
        projection_weight, out_weight, gate_up_weight, down_turned,
    )

    (low_out,) = gate([low_out], [pack1, pack2, cosine], "out_after_pack")
    pack3 = swap(pack2, "fsdp", 1)
    out2 = swap(low_out, "fsdp", 2)
    out1 = swap(low_out, "fsdp", 1)

    (a, q, k, v, lifted0, lifted1, lifted2, inv, o, weight_full, gains) = kernel_call(
        forward_kernel,
        [
            shaped((count, MODEL_WIDTH), bf16),
            shaped((count, q_wide), bf16),
            shaped((count, kv_wide), bf16),
            shaped((count, kv_wide), bf16),
        ]
        + [shaped((CLUSTER, count, count), bf16)] * 3
        + [
            shaped((count, q_wide), f32),
            shaped((count, q_wide), bf16),
            shaped((MODEL_WIDTH, wide), bf16),
            shaped((2, q_wide), f32),
        ],
        "attention_forward", 4e9,
    )(where, tokens_low, cosine, sine, mask, pack, pack1, pack2, pack3)

    half, low_gate_up, low_down = gate([half, low_gate_up, low_down], [out2, pack3], "feed_after_out")
    out3 = swap(out2, "fsdp", 1)
    half_across = swap(half, "fsdp", 2)
    gate_up1 = swap(low_gate_up, "fsdp", 1)
    down1 = swap(low_down, "fsdp", 1)

    h, a2, a2_shift, a2_turned, out_full = kernel_call(
        project_kernel,
        [
            shaped((count, MODEL_WIDTH), f32),
            shaped((count, MODEL_WIDTH), bf16),
            shaped((count, q_wide), bf16),
            shaped((MODEL_WIDTH, count), bf16),
            shaped((MODEL_WIDTH, MODEL_WIDTH), bf16),
        ],
        "project", 3e8,
    )(where, tokens_low, o, gains, low_out, out1, out2, out3)

    (low_down,) = gate([low_down], [half_across, o], "down_after_gate_up")
    half_beside = swap(half_across, "rep", extra)
    down2 = swap(low_down, "fsdp", 2)
    half_across3 = swap(half_across, "fsdp", 1)
    half_beside3 = swap(half_beside, "fsdp", 1)
    down3 = swap(down2, "fsdp", 1)
    gate_ups = {0: [low_gate_up], 1: [gate_up1], 2: [half_across, half_beside], 3: [half_across3, half_beside3]}
    downs = {0: low_down, 1: down1, 2: down2, 3: down3}

    gate_up_block = (groups, 2 * MODEL_WIDTH // groups, ff_rows)
    down_block = (groups, MODEL_WIDTH // groups, ff_rows)
    grad_gate_ups = {}
    grad_downs = {}
    total, accumulated = h, []
    for chunks in ((0, 1), (2,), (3,)):
        first, last = chunks[0] == 0, chunks[0] == 3
        blocks = [shaped(shape, bf16) for _ in chunks for shape in (gate_up_block, down_block)]
        results = kernel_call(
            functools.partial(feed_kernel, groups, chunks, first, last),
            [
                shaped((MODEL_WIDTH, count), bf16) if last else shaped((count, MODEL_WIDTH), f32),
                shaped((count, MODEL_WIDTH), f32),
                shaped((count, q_wide), f32),
            ] + blocks,
            "feed_" + "".join(str(j) for j in chunks), 2.1e9 * len(chunks),
            scratch=[] if first else [pltpu.VMEM((ff_rows, 2 * MODEL_WIDTH), bf16)],
            after=(gate_up_zero, down_zero) if last else (),
        )(
            where, a2, a2_shift, a2_turned, e, e_turned, total, *accumulated,
            *[part for j in chunks for part in gate_ups[j]], *[downs[j] for j in chunks],
        )
        total, accumulated = results[0], results[1:3]
        for c, j in enumerate(chunks):
            grad_gate_ups[j] = results[3 + 2 * c]
            grad_downs[j] = results[4 + 2 * c]
        if first:
            gate_up_zero = core_sum(grad_gate_ups, 0)
            down_zero = core_sum(grad_downs, 0)
    output = total.T

    gate_up_two = core_sum(grad_gate_ups, 2)
    down_two = core_sum(grad_downs, 2)
    gate_up_parts = replica_first(gate_up_zero, gate_up_two, extra, groups)
    down_parts = replica_first(down_zero, down_two, extra, groups)

    out_block = (groups, shard_rows, LANES)
    dh, dol, gain_two, *grad_outs = kernel_call(
        functools.partial(middle_kernel, groups),
        [
            shaped((count, MODEL_WIDTH), f32),
            shaped((count, q_wide), bf16),
            shaped((1, MODEL_WIDTH), f32),
        ] + [shaped(out_block, bf16)] * 4,
        "middle", 1e9,
        scratch=[pltpu.VMEM((MODEL_WIDTH, groups * LANES), bf16)],
    )(where, *accumulated, h, e, gains, o, inv, out_full)
    out_zero, out_two = core_sum(grad_outs, 0), core_sum(grad_outs, 2)
    out_parts = group_first(out_zero, out_two, extra, groups)

    dqs, dks, dvs = [], [], []
    for g, lifted in enumerate((lifted0, lifted1, lifted2)):
        dq, dk, dv = kernel_call(
            functools.partial(attention_back_kernel, g),
            [shaped((CLUSTER, count, LANES), f32), shaped((count, LANES), f32), shaped((count, LANES), f32)],
            "attention_back_" + str(g), 2e9,
            after=((gate_up_two, down_two), (out_zero, out_two, *dqs), tuple(dqs))[g],
        )(where, q, k, v, lifted, o, dol)
        dqs.append(dq)
        dks.append(dk)
        dvs.append(dv)

    message = 2 * groups * shard_rows + SMALL_ROWS
    sent, kept, tokens_grad = kernel_call(
        functools.partial(last_kernel, groups),
        [
            shaped((message, LANES), bf16),
            shaped((message, LANES), bf16),
            shaped((MODEL_WIDTH, count), bf16),
        ],
        "last", 2e9,
        scratch=[pltpu.VMEM((MODEL_WIDTH, groups * LANES), bf16)],
    )(where, *dqs, *dks, *dvs, cosine, sine, a, tokens_low, dh, weight_full, gains, gain_two)

    steps = [("fsdp", 1), ("fsdp", 2)]
    steps += [("rep", extra << i) for i in range(groups.bit_length() - 1)]
    for at, (axis, bit) in enumerate(steps):
        if at:
            part = (kept.shape[0] - SMALL_ROWS) // 2 + SMALL_ROWS
            sent, kept = kernel_call(
                halve_kernel, [shaped((part, LANES), bf16)] * 2, "halve_" + str(at), 1e5
            )(where, kept, came)
        came = swap(sent, axis, bit)
    qkv_parts = finish_parts(kept, came, extra)

    def weight_step(parts, dim, own, first, second, rate, name):
        parts = [part[0] for part in parts]
        if extra > 1:
            width = own.shape[dim]
            parts = [lax.dynamic_slice_in_dim(parts[0], (replica % extra) * width, width, dim)]
        return kernel_call(
            functools.partial(weight_step_kernel, rate, len(parts)),
            [shaped(first.shape, f32)] * 3, name, 1e6,
        )(where, *parts, own, first, second)

    gate_up_new = weight_step(
        finish_parts(*gate_up_parts, extra), 0, own_gate_up, gate_up_first.T, gate_up_second.T,
        rates[2], "gate_up_step",
    )
    down_new = weight_step(
        finish_parts(*down_parts, extra), 0, own_down, down_first.T, down_second.T, rates[3], "down_step"
    )
    out_new = weight_step(
        finish_parts(*out_parts, extra), 1, own_out, out_first, out_second, rates[1], "out_step"
    )
    if extra > 1:
        (term,) = qkv_parts
        width = own_qkv.shape[1]
        own = lax.dynamic_slice_in_dim(term[:-SMALL_ROWS], (replica % extra) * width, width, 1)
        own = jnp.pad(own, ((0, 0), (0, LANES - width)))
        qkv_parts = [jnp.concatenate([own, term[-SMALL_ROWS:]])]
    vectors = (norm_gains, gains_first, gains_second, projection_bias, bias_first_moment, bias_second_moment)
    news = kernel_call(
        functools.partial(final_kernel, (rates[0], rates[4], rates[5]), len(qkv_parts)),
        [shaped(own_qkv.shape, f32)] * 3 + [shaped(vector.shape, f32) for vector in vectors],
        "final_step", 1e6,
    )(where, *qkv_parts, own_qkv, projection_first_moment, projection_second_moment, *vectors)
    return (
        output,
        tokens_grad.T,
        *news[:3],
        *out_new,
        *[new.T for new in gate_up_new],
        *[new.T for new in down_new],
        *news[3:],
    )


def solution(mesh):
    rows = P(("rep", "fsdp"), None)
    weight = P("fsdp", None)
    state = P("fsdp", "rep")
    vector = P("fsdp")
    states = (state,) * 4 + (vector,) * 2
    in_specs = (rows, P(("rep", "fsdp")), rows) + (weight,) * 4 + (vector,) * 2 + states + states
    out_specs = (rows, rows) + (state,) * 12 + (vector,) * 6
    return jax.shard_map(
        on_device, mesh=mesh, in_specs=in_specs, out_specs=out_specs, check_vma=False
    )
```

```python
import functools
import math

import jax
import jax.numpy as jnp
from jax import lax
from jax.experimental import pallas as pl
from jax.experimental.pallas import tpu as pltpu
from jax.sharding import PartitionSpec as P

MODEL_WIDTH = 576
QUERY_HEADS = 9
KEY_VALUE_HEADS = 3
HEAD_SIZE = 64
FF = 1536
STEP = 10

norm_eps = 1e-05
rope_base = 100000.0
beta_one = 0.9
beta_two = 0.95
adam_eps = 1e-08
decay_rate = 0.1

LANES = 128
QKV_WIDTH = (QUERY_HEADS + 2 * KEY_VALUE_HEADS) * HEAD_SIZE
CLUSTER = QUERY_HEADS // KEY_VALUE_HEADS
SMALL_ROWS = 32
ROW_BLOCK = 256
OUT_ROW = MODEL_WIDTH // 4
bf16 = jnp.bfloat16
f32 = jnp.float32


def learn_rates():
    out_fan = max(QUERY_HEADS * HEAD_SIZE // 16, 1)
    return (MODEL_WIDTH ** (-0.5), out_fan ** (-0.5), MODEL_WIDTH ** (-0.5), FF ** (-0.5), 0.5, 0.5)


def adam_update(weight, first_moment, second_moment, gradient, step_rate):
    first_new = beta_one * first_moment + (1.0 - beta_one) * gradient
    second_new = beta_two * second_moment + (1.0 - beta_two) * gradient * gradient
    first_fix = 1.0 - beta_one**STEP
    second_fix = 1.0 - beta_two**STEP
    direction = first_new / first_fix / (jnp.sqrt(second_new / second_fix) + adam_eps)
    return (first_new, second_new, weight - step_rate * (direction + decay_rate * weight))


def dot_plain(left, right):
    return lax.dot_general(left, right, (((1,), (0,)), ((), ())), preferred_element_type=f32)


def dot_last(left, right):
    return lax.dot_general(left, right, (((1,), (1,)), ((), ())), preferred_element_type=f32)


def dot_first(left, right):
    return lax.dot_general(left, right, (((0,), (0,)), ((), ())), preferred_element_type=f32)


def kernel_call(body, outs, name, time, scratch=(), vmem=12, after=()):
    def call(scalars, *arrays):
        count = len(after)

        def run(*refs):
            body(refs[0], *refs[1 + count :])

        return pl.pallas_call(
            run,
            out_shape=tuple(outs),
            in_specs=[pl.BlockSpec(memory_space=pltpu.SMEM)]
            + [pl.BlockSpec(memory_space=pl.ANY)] * count
            + [pl.BlockSpec(memory_space=pltpu.VMEM)] * len(arrays),
            out_specs=tuple(pl.BlockSpec(memory_space=pltpu.VMEM) for _ in outs),
            scratch_shapes=list(scratch),
            name=name,
            compiler_params=pltpu.CompilerParams(vmem_limit_bytes=vmem * 2**20),
            cost_estimate=pl.CostEstimate(
                flops=int(time * 1.15e9), bytes_accessed=0, transcendentals=0
            ),
        )(scalars, *after, *arrays)

    return call


def gate(values, after, name):
    def nothing(*refs):
        pass

    result = pl.pallas_call(
        nothing,
        out_shape=tuple(shaped(v.shape, v.dtype) for v in values),
        in_specs=[pl.BlockSpec(memory_space=pl.ANY)] * (len(values) + len(after)),
        out_specs=tuple(pl.BlockSpec(memory_space=pl.ANY) for _ in values),
        input_output_aliases={i: i for i in range(len(values))},
        name=name,
        compiler_params=pltpu.CompilerParams(vmem_limit_bytes=2**20),
        cost_estimate=pl.CostEstimate(flops=0, bytes_accessed=0, transcendentals=0),
    )(*values, *after)
    return list(result)


def shaped(shape, dtype):
    return jax.ShapeDtypeStruct(tuple(shape), dtype)


def lane_index(shape):
    return lax.broadcasted_iota(jnp.int32, shape, len(shape) - 1)


def lower_half(shape):
    return lane_index(shape) < HEAD_SIZE


def swap_pairs(block):
    first = (lane_index(block.shape) & (HEAD_SIZE // 2)) == 0
    ahead = pltpu.roll(block, LANES - HEAD_SIZE // 2, 1)
    behind = pltpu.roll(block, HEAD_SIZE // 2, 1)
    return jnp.where(first, ahead, behind)


def both_halves(block, upper):
    other = pltpu.roll(block, HEAD_SIZE, 1)
    low = lower_half(block.shape)
    return jnp.where(low, other, block) if upper else jnp.where(low, block, other)


def cut_lanes(blocks, start, width):
    at, offset = divmod(start, LANES)
    lane = lane_index(blocks[0].shape)
    part = blocks[at]
    if offset:
        part = pltpu.roll(part, LANES - offset, 1)
        if offset + width > LANES:
            after = pltpu.roll(blocks[at + 1], LANES - offset, 1)
            part = jnp.where(lane < LANES - offset, part, after)
    if width < LANES:
        part = jnp.where(lane < width, part, 0.0)
    return part


def lane_blocks(values):
    width = values.shape[1]
    full = width // LANES
    blocks = [values[:, i * LANES : (i + 1) * LANES] for i in range(full)]
    if width % LANES:
        rest = values[:, full * LANES :]
        fill = jnp.zeros((values.shape[0], LANES - width % LANES), values.dtype)
        blocks.append(jnp.concatenate([rest, fill], axis=1))
    return blocks


def block_place(block, mine, groups):
    away = mine ^ block
    place = 0
    bit = 1
    while bit < groups:
        place = place * 2 + jnp.where((away & bit) == 0, 0, 1)
        bit *= 2
    return place


def own_rows(ref, replica, width):
    if width % 8 == 0:
        return ref[pl.ds(pl.multiple_of(replica * width, 8), width), :]
    rows = ref.shape[0]
    return pltpu.roll(ref[...], rows - replica * width, 0)[:width]


def pack_kernel(where_ref, qkv_ref, gains_ref, bias_ref, pack_ref):
    rows = qkv_ref.shape[0]
    pack_ref[:rows, :QKV_WIDTH] = qkv_ref[...].astype(bf16)
    pack_ref[:rows, QKV_WIDTH:] = jnp.zeros((rows, pack_ref.shape[1] - QKV_WIDTH), bf16)
    spare = pack_ref.shape[0] - rows
    bias, gains = (ref[...].reshape(1, ref.shape[0]) for ref in (bias_ref, gains_ref))
    extra = jnp.concatenate(lane_blocks(bias) + lane_blocks(gains), axis=1)
    line = jnp.concatenate(
        [extra, jnp.zeros((1, pack_ref.shape[1] - extra.shape[1]), f32)], axis=1
    )
    pack_ref[rows:, :] = jnp.broadcast_to(line, (spare, line.shape[1])).astype(bf16)


def tables_kernel(
    where_ref, segments_ref, tokens_turned_ref, e_turned_ref, qkv_ref, out_ref, gate_up_ref, down_ref,
    cos_ref, sin_ref, mask_ref, tokens_ref, e_ref, low_out_ref, low_gate_up_ref, half_ref, low_down_ref,
    own_qkv_ref, own_out_ref, own_gate_up_ref, own_down_ref, turned_ref,
):
    tokens = segments_ref.shape[0]
    row = segments_ref[...].reshape(1, tokens).astype(f32)
    column = jnp.broadcast_to(row, (LANES, tokens)).T[:, :1]
    query = lax.broadcasted_iota(jnp.int32, (tokens, tokens), 0)
    key = lax.broadcasted_iota(jnp.int32, (tokens, tokens), 1)
    same = column == row
    earlier = jnp.sum(jnp.where(same & (key < query), 1.0, 0.0), axis=1, keepdims=True)
    mask_ref[...] = jnp.where(same & (key <= query), 0.0, -1e30)
    lane = lane_index((tokens, LANES))
    exponent = (lane & (HEAD_SIZE // 2 - 1)).astype(f32) * (2.0 / HEAD_SIZE)
    frequency = jnp.exp(exponent * (-math.log(rope_base)))
    angles = earlier * frequency
    cos_ref[...] = jnp.cos(angles)
    sine = jnp.sin(angles)
    sin_ref[...] = jnp.where((lane & (HEAD_SIZE // 2)) == 0, -sine, sine)
    tokens_ref[...] = tokens_turned_ref[...].astype(f32).T.astype(bf16)
    e_ref[...] = e_turned_ref[...].astype(f32).T.astype(bf16)

    low_out_ref[...] = out_ref[...].astype(bf16)
    gate_up = gate_up_ref[...]
    low_gate_up_ref[...] = gate_up.astype(bf16)
    rows = half_ref.shape[0]
    start = pl.multiple_of((where_ref[1] & 1) * rows, 16)
    half_ref[...] = gate_up_ref[pl.ds(start, rows), :].astype(bf16)
    low_down_ref[...] = down_ref[...].astype(bf16)
    replica = where_ref[2]
    turned_ref[...] = gate_up.T
    width = own_gate_up_ref.shape[0]
    own_gate_up_ref[...] = own_rows(turned_ref, replica, width)
    width = own_down_ref.shape[0]
    own_down_ref[...] = own_rows(down_ref, replica, width)
    for ref, own in ((qkv_ref, own_qkv_ref), (out_ref, own_out_ref)):
        width = own.shape[1]
        wide = jnp.concatenate(lane_blocks(ref[...]), axis=1)
        own[...] = pltpu.roll(wide, wide.shape[1] - replica * width, 1)[:, :width]


def forward_kernel(
    where_ref, tokens_ref, cos_ref, sin_ref, mask_ref, pack0, pack1, pack2, pack3,
    a_ref, q_ref, k_ref, v_ref, e0_ref, e1_ref, e2_ref, inv_ref, o_ref, weight_ref, gains_ref,
):
    me = where_ref[0]
    tokens = tokens_ref.shape[0]
    shard_rows = MODEL_WIDTH // 4
    packs = (pack0, pack1, pack2, pack3)
    lines = []
    for j in range(4):
        start = pl.multiple_of((me ^ j) * shard_rows, 16)
        weight_ref[pl.ds(start, shard_rows), :] = packs[j][:shard_rows, :]
        lines.append(packs[j][shard_rows:, :].astype(f32)[:1, :])
    bias_wide = lane_index((1, LANES)) * 0.0
    ordered = []
    for s in range(4):
        line = jnp.where((me ^ s) == 0, lines[0], 0.0)
        for j in range(1, 4):
            line = jnp.where((me ^ s) == j, lines[j], line)
        ordered.append(line)
    bias_blocks = [bias_wide for _ in range(weight_ref.shape[1] // LANES)]
    gain_blocks = [[bias_wide for _ in range(5)] for _ in range(2)]
    lane = lane_index((1, LANES))

    def put(blocks, source, width, start):
        done = 0
        while done < width:
            at, offset = divmod(start + done, LANES)
            count = min(LANES - offset, width - done)
            from_at, from_offset = divmod(done, LANES)
            count = min(count, LANES - from_offset)
            turn = (offset - from_offset) % LANES
            part = source[from_at]
            if turn:
                part = pltpu.roll(part, turn, 1)
            blocks[at] = jnp.where((lane >= offset) & (lane < offset + count), part, blocks[at])
            done += count

    bias_each = QKV_WIDTH // 4
    gain_each = 2 * MODEL_WIDTH // 4
    bias_lanes = -(-bias_each // LANES) * LANES
    for s in range(4):
        pieces = [ordered[s][:, i * LANES : (i + 1) * LANES] for i in range(8)]
        put(bias_blocks, pieces, bias_each, s * bias_each)
        put(gain_blocks[s // 2], pieces[bias_lanes // LANES :], gain_each, (s % 2) * gain_each)
    gains = [jnp.concatenate(blocks, axis=1) for blocks in gain_blocks]
    for i in range(2):
        gains_ref[i : i + 1, :] = gains[i]
    bias = jnp.concatenate(bias_blocks, axis=1)

    x = tokens_ref[...].astype(f32)
    inverse = lax.rsqrt(jnp.mean(x * x, axis=1, keepdims=True) + norm_eps)
    a = (x * inverse * gains[0][:, :MODEL_WIDTH]).astype(bf16)
    a_ref[...] = a
    p = dot_plain(a, weight_ref[...]) + bias
    cosine, sine = cos_ref[...], sin_ref[...]
    blocks = [p[:, i * LANES : (i + 1) * LANES] for i in range(8)]
    for i in range(6):
        blocks[i] = blocks[i] * cosine + swap_pairs(blocks[i]) * sine
    low = lower_half((tokens, LANES))
    for i in range(5):
        scaled = blocks[i] * HEAD_SIZE ** (-0.5)
        if i == 4:
            scaled = jnp.where(low, scaled, 0.0)
        q_ref[:, i * LANES : (i + 1) * LANES] = scaled.astype(bf16)
    keys = [both_halves(blocks[4], True), both_halves(blocks[5], False), both_halves(blocks[5], True)]
    values = [both_halves(blocks[6], False), both_halves(blocks[6], True), both_halves(blocks[7], False)]
    for g in range(KEY_VALUE_HEADS):
        k_ref[:, g * LANES : (g + 1) * LANES] = keys[g].astype(bf16)
        v_ref[:, g * LANES : (g + 1) * LANES] = values[g].astype(bf16)

    e_refs = (e0_ref, e1_ref, e2_ref)
    step = ROW_BLOCK
    low = lower_half((step, LANES))
    for at in range(tokens // step):
        rows = slice(at * step, (at + 1) * step)
        seen = (at + 1) * step
        mixed = []
        inverses = []
        for g in range(KEY_VALUE_HEADS):
            stack = head_stack(q_ref, rows, g)
            scores = dot_last(stack, k_ref[:seen, g * LANES : (g + 1) * LANES])
            scores = scores.reshape(CLUSTER, step, seen) + mask_ref[rows, :seen][None]
            lifted = jnp.exp(scores - jnp.max(scores, axis=2, keepdims=True))
            total = jnp.sum(lifted, axis=2, keepdims=True)
            kept = lifted.astype(bf16)
            e_refs[g][:, rows, :seen] = kept
            gathered = dot_plain(
                kept.reshape(CLUSTER * step, seen), v_ref[:seen, g * LANES : (g + 1) * LANES]
            ).reshape(CLUSTER, step, LANES)
            inverse_total = jnp.broadcast_to(1.0 / total, gathered.shape)
            gathered = gathered * inverse_total
            for t in range(CLUSTER):
                mixed.append(gathered[t])
                inverses.append(inverse_total[t])
        for i in range(5):
            second = mixed[2 * i + 1] if 2 * i + 1 < QUERY_HEADS else 0.0
            part = jnp.where(low, mixed[2 * i], second)
            o_ref[rows, i * LANES : (i + 1) * LANES] = part.astype(bf16)
            second = inverses[2 * i + 1] if 2 * i + 1 < QUERY_HEADS else 0.0
            inv_ref[rows, i * LANES : (i + 1) * LANES] = jnp.where(low, inverses[2 * i], second)


def project_kernel(
    where_ref, tokens_ref, o_ref, gains_ref, out0, out1, out2, out3,
    h_ref, a2_ref, a2_shift_ref, a2_turned_ref, out_weight_ref,
):
    me = where_ref[0]
    tokens = tokens_ref.shape[0]
    shard_rows = out0.shape[0]
    for j, out in enumerate((out0, out1, out2, out3)):
        start = pl.multiple_of((me ^ j) * shard_rows, 16)
        out_weight_ref[pl.ds(start, shard_rows), :] = out[...]
    x = tokens_ref[...].astype(f32)
    h = x + dot_plain(o_ref[:, :MODEL_WIDTH], out_weight_ref[...])
    h_ref[...] = h
    inverse = lax.rsqrt(jnp.mean(h * h, axis=1, keepdims=True) + norm_eps)
    a2 = h * inverse * gains_ref[1:2, :MODEL_WIDTH]
    a2_ref[...] = a2.astype(bf16)
    a2_blocks = lane_blocks(a2)
    low = lower_half((tokens, LANES))
    before = jnp.zeros((tokens, LANES), f32)
    for i in range(5):
        part = jnp.where(low, pltpu.roll(before, HEAD_SIZE, 1), pltpu.roll(a2_blocks[i], HEAD_SIZE, 1))
        a2_shift_ref[:, i * LANES : (i + 1) * LANES] = part.astype(bf16)
        before = a2_blocks[i]
    a2_turned_ref[...] = a2.T.astype(bf16)


def head_stack(ref, rows, g):
    parts = []
    for t in range(CLUSTER):
        head = g * CLUSTER + t
        block = ref[rows, (head // 2) * LANES : (head // 2 + 1) * LANES]
        low = lower_half(block.shape)
        keep = low if head % 2 == 0 else jnp.logical_not(low)
        parts.append(jnp.where(keep, block, jnp.zeros_like(block)))
    return jnp.concatenate(parts, axis=0)


def feed_kernel(groups, chunks, first, last, halved, *refs):
    refs = list(refs)

    def take(count):
        taken = refs[:count]
        del refs[:count]
        return taken

    (where_ref, a2_ref, a2_shift_ref, a2_turned_ref, e_ref, e_turned_ref, base_ref) = take(7)
    gate_in, shift_in = (None, None) if first else take(2)
    gate_ups = [take(2 if halved else 1) for _ in chunks]
    downs = take(len(chunks))
    total_ref, gate_acc, shift_acc = take(3)
    mine = where_ref[1]
    total = base_ref[...]
    for c in range(len(chunks)):
        grad_gate_up_ref, grad_down_ref = take(2)
        down = downs[c]
        if not halved:
            gate_up = gate_ups[c][0]
        else:
            gate_up = refs[-1]
            rows = gate_ups[c][0].shape[0]
            for half in range(2):
                start = pl.multiple_of(((mine & 1) ^ half) * rows, 16)
                gate_up[pl.ds(start, rows), :] = gate_ups[c][half][...]
        gate_weights = gate_up[:, :MODEL_WIDTH]
        up_weights = gate_up[:, MODEL_WIDTH - HEAD_SIZE :]
        gate = dot_last(a2_ref[...], gate_weights)
        up = dot_last(a2_shift_ref[...], up_weights)
        sigma = 1.0 / (1.0 + jnp.exp(-gate))
        active = gate * sigma
        hidden = (active * up).astype(bf16)
        total = total + dot_last(hidden, down[...])
        grad_hidden = dot_plain(e_ref[...], down[...])
        grad_gate = (grad_hidden * up * (sigma * (1.0 + gate * (1.0 - sigma)))).astype(bf16)
        grad_up = (grad_hidden * active).astype(bf16)
        width = grad_gate_up_ref.shape[1]
        half = groups // 2
        for turned, offset in ((dot_plain(a2_turned_ref[...], grad_gate), 0),
                               (dot_plain(a2_turned_ref[...], grad_up), half)):
            for b in range(half):
                grad_gate_up_ref[block_place(b + offset, mine, groups)] = turned[
                    b * width : (b + 1) * width
                ].astype(bf16)
        turned = dot_plain(e_turned_ref[...], hidden)
        width = grad_down_ref.shape[1]
        for b in range(groups):
            grad_down_ref[block_place(b, mine, groups)] = turned[
                b * width : (b + 1) * width
            ].astype(bf16)
        gate_part = dot_plain(grad_gate, gate_weights)
        shift_part = dot_plain(grad_up, up_weights)
        if c == 0 and first:
            gate_acc[...] = gate_part
            shift_acc[...] = shift_part
        elif c == 0:
            gate_acc[...] = gate_in[...] + gate_part
            shift_acc[...] = shift_in[...] + shift_part
        else:
            gate_acc[...] = gate_acc[...] + gate_part
            shift_acc[...] = shift_acc[...] + shift_part
    total_ref[...] = total.T.astype(bf16) if last else total


def middle_kernel(
    groups, where_ref, gate_acc, shift_acc, h_ref, e_ref, gains_ref, o_ref, inv_ref, out_weight_ref,
    dh_ref, dol_ref, small_ref, grad0, grad1, grad2, grad3, held_ref,
):
    me, mine = where_ref[0], where_ref[1]
    tokens = h_ref.shape[0]
    gain = gains_ref[1:2, :MODEL_WIDTH]
    h = h_ref[...]
    low = lower_half((tokens, LANES))
    shifted = [shift_acc[:, i * LANES : (i + 1) * LANES] for i in range(5)]
    parts = []
    for i in range(5):
        part = pltpu.roll(shifted[i], HEAD_SIZE, 1)
        after = pltpu.roll(shifted[i + 1], HEAD_SIZE, 1) if i < 4 else 0.0
        parts.append(jnp.where(low, part, after))
    da2 = gate_acc[...] + jnp.concatenate(parts, axis=1)[:, :MODEL_WIDTH]
    inverse = lax.rsqrt(jnp.mean(h * h, axis=1, keepdims=True) + norm_eps)
    weighted = da2 * gain
    inner = jnp.mean(weighted * h, axis=1, keepdims=True)
    dh = e_ref[...].astype(f32) + inverse * weighted - h * (inverse * inverse * inverse) * inner
    dh_ref[...] = dh
    small_ref[...] = jnp.sum(da2 * h * inverse, axis=0, keepdims=True)
    dhl = dh.astype(bf16)
    spread = dhl.astype(f32)
    blocks = lane_blocks(spread)
    width = MODEL_WIDTH // groups
    chosen = jnp.concatenate(
        [cut_lanes(blocks, b * width, width).astype(bf16) for b in range(groups)], axis=1
    )
    held_ref[...] = dot_first(o_ref[:, :MODEL_WIDTH], chosen).astype(bf16)
    rows = grad0.shape[1]
    for j, grad in enumerate((grad0, grad1, grad2, grad3)):
        start = pl.multiple_of((me ^ j) * rows, 16)
        for b in range(groups):
            grad[block_place(b, mine, groups)] = held_ref[
                pl.ds(start, rows), b * LANES : (b + 1) * LANES
            ]
    dol = dot_last(dhl, out_weight_ref[...])
    dol_blocks = lane_blocks(dol.astype(bf16).astype(f32))
    for i in range(5):
        lanes = slice(i * LANES, (i + 1) * LANES)
        dol_ref[:, lanes] = (dol_blocks[i] * inv_ref[:, lanes]).astype(bf16)


def attention_back_kernel(g, where_ref, q_ref, k_ref, v_ref, lifted_ref, o_ref, dol_ref, dq_ref, dk_ref, dv_ref):
    tokens = q_ref.shape[0]
    step = ROW_BLOCK
    lanes = slice(g * LANES, (g + 1) * LANES)
    dk = None
    dv = None
    for at in reversed(range(tokens // step)):
        rows = slice(at * step, (at + 1) * step)
        seen = (at + 1) * step
        q_stack = head_stack(q_ref, rows, g)
        o_stack = head_stack(o_ref, rows, g)
        dol_stack = head_stack(dol_ref, rows, g)
        lifted = lifted_ref[:, rows, :seen].reshape(CLUSTER * step, seen)
        inner = jnp.sum(o_stack.astype(f32) * dol_stack.astype(f32), axis=1, keepdims=True)
        grad = dot_last(dol_stack, v_ref[:seen, lanes])
        dsl = (lifted.astype(f32) * (grad - inner)).astype(bf16)
        dq = dot_plain(dsl, k_ref[:seen, lanes]) * HEAD_SIZE ** (-0.5)
        dq_ref[:, rows, :] = dq.reshape(CLUSTER, step, LANES)
        dk_part = dot_first(q_stack, dsl)
        dv_part = dot_first(dol_stack, lifted)
        if dk is None:
            dk, dv = dk_part, dv_part
        else:
            dk = jnp.concatenate([dk[:, :seen] + dk_part, dk[:, seen:]], axis=1)
            dv = jnp.concatenate([dv[:, :seen] + dv_part, dv[:, seen:]], axis=1)
    dk = dk.T
    dv = dv.T
    dk_ref[...] = dk + pltpu.roll(dk, HEAD_SIZE, 1)
    dv_ref[...] = dv + pltpu.roll(dv, HEAD_SIZE, 1)


def last_kernel(
    groups, where_ref, dq0, dq1, dq2, dk0, dk1, dk2, dv0, dv1, dv2, cos_ref, sin_ref,
    a_ref, tokens_ref, dh_ref, weight_ref, gains_ref, gain_two_ref,
    sent_ref, kept_ref, tokens_grad_ref, held_ref,
):
    me, mine = where_ref[0], where_ref[1]
    tokens = tokens_ref.shape[0]
    low = lower_half((tokens, LANES))
    heads = [ref[t] for ref in (dq0, dq1, dq2) for t in range(CLUSTER)]
    blocks = [jnp.where(low, heads[2 * i], heads[2 * i + 1]) for i in range(4)]
    blocks.append(jnp.where(low, heads[8], dk0[...]))
    blocks.append(jnp.where(low, dk1[...], dk2[...]))
    cosine, sine = cos_ref[...], sin_ref[...]
    blocks = [block * cosine - swap_pairs(block) * sine for block in blocks]
    blocks.append(jnp.where(low, dv0[...], dv1[...]))
    blocks.append(jnp.where(low, dv2[...], 0.0))
    low_blocks = [block.astype(bf16) for block in blocks]
    blocks = [block.astype(f32) for block in low_blocks]
    dpl = jnp.concatenate(low_blocks, axis=1)
    width = QKV_WIDTH // groups
    chosen = jnp.concatenate(
        [cut_lanes(blocks, b * width, width).astype(bf16) for b in range(groups)], axis=1
    )
    held_ref[...] = dot_first(a_ref[...], chosen).astype(bf16)
    rows = held_ref.shape[0] // 4
    for j in range(4):
        start = pl.multiple_of((me ^ j) * rows, 16)
        target = sent_ref if j % 2 else kept_ref
        half = groups // 2
        for b in range(groups):
            place = block_place(b, mine, groups)
            beyond = jnp.where((place & half) == 0, 0, half)
            to = pl.multiple_of((place + beyond + (j // 2) * half) * rows, 16)
            target[pl.ds(to, rows), :] = held_ref[pl.ds(start, rows), b * LANES : (b + 1) * LANES]

    bias_blocks = [jnp.sum(block, axis=0, keepdims=True) for block in blocks]
    x = tokens_ref[...].astype(f32)
    inverse = lax.rsqrt(jnp.mean(x * x, axis=1, keepdims=True) + norm_eps)
    da = dot_last(dpl, weight_ref[...])
    gain_one_blocks = lane_blocks(jnp.sum(da * x * inverse, axis=0, keepdims=True))
    gain_two_blocks = lane_blocks(gain_two_ref[...])
    weighted = da * gains_ref[0:1, :MODEL_WIDTH]
    inner = jnp.mean(weighted * x, axis=1, keepdims=True)
    tokens_grad = dh_ref[...] + inverse * weighted - x * (inverse * inverse * inverse) * inner
    tokens_grad_ref[...] = tokens_grad.T.astype(bf16)

    gain_each = 2 * MODEL_WIDTH // 4
    bias_each = QKV_WIDTH // 4
    lines = []
    for s in range(4):
        source = gain_one_blocks if s < 2 else gain_two_blocks
        count = 0
        for t in range(0, gain_each, LANES):
            lines.append(cut_lanes(source, (s % 2) * gain_each + t, min(LANES, gain_each - t)))
            count += 1
        for t in range(0, bias_each, LANES):
            lines.append(cut_lanes(bias_blocks, s * bias_each + t, min(LANES, bias_each - t)))
            count += 1
        lines += [jnp.zeros((1, LANES), f32)] * (SMALL_ROWS // 4 - count)
    small = jnp.concatenate(lines, axis=0).astype(bf16)
    sent_ref[2 * groups * rows :, :] = small
    kept_ref[2 * groups * rows :, :] = small


def halve_kernel(where_ref, kept_ref, came_ref, sent_ref, left_ref):
    part = left_ref.shape[0] - SMALL_ROWS
    total = kept_ref[...].astype(f32) + came_ref[...].astype(f32)
    total = total.astype(bf16)
    left_ref[:part, :] = total[:part]
    left_ref[part:, :] = total[2 * part :]
    sent_ref[...] = total[part:]


def fold_first_kernel(
    where_ref, gate_kept, gate_came, gate_across, down_kept, down_came, out_kept, out_came,
    qkv_kept, qkv_came, left_ref, sent_ref,
):
    blocks, rows = gate_kept.shape[:2]
    half = blocks // 2
    thin = down_kept.shape[1]
    qkv = qkv_kept[...].astype(f32) + qkv_came[...].astype(f32)
    small = qkv[blocks * rows :].astype(bf16)
    for b in range(blocks):
        ref, at = (left_ref, b) if b < half else (sent_ref, b - half)
        gate_up = gate_kept[b].astype(f32) + gate_came[b].astype(f32) + gate_across[b].astype(f32)
        ref[at, :rows, :] = gate_up.astype(bf16)
        out = out_kept[b].astype(f32) + out_came[b].astype(f32)
        ref[at, rows : 2 * rows, :LANES] = out.astype(bf16)
        ref[at, rows : 2 * rows, LANES : 2 * LANES] = qkv[b * rows : (b + 1) * rows].astype(bf16)
        ref[at, rows : 2 * rows, 2 * LANES :] = jnp.zeros((rows, LANES), bf16)
        if at == 0:
            ref[at, rows : rows + SMALL_ROWS, 2 * LANES :] = small
        down = down_kept[b].astype(f32) + down_came[b].astype(f32)
        spare = ref.shape[1] - 2 * rows - thin
        down = jnp.concatenate([down, jnp.zeros((spare, down.shape[1]), f32)], axis=0)
        ref[at, 2 * rows :, :] = down.astype(bf16)


def fold_kernel(where_ref, kept_ref, came_ref, left_ref, sent_ref):
    half = left_ref.shape[0]
    for b in range(2 * half):
        total = (kept_ref[b].astype(f32) + came_ref[b].astype(f32)).astype(bf16)
        if b < half:
            left_ref[b] = total
        else:
            sent_ref[b - half] = total
        if b == 0:
            small = total[OUT_ROW : OUT_ROW + SMALL_ROWS, 2 * LANES :]
    sent_ref[0, OUT_ROW : OUT_ROW + SMALL_ROWS, 2 * LANES :] = small


def final_kernel(step_rates, parts, where_ref, *refs):
    total = refs[0][0].astype(f32)
    for ref in refs[1:parts]:
        total = total + ref[0].astype(f32)
    refs = refs[parts:]
    count = len(refs) // 2
    ins, outs = refs[:count], refs[count:]

    def step(at, gradient, rate):
        new = adam_update(ins[at][...], ins[at + 1][...], ins[at + 2][...], gradient, rate)
        for i in range(3):
            outs[at + i][...] = new[i]

    middle = total[OUT_ROW : 2 * OUT_ROW]
    step(0, middle[:, LANES : LANES + ins[0].shape[1]], step_rates[0])
    step(3, middle[:, : ins[3].shape[1]], step_rates[1])
    step(6, total[: ins[6].shape[0]], step_rates[2])
    step(9, total[2 * OUT_ROW : 2 * OUT_ROW + ins[9].shape[0]], step_rates[3])
    me = where_ref[0]
    each = SMALL_ROWS // 4
    small = middle[:SMALL_ROWS, 2 * LANES :]
    mine = small[:each]
    for s in range(1, 4):
        mine = jnp.where(me == s, small[s * each : (s + 1) * each], mine)
    line = 0
    for at in (12, 15):
        width = ins[at].shape[0]
        lines = -(-width // LANES)
        wide = jnp.concatenate([mine[line + t : line + t + 1, :] for t in range(lines)], axis=1)
        line += lines
        step(at, wide[:, :width].reshape(width), step_rates[4 if at == 12 else 5])


def swap(values, axis, bit):
    size = lax.axis_size(axis)
    return lax.ppermute(values, axis, [(i, i ^ bit) for i in range(size)])


def add_low(left, right):
    return (left.astype(f32) + right.astype(f32)).astype(bf16)


def halves(values):
    half = values.shape[0] // 2
    return values[:half], values[half:]


def core_sum(chunks, at):
    return add_low(chunks[at], swap(chunks[at + 1], "fsdp", 1))


def own_block(total, extra, widths):
    bit = 1
    while bit < extra:
        total = total + swap(total, "rep", bit)
        bit *= 2
    at = lax.axis_index("rep") % extra
    qkv, out, gate_up, down = widths

    def take(part, width, dim):
        own = lax.dynamic_slice_in_dim(part, at * width, width, dim)
        fill = [(0, 0), (0, 0)]
        fill[dim] = (0, part.shape[dim] - width)
        return jnp.pad(own, fill)

    middle = total[OUT_ROW : 2 * OUT_ROW]
    middle = jnp.concatenate(
        [take(middle[:, :LANES], out, 1), take(middle[:, LANES : 2 * LANES], qkv, 1), middle[:, 2 * LANES :]],
        axis=1,
    )
    return jnp.concatenate(
        [take(total[:OUT_ROW], gate_up, 0), middle, take(total[2 * OUT_ROW :], down, 0)]
    )


def on_device(
    tokens,
    segments,
    cotangent,
    projection_weight,
    out_weight,
    gate_up_weight,
    down_weight,
    norm_gains,
    projection_bias,
    projection_first_moment,
    out_first,
    gate_up_first,
    down_first,
    gains_first,
    bias_first_moment,
    projection_second_moment,
    out_second,
    gate_up_second,
    down_second,
    gains_second,
    bias_second_moment,
):
    count = tokens.shape[0]
    replicas = lax.axis_size("rep")
    groups = min(replicas, 8)
    extra = replicas // groups
    replica = lax.axis_index("rep")
    where = jnp.stack([lax.axis_index("fsdp"), replica // extra, replica]).astype(jnp.int32)
    rates = learn_rates()
    wide = 1024
    shard_rows, ff_rows = projection_weight.shape[0], gate_up_weight.shape[0]
    q_wide = 5 * LANES
    kv_wide = KEY_VALUE_HEADS * LANES
    tokens_turned, e_turned, down_turned = tokens.T, cotangent.T, down_weight.T

    pack = kernel_call(
        pack_kernel, [shaped((shard_rows + 16, wide), bf16)], "pack_attention", 1.0
    )(where, projection_weight, norm_gains, projection_bias)[0]
    pack2 = swap(pack, "fsdp", 2)
    pack1 = swap(pack, "fsdp", 1)

    (cosine, sine, mask, tokens_low, e, low_out, low_gate_up, half, low_down,
     own_qkv, own_out, own_gate_up, own_down) = kernel_call(
        tables_kernel,
        [
            shaped((count, LANES), f32),
            shaped((count, LANES), f32),
            shaped((count, count), f32),
            shaped((count, MODEL_WIDTH), bf16),
            shaped((count, MODEL_WIDTH), bf16),
            shaped(out_weight.shape, bf16),
            shaped((ff_rows, 2 * MODEL_WIDTH), bf16),
            shaped((ff_rows // 2, 2 * MODEL_WIDTH), bf16),
            shaped((MODEL_WIDTH, ff_rows), bf16),
            shaped(projection_first_moment.shape, f32),
            shaped(out_first.shape, f32),
            shaped(gate_up_first.shape[::-1], f32),
            shaped(down_first.shape[::-1], f32),
        ],
        "tables", 3.0,
        scratch=[pltpu.VMEM((2 * MODEL_WIDTH, ff_rows), f32)], after=(pack,),
    )(
        where, segments, tokens_turned, e_turned,
        projection_weight, out_weight, gate_up_weight, down_turned,
    )

    pack2, low_out, half = gate([pack2, low_out, half], [pack1, cosine], "after_pack")
    pack3 = swap(pack2, "fsdp", 1)
    out2 = swap(low_out, "fsdp", 2)
    half_across = swap(half, "fsdp", 2)
    out1 = swap(low_out, "fsdp", 1)
    gate_up1 = swap(low_gate_up, "fsdp", 1)
    down1 = swap(low_down, "fsdp", 1)

    (a, q, k, v, lifted0, lifted1, lifted2, inv, o, weight_full, gains) = kernel_call(
        forward_kernel,
        [
            shaped((count, MODEL_WIDTH), bf16),
            shaped((count, q_wide), bf16),
            shaped((count, kv_wide), bf16),
            shaped((count, kv_wide), bf16),
        ]
        + [shaped((CLUSTER, count, count), bf16)] * 3
        + [
            shaped((count, q_wide), f32),
            shaped((count, q_wide), bf16),
            shaped((MODEL_WIDTH, wide), bf16),
            shaped((2, q_wide), f32),
        ],
        "attention_forward", 8.0,
    )(where, tokens_low, cosine, sine, mask, pack, pack1, pack2, pack3)

    out2, low_down_late = gate([out2, low_down], [o, down1], "after_attention")
    out3 = swap(out2, "fsdp", 1)
    down2 = swap(low_down_late, "fsdp", 2)

    h, a2, a2_shift, a2_turned, out_full = kernel_call(
        project_kernel,
        [
            shaped((count, MODEL_WIDTH), f32),
            shaped((count, MODEL_WIDTH), bf16),
            shaped((count, q_wide), bf16),
            shaped((MODEL_WIDTH, count), bf16),
            shaped((MODEL_WIDTH, MODEL_WIDTH), bf16),
        ],
        "project", 2.3,
    )(where, tokens_low, o, gains, low_out, out1, out2, out3)

    (half_across,) = gate([half_across], [h], "after_project")
    half_beside = swap(half_across, "rep", extra)
    half_across3 = swap(half_across, "fsdp", 1)
    half_beside3 = swap(half_beside, "fsdp", 1)
    down3 = swap(down2, "fsdp", 1)
    gate_ups = {0: [low_gate_up], 1: [gate_up1], 2: [half_across, half_beside], 3: [half_across3, half_beside3]}
    downs = {0: low_down_late, 1: down1, 2: down2, 3: down3}

    gate_up_block = (groups, 2 * MODEL_WIDTH // groups, ff_rows)
    down_block = (groups, MODEL_WIDTH // groups, ff_rows)
    grad_gate_ups = {}
    grad_downs = {}
    total, accumulated = h, []
    for chunks in ((1,), (0,), (3,), (2,)):
        first, last = chunks[0] == 1, chunks[0] == 2
        blocks = [shaped(shape, bf16) for _ in chunks for shape in (gate_up_block, down_block)]
        results = kernel_call(
            functools.partial(feed_kernel, groups, chunks, first, last, chunks[0] > 1),
            [
                shaped((MODEL_WIDTH, count), bf16) if last else shaped((count, MODEL_WIDTH), f32),
                shaped((count, MODEL_WIDTH), f32),
                shaped((count, q_wide), f32),
            ] + blocks,
            "feed_" + "".join(str(j) for j in chunks), 4.5 * len(chunks),
            scratch=[pltpu.VMEM((ff_rows, 2 * MODEL_WIDTH), bf16)] if chunks[0] > 1 else [],
            after=(gate_up_zero, down_zero) if chunks[0] == 3 else (),
        )(
            where, a2, a2_shift, a2_turned, e, e_turned, total, *accumulated,
            *[part for j in chunks for part in gate_ups[j]], *[downs[j] for j in chunks],
        )
        total, accumulated = results[0], results[1:3]
        for c, j in enumerate(chunks):
            grad_gate_ups[j] = results[3 + 2 * c]
            grad_downs[j] = results[4 + 2 * c]
        if chunks[0] == 0:
            gate_up_zero = core_sum(grad_gate_ups, 0)
            down_zero = core_sum(grad_downs, 0)
            zero_kept, zero_sent = halves(gate_up_zero)
            zero_came = swap(zero_sent, "rep", extra)
    output = total.T

    gate_up_two = core_sum(grad_gate_ups, 2)
    down_two = core_sum(grad_downs, 2)
    two_kept, two_sent = halves(gate_up_two)
    two_came = swap(two_sent, "rep", extra)
    down_came = swap(down_two, "fsdp", 2)

    out_block = (groups, shard_rows, LANES)
    dh, dol, gain_two, *grad_outs = kernel_call(
        functools.partial(middle_kernel, groups),
        [
            shaped((count, MODEL_WIDTH), f32),
            shaped((count, q_wide), bf16),
            shaped((1, MODEL_WIDTH), f32),
        ] + [shaped(out_block, bf16)] * 4,
        "middle", 4.2, after=(gate_up_two, down_two, zero_came),
        scratch=[pltpu.VMEM((MODEL_WIDTH, groups * LANES), bf16)],
    )(where, *accumulated, h, e, gains, o, inv, out_full)
    out_zero, out_two = core_sum(grad_outs, 0), core_sum(grad_outs, 2)
    out_came = swap(out_two, "fsdp", 2)

    dqs, dks, dvs = [], [], []
    waits = ((), (out_zero, out_two), ())
    for g, lifted in enumerate((lifted0, lifted1, lifted2)):
        dq, dk, dv = kernel_call(
            functools.partial(attention_back_kernel, g),
            [shaped((CLUSTER, count, LANES), f32), shaped((count, LANES), f32), shaped((count, LANES), f32)],
            "attention_back_" + str(g), 2.2,
            after=waits[g] + tuple(dqs),
        )(where, q, k, v, lifted, o, dol)
        dqs.append(dq)
        dks.append(dk)
        dvs.append(dv)

    two = add_low(two_kept, two_came)
    gate_up_across = swap(two, "fsdp", 2)
    (down_zero,) = gate([down_zero], [dqs[1]], "after_back")
    down_kept, down_sent = halves(add_low(down_zero, down_came))
    down_came = swap(down_sent, "rep", extra)

    message = 2 * groups * shard_rows + SMALL_ROWS
    sent, kept, tokens_grad = kernel_call(
        functools.partial(last_kernel, groups),
        [
            shaped((message, LANES), bf16),
            shaped((message, LANES), bf16),
            shaped((MODEL_WIDTH, count), bf16),
        ],
        "last", 5.0, after=(two, down_sent),
        scratch=[pltpu.VMEM((MODEL_WIDTH, groups * LANES), bf16)],
    )(where, *dqs, *dks, *dvs, cosine, sine, a, tokens_low, dh, weight_full, gains, gain_two)

    (out_zero,) = gate([out_zero], [sent], "after_last")
    out_kept, out_sent = halves(add_low(out_zero, out_came))
    out_came = swap(out_sent, "rep", extra)
    steps = [("fsdp", 1), ("rep", extra), ("fsdp", 2)]
    for at, (axis, bit) in enumerate(steps):
        if at:
            part = (kept.shape[0] - SMALL_ROWS) // 2 + SMALL_ROWS
            sent, kept = kernel_call(
                halve_kernel, [shaped((part, LANES), bf16)] * 2, "halve_" + str(at), 0.6,
                after=(gate_up_across,) if at == 2 else (),
            )(where, kept, came)
        came = swap(sent, axis, bit)

    rows = 2 * OUT_ROW + 80
    half_blocks = groups // 4
    left, sent = kernel_call(
        fold_first_kernel, [shaped((half_blocks, rows, ff_rows), bf16)] * 2, "fold_first", 1.0
    )(
        where, zero_kept, zero_came, gate_up_across, down_kept, down_came, out_kept, out_came, kept, came
    )
    bit = 2
    came = swap(sent, "rep", bit * extra)
    while half_blocks > 1:
        half_blocks //= 2
        bit *= 2
        left, sent = kernel_call(
            fold_kernel, [shaped((half_blocks, rows, ff_rows), bf16)] * 2, "fold_" + str(bit), 1.0
        )(where, left, came)
        came = swap(sent, "rep", bit * extra)
    parts = [left, came]
    owns = (own_qkv, own_out, own_gate_up, own_down)
    if extra > 1:
        widths = (own_qkv.shape[1], own_out.shape[1], own_gate_up.shape[0], own_down.shape[0])
        parts = [own_block((left.astype(f32) + came.astype(f32))[0], extra, widths)[None]]
    states = (
        own_qkv, projection_first_moment, projection_second_moment,
        own_out, out_first, out_second,
        own_gate_up, gate_up_first.T, gate_up_second.T,
        own_down, down_first.T, down_second.T,
        norm_gains, gains_first, gains_second,
        projection_bias, bias_first_moment, bias_second_moment,
    )
    news = kernel_call(
        functools.partial(final_kernel, rates, len(parts)),
        [shaped(state.shape, f32) for state in states], "final_step", 3.0,
    )(where, *parts, *states)
    return (
        output,
        tokens_grad.T,
        *news[:6],
        *[new.T for new in news[6:12]],
        *news[12:],
    )


def solution(mesh):
    rows = P(("rep", "fsdp"), None)
    weight = P("fsdp", None)
    state = P("fsdp", "rep")
    vector = P("fsdp")
    states = (state,) * 4 + (vector,) * 2
    in_specs = (rows, P(("rep", "fsdp")), rows) + (weight,) * 4 + (vector,) * 2 + states + states
    out_specs = (rows, rows) + (state,) * 12 + (vector,) * 6
    return jax.shard_map(
        on_device, mesh=mesh, in_specs=in_specs, out_specs=out_specs, check_vma=False
    )
```

```python
import functools
import math

import jax
import jax.numpy as jnp
from jax import lax
from jax.experimental import pallas as pl
from jax.experimental.pallas import tpu as pltpu
from jax.sharding import PartitionSpec as P

MODEL_WIDTH = 576
QUERY_HEADS = 9
KEY_VALUE_HEADS = 3
HEAD_SIZE = 64
FF = 1536
STEP = 10

norm_eps = 1e-05
rope_base = 100000.0
beta_one = 0.9
beta_two = 0.95
adam_eps = 1e-08
decay_rate = 0.1

LANES = 128
QKV_WIDTH = (QUERY_HEADS + 2 * KEY_VALUE_HEADS) * HEAD_SIZE
CLUSTER = QUERY_HEADS // KEY_VALUE_HEADS
SMALL_ROWS = 32
ROW_BLOCK = 256
OUT_ROW = MODEL_WIDTH // 4
GATE_PARTS = 2
DOWN_PARTS = 1
DOWN_ROWS = 80
bf16 = jnp.bfloat16
f32 = jnp.float32


def learn_rates():
    out_fan = max(QUERY_HEADS * HEAD_SIZE // 16, 1)
    return (MODEL_WIDTH ** (-0.5), out_fan ** (-0.5), MODEL_WIDTH ** (-0.5), FF ** (-0.5), 0.5, 0.5)


def adam_update(weight, first_moment, second_moment, gradient, step_rate):
    first_new = beta_one * first_moment + (1.0 - beta_one) * gradient
    second_new = beta_two * second_moment + (1.0 - beta_two) * gradient * gradient
    first_fix = 1.0 - beta_one**STEP
    second_fix = 1.0 - beta_two**STEP
    direction = first_new / first_fix / (jnp.sqrt(second_new / second_fix) + adam_eps)
    return (first_new, second_new, weight - step_rate * (direction + decay_rate * weight))


def dot_plain(left, right):
    return lax.dot_general(left, right, (((1,), (0,)), ((), ())), preferred_element_type=f32)


def dot_last(left, right):
    return lax.dot_general(left, right, (((1,), (1,)), ((), ())), preferred_element_type=f32)


def dot_first(left, right):
    return lax.dot_general(left, right, (((0,), (0,)), ((), ())), preferred_element_type=f32)


def kernel_call(body, outs, name, time, scratch=(), vmem=12, after=()):
    def call(scalars, *arrays):
        count = len(after)

        def run(*refs):
            body(refs[0], *refs[1 + count :])

        return pl.pallas_call(
            run,
            out_shape=tuple(outs),
            in_specs=[pl.BlockSpec(memory_space=pltpu.SMEM)]
            + [pl.BlockSpec(memory_space=pl.ANY)] * count
            + [pl.BlockSpec(memory_space=pltpu.VMEM)] * len(arrays),
            out_specs=tuple(pl.BlockSpec(memory_space=pltpu.VMEM) for _ in outs),
            scratch_shapes=list(scratch),
            name=name,
            compiler_params=pltpu.CompilerParams(vmem_limit_bytes=vmem * 2**20),
            cost_estimate=pl.CostEstimate(
                flops=int(time * 1.15e9), bytes_accessed=0, transcendentals=0
            ),
        )(scalars, *after, *arrays)

    return call


def gate(values, after, name):
    def nothing(*refs):
        pass

    result = pl.pallas_call(
        nothing,
        out_shape=tuple(shaped(v.shape, v.dtype) for v in values),
        in_specs=[pl.BlockSpec(memory_space=pl.ANY)] * (len(values) + len(after)),
        out_specs=tuple(pl.BlockSpec(memory_space=pl.ANY) for _ in values),
        input_output_aliases={i: i for i in range(len(values))},
        name=name,
        compiler_params=pltpu.CompilerParams(vmem_limit_bytes=2**20),
        cost_estimate=pl.CostEstimate(flops=0, bytes_accessed=0, transcendentals=0),
    )(*values, *after)
    return list(result)


def shaped(shape, dtype):
    return jax.ShapeDtypeStruct(tuple(shape), dtype)


def lane_index(shape):
    return lax.broadcasted_iota(jnp.int32, shape, len(shape) - 1)


def lower_half(shape):
    return lane_index(shape) < HEAD_SIZE


def swap_pairs(block):
    first = (lane_index(block.shape) & (HEAD_SIZE // 2)) == 0
    ahead = pltpu.roll(block, LANES - HEAD_SIZE // 2, 1)
    behind = pltpu.roll(block, HEAD_SIZE // 2, 1)
    return jnp.where(first, ahead, behind)


def both_halves(block, upper):
    other = pltpu.roll(block, HEAD_SIZE, 1)
    low = lower_half(block.shape)
    return jnp.where(low, other, block) if upper else jnp.where(low, block, other)


def cut_lanes(blocks, start, width):
    at, offset = divmod(start, LANES)
    lane = lane_index(blocks[0].shape)
    part = blocks[at]
    if offset:
        part = pltpu.roll(part, LANES - offset, 1)
        if offset + width > LANES:
            after = pltpu.roll(blocks[at + 1], LANES - offset, 1)
            part = jnp.where(lane < LANES - offset, part, after)
    if width < LANES:
        part = jnp.where(lane < width, part, 0.0)
    return part


def lane_blocks(values):
    width = values.shape[1]
    full = width // LANES
    blocks = [values[:, i * LANES : (i + 1) * LANES] for i in range(full)]
    if width % LANES:
        rest = values[:, full * LANES :]
        fill = jnp.zeros((values.shape[0], LANES - width % LANES), values.dtype)
        blocks.append(jnp.concatenate([rest, fill], axis=1))
    return blocks


def block_place(block, mine, groups):
    away = mine ^ block
    place = 0
    bit = 1
    while bit < groups:
        place = place * 2 + jnp.where((away & bit) == 0, 0, 1)
        bit *= 2
    return place


def own_rows(ref, replica, width):
    if width % 8 == 0:
        return ref[pl.ds(pl.multiple_of(replica * width, 8), width), :]
    rows = ref.shape[0]
    return pltpu.roll(ref[...], rows - replica * width, 0)[:width]


def pack_kernel(qkv_hbm, gains_hbm, bias_hbm, pack_ref, qkv_ref, gains_ref, bias_ref, sems):
    copies = [
        pltpu.make_async_copy(source, target, sems.at[i])
        for i, (source, target) in enumerate(
            ((qkv_hbm, qkv_ref), (gains_hbm, gains_ref), (bias_hbm, bias_ref))
        )
    ]
    for copy in copies:
        copy.start()
    for copy in copies:
        copy.wait()
    rows = qkv_ref.shape[0]
    pack_ref[:rows, :QKV_WIDTH] = qkv_ref[...].astype(bf16)
    pack_ref[:rows, QKV_WIDTH:] = jnp.zeros((rows, pack_ref.shape[1] - QKV_WIDTH), bf16)
    spare = pack_ref.shape[0] - rows
    bias, gains = (ref[...].reshape(1, ref.shape[0]) for ref in (bias_ref, gains_ref))
    extra = jnp.concatenate(lane_blocks(bias) + lane_blocks(gains), axis=1)
    line = jnp.concatenate(
        [extra, jnp.zeros((1, pack_ref.shape[1] - extra.shape[1]), f32)], axis=1
    )
    pack_ref[rows:, :] = jnp.broadcast_to(line, (spare, line.shape[1])).astype(bf16)


def pack_attention(weight, gains, bias, wide):
    return pl.pallas_call(
        pack_kernel,
        out_shape=shaped((weight.shape[0] + 16, wide), bf16),
        in_specs=[pl.BlockSpec(memory_space=pl.ANY)] * 3,
        out_specs=pl.BlockSpec(memory_space=pltpu.VMEM),
        scratch_shapes=[
            pltpu.VMEM(weight.shape, f32),
            pltpu.VMEM(gains.shape, f32),
            pltpu.VMEM(bias.shape, f32),
            pltpu.SemaphoreType.DMA((3,)),
        ],
        name="pack_attention",
        compiler_params=pltpu.CompilerParams(vmem_limit_bytes=8 * 2**20),
        cost_estimate=pl.CostEstimate(flops=10**9, bytes_accessed=0, transcendentals=0),
    )(weight, gains, bias)


def tables_kernel(
    where_ref, segments_ref, tokens_turned_ref, e_turned_ref, qkv_ref, out_ref, gate_up_ref, down_ref,
    cos_ref, sin_ref, mask_ref, tokens_ref, e_ref, low_out_ref, low_gate_up_ref, half_ref, low_down_ref,
    own_qkv_ref, own_out_ref, own_gate_up_ref, own_down_ref, turned_ref,
):
    tokens = segments_ref.shape[0]
    row = segments_ref[...].reshape(1, tokens).astype(f32)
    column = jnp.broadcast_to(row, (LANES, tokens)).T[:, :1]
    query = lax.broadcasted_iota(jnp.int32, (tokens, tokens), 0)
    key = lax.broadcasted_iota(jnp.int32, (tokens, tokens), 1)
    same = column == row
    earlier = jnp.sum(jnp.where(same & (key < query), 1.0, 0.0), axis=1, keepdims=True)
    mask_ref[...] = jnp.where(same & (key <= query), 0.0, -1e30)
    lane = lane_index((tokens, LANES))
    exponent = (lane & (HEAD_SIZE // 2 - 1)).astype(f32) * (2.0 / HEAD_SIZE)
    frequency = jnp.exp(exponent * (-math.log(rope_base)))
    angles = earlier * frequency
    cos_ref[...] = jnp.cos(angles)
    sine = jnp.sin(angles)
    sin_ref[...] = jnp.where((lane & (HEAD_SIZE // 2)) == 0, -sine, sine)
    tokens_ref[...] = tokens_turned_ref[...].astype(f32).T.astype(bf16)
    e_ref[...] = e_turned_ref[...].astype(f32).T.astype(bf16)

    low_out_ref[...] = out_ref[...].astype(bf16)
    gate_up = gate_up_ref[...]
    low_gate_up_ref[...] = gate_up.astype(bf16)
    rows = half_ref.shape[0]
    start = pl.multiple_of((where_ref[1] & 1) * rows, 16)
    half_ref[...] = gate_up_ref[pl.ds(start, rows), :].astype(bf16)
    low_down_ref[...] = down_ref[...].astype(bf16)
    replica = where_ref[2]
    turned_ref[...] = gate_up.T
    width = own_gate_up_ref.shape[0]
    own_gate_up_ref[...] = own_rows(turned_ref, replica, width)
    width = own_down_ref.shape[0]
    own_down_ref[...] = own_rows(down_ref, replica, width)
    for ref, own in ((qkv_ref, own_qkv_ref), (out_ref, own_out_ref)):
        width = own.shape[1]
        wide = jnp.concatenate(lane_blocks(ref[...]), axis=1)
        own[...] = pltpu.roll(wide, wide.shape[1] - replica * width, 1)[:, :width]


def forward_kernel(
    where_ref, tokens_ref, cos_ref, sin_ref, mask_ref, pack0, pack1, pack2, pack3,
    a_ref, q_ref, k_ref, v_ref, e0_ref, e1_ref, e2_ref, inv_ref, o_ref, weight_ref, gains_ref,
):
    me = where_ref[0]
    tokens = tokens_ref.shape[0]
    shard_rows = MODEL_WIDTH // 4
    packs = (pack0, pack1, pack2, pack3)
    lines = []
    for j in range(4):
        start = pl.multiple_of((me ^ j) * shard_rows, 16)
        weight_ref[pl.ds(start, shard_rows), :] = packs[j][:shard_rows, :]
        lines.append(packs[j][shard_rows:, :].astype(f32)[:1, :])
    bias_wide = lane_index((1, LANES)) * 0.0
    ordered = []
    for s in range(4):
        line = jnp.where((me ^ s) == 0, lines[0], 0.0)
        for j in range(1, 4):
            line = jnp.where((me ^ s) == j, lines[j], line)
        ordered.append(line)
    bias_blocks = [bias_wide for _ in range(weight_ref.shape[1] // LANES)]
    gain_blocks = [[bias_wide for _ in range(5)] for _ in range(2)]
    lane = lane_index((1, LANES))

    def put(blocks, source, width, start):
        done = 0
        while done < width:
            at, offset = divmod(start + done, LANES)
            count = min(LANES - offset, width - done)
            from_at, from_offset = divmod(done, LANES)
            count = min(count, LANES - from_offset)
            turn = (offset - from_offset) % LANES
            part = source[from_at]
            if turn:
                part = pltpu.roll(part, turn, 1)
            blocks[at] = jnp.where((lane >= offset) & (lane < offset + count), part, blocks[at])
            done += count

    bias_each = QKV_WIDTH // 4
    gain_each = 2 * MODEL_WIDTH // 4
    bias_lanes = -(-bias_each // LANES) * LANES
    for s in range(4):
        pieces = [ordered[s][:, i * LANES : (i + 1) * LANES] for i in range(8)]
        put(bias_blocks, pieces, bias_each, s * bias_each)
        put(gain_blocks[s // 2], pieces[bias_lanes // LANES :], gain_each, (s % 2) * gain_each)
    gains = [jnp.concatenate(blocks, axis=1) for blocks in gain_blocks]
    for i in range(2):
        gains_ref[i : i + 1, :] = gains[i]
    bias = jnp.concatenate(bias_blocks, axis=1)

    x = tokens_ref[...].astype(f32)
    inverse = lax.rsqrt(jnp.mean(x * x, axis=1, keepdims=True) + norm_eps)
    a = (x * inverse * gains[0][:, :MODEL_WIDTH]).astype(bf16)
    a_ref[...] = a
    p = dot_plain(a, weight_ref[...]) + bias
    cosine, sine = cos_ref[...], sin_ref[...]
    blocks = [p[:, i * LANES : (i + 1) * LANES] for i in range(8)]
    for i in range(6):
        blocks[i] = blocks[i] * cosine + swap_pairs(blocks[i]) * sine
    low = lower_half((tokens, LANES))
    for i in range(5):
        scaled = blocks[i] * HEAD_SIZE ** (-0.5)
        if i == 4:
            scaled = jnp.where(low, scaled, 0.0)
        q_ref[:, i * LANES : (i + 1) * LANES] = scaled.astype(bf16)
    keys = [both_halves(blocks[4], True), both_halves(blocks[5], False), both_halves(blocks[5], True)]
    values = [both_halves(blocks[6], False), both_halves(blocks[6], True), both_halves(blocks[7], False)]
    for g in range(KEY_VALUE_HEADS):
        k_ref[:, g * LANES : (g + 1) * LANES] = keys[g].astype(bf16)
        v_ref[:, g * LANES : (g + 1) * LANES] = values[g].astype(bf16)

    e_refs = (e0_ref, e1_ref, e2_ref)
    step = ROW_BLOCK
    low = lower_half((step, LANES))
    for at in range(tokens // step):
        rows = slice(at * step, (at + 1) * step)
        seen = (at + 1) * step
        mixed = []
        inverses = []
        for g in range(KEY_VALUE_HEADS):
            stack = head_stack(q_ref, rows, g)
            scores = dot_last(stack, k_ref[:seen, g * LANES : (g + 1) * LANES])
            scores = scores.reshape(CLUSTER, step, seen) + mask_ref[rows, :seen][None]
            lifted = jnp.exp(scores - jnp.max(scores, axis=2, keepdims=True))
            total = jnp.sum(lifted, axis=2, keepdims=True)
            kept = lifted.astype(bf16)
            e_refs[g][:, rows, :seen] = kept
            gathered = dot_plain(
                kept.reshape(CLUSTER * step, seen), v_ref[:seen, g * LANES : (g + 1) * LANES]
            ).reshape(CLUSTER, step, LANES)
            inverse_total = jnp.broadcast_to(1.0 / total, gathered.shape)
            gathered = gathered * inverse_total
            for t in range(CLUSTER):
                mixed.append(gathered[t])
                inverses.append(inverse_total[t])
        for i in range(5):
            second = mixed[2 * i + 1] if 2 * i + 1 < QUERY_HEADS else 0.0
            part = jnp.where(low, mixed[2 * i], second)
            o_ref[rows, i * LANES : (i + 1) * LANES] = part.astype(bf16)
            second = inverses[2 * i + 1] if 2 * i + 1 < QUERY_HEADS else 0.0
            inv_ref[rows, i * LANES : (i + 1) * LANES] = jnp.where(low, inverses[2 * i], second)


def project_kernel(
    where_ref, tokens_ref, o_ref, gains_ref, out0, out1, out2, out3,
    h_ref, a2_ref, a2_shift_ref, a2_turned_ref, out_weight_ref,
):
    me = where_ref[0]
    tokens = tokens_ref.shape[0]
    shard_rows = out0.shape[0]
    for j, out in enumerate((out0, out1, out2, out3)):
        start = pl.multiple_of((me ^ j) * shard_rows, 16)
        out_weight_ref[pl.ds(start, shard_rows), :] = out[...]
    x = tokens_ref[...].astype(f32)
    h = x + dot_plain(o_ref[:, :MODEL_WIDTH], out_weight_ref[...])
    h_ref[...] = h
    inverse = lax.rsqrt(jnp.mean(h * h, axis=1, keepdims=True) + norm_eps)
    a2 = h * inverse * gains_ref[1:2, :MODEL_WIDTH]
    a2_ref[...] = a2.astype(bf16)
    a2_blocks = lane_blocks(a2)
    low = lower_half((tokens, LANES))
    before = jnp.zeros((tokens, LANES), f32)
    for i in range(5):
        part = jnp.where(low, pltpu.roll(before, HEAD_SIZE, 1), pltpu.roll(a2_blocks[i], HEAD_SIZE, 1))
        a2_shift_ref[:, i * LANES : (i + 1) * LANES] = part.astype(bf16)
        before = a2_blocks[i]
    a2_turned_ref[...] = a2.T.astype(bf16)


def head_stack(ref, rows, g):
    parts = []
    for t in range(CLUSTER):
        head = g * CLUSTER + t
        block = ref[rows, (head // 2) * LANES : (head // 2 + 1) * LANES]
        low = lower_half(block.shape)
        keep = low if head % 2 == 0 else jnp.logical_not(low)
        parts.append(jnp.where(keep, block, jnp.zeros_like(block)))
    return jnp.concatenate(parts, axis=0)


def feed_kernel(groups, chunks, first, last, halved, *refs):
    refs = list(refs)

    def take(count):
        taken = refs[:count]
        del refs[:count]
        return taken

    (where_ref, a2_ref, a2_shift_ref, a2_turned_ref, e_ref, e_turned_ref, base_ref) = take(7)
    gate_in, shift_in = (None, None) if first else take(2)
    gate_ups = [take(2 if halved else 1) for _ in chunks]
    downs = take(len(chunks))
    total_ref, gate_acc, shift_acc = take(3)
    mine = where_ref[1]
    total = base_ref[...]
    for c in range(len(chunks)):
        gate_outs, down_outs = take(GATE_PARTS), take(DOWN_PARTS)
        down = downs[c]
        if not halved:
            gate_up = gate_ups[c][0]
        else:
            gate_up = refs[-1]
            rows = gate_ups[c][0].shape[0]
            for half in range(2):
                start = pl.multiple_of(((mine & 1) ^ half) * rows, 16)
                gate_up[pl.ds(start, rows), :] = gate_ups[c][half][...]
        gate_weights = gate_up[:, :MODEL_WIDTH]
        up_weights = gate_up[:, MODEL_WIDTH - HEAD_SIZE :]
        gate = dot_last(a2_ref[...], gate_weights)
        up = dot_last(a2_shift_ref[...], up_weights)
        sigma = 1.0 / (1.0 + jnp.exp(-gate))
        active = gate * sigma
        hidden = (active * up).astype(bf16)
        total = total + dot_last(hidden, down[...])
        grad_hidden = dot_plain(e_ref[...], down[...])
        grad_gate = (grad_hidden * up * (sigma * (1.0 + gate * (1.0 - sigma)))).astype(bf16)
        grad_up = (grad_hidden * active).astype(bf16)
        half = groups // 2
        each, width = gate_outs[0].shape[:2]
        for turned, offset in ((dot_plain(a2_turned_ref[...], grad_gate), 0),
                               (dot_plain(a2_turned_ref[...], grad_up), half)):
            for b in range(half):
                at, inner = divmod(b + offset, each)
                gate_outs[at][inner] = turned[b * width : (b + 1) * width].astype(bf16)
        turned = dot_plain(e_turned_ref[...], hidden)
        each, width = down_outs[0].shape[:2]
        for b in range(groups):
            at, inner = divmod(b, each)
            down_outs[at][inner] = turned[b * width : (b + 1) * width].astype(bf16)
        gate_part = dot_plain(grad_gate, gate_weights)
        shift_part = dot_plain(grad_up, up_weights)
        if c == 0 and first:
            gate_acc[...] = gate_part
            shift_acc[...] = shift_part
        elif c == 0:
            gate_acc[...] = gate_in[...] + gate_part
            shift_acc[...] = shift_in[...] + shift_part
        else:
            gate_acc[...] = gate_acc[...] + gate_part
            shift_acc[...] = shift_acc[...] + shift_part
    total_ref[...] = total.T.astype(bf16) if last else total


def core_sum_kernel(groups, where_ref, *refs):
    mine = where_ref[1]
    gates, downs = refs[:GATE_PARTS], refs[GATE_PARTS : GATE_PARTS + DOWN_PARTS]
    refs = refs[GATE_PARTS + DOWN_PARTS :]
    gates_came, downs_came = refs[:GATE_PARTS], refs[GATE_PARTS : GATE_PARTS + DOWN_PARTS]
    gate_kept, gate_sent, down_total, held_ref = refs[GATE_PARTS + DOWN_PARTS :]
    for parts, came, target in ((gates, gates_came, held_ref), (downs, downs_came, down_total)):
        each = parts[0].shape[0]
        for b in range(groups):
            at, inner = divmod(b, each)
            total = parts[at][inner].astype(f32) + came[at][inner].astype(f32)
            target[block_place(b, mine, groups)] = total.astype(bf16)
    half = groups // 2
    gate_kept[...] = held_ref[:half]
    gate_sent[...] = held_ref[half:]


def write_message(held_ref, sent_refs, kept_ref, me, groups):
    rows = held_ref.shape[0] // 4
    each = 2 * groups // len(sent_refs)
    for j in range(4):
        start = pl.multiple_of((me ^ j) * rows, 16)
        for b in range(groups):
            block = held_ref[pl.ds(start, rows), b * LANES : (b + 1) * LANES]
            to = (j // 2) * groups + b
            if j % 2:
                at, to = divmod(to, each)
                sent_refs[at][to * rows : (to + 1) * rows, :] = block
            else:
                kept_ref[to * rows : (to + 1) * rows, :] = block


def middle_kernel(
    groups, where_ref, gate_acc, shift_acc, h_ref, e_ref, gains_ref, o_ref, inv_ref, out_weight_ref,
    dh_ref, dol_ref, small_ref, sent0, sent1, kept_ref, held_ref,
):
    me = where_ref[0]
    tokens = h_ref.shape[0]
    gain = gains_ref[1:2, :MODEL_WIDTH]
    h = h_ref[...]
    low = lower_half((tokens, LANES))
    shifted = [shift_acc[:, i * LANES : (i + 1) * LANES] for i in range(5)]
    parts = []
    for i in range(5):
        part = pltpu.roll(shifted[i], HEAD_SIZE, 1)
        after = pltpu.roll(shifted[i + 1], HEAD_SIZE, 1) if i < 4 else 0.0
        parts.append(jnp.where(low, part, after))
    da2 = gate_acc[...] + jnp.concatenate(parts, axis=1)[:, :MODEL_WIDTH]
    inverse = lax.rsqrt(jnp.mean(h * h, axis=1, keepdims=True) + norm_eps)
    weighted = da2 * gain
    inner = jnp.mean(weighted * h, axis=1, keepdims=True)
    dh = e_ref[...].astype(f32) + inverse * weighted - h * (inverse * inverse * inverse) * inner
    dh_ref[...] = dh
    small_ref[...] = jnp.sum(da2 * h * inverse, axis=0, keepdims=True)
    dhl = dh.astype(bf16)
    spread = dhl.astype(f32)
    blocks = lane_blocks(spread)
    width = MODEL_WIDTH // groups
    chosen = jnp.concatenate(
        [cut_lanes(blocks, b * width, width).astype(bf16) for b in range(groups)], axis=1
    )
    held_ref[...] = dot_first(o_ref[:, :MODEL_WIDTH], chosen).astype(bf16)
    write_message(held_ref, (sent0, sent1), kept_ref, me, groups)
    dol = dot_last(dhl, out_weight_ref[...])
    dol_blocks = lane_blocks(dol.astype(bf16).astype(f32))
    for i in range(5):
        lanes = slice(i * LANES, (i + 1) * LANES)
        dol_ref[:, lanes] = (dol_blocks[i] * inv_ref[:, lanes]).astype(bf16)


def attention_back_kernel(g, where_ref, q_ref, k_ref, v_ref, lifted_ref, o_ref, dol_ref, dq_ref, dk_ref, dv_ref):
    tokens = q_ref.shape[0]
    step = ROW_BLOCK
    lanes = slice(g * LANES, (g + 1) * LANES)
    dk = None
    dv = None
    for at in reversed(range(tokens // step)):
        rows = slice(at * step, (at + 1) * step)
        seen = (at + 1) * step
        q_stack = head_stack(q_ref, rows, g)
        o_stack = head_stack(o_ref, rows, g)
        dol_stack = head_stack(dol_ref, rows, g)
        lifted = lifted_ref[:, rows, :seen].reshape(CLUSTER * step, seen)
        inner = jnp.sum(o_stack.astype(f32) * dol_stack.astype(f32), axis=1, keepdims=True)
        grad = dot_last(dol_stack, v_ref[:seen, lanes])
        dsl = (lifted.astype(f32) * (grad - inner)).astype(bf16)
        dq = dot_plain(dsl, k_ref[:seen, lanes]) * HEAD_SIZE ** (-0.5)
        dq_ref[:, rows, :] = dq.reshape(CLUSTER, step, LANES)
        dk_part = dot_first(q_stack, dsl)
        dv_part = dot_first(dol_stack, lifted)
        if dk is None:
            dk, dv = dk_part, dv_part
        else:
            dk = jnp.concatenate([dk[:, :seen] + dk_part, dk[:, seen:]], axis=1)
            dv = jnp.concatenate([dv[:, :seen] + dv_part, dv[:, seen:]], axis=1)
    dk = dk.T
    dv = dv.T
    dk_ref[...] = dk + pltpu.roll(dk, HEAD_SIZE, 1)
    dv_ref[...] = dv + pltpu.roll(dv, HEAD_SIZE, 1)


def last_kernel(
    groups, where_ref, dq0, dq1, dq2, dk0, dk1, dk2, dv0, dv1, dv2, cos_ref, sin_ref,
    a_ref, tokens_ref, dh_ref, weight_ref, gains_ref, gain_two_ref,
    sent0, sent1, kept_ref, tokens_grad_ref, held_ref,
):
    me = where_ref[0]
    tokens = tokens_ref.shape[0]
    low = lower_half((tokens, LANES))
    heads = [ref[t] for ref in (dq0, dq1, dq2) for t in range(CLUSTER)]
    blocks = [jnp.where(low, heads[2 * i], heads[2 * i + 1]) for i in range(4)]
    blocks.append(jnp.where(low, heads[8], dk0[...]))
    blocks.append(jnp.where(low, dk1[...], dk2[...]))
    cosine, sine = cos_ref[...], sin_ref[...]
    blocks = [block * cosine - swap_pairs(block) * sine for block in blocks]
    blocks.append(jnp.where(low, dv0[...], dv1[...]))
    blocks.append(jnp.where(low, dv2[...], 0.0))
    low_blocks = [block.astype(bf16) for block in blocks]
    blocks = [block.astype(f32) for block in low_blocks]
    dpl = jnp.concatenate(low_blocks, axis=1)
    width = QKV_WIDTH // groups
    chosen = jnp.concatenate(
        [cut_lanes(blocks, b * width, width).astype(bf16) for b in range(groups)], axis=1
    )
    held_ref[...] = dot_first(a_ref[...], chosen).astype(bf16)
    write_message(held_ref, (sent0, sent1), kept_ref, me, groups)
    rows = held_ref.shape[0] // 4

    bias_blocks = [jnp.sum(block, axis=0, keepdims=True) for block in blocks]
    x = tokens_ref[...].astype(f32)
    inverse = lax.rsqrt(jnp.mean(x * x, axis=1, keepdims=True) + norm_eps)
    da = dot_last(dpl, weight_ref[...])
    gain_one_blocks = lane_blocks(jnp.sum(da * x * inverse, axis=0, keepdims=True))
    gain_two_blocks = lane_blocks(gain_two_ref[...])
    weighted = da * gains_ref[0:1, :MODEL_WIDTH]
    inner = jnp.mean(weighted * x, axis=1, keepdims=True)
    tokens_grad = dh_ref[...] + inverse * weighted - x * (inverse * inverse * inverse) * inner
    tokens_grad_ref[...] = tokens_grad.T.astype(bf16)

    gain_each = 2 * MODEL_WIDTH // 4
    bias_each = QKV_WIDTH // 4
    lines = []
    for s in range(4):
        source = gain_one_blocks if s < 2 else gain_two_blocks
        count = 0
        for t in range(0, gain_each, LANES):
            lines.append(cut_lanes(source, (s % 2) * gain_each + t, min(LANES, gain_each - t)))
            count += 1
        for t in range(0, bias_each, LANES):
            lines.append(cut_lanes(bias_blocks, s * bias_each + t, min(LANES, bias_each - t)))
            count += 1
        lines += [jnp.zeros((1, LANES), f32)] * (SMALL_ROWS // 4 - count)
    small = jnp.concatenate(lines, axis=0).astype(bf16)
    sent1[groups * rows :, :] = small
    kept_ref[2 * groups * rows :, :] = small


def place_sum(held_ref, kept_ref, came_refs, mine, groups, rows):
    half = groups // 2
    each = 2 * groups // len(came_refs)
    for j in range(2):
        for b in range(groups):
            at = j * groups + b
            part, inner = divmod(at, each)
            total = kept_ref[at * rows : (at + 1) * rows, :].astype(f32)
            total = total + came_refs[part][inner * rows : (inner + 1) * rows, :].astype(f32)
            place = block_place(b, mine, groups)
            beyond = jnp.where((place & half) == 0, 0, half)
            to = pl.multiple_of((place + beyond + j * half) * rows, 16)
            held_ref[pl.ds(to, rows), :] = total.astype(bf16)


def halve_first_kernel(groups, where_ref, kept_ref, came0, came1, sent_ref, left_ref, held_ref):
    rows = OUT_ROW
    part = groups * rows
    place_sum(held_ref, kept_ref, (came0, came1), where_ref[1], groups, rows)
    small = kept_ref[2 * part :, :].astype(f32) + came1[part:, :].astype(f32)
    for ref, start in ((left_ref, 0), (sent_ref, part)):
        ref[:part, :] = held_ref[start : start + part, :]
        ref[part:, :] = small.astype(bf16)


def down_out_kernel(groups, where_ref, down_zero, down_came, kept_ref, came0, came1, sent_ref, left_ref, held_ref):
    rows = OUT_ROW
    part = groups * rows
    place_sum(held_ref, kept_ref, (came0, came1), where_ref[1], groups, rows)
    thin = down_zero.shape[1]
    lanes = down_zero.shape[2] // LANES
    fill = jnp.zeros((DOWN_ROWS - thin, LANES), f32)
    for ref, start, first in ((left_ref, 0, 0), (sent_ref, part, groups // 2)):
        ref[:part, :] = held_ref[start : start + part, :]
        for b in range(groups // 2):
            total = down_zero[first + b].astype(f32) + down_came[first + b].astype(f32)
            for i in range(lanes):
                to = part + (b * lanes + i) * DOWN_ROWS
                block = jnp.concatenate([total[:, i * LANES : (i + 1) * LANES], fill], axis=0)
                ref[to : to + DOWN_ROWS, :] = block.astype(bf16)


def halve_kernel(small_rows, where_ref, kept_ref, came_ref, sent_ref, left_ref):
    part = left_ref.shape[0] - small_rows
    rows = 2 * part + small_rows
    total = kept_ref[:rows, :].astype(f32) + came_ref[:rows, :].astype(f32)
    total = total.astype(bf16)
    left_ref[:part, :] = total[:part]
    sent_ref[:part, :] = total[part : 2 * part]
    if small_rows:
        left_ref[part:, :] = total[2 * part :]
        sent_ref[part:, :] = total[2 * part :]


def fold_feed_kernel(where_ref, gate_kept, gate_came, gate_across, low_kept, low_came, left_ref, sent_ref):
    blocks, rows = gate_kept.shape[:2]
    half = blocks // 2
    lanes = gate_kept.shape[2] // LANES
    first = low_kept.shape[0] - blocks * lanes * DOWN_ROWS
    for b in range(blocks):
        ref, at = (left_ref, b) if b < half else (sent_ref, b - half)
        gate_up = gate_kept[b].astype(f32) + gate_came[b].astype(f32) + gate_across[b].astype(f32)
        ref[at, :rows, :] = gate_up.astype(bf16)
        for i in range(lanes):
            start = first + (b * lanes + i) * DOWN_ROWS
            down = low_kept[start : start + DOWN_ROWS, :].astype(f32)
            down = down + low_came[start : start + DOWN_ROWS, :].astype(f32)
            ref[at, rows:, i * LANES : (i + 1) * LANES] = down.astype(bf16)


def fold_attention_kernel(where_ref, out_kept, out_came, qkv_kept, qkv_came, left_ref, sent_ref):
    rows = OUT_ROW
    blocks = out_kept.shape[0] // rows
    half = blocks // 2
    out = (out_kept[...].astype(f32) + out_came[...].astype(f32)).astype(bf16)
    qkv = (qkv_kept[...].astype(f32) + qkv_came[...].astype(f32)).astype(bf16)
    small = qkv[blocks * rows :]
    for b in range(blocks):
        ref, at = (left_ref, b) if b < half else (sent_ref, b - half)
        ref[at, :rows, :LANES] = out[b * rows : (b + 1) * rows]
        ref[at, :rows, LANES:] = qkv[b * rows : (b + 1) * rows]
        ref[at, rows:, :LANES] = small
        ref[at, rows:, LANES:] = jnp.zeros((SMALL_ROWS, LANES), bf16)


def fold_kernel(where_ref, kept_ref, came_ref, left_ref, sent_ref):
    half = left_ref.shape[0]
    for b in range(half):
        left_ref[b] = (kept_ref[b].astype(f32) + came_ref[b].astype(f32)).astype(bf16)
        at = b + half
        sent_ref[b] = (kept_ref[at].astype(f32) + came_ref[at].astype(f32)).astype(bf16)


def read_total(refs, parts):
    total = refs[0][0].astype(f32)
    for ref in refs[1:parts]:
        total = total + ref[0].astype(f32)
    return total


def step_with(refs):
    count = len(refs) // 2
    ins, outs = refs[:count], refs[count:]

    def step(at, gradient, rate):
        new = adam_update(ins[at][...], ins[at + 1][...], ins[at + 2][...], gradient, rate)
        for i in range(3):
            outs[at + i][...] = new[i]

    return ins, step


def feed_step_kernel(step_rates, parts, where_ref, *refs):
    total = read_total(refs, parts)
    ins, step = step_with(refs[parts:])
    step(0, total[: ins[0].shape[0]], step_rates[2])
    step(3, total[OUT_ROW : OUT_ROW + ins[3].shape[0]], step_rates[3])


def attention_step_kernel(step_rates, parts, where_ref, *refs):
    total = read_total(refs, parts)
    ins, step = step_with(refs[parts:])
    step(0, total[:OUT_ROW, LANES : LANES + ins[0].shape[1]], step_rates[0])
    step(3, total[:OUT_ROW, : ins[3].shape[1]], step_rates[1])
    me = where_ref[0]
    each = SMALL_ROWS // 4
    small = total[OUT_ROW:, :LANES]
    mine = small[:each]
    for s in range(1, 4):
        mine = jnp.where(me == s, small[s * each : (s + 1) * each], mine)
    line = 0
    for at in (6, 9):
        width = ins[at].shape[0]
        lines = -(-width // LANES)
        wide = jnp.concatenate([mine[line + t : line + t + 1, :] for t in range(lines)], axis=1)
        line += lines
        step(at, wide[:, :width].reshape(width), step_rates[4 if at == 6 else 5])


def swap(values, axis, bit):
    size = lax.axis_size(axis)
    return lax.ppermute(values, axis, [(i, i ^ bit) for i in range(size)])


def add_low(left, right):
    return (left.astype(f32) + right.astype(f32)).astype(bf16)


def halves(values):
    half = values.shape[0] // 2
    return values[:half], values[half:]


def own_term(total, extra, places):
    bit = 1
    while bit < extra:
        total = total + swap(total, "rep", bit)
        bit *= 2
    at = lax.axis_index("rep") % extra
    result = total
    for row, rows, lane, lanes, dim, width in places:
        part = total[row : row + rows, lane : lane + lanes]
        own = lax.dynamic_slice_in_dim(part, at * width, width, dim)
        result = lax.dynamic_update_slice(result, own, (row, lane))
    return result[None]


def finish(left, came, extra, places):
    if extra == 1:
        return [left, came]
    return [own_term((left.astype(f32) + came.astype(f32))[0], extra, places)]


def on_device(
    tokens,
    segments,
    cotangent,
    projection_weight,
    out_weight,
    gate_up_weight,
    down_weight,
    norm_gains,
    projection_bias,
    projection_first_moment,
    out_first,
    gate_up_first,
    down_first,
    gains_first,
    bias_first_moment,
    projection_second_moment,
    out_second,
    gate_up_second,
    down_second,
    gains_second,
    bias_second_moment,
):
    count = tokens.shape[0]
    replicas = lax.axis_size("rep")
    groups = min(replicas, 8)
    extra = replicas // groups
    replica = lax.axis_index("rep")
    where = jnp.stack([lax.axis_index("fsdp"), replica // extra, replica]).astype(jnp.int32)
    rates = learn_rates()
    wide = 1024
    shard_rows, ff_rows = projection_weight.shape[0], gate_up_weight.shape[0]
    q_wide = 5 * LANES
    kv_wide = KEY_VALUE_HEADS * LANES
    tokens_turned, e_turned, down_turned = tokens.T, cotangent.T, down_weight.T

    pack = pack_attention(projection_weight, norm_gains, projection_bias, wide)
    pack2 = swap(pack, "fsdp", 2)
    pack1 = swap(pack, "fsdp", 1)

    (cosine, sine, mask, tokens_low, e, low_out, low_gate_up, half, low_down,
     own_qkv, own_out, own_gate_up, own_down) = kernel_call(
        tables_kernel,
        [
            shaped((count, LANES), f32),
            shaped((count, LANES), f32),
            shaped((count, count), f32),
            shaped((count, MODEL_WIDTH), bf16),
            shaped((count, MODEL_WIDTH), bf16),
            shaped(out_weight.shape, bf16),
            shaped((ff_rows, 2 * MODEL_WIDTH), bf16),
            shaped((ff_rows // 2, 2 * MODEL_WIDTH), bf16),
            shaped((MODEL_WIDTH, ff_rows), bf16),
            shaped(projection_first_moment.shape, f32),
            shaped(out_first.shape, f32),
            shaped(gate_up_first.shape[::-1], f32),
            shaped(down_first.shape[::-1], f32),
        ],
        "tables", 3.0,
        scratch=[pltpu.VMEM((2 * MODEL_WIDTH, ff_rows), f32)], after=(pack,),
    )(
        where, segments, tokens_turned, e_turned,
        projection_weight, out_weight, gate_up_weight, down_turned,
    )

    pack2, low_out, half = gate([pack2, low_out, half], [pack1, cosine], "after_pack")
    pack3 = swap(pack2, "fsdp", 1)
    out2 = swap(low_out, "fsdp", 2)
    half_across = swap(half, "fsdp", 2)
    out1 = swap(low_out, "fsdp", 1)
    gate_up1 = swap(low_gate_up, "fsdp", 1)
    down1 = swap(low_down, "fsdp", 1)

    (a, q, k, v, lifted0, lifted1, lifted2, inv, o, weight_full, gains) = kernel_call(
        forward_kernel,
        [
            shaped((count, MODEL_WIDTH), bf16),
            shaped((count, q_wide), bf16),
            shaped((count, kv_wide), bf16),
            shaped((count, kv_wide), bf16),
        ]
        + [shaped((CLUSTER, count, count), bf16)] * 3
        + [
            shaped((count, q_wide), f32),
            shaped((count, q_wide), bf16),
            shaped((MODEL_WIDTH, wide), bf16),
            shaped((2, q_wide), f32),
        ],
        "attention_forward", 6.0,
    )(where, tokens_low, cosine, sine, mask, pack, pack1, pack2, pack3)

    out2, low_down_late = gate([out2, low_down], [o, down1], "after_attention")
    out3 = swap(out2, "fsdp", 1)
    down2 = swap(low_down_late, "fsdp", 2)

    h, a2, a2_shift, a2_turned, out_full = kernel_call(
        project_kernel,
        [
            shaped((count, MODEL_WIDTH), f32),
            shaped((count, MODEL_WIDTH), bf16),
            shaped((count, q_wide), bf16),
            shaped((MODEL_WIDTH, count), bf16),
            shaped((MODEL_WIDTH, MODEL_WIDTH), bf16),
        ],
        "project", 2.0,
    )(where, tokens_low, o, gains, low_out, out1, out2, out3)

    (half_across,) = gate([half_across], [h], "after_project")
    half_beside = swap(half_across, "rep", extra)
    half_across3 = swap(half_across, "fsdp", 1)
    gate_ups = {0: [low_gate_up], 1: [gate_up1]}
    downs = {0: low_down_late, 1: down1}

    gate_up_part = (groups // GATE_PARTS, 2 * MODEL_WIDTH // groups, ff_rows)
    down_part = (groups // DOWN_PARTS, MODEL_WIDTH // groups, ff_rows)
    half_block = (groups // 2,) + gate_up_part[1:]
    parts = [shaped(gate_up_part, bf16)] * GATE_PARTS + [shaped(down_part, bf16)] * DOWN_PARTS

    def core_sum(own, sent, name):
        came = [swap(part, "fsdp", 1) for part in sent]
        return kernel_call(
            functools.partial(core_sum_kernel, groups),
            [shaped(half_block, bf16), shaped(half_block, bf16), shaped((groups,) + down_part[1:], bf16)],
            name, 0.2, scratch=[pltpu.VMEM((groups,) + gate_up_part[1:], bf16)],
        )(where, *own, *came)

    grads = {}
    total, accumulated = h, []
    for j in (1, 0, 3, 2):
        first, last = j == 1, j == 2
        waits = (half_across,) if first else (zero_sent,) if j == 3 else ()
        total, *results = kernel_call(
            functools.partial(feed_kernel, groups, (j,), first, last, j > 1),
            [
                shaped((MODEL_WIDTH, count), bf16) if last else shaped((count, MODEL_WIDTH), f32),
                shaped((count, MODEL_WIDTH), f32),
                shaped((count, q_wide), f32),
            ] + parts,
            "feed_" + str(j), 0.5,
            scratch=[pltpu.VMEM((ff_rows, 2 * MODEL_WIDTH), bf16)] if j > 1 else [],
            after=waits,
        )(
            where, a2, a2_shift, a2_turned, e, e_turned, total, *accumulated, *gate_ups[j], downs[j],
        )
        accumulated, grads[j] = results[:2], results[2:]
        if j == 0:
            half_beside, down2 = gate([half_beside, down2], [total], "after_feed_0")
            gate_ups[2] = [half_across, half_beside]
            gate_ups[3] = [half_across3, swap(half_beside, "fsdp", 1)]
            downs[2], downs[3] = down2, swap(down2, "fsdp", 1)
            zero_kept, zero_sent, down_zero = core_sum(grads[0], grads[1], "core_sum_0")
            zero_came = swap(zero_sent, "rep", extra)
    output = total.T

    two_kept, two_sent, down_two = core_sum(grads[2], grads[3], "core_sum_2")
    two_came = swap(two_sent, "rep", extra)
    down_came = swap(down_two, "fsdp", 2)

    message = 2 * groups * shard_rows
    dh, dol, gain_two, *out_parts = kernel_call(
        functools.partial(middle_kernel, groups),
        [
            shaped((count, MODEL_WIDTH), f32),
            shaped((count, q_wide), bf16),
            shaped((1, MODEL_WIDTH), f32),
            shaped((message // 2, LANES), bf16),
            shaped((message // 2, LANES), bf16),
            shaped((message, LANES), bf16),
        ],
        "middle", 0.5, after=(two_sent, down_two),
        scratch=[pltpu.VMEM((MODEL_WIDTH, groups * LANES), bf16)],
    )(where, *accumulated, h, e, gains, o, inv, out_full)

    def halve(kept, came, small_rows, name, after=()):
        part = (kept.shape[0] - small_rows) // 2 + small_rows
        return kernel_call(
            functools.partial(halve_kernel, small_rows),
            [shaped((part, LANES), bf16)] * 2, name, 0.3, after=after,
        )(where, kept, came)

    *out_sent, out_kept = out_parts
    out_came = [swap(part, "fsdp", 1) for part in out_sent]

    dqs, dks, dvs = [], [], []
    waits = ()
    for g, lifted in enumerate((lifted0, lifted1, lifted2)):
        if g == 2:
            two_kept, down_zero = gate([two_kept, down_zero], [dqs[1]], "after_back")
            two = add_low(two_kept, two_came)
            gate_up_across = swap(two, "fsdp", 2)
            low_rows = message // 2 + groups // 2 * (ff_rows // LANES) * DOWN_ROWS
            low_sent, low_kept = kernel_call(
                functools.partial(down_out_kernel, groups),
                [shaped((low_rows, LANES), bf16)] * 2, "down_out", 0.2,
                scratch=[pltpu.VMEM((message, LANES), bf16)],
            )(where, down_zero, down_came, out_kept, *out_came)
            low_came = swap(low_sent, "rep", extra)
            waits = (two, low_sent)
        dq, dk, dv = kernel_call(
            functools.partial(attention_back_kernel, g),
            [shaped((CLUSTER, count, LANES), f32), shaped((count, LANES), f32), shaped((count, LANES), f32)],
            "attention_back_" + str(g), 0.2, after=waits + tuple(dqs),
        )(where, q, k, v, lifted, o, dol)
        dqs.append(dq)
        dks.append(dk)
        dvs.append(dv)

    *sent, kept, tokens_grad = kernel_call(
        functools.partial(last_kernel, groups),
        [
            shaped((message // 2, LANES), bf16),
            shaped((message // 2 + SMALL_ROWS, LANES), bf16),
            shaped((message + SMALL_ROWS, LANES), bf16),
            shaped((MODEL_WIDTH, count), bf16),
        ],
        "last", 0.2,
        scratch=[pltpu.VMEM((MODEL_WIDTH, groups * LANES), bf16)],
    )(where, *dqs, *dks, *dvs, cosine, sine, a, tokens_low, dh, weight_full, gains, gain_two)
    came = [swap(part, "fsdp", 1) for part in sent]

    quarter = groups // 4
    rows = OUT_ROW + DOWN_ROWS
    feed_left, feed_sent = kernel_call(
        fold_feed_kernel, [shaped((quarter, rows, ff_rows), bf16)] * 2, "fold_feed", 0.5, after=(sent[0],)
    )(where, zero_kept, zero_came, gate_up_across, low_kept, low_came)
    feed_came = swap(feed_sent, "rep", 2 * extra)
    out_sent, out_kept = kernel_call(
        functools.partial(halve_kernel, 0),
        [shaped((message // 4, LANES), bf16)] * 2, "out_halve", 0.3, after=(feed_sent,),
    )(where, low_kept, low_came)
    out_came = swap(out_sent, "fsdp", 2)
    sent, kept = kernel_call(
        functools.partial(halve_first_kernel, groups),
        [shaped((message // 2 + SMALL_ROWS, LANES), bf16)] * 2, "halve_first", 0.3, after=(out_sent,),
        scratch=[pltpu.VMEM((message, LANES), bf16)],
    )(where, kept, *came)
    came = swap(sent, "rep", extra)

    def fold(left, came, name, after=()):
        half = left.shape[0] // 2
        return kernel_call(
            fold_kernel, [shaped((half,) + left.shape[1:], bf16)] * 2, name, 0.3, after=after
        )(where, left, came)

    bits = [1 << i for i in range(2, groups.bit_length() - 1)]
    for bit in bits:
        feed_left, feed_sent = fold(feed_left, feed_came, "fold_feed_" + str(bit), (sent,))
        feed_came = swap(feed_sent, "rep", bit * extra)
    sent, kept = halve(kept, came, SMALL_ROWS, "halve_2", (feed_sent,))
    came = swap(sent, "fsdp", 2)
    left, sent = kernel_call(
        fold_attention_kernel,
        [shaped((quarter, OUT_ROW + SMALL_ROWS, 2 * LANES), bf16)] * 2, "fold_attention", 0.5,
    )(where, out_kept, out_came, kept, came)
    came = swap(sent, "rep", 2 * extra)
    feed_states = (
        own_gate_up, gate_up_first.T, gate_up_second.T, own_down, down_first.T, down_second.T,
    )
    wide_gate, wide_down = own_gate_up.shape[0] * extra, own_down.shape[0] * extra
    feed_parts = finish(feed_left, feed_came, extra, (
        (0, wide_gate, 0, ff_rows, 0, own_gate_up.shape[0]),
        (OUT_ROW, wide_down, 0, ff_rows, 0, own_down.shape[0]),
    ))
    feed_news = kernel_call(
        functools.partial(feed_step_kernel, rates, len(feed_parts)),
        [shaped(state.shape, f32) for state in feed_states], "feed_step", 0.5, after=(sent,),
    )(where, *feed_parts, *feed_states)
    for bit in bits:
        left, sent = fold(left, came, "fold_attention_" + str(bit), (feed_news[0],))
        came = swap(sent, "rep", bit * extra)

    states = (
        own_qkv, projection_first_moment, projection_second_moment,
        own_out, out_first, out_second,
        norm_gains, gains_first, gains_second,
        projection_bias, bias_first_moment, bias_second_moment,
    )
    parts = finish(left, came, extra, (
        (0, OUT_ROW, LANES, own_qkv.shape[1] * extra, 1, own_qkv.shape[1]),
        (0, OUT_ROW, 0, own_out.shape[1] * extra, 1, own_out.shape[1]),
    ))
    news = kernel_call(
        functools.partial(attention_step_kernel, rates, len(parts)),
        [shaped(state.shape, f32) for state in states], "attention_step", 1.0,
    )(where, *parts, *states)
    return (
        output,
        tokens_grad.T,
        *news[:6],
        *[new.T for new in feed_news],
        *news[6:],
    )


def solution(mesh):
    rows = P(("rep", "fsdp"), None)
    weight = P("fsdp", None)
    state = P("fsdp", "rep")
    vector = P("fsdp")
    states = (state,) * 4 + (vector,) * 2
    in_specs = (rows, P(("rep", "fsdp")), rows) + (weight,) * 4 + (vector,) * 2 + states + states
    out_specs = (rows, rows) + (state,) * 12 + (vector,) * 6
    return jax.shard_map(
        on_device, mesh=mesh, in_specs=in_specs, out_specs=out_specs, check_vma=False
    )
```

```python
import functools
import math

import jax
import jax.numpy as jnp
from jax import lax
from jax.experimental import pallas as pl
from jax.experimental.pallas import tpu as pltpu
from jax.sharding import PartitionSpec as P

MODEL_WIDTH = 576
QUERY_HEADS = 9
KEY_VALUE_HEADS = 3
HEAD_SIZE = 64
FF = 1536
STEP = 10

norm_eps = 1e-05
rope_base = 100000.0
beta_one = 0.9
beta_two = 0.95
adam_eps = 1e-08
decay_rate = 0.1

LANES = 128
QKV_WIDTH = (QUERY_HEADS + 2 * KEY_VALUE_HEADS) * HEAD_SIZE
CLUSTER = QUERY_HEADS // KEY_VALUE_HEADS
SMALL_ROWS = 32
ROW_BLOCK = 256
OUT_ROW = MODEL_WIDTH // 4
DOWN_ROWS = 80
bf16 = jnp.bfloat16
f32 = jnp.float32


def learn_rates():
    out_fan = max(QUERY_HEADS * HEAD_SIZE // 16, 1)
    return (MODEL_WIDTH ** (-0.5), out_fan ** (-0.5), MODEL_WIDTH ** (-0.5), FF ** (-0.5), 0.5, 0.5)


def adam_update(weight, first_moment, second_moment, gradient, step_rate):
    first_new = beta_one * first_moment + (1.0 - beta_one) * gradient
    second_new = beta_two * second_moment + (1.0 - beta_two) * gradient * gradient
    first_fix = 1.0 - beta_one**STEP
    second_fix = 1.0 - beta_two**STEP
    direction = first_new / first_fix / (jnp.sqrt(second_new / second_fix) + adam_eps)
    return (first_new, second_new, weight - step_rate * (direction + decay_rate * weight))


def dot_plain(left, right):
    return lax.dot_general(left, right, (((1,), (0,)), ((), ())), preferred_element_type=f32)


def dot_last(left, right):
    return lax.dot_general(left, right, (((1,), (1,)), ((), ())), preferred_element_type=f32)


def dot_first(left, right):
    return lax.dot_general(left, right, (((0,), (0,)), ((), ())), preferred_element_type=f32)


def kernel_call(body, outs, name, time, scratch=(), vmem=12, after=()):
    def call(scalars, *arrays):
        count = len(after)

        def run(*refs):
            body(refs[0], *refs[1 + count :])

        return pl.pallas_call(
            run,
            out_shape=tuple(outs),
            in_specs=[pl.BlockSpec(memory_space=pltpu.SMEM)]
            + [pl.BlockSpec(memory_space=pl.ANY)] * count
            + [pl.BlockSpec(memory_space=pltpu.VMEM)] * len(arrays),
            out_specs=tuple(pl.BlockSpec(memory_space=pltpu.VMEM) for _ in outs),
            scratch_shapes=list(scratch),
            name=name,
            compiler_params=pltpu.CompilerParams(vmem_limit_bytes=vmem * 2**20),
            cost_estimate=pl.CostEstimate(
                flops=int(time * 1.15e9), bytes_accessed=0, transcendentals=0
            ),
        )(scalars, *after, *arrays)

    return call


def gate(values, after, name):
    def nothing(*refs):
        pass

    result = pl.pallas_call(
        nothing,
        out_shape=tuple(shaped(v.shape, v.dtype) for v in values),
        in_specs=[pl.BlockSpec(memory_space=pl.ANY)] * (len(values) + len(after)),
        out_specs=tuple(pl.BlockSpec(memory_space=pl.ANY) for _ in values),
        input_output_aliases={i: i for i in range(len(values))},
        name=name,
        compiler_params=pltpu.CompilerParams(vmem_limit_bytes=2**20),
        cost_estimate=pl.CostEstimate(flops=0, bytes_accessed=0, transcendentals=0),
    )(*values, *after)
    return list(result)


def shaped(shape, dtype):
    return jax.ShapeDtypeStruct(tuple(shape), dtype)


def lane_index(shape):
    return lax.broadcasted_iota(jnp.int32, shape, len(shape) - 1)


def lower_half(shape):
    return lane_index(shape) < HEAD_SIZE


def swap_pairs(block):
    first = (lane_index(block.shape) & (HEAD_SIZE // 2)) == 0
    ahead = pltpu.roll(block, LANES - HEAD_SIZE // 2, 1)
    behind = pltpu.roll(block, HEAD_SIZE // 2, 1)
    return jnp.where(first, ahead, behind)


def both_halves(block, upper):
    other = pltpu.roll(block, HEAD_SIZE, 1)
    low = lower_half(block.shape)
    return jnp.where(low, other, block) if upper else jnp.where(low, block, other)


def cut_lanes(blocks, start, width):
    at, offset = divmod(start, LANES)
    lane = lane_index(blocks[0].shape)
    part = blocks[at]
    if offset:
        part = pltpu.roll(part, LANES - offset, 1)
        if offset + width > LANES:
            after = pltpu.roll(blocks[at + 1], LANES - offset, 1)
            part = jnp.where(lane < LANES - offset, part, after)
    if width < LANES:
        part = jnp.where(lane < width, part, 0.0)
    return part


def lane_blocks(values):
    width = values.shape[1]
    full = width // LANES
    blocks = [values[:, i * LANES : (i + 1) * LANES] for i in range(full)]
    if width % LANES:
        rest = values[:, full * LANES :]
        fill = jnp.zeros((values.shape[0], LANES - width % LANES), values.dtype)
        blocks.append(jnp.concatenate([rest, fill], axis=1))
    return blocks


def block_place(block, mine, groups):
    away = mine ^ block
    place = 0
    bit = 1
    while bit < groups:
        place = place * 2 + jnp.where((away & bit) == 0, 0, 1)
        bit *= 2
    return place


def own_rows(ref, replica, width):
    if width % 8 == 0:
        return ref[pl.ds(pl.multiple_of(replica * width, 8), width), :]
    rows = ref.shape[0]
    return pltpu.roll(ref[...], rows - replica * width, 0)[:width]


def pack_kernel(qkv_hbm, gains_hbm, bias_hbm, pack_ref, qkv_ref, gains_ref, bias_ref, sems):
    copies = [
        pltpu.make_async_copy(source, target, sems.at[i])
        for i, (source, target) in enumerate(
            ((qkv_hbm, qkv_ref), (gains_hbm, gains_ref), (bias_hbm, bias_ref))
        )
    ]
    for copy in copies:
        copy.start()
    for copy in copies:
        copy.wait()
    rows = qkv_ref.shape[0]
    pack_ref[:rows, :QKV_WIDTH] = qkv_ref[...].astype(bf16)
    pack_ref[:rows, QKV_WIDTH:] = jnp.zeros((rows, pack_ref.shape[1] - QKV_WIDTH), bf16)
    spare = pack_ref.shape[0] - rows
    bias, gains = (ref[...].reshape(1, ref.shape[0]) for ref in (bias_ref, gains_ref))
    extra = jnp.concatenate(lane_blocks(bias) + lane_blocks(gains), axis=1)
    line = jnp.concatenate(
        [extra, jnp.zeros((1, pack_ref.shape[1] - extra.shape[1]), f32)], axis=1
    )
    pack_ref[rows:, :] = jnp.broadcast_to(line, (spare, line.shape[1])).astype(bf16)


def pack_attention(weight, gains, bias, wide):
    return pl.pallas_call(
        pack_kernel,
        out_shape=shaped((weight.shape[0] + 16, wide), bf16),
        in_specs=[pl.BlockSpec(memory_space=pl.ANY)] * 3,
        out_specs=pl.BlockSpec(memory_space=pltpu.VMEM),
        scratch_shapes=[
            pltpu.VMEM(weight.shape, f32),
            pltpu.VMEM(gains.shape, f32),
            pltpu.VMEM(bias.shape, f32),
            pltpu.SemaphoreType.DMA((3,)),
        ],
        name="pack_attention",
        compiler_params=pltpu.CompilerParams(vmem_limit_bytes=60 * 2**20),
        cost_estimate=pl.CostEstimate(flops=10**9, bytes_accessed=0, transcendentals=0),
    )(weight, gains, bias)


def tables_kernel(
    where_ref, segments_ref, tokens_turned_ref, e_turned_ref, qkv_ref, out_ref, gate_up_ref, down_ref,
    cos_ref, sin_ref, mask_ref, tokens_ref, e_ref, low_out_ref, low_gate_up_ref, half_ref, low_down_ref,
    own_qkv_ref, own_out_ref, own_gate_up_ref, own_down_ref, turned_ref,
):
    tokens = segments_ref.shape[0]
    row = segments_ref[...].reshape(1, tokens).astype(f32)
    column = jnp.broadcast_to(row, (LANES, tokens)).T[:, :1]
    query = lax.broadcasted_iota(jnp.int32, (tokens, tokens), 0)
    key = lax.broadcasted_iota(jnp.int32, (tokens, tokens), 1)
    same = column == row
    earlier = jnp.sum(jnp.where(same & (key < query), 1.0, 0.0), axis=1, keepdims=True)
    mask_ref[...] = jnp.where(same & (key <= query), 0.0, -1e30)
    lane = lane_index((tokens, LANES))
    exponent = (lane & (HEAD_SIZE // 2 - 1)).astype(f32) * (2.0 / HEAD_SIZE)
    frequency = jnp.exp(exponent * (-math.log(rope_base)))
    angles = earlier * frequency
    cos_ref[...] = jnp.cos(angles)
    sine = jnp.sin(angles)
    sin_ref[...] = jnp.where((lane & (HEAD_SIZE // 2)) == 0, -sine, sine)
    tokens_ref[...] = tokens_turned_ref[...].astype(f32).T.astype(bf16)
    e_ref[...] = e_turned_ref[...].astype(f32).T.astype(bf16)

    low_out_ref[...] = out_ref[...].astype(bf16)
    gate_up = gate_up_ref[...]
    low_gate_up_ref[...] = gate_up.astype(bf16)
    rows = half_ref.shape[0]
    start = pl.multiple_of((where_ref[1] & 1) * rows, 16)
    half_ref[...] = gate_up_ref[pl.ds(start, rows), :].astype(bf16)
    low_down_ref[...] = down_ref[...].astype(bf16)
    replica = where_ref[2]
    turned_ref[...] = gate_up.T
    width = own_gate_up_ref.shape[0]
    own_gate_up_ref[...] = own_rows(turned_ref, replica, width)
    width = own_down_ref.shape[0]
    own_down_ref[...] = own_rows(down_ref, replica, width)
    for ref, own in ((qkv_ref, own_qkv_ref), (out_ref, own_out_ref)):
        width = own.shape[1]
        wide = jnp.concatenate(lane_blocks(ref[...]), axis=1)
        own[...] = pltpu.roll(wide, wide.shape[1] - replica * width, 1)[:, :width]


def forward_kernel(
    where_ref, tokens_ref, cos_ref, sin_ref, mask_ref, pack0, pack1, pack2, pack3,
    a_ref, q_ref, k_ref, v_ref, e0_ref, e1_ref, e2_ref, inv_ref, o_ref, weight_ref, gains_ref,
):
    me = where_ref[0]
    tokens = tokens_ref.shape[0]
    shard_rows = MODEL_WIDTH // 4
    packs = (pack0, pack1, pack2, pack3)
    lines = []
    for j in range(4):
        start = pl.multiple_of((me ^ j) * shard_rows, 16)
        weight_ref[pl.ds(start, shard_rows), :] = packs[j][:shard_rows, :]
        lines.append(packs[j][shard_rows:, :].astype(f32)[:1, :])
    bias_wide = lane_index((1, LANES)) * 0.0
    ordered = []
    for s in range(4):
        line = jnp.where((me ^ s) == 0, lines[0], 0.0)
        for j in range(1, 4):
            line = jnp.where((me ^ s) == j, lines[j], line)
        ordered.append(line)
    bias_blocks = [bias_wide for _ in range(weight_ref.shape[1] // LANES)]
    gain_blocks = [[bias_wide for _ in range(5)] for _ in range(2)]
    lane = lane_index((1, LANES))

    def put(blocks, source, width, start):
        done = 0
        while done < width:
            at, offset = divmod(start + done, LANES)
            count = min(LANES - offset, width - done)
            from_at, from_offset = divmod(done, LANES)
            count = min(count, LANES - from_offset)
            turn = (offset - from_offset) % LANES
            part = source[from_at]
            if turn:
                part = pltpu.roll(part, turn, 1)
            blocks[at] = jnp.where((lane >= offset) & (lane < offset + count), part, blocks[at])
            done += count

    bias_each = QKV_WIDTH // 4
    gain_each = 2 * MODEL_WIDTH // 4
    bias_lanes = -(-bias_each // LANES) * LANES
    for s in range(4):
        pieces = [ordered[s][:, i * LANES : (i + 1) * LANES] for i in range(8)]
        put(bias_blocks, pieces, bias_each, s * bias_each)
        put(gain_blocks[s // 2], pieces[bias_lanes // LANES :], gain_each, (s % 2) * gain_each)
    gains = [jnp.concatenate(blocks, axis=1) for blocks in gain_blocks]
    for i in range(2):
        gains_ref[i : i + 1, :] = gains[i]
    bias = jnp.concatenate(bias_blocks, axis=1)

    x = tokens_ref[...].astype(f32)
    inverse = lax.rsqrt(jnp.mean(x * x, axis=1, keepdims=True) + norm_eps)
    a = (x * inverse * gains[0][:, :MODEL_WIDTH]).astype(bf16)
    a_ref[...] = a
    p = dot_plain(a, weight_ref[...]) + bias
    cosine, sine = cos_ref[...], sin_ref[...]
    blocks = [p[:, i * LANES : (i + 1) * LANES] for i in range(8)]
    for i in range(6):
        blocks[i] = blocks[i] * cosine + swap_pairs(blocks[i]) * sine
    low = lower_half((tokens, LANES))
    for i in range(5):
        scaled = blocks[i] * HEAD_SIZE ** (-0.5)
        if i == 4:
            scaled = jnp.where(low, scaled, 0.0)
        q_ref[:, i * LANES : (i + 1) * LANES] = scaled.astype(bf16)
    keys = [both_halves(blocks[4], True), both_halves(blocks[5], False), both_halves(blocks[5], True)]
    values = [both_halves(blocks[6], False), both_halves(blocks[6], True), both_halves(blocks[7], False)]
    for g in range(KEY_VALUE_HEADS):
        k_ref[:, g * LANES : (g + 1) * LANES] = keys[g].astype(bf16)
        v_ref[:, g * LANES : (g + 1) * LANES] = values[g].astype(bf16)

    e_refs = (e0_ref, e1_ref, e2_ref)
    step = ROW_BLOCK
    low = lower_half((step, LANES))
    for at in range(tokens // step):
        rows = slice(at * step, (at + 1) * step)
        seen = (at + 1) * step
        mixed = []
        inverses = []
        for g in range(KEY_VALUE_HEADS):
            stack = head_stack(q_ref, rows, g)
            scores = dot_last(stack, k_ref[:seen, g * LANES : (g + 1) * LANES])
            scores = scores.reshape(CLUSTER, step, seen) + mask_ref[rows, :seen][None]
            lifted = jnp.exp(scores - jnp.max(scores, axis=2, keepdims=True))
            total = jnp.sum(lifted, axis=2, keepdims=True)
            kept = lifted.astype(bf16)
            e_refs[g][:, rows, :seen] = kept
            gathered = dot_plain(
                kept.reshape(CLUSTER * step, seen), v_ref[:seen, g * LANES : (g + 1) * LANES]
            ).reshape(CLUSTER, step, LANES)
            inverse_total = jnp.broadcast_to(1.0 / total, gathered.shape)
            gathered = gathered * inverse_total
            for t in range(CLUSTER):
                mixed.append(gathered[t])
                inverses.append(inverse_total[t])
        for i in range(5):
            second = mixed[2 * i + 1] if 2 * i + 1 < QUERY_HEADS else 0.0
            part = jnp.where(low, mixed[2 * i], second)
            o_ref[rows, i * LANES : (i + 1) * LANES] = part.astype(bf16)
            second = inverses[2 * i + 1] if 2 * i + 1 < QUERY_HEADS else 0.0
            inv_ref[rows, i * LANES : (i + 1) * LANES] = jnp.where(low, inverses[2 * i], second)


def project_kernel(
    where_ref, tokens_ref, o_ref, gains_ref, out0, out1, out2, out3,
    h_ref, a2_ref, a2_shift_ref, a2_turned_ref, out_weight_ref,
):
    me = where_ref[0]
    tokens = tokens_ref.shape[0]
    shard_rows = out0.shape[0]
    for j, out in enumerate((out0, out1, out2, out3)):
        start = pl.multiple_of((me ^ j) * shard_rows, 16)
        out_weight_ref[pl.ds(start, shard_rows), :] = out[...]
    x = tokens_ref[...].astype(f32)
    h = x + dot_plain(o_ref[:, :MODEL_WIDTH], out_weight_ref[...])
    h_ref[...] = h
    inverse = lax.rsqrt(jnp.mean(h * h, axis=1, keepdims=True) + norm_eps)
    a2 = h * inverse * gains_ref[1:2, :MODEL_WIDTH]
    a2_ref[...] = a2.astype(bf16)
    a2_blocks = lane_blocks(a2)
    low = lower_half((tokens, LANES))
    before = jnp.zeros((tokens, LANES), f32)
    for i in range(5):
        part = jnp.where(low, pltpu.roll(before, HEAD_SIZE, 1), pltpu.roll(a2_blocks[i], HEAD_SIZE, 1))
        a2_shift_ref[:, i * LANES : (i + 1) * LANES] = part.astype(bf16)
        before = a2_blocks[i]
    a2_turned_ref[...] = a2.T.astype(bf16)


def head_stack(ref, rows, g):
    parts = []
    for t in range(CLUSTER):
        head = g * CLUSTER + t
        block = ref[rows, (head // 2) * LANES : (head // 2 + 1) * LANES]
        low = lower_half(block.shape)
        keep = low if head % 2 == 0 else jnp.logical_not(low)
        parts.append(jnp.where(keep, block, jnp.zeros_like(block)))
    return jnp.concatenate(parts, axis=0)


def feed_kernel(groups, chunks, first, last, halved, parts, *refs):
    refs = list(refs)

    def take(count):
        taken = refs[:count]
        del refs[:count]
        return taken

    (where_ref, a2_ref, a2_shift_ref, a2_turned_ref, e_ref, e_turned_ref, base_ref) = take(7)
    gate_in, shift_in = (None, None) if first else take(2)
    gate_ups = [take(2 if halved else 1) for _ in chunks]
    downs = take(len(chunks))
    total_ref, gate_acc, shift_acc = take(3)
    mine = where_ref[1]
    total = base_ref[...]
    for c in range(len(chunks)):
        outs = take(parts)
        down = downs[c]
        if not halved:
            gate_up = gate_ups[c][0]
        else:
            gate_up = refs[-1]
            rows = gate_ups[c][0].shape[0]
            for half in range(2):
                start = pl.multiple_of(((mine & 1) ^ half) * rows, 16)
                gate_up[pl.ds(start, rows), :] = gate_ups[c][half][...]
        gate_weights = gate_up[:, :MODEL_WIDTH]
        up_weights = gate_up[:, MODEL_WIDTH - HEAD_SIZE :]
        gate = dot_last(a2_ref[...], gate_weights)
        up = dot_last(a2_shift_ref[...], up_weights)
        sigma = 1.0 / (1.0 + jnp.exp(-gate))
        active = gate * sigma
        hidden = (active * up).astype(bf16)
        total = total + dot_last(hidden, down[...])
        grad_hidden = dot_plain(e_ref[...], down[...])
        grad_gate = (grad_hidden * up * (sigma * (1.0 + gate * (1.0 - sigma)))).astype(bf16)
        grad_up = (grad_hidden * active).astype(bf16)
        half = groups // 2
        each = groups // parts
        width = OUT_ROW
        block_rows = OUT_ROW + DOWN_ROWS
        for turned, offset in ((dot_plain(a2_turned_ref[...], grad_gate), 0),
                               (dot_plain(a2_turned_ref[...], grad_up), half)):
            for b in range(half):
                at, inner = divmod(b + offset, each)
                to = inner * block_rows
                outs[at][to : to + width, :] = turned[b * width : (b + 1) * width].astype(bf16)
        turned = dot_plain(e_turned_ref[...], hidden)
        thin = MODEL_WIDTH // groups
        fill = jnp.zeros((DOWN_ROWS - thin, turned.shape[1]), f32)
        for b in range(groups):
            at, inner = divmod(b, each)
            block = jnp.concatenate([turned[b * thin : (b + 1) * thin], fill], axis=0)
            to = inner * block_rows + width
            outs[at][to : to + DOWN_ROWS, :] = block.astype(bf16)
        gate_part = dot_plain(grad_gate, gate_weights)
        shift_part = dot_plain(grad_up, up_weights)
        if c == 0 and first:
            gate_acc[...] = gate_part
            shift_acc[...] = shift_part
        elif c == 0:
            gate_acc[...] = gate_in[...] + gate_part
            shift_acc[...] = shift_in[...] + shift_part
        else:
            gate_acc[...] = gate_acc[...] + gate_part
            shift_acc[...] = shift_acc[...] + shift_part
    total_ref[...] = total.T.astype(bf16) if last else total


def core_sum_kernel(groups, parts, where_ref, *refs):
    mine = where_ref[1]
    own, came = refs[:parts], refs[parts : 2 * parts]
    gate_kept, gate_sent, down_total, held_ref = refs[2 * parts :]
    each = groups // parts
    block_rows = OUT_ROW + DOWN_ROWS
    for b in range(groups):
        at, inner = divmod(b, each)
        place = block_place(b, mine, groups)
        rows = slice(inner * block_rows, inner * block_rows + OUT_ROW)
        total = own[at][rows, :].astype(f32) + came[at][rows, :].astype(f32)
        held_ref[place] = total.astype(bf16)
        rows = slice(inner * block_rows + OUT_ROW, (inner + 1) * block_rows)
        total = own[at][rows, :].astype(f32) + came[at][rows, :].astype(f32)
        down_total[pl.ds(pl.multiple_of(place * DOWN_ROWS, 16), DOWN_ROWS), :] = total.astype(bf16)
    half = groups // 2
    gate_kept[...] = held_ref[:half]
    gate_sent[...] = held_ref[half:]


def write_message(held_ref, sent_refs, kept_ref, me, groups):
    rows = held_ref.shape[0] // 4
    each = 2 * groups // len(sent_refs)
    for j in range(4):
        start = pl.multiple_of((me ^ j) * rows, 16)
        for b in range(groups):
            block = held_ref[pl.ds(start, rows), b * LANES : (b + 1) * LANES]
            to = (j // 2) * groups + b
            if j % 2:
                at, to = divmod(to, each)
                sent_refs[at][to * rows : (to + 1) * rows, :] = block
            else:
                kept_ref[to * rows : (to + 1) * rows, :] = block


def middle_kernel(
    groups, where_ref, gate_acc, shift_acc, h_ref, e_ref, gains_ref, o_ref, inv_ref, out_weight_ref,
    dh_ref, dol_ref, small_ref, sent0, sent1, kept_ref, held_ref,
):
    me = where_ref[0]
    tokens = h_ref.shape[0]
    gain = gains_ref[1:2, :MODEL_WIDTH]
    h = h_ref[...]
    low = lower_half((tokens, LANES))
    shifted = [shift_acc[:, i * LANES : (i + 1) * LANES] for i in range(5)]
    parts = []
    for i in range(5):
        part = pltpu.roll(shifted[i], HEAD_SIZE, 1)
        after = pltpu.roll(shifted[i + 1], HEAD_SIZE, 1) if i < 4 else 0.0
        parts.append(jnp.where(low, part, after))
    da2 = gate_acc[...] + jnp.concatenate(parts, axis=1)[:, :MODEL_WIDTH]
    inverse = lax.rsqrt(jnp.mean(h * h, axis=1, keepdims=True) + norm_eps)
    weighted = da2 * gain
    inner = jnp.mean(weighted * h, axis=1, keepdims=True)
    dh = e_ref[...].astype(f32) + inverse * weighted - h * (inverse * inverse * inverse) * inner
    dh_ref[...] = dh
    small_ref[...] = jnp.sum(da2 * h * inverse, axis=0, keepdims=True)
    dhl = dh.astype(bf16)
    spread = dhl.astype(f32)
    blocks = lane_blocks(spread)
    width = MODEL_WIDTH // groups
    chosen = jnp.concatenate(
        [cut_lanes(blocks, b * width, width).astype(bf16) for b in range(groups)], axis=1
    )
    held_ref[...] = dot_first(o_ref[:, :MODEL_WIDTH], chosen).astype(bf16)
    write_message(held_ref, (sent0, sent1), kept_ref, me, groups)
    dol = dot_last(dhl, out_weight_ref[...])
    dol_blocks = lane_blocks(dol.astype(bf16).astype(f32))
    for i in range(5):
        lanes = slice(i * LANES, (i + 1) * LANES)
        dol_ref[:, lanes] = (dol_blocks[i] * inv_ref[:, lanes]).astype(bf16)


def attention_back_kernel(g, where_ref, q_ref, k_ref, v_ref, lifted_ref, o_ref, dol_ref, dq_ref, dk_ref, dv_ref):
    tokens = q_ref.shape[0]
    step = ROW_BLOCK
    lanes = slice(g * LANES, (g + 1) * LANES)
    dk = None
    dv = None
    for at in reversed(range(tokens // step)):
        rows = slice(at * step, (at + 1) * step)
        seen = (at + 1) * step
        q_stack = head_stack(q_ref, rows, g)
        o_stack = head_stack(o_ref, rows, g)
        dol_stack = head_stack(dol_ref, rows, g)
        lifted = lifted_ref[:, rows, :seen].reshape(CLUSTER * step, seen)
        inner = jnp.sum(o_stack.astype(f32) * dol_stack.astype(f32), axis=1, keepdims=True)
        grad = dot_last(dol_stack, v_ref[:seen, lanes])
        dsl = (lifted.astype(f32) * (grad - inner)).astype(bf16)
        dq = dot_plain(dsl, k_ref[:seen, lanes]) * HEAD_SIZE ** (-0.5)
        dq_ref[:, rows, :] = dq.reshape(CLUSTER, step, LANES)
        dk_part = dot_first(q_stack, dsl)
        dv_part = dot_first(dol_stack, lifted)
        if dk is None:
            dk, dv = dk_part, dv_part
        else:
            dk = jnp.concatenate([dk[:, :seen] + dk_part, dk[:, seen:]], axis=1)
            dv = jnp.concatenate([dv[:, :seen] + dv_part, dv[:, seen:]], axis=1)
    dk = dk.T
    dv = dv.T
    dk_ref[...] = dk + pltpu.roll(dk, HEAD_SIZE, 1)
    dv_ref[...] = dv + pltpu.roll(dv, HEAD_SIZE, 1)


def last_kernel(
    groups, where_ref, dq0, dq1, dq2, dk0, dk1, dk2, dv0, dv1, dv2, cos_ref, sin_ref,
    a_ref, sent0, sent1, kept_ref, dpl_ref, bias_ref, held_ref,
):
    me = where_ref[0]
    tokens = a_ref.shape[0]
    low = lower_half((tokens, LANES))
    heads = [ref[t] for ref in (dq0, dq1, dq2) for t in range(CLUSTER)]
    blocks = [jnp.where(low, heads[2 * i], heads[2 * i + 1]) for i in range(4)]
    blocks.append(jnp.where(low, heads[8], dk0[...]))
    blocks.append(jnp.where(low, dk1[...], dk2[...]))
    cosine, sine = cos_ref[...], sin_ref[...]
    blocks = [block * cosine - swap_pairs(block) * sine for block in blocks]
    blocks.append(jnp.where(low, dv0[...], dv1[...]))
    blocks.append(jnp.where(low, dv2[...], 0.0))
    low_blocks = [block.astype(bf16) for block in blocks]
    blocks = [block.astype(f32) for block in low_blocks]
    dpl_ref[...] = jnp.concatenate(low_blocks, axis=1)
    width = QKV_WIDTH // groups
    chosen = jnp.concatenate(
        [cut_lanes(blocks, b * width, width).astype(bf16) for b in range(groups)], axis=1
    )
    held_ref[...] = dot_first(a_ref[...], chosen).astype(bf16)
    write_message(held_ref, (sent0, sent1), kept_ref, me, groups)
    bias_ref[...] = jnp.concatenate([jnp.sum(block, axis=0, keepdims=True) for block in blocks], axis=1)


def input_kernel(
    where_ref, dpl_ref, bias_ref, tokens_ref, dh_ref, weight_ref, gains_ref, gain_two_ref,
    tokens_grad_ref, small_ref,
):
    bias_blocks = lane_blocks(bias_ref[...])
    x = tokens_ref[...].astype(f32)
    inverse = lax.rsqrt(jnp.mean(x * x, axis=1, keepdims=True) + norm_eps)
    da = dot_last(dpl_ref[...], weight_ref[...])
    gain_one_blocks = lane_blocks(jnp.sum(da * x * inverse, axis=0, keepdims=True))
    gain_two_blocks = lane_blocks(gain_two_ref[...])
    weighted = da * gains_ref[0:1, :MODEL_WIDTH]
    inner = jnp.mean(weighted * x, axis=1, keepdims=True)
    tokens_grad = dh_ref[...] + inverse * weighted - x * (inverse * inverse * inverse) * inner
    tokens_grad_ref[...] = tokens_grad.T.astype(bf16)

    gain_each = 2 * MODEL_WIDTH // 4
    bias_each = QKV_WIDTH // 4
    lines = []
    for s in range(4):
        source = gain_one_blocks if s < 2 else gain_two_blocks
        count = 0
        for t in range(0, gain_each, LANES):
            lines.append(cut_lanes(source, (s % 2) * gain_each + t, min(LANES, gain_each - t)))
            count += 1
        for t in range(0, bias_each, LANES):
            lines.append(cut_lanes(bias_blocks, s * bias_each + t, min(LANES, bias_each - t)))
            count += 1
        lines += [jnp.zeros((1, LANES), f32)] * (SMALL_ROWS // 4 - count)
    small_ref[...] = jnp.concatenate(lines, axis=0).astype(bf16)


def place_sum(held_ref, kept_ref, came_refs, mine, groups, rows):
    half = groups // 2
    each = 2 * groups // len(came_refs)
    for j in range(2):
        for b in range(groups):
            at = j * groups + b
            part, inner = divmod(at, each)
            total = kept_ref[at * rows : (at + 1) * rows, :].astype(f32)
            total = total + came_refs[part][inner * rows : (inner + 1) * rows, :].astype(f32)
            place = block_place(b, mine, groups)
            beyond = jnp.where((place & half) == 0, 0, half)
            to = pl.multiple_of((place + beyond + j * half) * rows, 16)
            held_ref[pl.ds(to, rows), :] = total.astype(bf16)


def halve_first_kernel(
    groups, where_ref, kept_ref, came0, came1, small_ref, small_came, sent_ref, left_ref, held_ref
):
    rows = OUT_ROW
    part = groups * rows
    place_sum(held_ref, kept_ref, (came0, came1), where_ref[1], groups, rows)
    small = small_ref[...].astype(f32) + small_came[...].astype(f32)
    for ref, start in ((left_ref, 0), (sent_ref, part)):
        ref[:part, :] = held_ref[start : start + part, :]
        ref[part:, :] = small.astype(bf16)


def down_out_kernel(groups, where_ref, down_zero, down_came, kept_ref, came0, came1, sent_ref, left_ref, held_ref):
    rows = OUT_ROW
    part = groups * rows
    place_sum(held_ref, kept_ref, (came0, came1), where_ref[1], groups, rows)
    lanes = down_zero.shape[1] // LANES
    for ref, start, first in ((left_ref, 0, 0), (sent_ref, part, groups // 2)):
        ref[:part, :] = held_ref[start : start + part, :]
        for b in range(groups // 2):
            rows = slice((first + b) * DOWN_ROWS, (first + b + 1) * DOWN_ROWS)
            total = down_zero[rows, :].astype(f32) + down_came[rows, :].astype(f32)
            for i in range(lanes):
                to = part + (b * lanes + i) * DOWN_ROWS
                ref[to : to + DOWN_ROWS, :] = total[:, i * LANES : (i + 1) * LANES].astype(bf16)


def halve_kernel(small_rows, where_ref, kept_ref, came_ref, sent_ref, left_ref):
    part = left_ref.shape[0] - small_rows
    rows = 2 * part + small_rows
    total = kept_ref[:rows, :].astype(f32) + came_ref[:rows, :].astype(f32)
    total = total.astype(bf16)
    left_ref[:part, :] = total[:part]
    sent_ref[:part, :] = total[part : 2 * part]
    if small_rows:
        left_ref[part:, :] = total[2 * part :]
        sent_ref[part:, :] = total[2 * part :]


def fold_feed_kernel(where_ref, gate_kept, gate_came, gate_across, low_kept, low_came, left_ref, sent_ref):
    blocks, rows = gate_kept.shape[:2]
    half = blocks // 2
    lanes = gate_kept.shape[2] // LANES
    first = low_kept.shape[0] - blocks * lanes * DOWN_ROWS
    for b in range(blocks):
        ref, at = (left_ref, b) if b < half else (sent_ref, b - half)
        gate_up = gate_kept[b].astype(f32) + gate_came[b].astype(f32) + gate_across[b].astype(f32)
        ref[at, :rows, :] = gate_up.astype(bf16)
        for i in range(lanes):
            start = first + (b * lanes + i) * DOWN_ROWS
            down = low_kept[start : start + DOWN_ROWS, :].astype(f32)
            down = down + low_came[start : start + DOWN_ROWS, :].astype(f32)
            ref[at, rows:, i * LANES : (i + 1) * LANES] = down.astype(bf16)


def fold_attention_kernel(where_ref, out_kept, out_came, qkv_kept, qkv_came, left_ref, sent_ref):
    rows = OUT_ROW
    blocks = out_kept.shape[0] // rows
    half = blocks // 2
    out = (out_kept[...].astype(f32) + out_came[...].astype(f32)).astype(bf16)
    qkv = (qkv_kept[...].astype(f32) + qkv_came[...].astype(f32)).astype(bf16)
    small = qkv[blocks * rows :]
    for b in range(blocks):
        ref, at = (left_ref, b) if b < half else (sent_ref, b - half)
        ref[at, :rows, :LANES] = out[b * rows : (b + 1) * rows]
        ref[at, :rows, LANES:] = qkv[b * rows : (b + 1) * rows]
        ref[at, rows:, :LANES] = small
        ref[at, rows:, LANES:] = jnp.zeros((SMALL_ROWS, LANES), bf16)


def fold_kernel(where_ref, kept_ref, came_ref, left_ref, sent_ref):
    half = left_ref.shape[0]
    for b in range(half):
        left_ref[b] = (kept_ref[b].astype(f32) + came_ref[b].astype(f32)).astype(bf16)
        at = b + half
        sent_ref[b] = (kept_ref[at].astype(f32) + came_ref[at].astype(f32)).astype(bf16)


def read_total(refs, parts):
    total = refs[0][0].astype(f32)
    for ref in refs[1:parts]:
        total = total + ref[0].astype(f32)
    return total


def step_with(refs):
    count = len(refs) // 2
    ins, outs = refs[:count], refs[count:]

    def step(at, gradient, rate):
        new = adam_update(ins[at][...], ins[at + 1][...], ins[at + 2][...], gradient, rate)
        for i in range(3):
            outs[at + i][...] = new[i]

    return ins, step


def feed_step_kernel(step_rates, parts, where_ref, *refs):
    total = read_total(refs, parts)
    ins, step = step_with(refs[parts:])
    step(0, total[: ins[0].shape[0]], step_rates[2])
    step(3, total[OUT_ROW : OUT_ROW + ins[3].shape[0]], step_rates[3])


def attention_step_kernel(step_rates, parts, where_ref, *refs):
    total = read_total(refs, parts)
    ins, step = step_with(refs[parts:])
    step(0, total[:OUT_ROW, LANES : LANES + ins[0].shape[1]], step_rates[0])
    step(3, total[:OUT_ROW, : ins[3].shape[1]], step_rates[1])
    me = where_ref[0]
    each = SMALL_ROWS // 4
    small = total[OUT_ROW:, :LANES]
    mine = small[:each]
    for s in range(1, 4):
        mine = jnp.where(me == s, small[s * each : (s + 1) * each], mine)
    line = 0
    for at in (6, 9):
        width = ins[at].shape[0]
        lines = -(-width // LANES)
        wide = jnp.concatenate([mine[line + t : line + t + 1, :] for t in range(lines)], axis=1)
        line += lines
        step(at, wide[:, :width].reshape(width), step_rates[4 if at == 6 else 5])


def swap(values, axis, bit):
    size = lax.axis_size(axis)
    return lax.ppermute(values, axis, [(i, i ^ bit) for i in range(size)])


def add_low(left, right):
    return (left.astype(f32) + right.astype(f32)).astype(bf16)


def halves(values):
    half = values.shape[0] // 2
    return values[:half], values[half:]


def own_term(total, extra, places):
    bit = 1
    while bit < extra:
        total = total + swap(total, "rep", bit)
        bit *= 2
    at = lax.axis_index("rep") % extra
    result = total
    for row, rows, lane, lanes, dim, width in places:
        part = total[row : row + rows, lane : lane + lanes]
        own = lax.dynamic_slice_in_dim(part, at * width, width, dim)
        result = lax.dynamic_update_slice(result, own, (row, lane))
    return result[None]


def finish(left, came, extra, places):
    if extra == 1:
        return [left, came]
    return [own_term((left.astype(f32) + came.astype(f32))[0], extra, places)]


def on_device(
    tokens,
    segments,
    cotangent,
    projection_weight,
    out_weight,
    gate_up_weight,
    down_weight,
    norm_gains,
    projection_bias,
    projection_first_moment,
    out_first,
    gate_up_first,
    down_first,
    gains_first,
    bias_first_moment,
    projection_second_moment,
    out_second,
    gate_up_second,
    down_second,
    gains_second,
    bias_second_moment,
):
    count = tokens.shape[0]
    replicas = lax.axis_size("rep")
    groups = min(replicas, 8)
    extra = replicas // groups
    replica = lax.axis_index("rep")
    where = jnp.stack([lax.axis_index("fsdp"), replica // extra, replica]).astype(jnp.int32)
    rates = learn_rates()
    wide = 1024
    shard_rows, ff_rows = projection_weight.shape[0], gate_up_weight.shape[0]
    q_wide = 5 * LANES
    kv_wide = KEY_VALUE_HEADS * LANES
    tokens_turned, e_turned, down_turned = tokens.T, cotangent.T, down_weight.T

    pack = pack_attention(projection_weight, norm_gains, projection_bias, wide)
    pack2 = swap(pack, "fsdp", 2)
    pack1 = swap(pack, "fsdp", 1)

    (cosine, sine, mask, tokens_low, e, low_out, low_gate_up, half, low_down,
     own_qkv, own_out, own_gate_up, own_down) = kernel_call(
        tables_kernel,
        [
            shaped((count, LANES), f32),
            shaped((count, LANES), f32),
            shaped((count, count), f32),
            shaped((count, MODEL_WIDTH), bf16),
            shaped((count, MODEL_WIDTH), bf16),
            shaped(out_weight.shape, bf16),
            shaped((ff_rows, 2 * MODEL_WIDTH), bf16),
            shaped((ff_rows // 2, 2 * MODEL_WIDTH), bf16),
            shaped((MODEL_WIDTH, ff_rows), bf16),
            shaped(projection_first_moment.shape, f32),
            shaped(out_first.shape, f32),
            shaped(gate_up_first.shape[::-1], f32),
            shaped(down_first.shape[::-1], f32),
        ],
        "tables", 3.0,
        scratch=[pltpu.VMEM((2 * MODEL_WIDTH, ff_rows), f32)], after=(pack,),
    )(
        where, segments, tokens_turned, e_turned,
        projection_weight, out_weight, gate_up_weight, down_turned,
    )

    pack2, low_out, half = gate([pack2, low_out, half], [pack1, cosine], "after_pack")
    pack3 = swap(pack2, "fsdp", 1)
    out2 = swap(low_out, "fsdp", 2)
    half_across = swap(half, "fsdp", 2)
    out1 = swap(low_out, "fsdp", 1)
    gate_up1 = swap(low_gate_up, "fsdp", 1)
    down1 = swap(low_down, "fsdp", 1)

    (a, q, k, v, lifted0, lifted1, lifted2, inv, o, weight_full, gains) = kernel_call(
        forward_kernel,
        [
            shaped((count, MODEL_WIDTH), bf16),
            shaped((count, q_wide), bf16),
            shaped((count, kv_wide), bf16),
            shaped((count, kv_wide), bf16),
        ]
        + [shaped((CLUSTER, count, count), bf16)] * 3
        + [
            shaped((count, q_wide), f32),
            shaped((count, q_wide), bf16),
            shaped((MODEL_WIDTH, wide), bf16),
            shaped((2, q_wide), f32),
        ],
        "attention_forward", 6.0,
    )(where, tokens_low, cosine, sine, mask, pack, pack1, pack2, pack3)

    (out2,) = gate([out2], [o], "after_attention")
    out3 = swap(out2, "fsdp", 1)

    h, a2, a2_shift, a2_turned, out_full = kernel_call(
        project_kernel,
        [
            shaped((count, MODEL_WIDTH), f32),
            shaped((count, MODEL_WIDTH), bf16),
            shaped((count, q_wide), bf16),
            shaped((MODEL_WIDTH, count), bf16),
            shaped((MODEL_WIDTH, MODEL_WIDTH), bf16),
        ],
        "project", 2.0,
    )(where, tokens_low, o, gains, low_out, out1, out2, out3)

    half_across, low_down_late = gate([half_across, low_down], [h, down1], "after_project")
    down2 = swap(low_down_late, "fsdp", 2)
    half_beside = swap(half_across, "rep", extra)
    half_across3 = swap(half_across, "fsdp", 1)
    gate_ups = {0: [low_gate_up], 1: [gate_up1]}
    downs = {0: low_down_late, 1: down1}

    gate_up_block = (2 * MODEL_WIDTH // groups, ff_rows)
    half_block = (groups // 2,) + gate_up_block

    def grad_parts(count):
        return [shaped((groups // count * (OUT_ROW + DOWN_ROWS), ff_rows), bf16)] * count

    def core_sum(own, sent, name, after=()):
        came = [swap(part, "fsdp", 1) for part in sent]
        return kernel_call(
            functools.partial(core_sum_kernel, groups, len(own)),
            [shaped(half_block, bf16), shaped(half_block, bf16), shaped((groups * DOWN_ROWS, ff_rows), bf16)],
            name, 0.2, scratch=[pltpu.VMEM((groups,) + gate_up_block, bf16)], after=after,
        )(where, *own, *came)

    grads = {}
    total, accumulated = h, []
    for j in (1, 0, 3, 2):
        first, last = j == 1, j == 2
        waits = (half_across,) if first else (zero_sent,) if j == 3 else ()
        parts = 4 if j > 1 else 2
        total, *results = kernel_call(
            functools.partial(feed_kernel, groups, (j,), first, last, j > 1, parts),
            [
                shaped((MODEL_WIDTH, count), bf16) if last else shaped((count, MODEL_WIDTH), f32),
                shaped((count, MODEL_WIDTH), f32),
                shaped((count, q_wide), f32),
            ] + grad_parts(parts),
            "feed_" + str(j), 0.5,
            scratch=[pltpu.VMEM((ff_rows, 2 * MODEL_WIDTH), bf16)] if j > 1 else [],
            after=waits,
        )(
            where, a2, a2_shift, a2_turned, e, e_turned, total, *accumulated, *gate_ups[j], downs[j],
        )
        accumulated, grads[j] = results[:2], results[2:]
        if j == 0:
            half_beside, down2 = gate([half_beside, down2], [total], "after_feed_0")
            gate_ups[2] = [half_across, half_beside]
            gate_ups[3] = [half_across3, swap(half_beside, "fsdp", 1)]
            downs[2], downs[3] = down2, swap(down2, "fsdp", 1)
            zero_kept, zero_sent, down_zero = core_sum(grads[0], grads[1], "core_sum_0")
            zero_came = swap(zero_sent, "rep", extra)
    output = total.T

    two_kept, two_sent, down_two = core_sum(grads[2], grads[3], "core_sum_2", (zero_came,))
    two_came = swap(two_sent, "rep", extra)
    down_came = swap(down_two, "fsdp", 2)

    message = 2 * groups * shard_rows
    dh, dol, gain_two, *out_parts = kernel_call(
        functools.partial(middle_kernel, groups),
        [
            shaped((count, MODEL_WIDTH), f32),
            shaped((count, q_wide), bf16),
            shaped((1, MODEL_WIDTH), f32),
            shaped((message // 2, LANES), bf16),
            shaped((message // 2, LANES), bf16),
            shaped((message, LANES), bf16),
        ],
        "middle", 0.5, after=(two_sent, down_two),
        scratch=[pltpu.VMEM((MODEL_WIDTH, groups * LANES), bf16)],
    )(where, *accumulated, h, e, gains, o, inv, out_full)

    def halve(kept, came, small_rows, name, after=()):
        part = (kept.shape[0] - small_rows) // 2 + small_rows
        return kernel_call(
            functools.partial(halve_kernel, small_rows),
            [shaped((part, LANES), bf16)] * 2, name, 0.3, after=after,
        )(where, kept, came)

    *out_sent, out_kept = out_parts
    out_came = [swap(part, "fsdp", 1) for part in out_sent]

    dqs, dks, dvs = [], [], []
    waits = ()
    for g, lifted in enumerate((lifted0, lifted1, lifted2)):
        if g == 2:
            two_kept, down_zero = gate([two_kept, down_zero], [dqs[1]], "after_back")
            two = add_low(two_kept, two_came)
            gate_up_across = swap(two, "fsdp", 2)
            low_rows = message // 2 + groups // 2 * (ff_rows // LANES) * DOWN_ROWS
            low_sent, low_kept = kernel_call(
                functools.partial(down_out_kernel, groups),
                [shaped((low_rows, LANES), bf16)] * 2, "down_out", 0.2,
                scratch=[pltpu.VMEM((message, LANES), bf16)],
            )(where, down_zero, down_came, out_kept, *out_came)
            low_came = swap(low_sent, "rep", extra)
            waits = (two, low_sent)
        dq, dk, dv = kernel_call(
            functools.partial(attention_back_kernel, g),
            [shaped((CLUSTER, count, LANES), f32), shaped((count, LANES), f32), shaped((count, LANES), f32)],
            "attention_back_" + str(g), 0.2, after=waits + tuple(dqs),
        )(where, q, k, v, lifted, o, dol)
        dqs.append(dq)
        dks.append(dk)
        dvs.append(dv)

    *sent, kept, dpl, bias_grad = kernel_call(
        functools.partial(last_kernel, groups),
        [
            shaped((message // 2, LANES), bf16),
            shaped((message // 2, LANES), bf16),
            shaped((message, LANES), bf16),
            shaped((count, wide), bf16),
            shaped((1, wide), f32),
        ],
        "last", 0.2,
        scratch=[pltpu.VMEM((MODEL_WIDTH, groups * LANES), bf16)],
    )(where, *dqs, *dks, *dvs, cosine, sine, a)
    came = [swap(part, "fsdp", 1) for part in sent]
    tokens_grad, small = kernel_call(
        input_kernel,
        [shaped((MODEL_WIDTH, count), bf16), shaped((SMALL_ROWS, LANES), bf16)], "input_gradient", 0.2,
    )(where, dpl, bias_grad, tokens_low, dh, weight_full, gains, gain_two)
    small_came = swap(small, "fsdp", 1)
    sent, kept = kernel_call(
        functools.partial(halve_first_kernel, groups),
        [shaped((message // 2 + SMALL_ROWS, LANES), bf16)] * 2, "halve_first", 0.3, after=(gate_up_across,),
        scratch=[pltpu.VMEM((message, LANES), bf16)],
    )(where, kept, *came, small, small_came)
    came = swap(sent, "rep", extra)

    quarter = groups // 4
    rows = OUT_ROW + DOWN_ROWS
    feed_left, feed_sent = kernel_call(
        fold_feed_kernel, [shaped((quarter, rows, ff_rows), bf16)] * 2, "fold_feed", 0.5, after=(sent,)
    )(where, zero_kept, zero_came, gate_up_across, low_kept, low_came)
    feed_came = swap(feed_sent, "rep", 2 * extra)
    out_sent, out_kept = kernel_call(
        functools.partial(halve_kernel, 0),
        [shaped((message // 4, LANES), bf16)] * 2, "out_halve", 0.3, after=(feed_sent,),
    )(where, low_kept, low_came)
    out_came = swap(out_sent, "fsdp", 2)
    sent, kept = halve(kept, came, SMALL_ROWS, "halve_2", (out_sent,))
    came = swap(sent, "fsdp", 2)

    def fold(left, came, name, after=()):
        half = left.shape[0] // 2
        return kernel_call(
            fold_kernel, [shaped((half,) + left.shape[1:], bf16)] * 2, name, 0.3, after=after
        )(where, left, came)

    bits = [1 << i for i in range(2, groups.bit_length() - 1)]
    for bit in bits:
        feed_left, feed_sent = fold(feed_left, feed_came, "fold_feed_" + str(bit), (sent,))
        feed_came = swap(feed_sent, "rep", bit * extra)
    left, sent = kernel_call(
        fold_attention_kernel,
        [shaped((quarter, OUT_ROW + SMALL_ROWS, 2 * LANES), bf16)] * 2, "fold_attention", 0.5, after=(feed_sent,),
    )(where, out_kept, out_came, kept, came)
    came = swap(sent, "rep", 2 * extra)
    for bit in bits:
        left, sent = fold(left, came, "fold_attention_" + str(bit), (feed_came,))
        came = swap(sent, "rep", bit * extra)

    feed_states = (
        own_gate_up, gate_up_first.T, gate_up_second.T, own_down, down_first.T, down_second.T,
    )
    wide_gate, wide_down = own_gate_up.shape[0] * extra, own_down.shape[0] * extra
    feed_parts = finish(feed_left, feed_came, extra, (
        (0, wide_gate, 0, ff_rows, 0, own_gate_up.shape[0]),
        (OUT_ROW, wide_down, 0, ff_rows, 0, own_down.shape[0]),
    ))
    feed_news = kernel_call(
        functools.partial(feed_step_kernel, rates, len(feed_parts)),
        [shaped(state.shape, f32) for state in feed_states], "feed_step", 0.5, after=(sent,),
    )(where, *feed_parts, *feed_states)
    states = (
        own_qkv, projection_first_moment, projection_second_moment,
        own_out, out_first, out_second,
        norm_gains, gains_first, gains_second,
        projection_bias, bias_first_moment, bias_second_moment,
    )
    parts = finish(left, came, extra, (
        (0, OUT_ROW, LANES, own_qkv.shape[1] * extra, 1, own_qkv.shape[1]),
        (0, OUT_ROW, 0, own_out.shape[1] * extra, 1, own_out.shape[1]),
    ))
    news = kernel_call(
        functools.partial(attention_step_kernel, rates, len(parts)),
        [shaped(state.shape, f32) for state in states], "attention_step", 1.0,
    )(where, *parts, *states)
    return (
        output,
        tokens_grad.T,
        *news[:6],
        *[new.T for new in feed_news],
        *news[6:],
    )


def solution(mesh):
    rows = P(("rep", "fsdp"), None)
    weight = P("fsdp", None)
    state = P("fsdp", "rep")
    vector = P("fsdp")
    states = (state,) * 4 + (vector,) * 2
    in_specs = (rows, P(("rep", "fsdp")), rows) + (weight,) * 4 + (vector,) * 2 + states + states
    out_specs = (rows, rows) + (state,) * 12 + (vector,) * 6
    return jax.shard_map(
        on_device, mesh=mesh, in_specs=in_specs, out_specs=out_specs, check_vma=False
    )
```

```python
import functools
import math

import jax
import jax.numpy as jnp
from jax import lax
from jax.experimental import pallas as pl
from jax.experimental.pallas import tpu as pltpu
from jax.sharding import PartitionSpec as P

MODEL_WIDTH = 576
QUERY_HEADS = 9
KEY_VALUE_HEADS = 3
HEAD_SIZE = 64
FF = 1536
STEP = 10

norm_eps = 1e-05
rope_base = 100000.0
beta_one = 0.9
beta_two = 0.95
adam_eps = 1e-08
decay_rate = 0.1

LANES = 128
QKV_WIDTH = (QUERY_HEADS + 2 * KEY_VALUE_HEADS) * HEAD_SIZE
CLUSTER = QUERY_HEADS // KEY_VALUE_HEADS
SMALL_ROWS = 32
ROW_BLOCK = 256
OUT_ROW = MODEL_WIDTH // 4
DOWN_ROWS = 80
bf16 = jnp.bfloat16
f32 = jnp.float32


def learn_rates():
    out_fan = max(QUERY_HEADS * HEAD_SIZE // 16, 1)
    return (MODEL_WIDTH ** (-0.5), out_fan ** (-0.5), MODEL_WIDTH ** (-0.5), FF ** (-0.5), 0.5, 0.5)


def adam_update(weight, first_moment, second_moment, gradient, step_rate):
    first_new = beta_one * first_moment + (1.0 - beta_one) * gradient
    second_new = beta_two * second_moment + (1.0 - beta_two) * gradient * gradient
    first_fix = 1.0 - beta_one**STEP
    second_fix = 1.0 - beta_two**STEP
    direction = first_new / first_fix / (jnp.sqrt(second_new / second_fix) + adam_eps)
    return (first_new, second_new, weight - step_rate * (direction + decay_rate * weight))


def dot_plain(left, right):
    return lax.dot_general(left, right, (((1,), (0,)), ((), ())), preferred_element_type=f32)


def dot_last(left, right):
    return lax.dot_general(left, right, (((1,), (1,)), ((), ())), preferred_element_type=f32)


def dot_first(left, right):
    return lax.dot_general(left, right, (((0,), (0,)), ((), ())), preferred_element_type=f32)


def kernel_call(body, outs, name, time, scratch=(), vmem=12, after=()):
    def call(scalars, *arrays):
        count = len(after)

        def run(*refs):
            body(refs[0], *refs[1 + count :])

        return pl.pallas_call(
            run,
            out_shape=tuple(outs),
            in_specs=[pl.BlockSpec(memory_space=pltpu.SMEM)]
            + [pl.BlockSpec(memory_space=pl.ANY)] * count
            + [pl.BlockSpec(memory_space=pltpu.VMEM)] * len(arrays),
            out_specs=tuple(pl.BlockSpec(memory_space=pltpu.VMEM) for _ in outs),
            scratch_shapes=list(scratch),
            name=name,
            compiler_params=pltpu.CompilerParams(vmem_limit_bytes=vmem * 2**20),
            cost_estimate=pl.CostEstimate(
                flops=int(time * 1.15e9), bytes_accessed=0, transcendentals=0
            ),
        )(scalars, *after, *arrays)

    return call


def gate(values, after, name):
    def nothing(*refs):
        pass

    result = pl.pallas_call(
        nothing,
        out_shape=tuple(shaped(v.shape, v.dtype) for v in values),
        in_specs=[pl.BlockSpec(memory_space=pl.ANY)] * (len(values) + len(after)),
        out_specs=tuple(pl.BlockSpec(memory_space=pl.ANY) for _ in values),
        input_output_aliases={i: i for i in range(len(values))},
        name=name,
        compiler_params=pltpu.CompilerParams(vmem_limit_bytes=2**20),
        cost_estimate=pl.CostEstimate(flops=0, bytes_accessed=0, transcendentals=0),
    )(*values, *after)
    return list(result)


def shaped(shape, dtype):
    return jax.ShapeDtypeStruct(tuple(shape), dtype)


def lane_index(shape):
    return lax.broadcasted_iota(jnp.int32, shape, len(shape) - 1)


def lower_half(shape):
    return lane_index(shape) < HEAD_SIZE


def swap_pairs(block):
    first = (lane_index(block.shape) & (HEAD_SIZE // 2)) == 0
    ahead = pltpu.roll(block, LANES - HEAD_SIZE // 2, 1)
    behind = pltpu.roll(block, HEAD_SIZE // 2, 1)
    return jnp.where(first, ahead, behind)


def both_halves(block, upper):
    other = pltpu.roll(block, HEAD_SIZE, 1)
    low = lower_half(block.shape)
    return jnp.where(low, other, block) if upper else jnp.where(low, block, other)


def cut_lanes(blocks, start, width):
    at, offset = divmod(start, LANES)
    lane = lane_index(blocks[0].shape)
    part = blocks[at]
    if offset:
        part = pltpu.roll(part, LANES - offset, 1)
        if offset + width > LANES:
            after = pltpu.roll(blocks[at + 1], LANES - offset, 1)
            part = jnp.where(lane < LANES - offset, part, after)
    if width < LANES:
        part = jnp.where(lane < width, part, 0.0)
    return part


def lane_blocks(values):
    width = values.shape[1]
    full = width // LANES
    blocks = [values[:, i * LANES : (i + 1) * LANES] for i in range(full)]
    if width % LANES:
        rest = values[:, full * LANES :]
        fill = jnp.zeros((values.shape[0], LANES - width % LANES), values.dtype)
        blocks.append(jnp.concatenate([rest, fill], axis=1))
    return blocks


def block_place(block, mine, groups):
    away = mine ^ block
    place = 0
    bit = 1
    while bit < groups:
        place = place * 2 + jnp.where((away & bit) == 0, 0, 1)
        bit *= 2
    return place


def own_rows(ref, replica, width):
    if width % 8 == 0:
        return ref[pl.ds(pl.multiple_of(replica * width, 8), width), :]
    rows = ref.shape[0]
    return pltpu.roll(ref[...], rows - replica * width, 0)[:width]


def pack_kernel(qkv_hbm, gains_hbm, bias_hbm, pack_ref, qkv_ref, gains_ref, bias_ref, sems):
    copies = [
        pltpu.make_async_copy(source, target, sems.at[i])
        for i, (source, target) in enumerate(
            ((qkv_hbm, qkv_ref), (gains_hbm, gains_ref), (bias_hbm, bias_ref))
        )
    ]
    for copy in copies:
        copy.start()
    for copy in copies:
        copy.wait()
    rows = qkv_ref.shape[0]
    pack_ref[:rows, :QKV_WIDTH] = qkv_ref[...].astype(bf16)
    pack_ref[:rows, QKV_WIDTH:] = jnp.zeros((rows, pack_ref.shape[1] - QKV_WIDTH), bf16)
    spare = pack_ref.shape[0] - rows
    bias, gains = (ref[...].reshape(1, ref.shape[0]) for ref in (bias_ref, gains_ref))
    extra = jnp.concatenate(lane_blocks(bias) + lane_blocks(gains), axis=1)
    line = jnp.concatenate(
        [extra, jnp.zeros((1, pack_ref.shape[1] - extra.shape[1]), f32)], axis=1
    )
    pack_ref[rows:, :] = jnp.broadcast_to(line, (spare, line.shape[1])).astype(bf16)


def pack_attention(weight, gains, bias, wide):
    return pl.pallas_call(
        pack_kernel,
        out_shape=shaped((weight.shape[0] + 16, wide), bf16),
        in_specs=[pl.BlockSpec(memory_space=pl.ANY)] * 3,
        out_specs=pl.BlockSpec(memory_space=pltpu.VMEM),
        scratch_shapes=[
            pltpu.VMEM(weight.shape, f32),
            pltpu.VMEM(gains.shape, f32),
            pltpu.VMEM(bias.shape, f32),
            pltpu.SemaphoreType.DMA((3,)),
        ],
        name="pack_attention",
        compiler_params=pltpu.CompilerParams(vmem_limit_bytes=60 * 2**20),
        cost_estimate=pl.CostEstimate(flops=10**9, bytes_accessed=0, transcendentals=0),
    )(weight, gains, bias)


def tables_kernel(
    where_ref, segments_ref, tokens_turned_ref, e_turned_ref, qkv_ref, out_ref, gate_up_ref, down_ref,
    cos_ref, sin_ref, mask_ref, tokens_ref, e_ref, low_out_ref, low_gate_up_ref, half_ref, low_down_ref,
    own_qkv_ref, own_out_ref, own_gate_up_ref, own_down_ref, turned_ref,
):
    tokens = segments_ref.shape[0]
    row = segments_ref[...].reshape(1, tokens).astype(f32)
    column = jnp.broadcast_to(row, (LANES, tokens)).T[:, :1]
    query = lax.broadcasted_iota(jnp.int32, (tokens, tokens), 0)
    key = lax.broadcasted_iota(jnp.int32, (tokens, tokens), 1)
    same = column == row
    earlier = jnp.sum(jnp.where(same & (key < query), 1.0, 0.0), axis=1, keepdims=True)
    mask_ref[...] = jnp.where(same & (key <= query), 0.0, -1e30)
    lane = lane_index((tokens, LANES))
    exponent = (lane & (HEAD_SIZE // 2 - 1)).astype(f32) * (2.0 / HEAD_SIZE)
    frequency = jnp.exp(exponent * (-math.log(rope_base)))
    angles = earlier * frequency
    cos_ref[...] = jnp.cos(angles)
    sine = jnp.sin(angles)
    sin_ref[...] = jnp.where((lane & (HEAD_SIZE // 2)) == 0, -sine, sine)
    tokens_ref[...] = tokens_turned_ref[...].astype(f32).T.astype(bf16)
    e_ref[...] = e_turned_ref[...].astype(f32).T.astype(bf16)

    low_out_ref[...] = out_ref[...].astype(bf16)
    gate_up = gate_up_ref[...]
    whole = MODEL_WIDTH // LANES * LANES
    blocks = [gate_up[:, i * LANES : (i + 1) * LANES] for i in range(gate_up.shape[1] // LANES)]
    low = lower_half(blocks[0].shape)
    low_gate_up_ref[:, :whole] = gate_up[:, :whole].astype(bf16)
    first = MODEL_WIDTH // LANES
    turned = [pltpu.roll(block, HEAD_SIZE, 1) for block in blocks[first:]]
    for i in range(first):
        block = jnp.where(low, turned[i], turned[i + 1])
        low_gate_up_ref[:, whole + i * LANES : whole + (i + 1) * LANES] = block.astype(bf16)
    low_gate_up_ref[:, 2 * whole :] = jnp.where(low, blocks[first], blocks[-1]).astype(bf16)
    rows = half_ref.shape[0]
    start = pl.multiple_of((where_ref[1] & 1) * rows, 16)
    half_ref[...] = low_gate_up_ref[pl.ds(start, rows), :]
    low_down_ref[...] = down_ref[...].astype(bf16)
    replica = where_ref[2]
    turned_ref[...] = gate_up.T
    width = own_gate_up_ref.shape[0]
    own_gate_up_ref[...] = own_rows(turned_ref, replica, width)
    width = own_down_ref.shape[0]
    own_down_ref[...] = own_rows(down_ref, replica, width)
    for ref, own in ((qkv_ref, own_qkv_ref), (out_ref, own_out_ref)):
        width = own.shape[1]
        wide = jnp.concatenate(lane_blocks(ref[...]), axis=1)
        own[...] = pltpu.roll(wide, wide.shape[1] - replica * width, 1)[:, :width]


def forward_kernel(
    where_ref, tokens_ref, cos_ref, sin_ref, mask_ref, pack0, pack1, pack2, pack3,
    a_ref, q_ref, k_ref, v_ref, e0_ref, e1_ref, e2_ref, inv_ref, o_ref, weight_ref, gains_ref,
):
    me = where_ref[0]
    tokens = tokens_ref.shape[0]
    shard_rows = MODEL_WIDTH // 4
    packs = (pack0, pack1, pack2, pack3)
    lines = []
    for j in range(4):
        start = pl.multiple_of((me ^ j) * shard_rows, 16)
        weight_ref[pl.ds(start, shard_rows), :] = packs[j][:shard_rows, :]
        lines.append(packs[j][shard_rows:, :].astype(f32)[:1, :])
    bias_wide = lane_index((1, LANES)) * 0.0
    ordered = []
    for s in range(4):
        line = jnp.where((me ^ s) == 0, lines[0], 0.0)
        for j in range(1, 4):
            line = jnp.where((me ^ s) == j, lines[j], line)
        ordered.append(line)
    bias_blocks = [bias_wide for _ in range(weight_ref.shape[1] // LANES)]
    gain_blocks = [[bias_wide for _ in range(5)] for _ in range(2)]
    lane = lane_index((1, LANES))

    def put(blocks, source, width, start):
        done = 0
        while done < width:
            at, offset = divmod(start + done, LANES)
            count = min(LANES - offset, width - done)
            from_at, from_offset = divmod(done, LANES)
            count = min(count, LANES - from_offset)
            turn = (offset - from_offset) % LANES
            part = source[from_at]
            if turn:
                part = pltpu.roll(part, turn, 1)
            blocks[at] = jnp.where((lane >= offset) & (lane < offset + count), part, blocks[at])
            done += count

    bias_each = QKV_WIDTH // 4
    gain_each = 2 * MODEL_WIDTH // 4
    bias_lanes = -(-bias_each // LANES) * LANES
    for s in range(4):
        pieces = [ordered[s][:, i * LANES : (i + 1) * LANES] for i in range(8)]
        put(bias_blocks, pieces, bias_each, s * bias_each)
        put(gain_blocks[s // 2], pieces[bias_lanes // LANES :], gain_each, (s % 2) * gain_each)
    gains = [jnp.concatenate(blocks, axis=1) for blocks in gain_blocks]
    for i in range(2):
        gains_ref[i : i + 1, :] = gains[i]
    bias = jnp.concatenate(bias_blocks, axis=1)

    x = tokens_ref[...].astype(f32)
    inverse = lax.rsqrt(jnp.mean(x * x, axis=1, keepdims=True) + norm_eps)
    a = (x * inverse * gains[0][:, :MODEL_WIDTH]).astype(bf16)
    a_ref[...] = a
    p = dot_plain(a, weight_ref[...]) + bias
    cosine, sine = cos_ref[...], sin_ref[...]
    blocks = [p[:, i * LANES : (i + 1) * LANES] for i in range(8)]
    for i in range(6):
        blocks[i] = blocks[i] * cosine + swap_pairs(blocks[i]) * sine
    low = lower_half((tokens, LANES))
    for i in range(5):
        scaled = blocks[i] * HEAD_SIZE ** (-0.5)
        if i == 4:
            scaled = jnp.where(low, scaled, 0.0)
        q_ref[:, i * LANES : (i + 1) * LANES] = scaled.astype(bf16)
    keys = [both_halves(blocks[4], True), both_halves(blocks[5], False), both_halves(blocks[5], True)]
    values = [both_halves(blocks[6], False), both_halves(blocks[6], True), both_halves(blocks[7], False)]
    for g in range(KEY_VALUE_HEADS):
        k_ref[:, g * LANES : (g + 1) * LANES] = keys[g].astype(bf16)
        v_ref[:, g * LANES : (g + 1) * LANES] = values[g].astype(bf16)

    e_refs = (e0_ref, e1_ref, e2_ref)
    step = ROW_BLOCK
    low = lower_half((step, LANES))
    for at in range(tokens // step):
        rows = slice(at * step, (at + 1) * step)
        seen = (at + 1) * step
        mixed = []
        inverses = []
        for g in range(KEY_VALUE_HEADS):
            stack = head_stack(q_ref, rows, g)
            scores = dot_last(stack, k_ref[:seen, g * LANES : (g + 1) * LANES])
            scores = scores.reshape(CLUSTER, step, seen) + mask_ref[rows, :seen][None]
            lifted = jnp.exp(scores - jnp.max(scores, axis=2, keepdims=True))
            total = jnp.sum(lifted, axis=2, keepdims=True)
            kept = lifted.astype(bf16)
            e_refs[g][:, rows, :seen] = kept
            gathered = dot_plain(
                kept.reshape(CLUSTER * step, seen), v_ref[:seen, g * LANES : (g + 1) * LANES]
            ).reshape(CLUSTER, step, LANES)
            inverse_total = jnp.broadcast_to(1.0 / total, gathered.shape)
            gathered = gathered * inverse_total
            for t in range(CLUSTER):
                mixed.append(gathered[t])
                inverses.append(inverse_total[t])
        for i in range(5):
            second = mixed[2 * i + 1] if 2 * i + 1 < QUERY_HEADS else 0.0
            part = jnp.where(low, mixed[2 * i], second)
            o_ref[rows, i * LANES : (i + 1) * LANES] = part.astype(bf16)
            second = inverses[2 * i + 1] if 2 * i + 1 < QUERY_HEADS else 0.0
            inv_ref[rows, i * LANES : (i + 1) * LANES] = jnp.where(low, inverses[2 * i], second)


def project_kernel(
    where_ref, tokens_ref, o_ref, gains_ref, out0, out1, out2, out3,
    h_ref, a2_ref, a2_turned_ref, out_weight_ref,
):
    me = where_ref[0]
    tokens = tokens_ref.shape[0]
    shard_rows = out0.shape[0]
    for j, out in enumerate((out0, out1, out2, out3)):
        start = pl.multiple_of((me ^ j) * shard_rows, 16)
        out_weight_ref[pl.ds(start, shard_rows), :] = out[...]
    x = tokens_ref[...].astype(f32)
    h = x + dot_plain(o_ref[:, :MODEL_WIDTH], out_weight_ref[...])
    h_ref[...] = h
    inverse = lax.rsqrt(jnp.mean(h * h, axis=1, keepdims=True) + norm_eps)
    a2 = h * inverse * gains_ref[1:2, :MODEL_WIDTH]
    for i, block in enumerate(lane_blocks(a2)):
        a2_ref[:, i * LANES : (i + 1) * LANES] = block.astype(bf16)
    a2_turned_ref[...] = a2.T.astype(bf16)


def head_stack(ref, rows, g):
    parts = []
    for t in range(CLUSTER):
        head = g * CLUSTER + t
        block = ref[rows, (head // 2) * LANES : (head // 2 + 1) * LANES]
        low = lower_half(block.shape)
        keep = low if head % 2 == 0 else jnp.logical_not(low)
        parts.append(jnp.where(keep, block, jnp.zeros_like(block)))
    return jnp.concatenate(parts, axis=0)


def feed_kernel(groups, first, last, halved, parts, *refs):
    refs = list(refs)

    def take(count):
        taken = refs[:count]
        del refs[:count]
        return taken

    where_ref, a2_ref, a2_turned_ref, e_ref, e_turned_ref, base_ref = take(6)
    acc_in = None if first else take(1)[0]
    gate_ups = take(2 if halved else 1)
    (down,) = take(1)
    total_ref, acc_ref = take(2)
    outs = take(parts)
    (stack,) = refs
    mine = where_ref[1]
    hidden_rows = down.shape[1]
    whole = MODEL_WIDTH // LANES * LANES
    for half, gate_up in enumerate(gate_ups):
        rows = gate_up.shape[0]
        start = pl.multiple_of(((mine & 1) ^ half) * rows, 16) if halved else 0
        rest = gate_up[:, 2 * whole :]
        turned = pltpu.roll(rest.astype(f32), HEAD_SIZE, 1).astype(bf16)
        stack[pl.ds(start, rows), :whole] = gate_up[:, :whole]
        stack[pl.ds(start, rows), whole:] = rest
        start = start + hidden_rows
        stack[pl.ds(start, rows), :whole] = gate_up[:, whole : 2 * whole]
        stack[pl.ds(start, rows), whole:] = turned
    both = dot_last(a2_ref[...], stack[...])
    gate, up = both[:, :hidden_rows], both[:, hidden_rows:]
    sigma = 1.0 / (1.0 + jnp.exp(-gate))
    active = gate * sigma
    hidden = (active * up).astype(bf16)
    grad_hidden = dot_plain(e_ref[...], down[...])
    grad_gate = (grad_hidden * up * (sigma * (1.0 + gate * (1.0 - sigma)))).astype(bf16)
    grad_up = (grad_hidden * active).astype(bf16)
    grads = jnp.concatenate([grad_gate, grad_up], axis=1)
    half = groups // 2
    each = groups // parts
    width = OUT_ROW
    block_rows = OUT_ROW + DOWN_ROWS
    turned = dot_plain(a2_turned_ref[...], grads)
    for b in range(groups):
        at, inner = divmod(b, each)
        row, lane = (b % half) * width, (b // half) * hidden_rows
        to = inner * block_rows
        block = turned[row : row + width, lane : lane + hidden_rows]
        outs[at][to : to + width, :] = block.astype(bf16)
    turned = dot_plain(e_turned_ref[...], hidden)
    thin = MODEL_WIDTH // groups
    fill = jnp.zeros((DOWN_ROWS - thin, turned.shape[1]), f32)
    for b in range(groups):
        at, inner = divmod(b, each)
        block = jnp.concatenate([turned[b * thin : (b + 1) * thin], fill], axis=0)
        to = inner * block_rows + width
        outs[at][to : to + DOWN_ROWS, :] = block.astype(bf16)
    part = dot_plain(grads, stack[...])
    acc_ref[...] = part if first else acc_in[...] + part
    total = base_ref[...] + dot_last(hidden, down[...])
    total_ref[...] = total.T.astype(bf16) if last else total


def core_sum_kernel(groups, parts, where_ref, *refs):
    mine = where_ref[1]
    own, came = refs[:parts], refs[parts : 2 * parts]
    gate_kept, gate_sent, down_total, held_ref = refs[2 * parts :]
    each = groups // parts
    block_rows = OUT_ROW + DOWN_ROWS
    for b in range(groups):
        at, inner = divmod(b, each)
        place = block_place(b, mine, groups)
        rows = slice(inner * block_rows, inner * block_rows + OUT_ROW)
        total = own[at][rows, :].astype(f32) + came[at][rows, :].astype(f32)
        held_ref[place] = total.astype(bf16)
        rows = slice(inner * block_rows + OUT_ROW, (inner + 1) * block_rows)
        total = own[at][rows, :].astype(f32) + came[at][rows, :].astype(f32)
        down_total[pl.ds(pl.multiple_of(place * DOWN_ROWS, 16), DOWN_ROWS), :] = total.astype(bf16)
    half = groups // 2
    gate_kept[...] = held_ref[:half]
    gate_sent[...] = held_ref[half:]


def write_message(held_ref, sent_refs, kept_ref, me, groups):
    rows = held_ref.shape[0] // 4
    each = 2 * groups // len(sent_refs)
    for j in range(4):
        start = pl.multiple_of((me ^ j) * rows, 16)
        for b in range(groups):
            block = held_ref[pl.ds(start, rows), b * LANES : (b + 1) * LANES]
            to = (j // 2) * groups + b
            if j % 2:
                at, to = divmod(to, each)
                sent_refs[at][to * rows : (to + 1) * rows, :] = block
            else:
                kept_ref[to * rows : (to + 1) * rows, :] = block


def middle_kernel(
    groups, where_ref, acc_ref, h_ref, e_ref, gains_ref, o_ref, inv_ref, out_weight_ref,
    dh_ref, dol_ref, small_ref, sent0, sent1, kept_ref, held_ref,
):
    me = where_ref[0]
    tokens = h_ref.shape[0]
    gain = gains_ref[1:2, :MODEL_WIDTH]
    h = h_ref[...]
    da2 = acc_ref[:, :MODEL_WIDTH]
    inverse = lax.rsqrt(jnp.mean(h * h, axis=1, keepdims=True) + norm_eps)
    weighted = da2 * gain
    inner = jnp.mean(weighted * h, axis=1, keepdims=True)
    dh = e_ref[...].astype(f32) + inverse * weighted - h * (inverse * inverse * inverse) * inner
    dh_ref[...] = dh
    small_ref[...] = jnp.sum(da2 * h * inverse, axis=0, keepdims=True)
    dhl = dh.astype(bf16)
    spread = dhl.astype(f32)
    blocks = lane_blocks(spread)
    width = MODEL_WIDTH // groups
    chosen = jnp.concatenate(
        [cut_lanes(blocks, b * width, width).astype(bf16) for b in range(groups)], axis=1
    )
    held_ref[...] = dot_first(o_ref[:, :MODEL_WIDTH], chosen).astype(bf16)
    write_message(held_ref, (sent0, sent1), kept_ref, me, groups)
    dol = dot_last(dhl, out_weight_ref[...])
    dol_blocks = lane_blocks(dol.astype(bf16).astype(f32))
    for i in range(5):
        lanes = slice(i * LANES, (i + 1) * LANES)
        dol_ref[:, lanes] = (dol_blocks[i] * inv_ref[:, lanes]).astype(bf16)


def attention_back_kernel(g, where_ref, q_ref, k_ref, v_ref, lifted_ref, o_ref, dol_ref, dq_ref, dk_ref, dv_ref):
    tokens = q_ref.shape[0]
    step = ROW_BLOCK
    lanes = slice(g * LANES, (g + 1) * LANES)
    dk = None
    dv = None
    for at in reversed(range(tokens // step)):
        rows = slice(at * step, (at + 1) * step)
        seen = (at + 1) * step
        q_stack = head_stack(q_ref, rows, g)
        o_stack = head_stack(o_ref, rows, g)
        dol_stack = head_stack(dol_ref, rows, g)
        lifted = lifted_ref[:, rows, :seen].reshape(CLUSTER * step, seen)
        inner = jnp.sum(o_stack.astype(f32) * dol_stack.astype(f32), axis=1, keepdims=True)
        grad = dot_last(dol_stack, v_ref[:seen, lanes])
        dsl = (lifted.astype(f32) * (grad - inner)).astype(bf16)
        dq = dot_plain(dsl, k_ref[:seen, lanes]) * HEAD_SIZE ** (-0.5)
        dq_ref[:, rows, :] = dq.reshape(CLUSTER, step, LANES)
        dk_part = dot_first(q_stack, dsl)
        dv_part = dot_first(dol_stack, lifted)
        if dk is None:
            dk, dv = dk_part, dv_part
        else:
            dk = jnp.concatenate([dk[:, :seen] + dk_part, dk[:, seen:]], axis=1)
            dv = jnp.concatenate([dv[:, :seen] + dv_part, dv[:, seen:]], axis=1)
    dk = dk.T
    dv = dv.T
    dk_ref[...] = dk + pltpu.roll(dk, HEAD_SIZE, 1)
    dv_ref[...] = dv + pltpu.roll(dv, HEAD_SIZE, 1)


def last_kernel(
    groups, where_ref, dq0, dq1, dq2, dk0, dk1, dk2, dv0, dv1, dv2, cos_ref, sin_ref,
    a_ref, sent0, sent1, kept_ref, dpl_ref, bias_ref, held_ref,
):
    me = where_ref[0]
    tokens = a_ref.shape[0]
    low = lower_half((tokens, LANES))
    heads = [ref[t] for ref in (dq0, dq1, dq2) for t in range(CLUSTER)]
    blocks = [jnp.where(low, heads[2 * i], heads[2 * i + 1]) for i in range(4)]
    blocks.append(jnp.where(low, heads[8], dk0[...]))
    blocks.append(jnp.where(low, dk1[...], dk2[...]))
    cosine, sine = cos_ref[...], sin_ref[...]
    blocks = [block * cosine - swap_pairs(block) * sine for block in blocks]
    blocks.append(jnp.where(low, dv0[...], dv1[...]))
    blocks.append(jnp.where(low, dv2[...], 0.0))
    low_blocks = [block.astype(bf16) for block in blocks]
    blocks = [block.astype(f32) for block in low_blocks]
    dpl_ref[...] = jnp.concatenate(low_blocks, axis=1)
    width = QKV_WIDTH // groups
    chosen = jnp.concatenate(
        [cut_lanes(blocks, b * width, width).astype(bf16) for b in range(groups)], axis=1
    )
    held_ref[...] = dot_first(a_ref[...], chosen).astype(bf16)
    write_message(held_ref, (sent0, sent1), kept_ref, me, groups)
    bias_ref[...] = jnp.concatenate([jnp.sum(block, axis=0, keepdims=True) for block in blocks], axis=1)


def input_kernel(where_ref, dpl_ref, bias_ref, tokens_ref, weight_ref, gain_two_ref, da_ref, small_ref):
    bias_blocks = lane_blocks(bias_ref[...])
    x = tokens_ref[...].astype(f32)
    inverse = lax.rsqrt(jnp.mean(x * x, axis=1, keepdims=True) + norm_eps)
    da = dot_last(dpl_ref[...], weight_ref[...])
    gain_one_blocks = lane_blocks(jnp.sum(da * x * inverse, axis=0, keepdims=True))
    gain_two_blocks = lane_blocks(gain_two_ref[...])
    da_ref[...] = da

    gain_each = 2 * MODEL_WIDTH // 4
    bias_each = QKV_WIDTH // 4
    lines = []
    for s in range(4):
        source = gain_one_blocks if s < 2 else gain_two_blocks
        count = 0
        for t in range(0, gain_each, LANES):
            lines.append(cut_lanes(source, (s % 2) * gain_each + t, min(LANES, gain_each - t)))
            count += 1
        for t in range(0, bias_each, LANES):
            lines.append(cut_lanes(bias_blocks, s * bias_each + t, min(LANES, bias_each - t)))
            count += 1
        lines += [jnp.zeros((1, LANES), f32)] * (SMALL_ROWS // 4 - count)
    small_ref[...] = jnp.concatenate(lines, axis=0).astype(bf16)


def tokens_kernel(where_ref, da_ref, tokens_ref, dh_ref, gains_ref, tokens_grad_ref):
    da = da_ref[...]
    x = tokens_ref[...].astype(f32)
    inverse = lax.rsqrt(jnp.mean(x * x, axis=1, keepdims=True) + norm_eps)
    weighted = da * gains_ref[0:1, :MODEL_WIDTH]
    inner = jnp.mean(weighted * x, axis=1, keepdims=True)
    tokens_grad = dh_ref[...] + inverse * weighted - x * (inverse * inverse * inverse) * inner
    tokens_grad_ref[...] = tokens_grad.T.astype(bf16)


def place_sum(held_ref, kept_ref, came_refs, mine, groups, rows):
    half = groups // 2
    each = 2 * groups // len(came_refs)
    for j in range(2):
        for b in range(groups):
            at = j * groups + b
            part, inner = divmod(at, each)
            total = kept_ref[at * rows : (at + 1) * rows, :].astype(f32)
            total = total + came_refs[part][inner * rows : (inner + 1) * rows, :].astype(f32)
            place = block_place(b, mine, groups)
            beyond = jnp.where((place & half) == 0, 0, half)
            to = pl.multiple_of((place + beyond + j * half) * rows, 16)
            held_ref[pl.ds(to, rows), :] = total.astype(bf16)


def halve_first_kernel(
    groups, where_ref, kept_ref, came0, came1, small_ref, small_came, sent_ref, left_ref, held_ref
):
    rows = OUT_ROW
    part = groups * rows
    place_sum(held_ref, kept_ref, (came0, came1), where_ref[1], groups, rows)
    small = small_ref[...].astype(f32) + small_came[...].astype(f32)
    for ref, start in ((left_ref, 0), (sent_ref, part)):
        ref[:part, :] = held_ref[start : start + part, :]
        ref[part:, :] = small.astype(bf16)


def down_out_kernel(groups, where_ref, down_zero, down_came, kept_ref, came0, came1, sent_ref, left_ref, held_ref):
    rows = OUT_ROW
    part = groups * rows
    place_sum(held_ref, kept_ref, (came0, came1), where_ref[1], groups, rows)
    lanes = down_zero.shape[1] // LANES
    for ref, start, first in ((left_ref, 0, 0), (sent_ref, part, groups // 2)):
        ref[:part, :] = held_ref[start : start + part, :]
        for b in range(groups // 2):
            rows = slice((first + b) * DOWN_ROWS, (first + b + 1) * DOWN_ROWS)
            total = down_zero[rows, :].astype(f32) + down_came[rows, :].astype(f32)
            for i in range(lanes):
                to = part + (b * lanes + i) * DOWN_ROWS
                ref[to : to + DOWN_ROWS, :] = total[:, i * LANES : (i + 1) * LANES].astype(bf16)


def halve_kernel(small_rows, where_ref, kept_ref, came_ref, sent_ref, left_ref):
    part = left_ref.shape[0] - small_rows
    rows = 2 * part + small_rows
    total = kept_ref[:rows, :].astype(f32) + came_ref[:rows, :].astype(f32)
    total = total.astype(bf16)
    left_ref[:part, :] = total[:part]
    sent_ref[:part, :] = total[part : 2 * part]
    if small_rows:
        left_ref[part:, :] = total[2 * part :]
        sent_ref[part:, :] = total[2 * part :]


def fold_feed_kernel(where_ref, gate_kept, gate_came, gate_across, low_kept, low_came, left_ref, sent_ref):
    blocks, rows = gate_kept.shape[:2]
    half = blocks // 2
    lanes = gate_kept.shape[2] // LANES
    first = low_kept.shape[0] - blocks * lanes * DOWN_ROWS
    for b in range(blocks):
        ref, at = (left_ref, b) if b < half else (sent_ref, b - half)
        gate_up = gate_kept[b].astype(f32) + gate_came[b].astype(f32) + gate_across[b].astype(f32)
        ref[at, :rows, :] = gate_up.astype(bf16)
        for i in range(lanes):
            start = first + (b * lanes + i) * DOWN_ROWS
            down = low_kept[start : start + DOWN_ROWS, :].astype(f32)
            down = down + low_came[start : start + DOWN_ROWS, :].astype(f32)
            ref[at, rows:, i * LANES : (i + 1) * LANES] = down.astype(bf16)


def fold_attention_kernel(where_ref, out_kept, out_came, qkv_kept, qkv_came, left_ref, sent_ref):
    rows = OUT_ROW
    blocks = out_kept.shape[0] // rows
    half = blocks // 2
    out = (out_kept[...].astype(f32) + out_came[...].astype(f32)).astype(bf16)
    qkv = (qkv_kept[...].astype(f32) + qkv_came[...].astype(f32)).astype(bf16)
    small = qkv[blocks * rows :].astype(f32)
    each = SMALL_ROWS // 4
    mine = small[:each]
    for s in range(1, 4):
        mine = jnp.where(where_ref[0] == s, small[s * each : (s + 1) * each], mine)
    mine = jnp.concatenate([mine, jnp.zeros_like(mine)], axis=0).astype(bf16)
    for b in range(blocks):
        ref, at = (left_ref, b) if b < half else (sent_ref, b - half)
        ref[at, :rows, :LANES] = out[b * rows : (b + 1) * rows]
        ref[at, :rows, LANES:] = qkv[b * rows : (b + 1) * rows]
        ref[at, rows:, :LANES] = mine
        ref[at, rows:, LANES:] = jnp.zeros_like(mine)


def fold_kernel(where_ref, kept_ref, came_ref, left_ref, sent_ref):
    half = left_ref.shape[0]
    for b in range(half):
        left_ref[b] = (kept_ref[b].astype(f32) + came_ref[b].astype(f32)).astype(bf16)
        at = b + half
        sent_ref[b] = (kept_ref[at].astype(f32) + came_ref[at].astype(f32)).astype(bf16)


def read_total(refs, parts):
    total = refs[0][0].astype(f32)
    for ref in refs[1:parts]:
        total = total + ref[0].astype(f32)
    return total


def step_with(refs):
    count = len(refs) // 2
    ins, outs = refs[:count], refs[count:]

    def step(at, gradient, rate):
        new = adam_update(ins[at][...], ins[at + 1][...], ins[at + 2][...], gradient, rate)
        for i in range(3):
            outs[at + i][...] = new[i]

    return ins, step


def feed_step_kernel(step_rates, parts, where_ref, *refs):
    total = read_total(refs, parts)
    ins, step = step_with(refs[parts:])
    step(0, total[: ins[0].shape[0]], step_rates[2])
    step(3, total[OUT_ROW : OUT_ROW + ins[3].shape[0]], step_rates[3])


def attention_step_kernel(step_rates, parts, where_ref, *refs):
    total = read_total(refs, parts)
    ins, step = step_with(refs[parts:])
    step(0, total[:OUT_ROW, LANES : LANES + ins[0].shape[1]], step_rates[0])
    step(3, total[:OUT_ROW, : ins[3].shape[1]], step_rates[1])
    mine = total[OUT_ROW:, :LANES]
    line = 0
    for at in (6, 9):
        width = ins[at].shape[0]
        lines = -(-width // LANES)
        wide = jnp.concatenate([mine[line + t : line + t + 1, :] for t in range(lines)], axis=1)
        line += lines
        step(at, wide[:, :width].reshape(width), step_rates[4 if at == 6 else 5])


def swap(values, axis, bit):
    size = lax.axis_size(axis)
    return lax.ppermute(values, axis, [(i, i ^ bit) for i in range(size)])


def add_low(left, right):
    return (left.astype(f32) + right.astype(f32)).astype(bf16)


def halves(values):
    half = values.shape[0] // 2
    return values[:half], values[half:]


def own_term(total, extra, places):
    bit = 1
    while bit < extra:
        total = total + swap(total, "rep", bit)
        bit *= 2
    at = lax.axis_index("rep") % extra
    result = total
    for row, rows, lane, lanes, dim, width in places:
        part = total[row : row + rows, lane : lane + lanes]
        own = lax.dynamic_slice_in_dim(part, at * width, width, dim)
        result = lax.dynamic_update_slice(result, own, (row, lane))
    return result[None]


def finish(left, came, extra, places):
    if extra == 1:
        return [left, came]
    return [own_term((left.astype(f32) + came.astype(f32))[0], extra, places)]


def on_device(
    tokens,
    segments,
    cotangent,
    projection_weight,
    out_weight,
    gate_up_weight,
    down_weight,
    norm_gains,
    projection_bias,
    projection_first_moment,
    out_first,
    gate_up_first,
    down_first,
    gains_first,
    bias_first_moment,
    projection_second_moment,
    out_second,
    gate_up_second,
    down_second,
    gains_second,
    bias_second_moment,
):
    count = tokens.shape[0]
    replicas = lax.axis_size("rep")
    groups = min(replicas, 8)
    extra = replicas // groups
    replica = lax.axis_index("rep")
    where = jnp.stack([lax.axis_index("fsdp"), replica // extra, replica]).astype(jnp.int32)
    rates = learn_rates()
    wide = 1024
    shard_rows, ff_rows = projection_weight.shape[0], gate_up_weight.shape[0]
    q_wide = 5 * LANES
    kv_wide = KEY_VALUE_HEADS * LANES
    tokens_turned, e_turned, down_turned = tokens.T, cotangent.T, down_weight.T

    pack = pack_attention(projection_weight, norm_gains, projection_bias, wide)
    pack2 = swap(pack, "fsdp", 2)
    pack1 = swap(pack, "fsdp", 1)

    (cosine, sine, mask, tokens_low, e, low_out, low_gate_up, half, low_down,
     own_qkv, own_out, own_gate_up, own_down) = kernel_call(
        tables_kernel,
        [
            shaped((count, LANES), f32),
            shaped((count, LANES), f32),
            shaped((count, count), f32),
            shaped((count, MODEL_WIDTH), bf16),
            shaped((count, MODEL_WIDTH), bf16),
            shaped(out_weight.shape, bf16),
            shaped((ff_rows, 2 * MODEL_WIDTH), bf16),
            shaped((ff_rows // 2, 2 * MODEL_WIDTH), bf16),
            shaped((MODEL_WIDTH, ff_rows), bf16),
            shaped(projection_first_moment.shape, f32),
            shaped(out_first.shape, f32),
            shaped(gate_up_first.shape[::-1], f32),
            shaped(down_first.shape[::-1], f32),
        ],
        "tables", 3.0,
        scratch=[pltpu.VMEM((2 * MODEL_WIDTH, ff_rows), f32)], after=(pack,),
    )(
        where, segments, tokens_turned, e_turned,
        projection_weight, out_weight, gate_up_weight, down_turned,
    )

    pack2, low_out, half = gate([pack2, low_out, half], [pack1, cosine], "after_pack")
    pack3 = swap(pack2, "fsdp", 1)
    out2 = swap(low_out, "fsdp", 2)
    half_across = swap(half, "fsdp", 2)
    out1 = swap(low_out, "fsdp", 1)
    gate_up1 = swap(low_gate_up, "fsdp", 1)
    down1 = swap(low_down, "fsdp", 1)

    (a, q, k, v, lifted0, lifted1, lifted2, inv, o, weight_full, gains) = kernel_call(
        forward_kernel,
        [
            shaped((count, MODEL_WIDTH), bf16),
            shaped((count, q_wide), bf16),
            shaped((count, kv_wide), bf16),
            shaped((count, kv_wide), bf16),
        ]
        + [shaped((CLUSTER, count, count), bf16)] * 3
        + [
            shaped((count, q_wide), f32),
            shaped((count, q_wide), bf16),
            shaped((MODEL_WIDTH, wide), bf16),
            shaped((2, q_wide), f32),
        ],
        "attention_forward", 6.0,
    )(where, tokens_low, cosine, sine, mask, pack, pack1, pack2, pack3)

    (out2,) = gate([out2], [o], "after_attention")
    out3 = swap(out2, "fsdp", 1)

    h, a2, a2_turned, out_full = kernel_call(
        project_kernel,
        [
            shaped((count, MODEL_WIDTH), f32),
            shaped((count, q_wide), bf16),
            shaped((MODEL_WIDTH, count), bf16),
            shaped((MODEL_WIDTH, MODEL_WIDTH), bf16),
        ],
        "project", 2.0,
    )(where, tokens_low, o, gains, low_out, out1, out2, out3)

    half_across, low_down_late = gate([half_across, low_down], [h, down1], "after_project")
    down2 = swap(low_down_late, "fsdp", 2)
    half_beside = swap(half_across, "rep", extra)
    half_across3 = swap(half_across, "fsdp", 1)
    gate_ups = {0: [low_gate_up], 1: [gate_up1]}
    downs = {0: low_down_late, 1: down1}

    gate_up_block = (2 * MODEL_WIDTH // groups, ff_rows)
    half_block = (groups // 2,) + gate_up_block

    def grad_parts(count):
        return [shaped((groups // count * (OUT_ROW + DOWN_ROWS), ff_rows), bf16)] * count

    def core_sum(own, sent, name, after=()):
        came = [swap(part, "fsdp", 1) for part in sent]
        return kernel_call(
            functools.partial(core_sum_kernel, groups, len(own)),
            [shaped(half_block, bf16), shaped(half_block, bf16), shaped((groups * DOWN_ROWS, ff_rows), bf16)],
            name, 0.2, scratch=[pltpu.VMEM((groups,) + gate_up_block, bf16)], after=after,
        )(where, *own, *came)

    grads = {}
    total, accumulated = h, []
    for j in (1, 0, 3, 2):
        first, last = j == 1, j == 2
        waits = (half_across,) if first else (zero_sent,) if j == 3 else ()
        parts = 4 if j > 1 else 2
        total, *results = kernel_call(
            functools.partial(feed_kernel, groups, first, last, j > 1, parts),
            [
                shaped((MODEL_WIDTH, count), bf16) if last else shaped((count, MODEL_WIDTH), f32),
                shaped((count, q_wide), f32),
            ] + grad_parts(parts),
            "feed_" + str(j), 0.5,
            scratch=[pltpu.VMEM((2 * ff_rows, q_wide), bf16)],
            after=waits,
        )(
            where, a2, a2_turned, e, e_turned, total, *accumulated, *gate_ups[j], downs[j],
        )
        accumulated, grads[j] = results[:1], results[1:]
        if j == 0:
            half_beside, down2 = gate([half_beside, down2], [total], "after_feed_0")
            gate_ups[2] = [half_across, half_beside]
            gate_ups[3] = [half_across3, swap(half_beside, "fsdp", 1)]
            downs[2], downs[3] = down2, swap(down2, "fsdp", 1)
            zero_kept, zero_sent, down_zero = core_sum(grads[0], grads[1], "core_sum_0")
            zero_came = swap(zero_sent, "rep", extra)
    output = total.T

    two_kept, two_sent, down_two = core_sum(grads[2], grads[3], "core_sum_2", (zero_came,))
    two_came = swap(two_sent, "rep", extra)
    down_came = swap(down_two, "fsdp", 2)

    message = 2 * groups * shard_rows
    dh, dol, gain_two, *out_parts = kernel_call(
        functools.partial(middle_kernel, groups),
        [
            shaped((count, MODEL_WIDTH), f32),
            shaped((count, q_wide), bf16),
            shaped((1, MODEL_WIDTH), f32),
            shaped((message // 2, LANES), bf16),
            shaped((message // 2, LANES), bf16),
            shaped((message, LANES), bf16),
        ],
        "middle", 0.5, after=(two_sent, down_two),
        scratch=[pltpu.VMEM((MODEL_WIDTH, groups * LANES), bf16)],
    )(where, *accumulated, h, e, gains, o, inv, out_full)

    def halve(kept, came, small_rows, name, after=()):
        part = (kept.shape[0] - small_rows) // 2 + small_rows
        return kernel_call(
            functools.partial(halve_kernel, small_rows),
            [shaped((part, LANES), bf16)] * 2, name, 0.3, after=after,
        )(where, kept, came)

    *out_sent, out_kept = out_parts
    out_came = [swap(part, "fsdp", 1) for part in out_sent]

    dqs, dks, dvs = [], [], []
    waits = ()
    for g, lifted in enumerate((lifted0, lifted1, lifted2)):
        if g == 2:
            two_kept, down_zero = gate([two_kept, down_zero], [dqs[1]], "after_back")
            two = add_low(two_kept, two_came)
            gate_up_across = swap(two, "fsdp", 2)
            low_rows = message // 2 + groups // 2 * (ff_rows // LANES) * DOWN_ROWS
            low_sent, low_kept = kernel_call(
                functools.partial(down_out_kernel, groups),
                [shaped((low_rows, LANES), bf16)] * 2, "down_out", 0.2,
                scratch=[pltpu.VMEM((message, LANES), bf16)],
            )(where, down_zero, down_came, out_kept, *out_came)
            low_came = swap(low_sent, "rep", extra)
            waits = (two, low_sent)
        dq, dk, dv = kernel_call(
            functools.partial(attention_back_kernel, g),
            [shaped((CLUSTER, count, LANES), f32), shaped((count, LANES), f32), shaped((count, LANES), f32)],
            "attention_back_" + str(g), 0.2, after=waits + tuple(dqs),
        )(where, q, k, v, lifted, o, dol)
        dqs.append(dq)
        dks.append(dk)
        dvs.append(dv)

    *sent, kept, dpl, bias_grad = kernel_call(
        functools.partial(last_kernel, groups),
        [
            shaped((message // 2, LANES), bf16),
            shaped((message // 2, LANES), bf16),
            shaped((message, LANES), bf16),
            shaped((count, wide), bf16),
            shaped((1, wide), f32),
        ],
        "last", 0.2,
        scratch=[pltpu.VMEM((MODEL_WIDTH, groups * LANES), bf16)],
    )(where, *dqs, *dks, *dvs, cosine, sine, a)
    came = [swap(part, "fsdp", 1) for part in sent]
    da, small = kernel_call(
        input_kernel,
        [shaped((count, MODEL_WIDTH), f32), shaped((SMALL_ROWS, LANES), bf16)], "input_gradient", 0.2,
    )(where, dpl, bias_grad, tokens_low, weight_full, gain_two)
    small_came = swap(small, "fsdp", 1)
    sent, kept = kernel_call(
        functools.partial(halve_first_kernel, groups),
        [shaped((message // 2 + SMALL_ROWS, LANES), bf16)] * 2, "halve_first", 0.3, after=(gate_up_across,),
        scratch=[pltpu.VMEM((message, LANES), bf16)],
    )(where, kept, *came, small, small_came)
    came = swap(sent, "rep", extra)

    quarter = groups // 4
    rows = OUT_ROW + DOWN_ROWS
    feed_left, feed_sent = kernel_call(
        fold_feed_kernel, [shaped((quarter, rows, ff_rows), bf16)] * 2, "fold_feed", 0.5, after=(sent,)
    )(where, zero_kept, zero_came, gate_up_across, low_kept, low_came)
    feed_came = swap(feed_sent, "rep", 2 * extra)
    out_sent, out_kept = kernel_call(
        functools.partial(halve_kernel, 0),
        [shaped((message // 4, LANES), bf16)] * 2, "out_halve", 0.3, after=(feed_sent,),
    )(where, low_kept, low_came)
    out_came = swap(out_sent, "fsdp", 2)
    (tokens_grad,) = kernel_call(
        tokens_kernel, [shaped((MODEL_WIDTH, count), bf16)], "tokens_gradient", 0.2, after=(out_sent,)
    )(where, da, tokens_low, dh, gains)
    sent, kept = halve(kept, came, SMALL_ROWS, "halve_2", (out_came, tokens_grad))
    came = swap(sent, "fsdp", 2)

    def fold(left, came, name, after=()):
        half = left.shape[0] // 2
        return kernel_call(
            fold_kernel, [shaped((half,) + left.shape[1:], bf16)] * 2, name, 0.3, after=after
        )(where, left, came)

    bits = [1 << i for i in range(2, groups.bit_length() - 1)]
    for bit in bits:
        feed_left, feed_sent = fold(feed_left, feed_came, "fold_feed_" + str(bit), (sent,))
        feed_came = swap(feed_sent, "rep", bit * extra)
    left, sent = kernel_call(
        fold_attention_kernel,
        [shaped((quarter, OUT_ROW + SMALL_ROWS // 2, 2 * LANES), bf16)] * 2, "fold_attention", 0.5, after=(feed_sent,),
    )(where, out_kept, out_came, kept, came)
    came = swap(sent, "rep", 2 * extra)
    for bit in bits:
        left, sent = fold(left, came, "fold_attention_" + str(bit), (feed_came,))
        came = swap(sent, "rep", bit * extra)

    feed_states = (
        own_gate_up, gate_up_first.T, gate_up_second.T, own_down, down_first.T, down_second.T,
    )
    wide_gate, wide_down = own_gate_up.shape[0] * extra, own_down.shape[0] * extra
    feed_parts = finish(feed_left, feed_came, extra, (
        (0, wide_gate, 0, ff_rows, 0, own_gate_up.shape[0]),
        (OUT_ROW, wide_down, 0, ff_rows, 0, own_down.shape[0]),
    ))
    feed_news = kernel_call(
        functools.partial(feed_step_kernel, rates, len(feed_parts)),
        [shaped(state.shape, f32) for state in feed_states], "feed_step", 0.5, after=(sent,),
    )(where, *feed_parts, *feed_states)
    states = (
        own_qkv, projection_first_moment, projection_second_moment,
        own_out, out_first, out_second,
        norm_gains, gains_first, gains_second,
        projection_bias, bias_first_moment, bias_second_moment,
    )
    parts = finish(left, came, extra, (
        (0, OUT_ROW, LANES, own_qkv.shape[1] * extra, 1, own_qkv.shape[1]),
        (0, OUT_ROW, 0, own_out.shape[1] * extra, 1, own_out.shape[1]),
    ))
    news = kernel_call(
        functools.partial(attention_step_kernel, rates, len(parts)),
        [shaped(state.shape, f32) for state in states], "attention_step", 1.0,
    )(where, *parts, *states)
    return (
        output,
        tokens_grad.T,
        *news[:6],
        *[new.T for new in feed_news],
        *news[6:],
    )


def solution(mesh):
    rows = P(("rep", "fsdp"), None)
    weight = P("fsdp", None)
    state = P("fsdp", "rep")
    vector = P("fsdp")
    states = (state,) * 4 + (vector,) * 2
    in_specs = (rows, P(("rep", "fsdp")), rows) + (weight,) * 4 + (vector,) * 2 + states + states
    out_specs = (rows, rows) + (state,) * 12 + (vector,) * 6
    return jax.shard_map(
        on_device, mesh=mesh, in_specs=in_specs, out_specs=out_specs, check_vma=False
    )
```

```python
import functools
import math

import jax
import jax.numpy as jnp
from jax import lax
from jax.experimental import pallas as pl
from jax.experimental.pallas import tpu as pltpu
from jax.sharding import PartitionSpec as P

MODEL_WIDTH = 576
QUERY_HEADS = 9
KEY_VALUE_HEADS = 3
HEAD_SIZE = 64
FF = 1536
STEP = 10

norm_eps = 1e-05
rope_base = 100000.0
beta_one = 0.9
beta_two = 0.95
adam_eps = 1e-08
decay_rate = 0.1

LANES = 128
QKV_WIDTH = (QUERY_HEADS + 2 * KEY_VALUE_HEADS) * HEAD_SIZE
CLUSTER = QUERY_HEADS // KEY_VALUE_HEADS
SMALL_ROWS = 32
ROW_BLOCK = 128
OUT_ROW = MODEL_WIDTH // 4
DOWN_ROWS = 80
bf16 = jnp.bfloat16
f32 = jnp.float32


def learn_rates():
    out_fan = max(QUERY_HEADS * HEAD_SIZE // 16, 1)
    return (MODEL_WIDTH ** (-0.5), out_fan ** (-0.5), MODEL_WIDTH ** (-0.5), FF ** (-0.5), 0.5, 0.5)


def adam_update(weight, first_moment, second_moment, gradient, step_rate):
    first_new = beta_one * first_moment + (1.0 - beta_one) * gradient
    second_new = beta_two * second_moment + (1.0 - beta_two) * gradient * gradient
    first_fix = 1.0 - beta_one**STEP
    second_fix = 1.0 - beta_two**STEP
    direction = first_new / first_fix / (jnp.sqrt(second_new / second_fix) + adam_eps)
    return (first_new, second_new, weight - step_rate * (direction + decay_rate * weight))


def dot_plain(left, right):
    return lax.dot_general(left, right, (((1,), (0,)), ((), ())), preferred_element_type=f32)


def dot_last(left, right):
    return lax.dot_general(left, right, (((1,), (1,)), ((), ())), preferred_element_type=f32)


def dot_first(left, right):
    return lax.dot_general(left, right, (((0,), (0,)), ((), ())), preferred_element_type=f32)


def kernel_call(body, outs, name, time, scratch=(), vmem=12, after=()):
    def call(scalars, *arrays):
        count = len(after)

        def run(*refs):
            body(refs[0], *refs[1 + count :])

        return pl.pallas_call(
            run,
            out_shape=tuple(outs),
            in_specs=[pl.BlockSpec(memory_space=pltpu.SMEM)]
            + [pl.BlockSpec(memory_space=pl.ANY)] * count
            + [pl.BlockSpec(memory_space=pltpu.VMEM)] * len(arrays),
            out_specs=tuple(pl.BlockSpec(memory_space=pltpu.VMEM) for _ in outs),
            scratch_shapes=list(scratch),
            name=name,
            compiler_params=pltpu.CompilerParams(vmem_limit_bytes=vmem * 2**20),
            cost_estimate=pl.CostEstimate(
                flops=int(time * 1.15e9), bytes_accessed=0, transcendentals=0
            ),
        )(scalars, *after, *arrays)

    return call


def gate(values, after, name):
    def nothing(*refs):
        pass

    result = pl.pallas_call(
        nothing,
        out_shape=tuple(shaped(v.shape, v.dtype) for v in values),
        in_specs=[pl.BlockSpec(memory_space=pl.ANY)] * (len(values) + len(after)),
        out_specs=tuple(pl.BlockSpec(memory_space=pl.ANY) for _ in values),
        input_output_aliases={i: i for i in range(len(values))},
        name=name,
        compiler_params=pltpu.CompilerParams(vmem_limit_bytes=2**20),
        cost_estimate=pl.CostEstimate(flops=0, bytes_accessed=0, transcendentals=0),
    )(*values, *after)
    return list(result)


def shaped(shape, dtype):
    return jax.ShapeDtypeStruct(tuple(shape), dtype)


def lane_index(shape):
    return lax.broadcasted_iota(jnp.int32, shape, len(shape) - 1)


def lower_half(shape):
    return lane_index(shape) < HEAD_SIZE


def swap_pairs(block):
    first = (lane_index(block.shape) & (HEAD_SIZE // 2)) == 0
    ahead = pltpu.roll(block, LANES - HEAD_SIZE // 2, 1)
    behind = pltpu.roll(block, HEAD_SIZE // 2, 1)
    return jnp.where(first, ahead, behind)


def both_halves(block, upper):
    other = pltpu.roll(block, HEAD_SIZE, 1)
    low = lower_half(block.shape)
    return jnp.where(low, other, block) if upper else jnp.where(low, block, other)


def cut_lanes(blocks, start, width):
    at, offset = divmod(start, LANES)
    lane = lane_index(blocks[0].shape)
    part = blocks[at]
    if offset:
        part = pltpu.roll(part, LANES - offset, 1)
        if offset + width > LANES:
            after = pltpu.roll(blocks[at + 1], LANES - offset, 1)
            part = jnp.where(lane < LANES - offset, part, after)
    if width < LANES:
        part = jnp.where(lane < width, part, 0.0)
    return part


def lane_blocks(values):
    width = values.shape[1]
    full = width // LANES
    blocks = [values[:, i * LANES : (i + 1) * LANES] for i in range(full)]
    if width % LANES:
        rest = values[:, full * LANES :]
        fill = jnp.zeros((values.shape[0], LANES - width % LANES), values.dtype)
        blocks.append(jnp.concatenate([rest, fill], axis=1))
    return blocks


def block_place(block, mine, groups):
    away = mine ^ block
    place = 0
    bit = 1
    while bit < groups:
        place = place * 2 + jnp.where((away & bit) == 0, 0, 1)
        bit *= 2
    return place


def own_rows(ref, replica, width):
    if width % 8 == 0:
        return ref[pl.ds(pl.multiple_of(replica * width, 8), width), :]
    rows = ref.shape[0]
    return pltpu.roll(ref[...], rows - replica * width, 0)[:width]


def pack_kernel(qkv_hbm, gains_hbm, bias_hbm, pack_ref, qkv_ref, gains_ref, bias_ref, sems):
    copies = [
        pltpu.make_async_copy(source, target, sems.at[i])
        for i, (source, target) in enumerate(
            ((qkv_hbm, qkv_ref), (gains_hbm, gains_ref), (bias_hbm, bias_ref))
        )
    ]
    for copy in copies:
        copy.start()
    for copy in copies:
        copy.wait()
    rows = qkv_ref.shape[0]
    pack_ref[:rows, :QKV_WIDTH] = qkv_ref[...].astype(bf16)
    pack_ref[:rows, QKV_WIDTH:] = jnp.zeros((rows, pack_ref.shape[1] - QKV_WIDTH), bf16)
    spare = pack_ref.shape[0] - rows
    bias, gains = (ref[...].reshape(1, ref.shape[0]) for ref in (bias_ref, gains_ref))
    extra = jnp.concatenate(lane_blocks(bias) + lane_blocks(gains), axis=1)
    line = jnp.concatenate(
        [extra, jnp.zeros((1, pack_ref.shape[1] - extra.shape[1]), f32)], axis=1
    )
    pack_ref[rows:, :] = jnp.broadcast_to(line, (spare, line.shape[1])).astype(bf16)


def pack_attention(weight, gains, bias, wide):
    return pl.pallas_call(
        pack_kernel,
        out_shape=shaped((weight.shape[0] + 16, wide), bf16),
        in_specs=[pl.BlockSpec(memory_space=pl.ANY)] * 3,
        out_specs=pl.BlockSpec(memory_space=pltpu.VMEM),
        scratch_shapes=[
            pltpu.VMEM(weight.shape, f32),
            pltpu.VMEM(gains.shape, f32),
            pltpu.VMEM(bias.shape, f32),
            pltpu.SemaphoreType.DMA((3,)),
        ],
        name="pack_attention",
        compiler_params=pltpu.CompilerParams(vmem_limit_bytes=60 * 2**20),
        cost_estimate=pl.CostEstimate(flops=10**9, bytes_accessed=0, transcendentals=0),
    )(weight, gains, bias)


def tables_kernel(
    where_ref, segments_ref, tokens_turned_ref, e_turned_ref, qkv_ref, out_ref, gate_up_ref, down_ref,
    cos_ref, sin_ref, mask_ref, tokens_ref, e_ref, low_out_ref, low_gate_up_ref, half_ref, low_down_ref,
    own_qkv_ref, own_out_ref, own_gate_up_ref, own_down_ref, turned_ref,
):
    tokens = segments_ref.shape[0]
    row = segments_ref[...].reshape(1, tokens).astype(f32)
    column = jnp.broadcast_to(row, (LANES, tokens)).T[:, :1]
    query = lax.broadcasted_iota(jnp.int32, (tokens, tokens), 0)
    key = lax.broadcasted_iota(jnp.int32, (tokens, tokens), 1)
    same = column == row
    earlier = jnp.sum(jnp.where(same & (key < query), 1.0, 0.0), axis=1, keepdims=True)
    mask_ref[...] = jnp.where(same & (key <= query), 0.0, -1e30)
    lane = lane_index((tokens, LANES))
    exponent = (lane & (HEAD_SIZE // 2 - 1)).astype(f32) * (2.0 / HEAD_SIZE)
    frequency = jnp.exp(exponent * (-math.log(rope_base)))
    angles = earlier * frequency
    cos_ref[...] = jnp.cos(angles)
    sine = jnp.sin(angles)
    sin_ref[...] = jnp.where((lane & (HEAD_SIZE // 2)) == 0, -sine, sine)
    tokens_ref[...] = tokens_turned_ref[...].astype(f32).T.astype(bf16)
    e_ref[...] = e_turned_ref[...].astype(f32).T.astype(bf16)

    low_out_ref[...] = out_ref[...].astype(bf16)
    gate_up = gate_up_ref[...]
    whole = MODEL_WIDTH // LANES * LANES
    blocks = [gate_up[:, i * LANES : (i + 1) * LANES] for i in range(gate_up.shape[1] // LANES)]
    low = lower_half(blocks[0].shape)
    low_gate_up_ref[:, :whole] = gate_up[:, :whole].astype(bf16)
    first = MODEL_WIDTH // LANES
    turned = [pltpu.roll(block, HEAD_SIZE, 1) for block in blocks[first:]]
    for i in range(first):
        block = jnp.where(low, turned[i], turned[i + 1])
        low_gate_up_ref[:, whole + i * LANES : whole + (i + 1) * LANES] = block.astype(bf16)
    low_gate_up_ref[:, 2 * whole :] = jnp.where(low, blocks[first], blocks[-1]).astype(bf16)
    rows = half_ref.shape[0]
    start = pl.multiple_of((where_ref[1] & 1) * rows, 16)
    half_ref[...] = low_gate_up_ref[pl.ds(start, rows), :]
    low_down_ref[...] = down_ref[...].astype(bf16)
    replica = where_ref[2]
    turned_ref[...] = gate_up.T
    width = own_gate_up_ref.shape[0]
    own_gate_up_ref[...] = own_rows(turned_ref, replica, width)
    width = own_down_ref.shape[0]
    own_down_ref[...] = own_rows(down_ref, replica, width)
    for ref, own in ((qkv_ref, own_qkv_ref), (out_ref, own_out_ref)):
        width = own.shape[1]
        wide = jnp.concatenate(lane_blocks(ref[...]), axis=1)
        own[...] = pltpu.roll(wide, wide.shape[1] - replica * width, 1)[:, :width]


def forward_kernel(
    where_ref, tokens_ref, cos_ref, sin_ref, mask_ref, pack0, pack1, pack2, pack3,
    a_ref, q_ref, k_ref, v_ref, e0_ref, e1_ref, e2_ref, inv_ref, o_ref, weight_ref, gains_ref,
):
    me = where_ref[0]
    tokens = tokens_ref.shape[0]
    shard_rows = MODEL_WIDTH // 4
    packs = (pack0, pack1, pack2, pack3)
    lines = []
    for j in range(4):
        start = pl.multiple_of((me ^ j) * shard_rows, 16)
        weight_ref[pl.ds(start, shard_rows), :] = packs[j][:shard_rows, :]
        lines.append(packs[j][shard_rows:, :].astype(f32)[:1, :])
    bias_wide = lane_index((1, LANES)) * 0.0
    ordered = []
    for s in range(4):
        line = jnp.where((me ^ s) == 0, lines[0], 0.0)
        for j in range(1, 4):
            line = jnp.where((me ^ s) == j, lines[j], line)
        ordered.append(line)
    bias_blocks = [bias_wide for _ in range(weight_ref.shape[1] // LANES)]
    gain_blocks = [[bias_wide for _ in range(5)] for _ in range(2)]
    lane = lane_index((1, LANES))

    def put(blocks, source, width, start):
        done = 0
        while done < width:
            at, offset = divmod(start + done, LANES)
            count = min(LANES - offset, width - done)
            from_at, from_offset = divmod(done, LANES)
            count = min(count, LANES - from_offset)
            turn = (offset - from_offset) % LANES
            part = source[from_at]
            if turn:
                part = pltpu.roll(part, turn, 1)
            blocks[at] = jnp.where((lane >= offset) & (lane < offset + count), part, blocks[at])
            done += count

    bias_each = QKV_WIDTH // 4
    gain_each = 2 * MODEL_WIDTH // 4
    bias_lanes = -(-bias_each // LANES) * LANES
    for s in range(4):
        pieces = [ordered[s][:, i * LANES : (i + 1) * LANES] for i in range(8)]
        put(bias_blocks, pieces, bias_each, s * bias_each)
        put(gain_blocks[s // 2], pieces[bias_lanes // LANES :], gain_each, (s % 2) * gain_each)
    gains = [jnp.concatenate(blocks, axis=1) for blocks in gain_blocks]
    for i in range(2):
        gains_ref[i : i + 1, :] = gains[i]
    bias = jnp.concatenate(bias_blocks, axis=1)

    x = tokens_ref[...].astype(f32)
    inverse = lax.rsqrt(jnp.mean(x * x, axis=1, keepdims=True) + norm_eps)
    a = (x * inverse * gains[0][:, :MODEL_WIDTH]).astype(bf16)
    a_ref[...] = a
    p = dot_plain(a, weight_ref[...]) + bias
    cosine, sine = cos_ref[...], sin_ref[...]
    blocks = [p[:, i * LANES : (i + 1) * LANES] for i in range(8)]
    for i in range(6):
        blocks[i] = blocks[i] * cosine + swap_pairs(blocks[i]) * sine
    low = lower_half((tokens, LANES))
    for i in range(5):
        scaled = blocks[i] * HEAD_SIZE ** (-0.5)
        if i == 4:
            scaled = jnp.where(low, scaled, 0.0)
        q_ref[:, i * LANES : (i + 1) * LANES] = scaled.astype(bf16)
    keys = [both_halves(blocks[4], True), both_halves(blocks[5], False), both_halves(blocks[5], True)]
    values = [both_halves(blocks[6], False), both_halves(blocks[6], True), both_halves(blocks[7], False)]
    for g in range(KEY_VALUE_HEADS):
        k_ref[:, g * LANES : (g + 1) * LANES] = keys[g].astype(bf16)
        v_ref[:, g * LANES : (g + 1) * LANES] = values[g].astype(bf16)

    e_refs = (e0_ref, e1_ref, e2_ref)
    step = ROW_BLOCK
    low = lower_half((step, LANES))
    for at in range(tokens // step):
        rows = slice(at * step, (at + 1) * step)
        seen = (at + 1) * step
        mixed = []
        inverses = []
        for g in range(KEY_VALUE_HEADS):
            stack = head_stack(q_ref, rows, g)
            scores = dot_last(stack, k_ref[:seen, g * LANES : (g + 1) * LANES])
            scores = scores.reshape(CLUSTER, step, seen) + mask_ref[rows, :seen][None]
            lifted = jnp.exp(scores - jnp.max(scores, axis=2, keepdims=True))
            total = jnp.sum(lifted, axis=2, keepdims=True)
            kept = lifted.astype(bf16)
            e_refs[g][:, rows, :seen] = kept
            gathered = dot_plain(
                kept.reshape(CLUSTER * step, seen), v_ref[:seen, g * LANES : (g + 1) * LANES]
            ).reshape(CLUSTER, step, LANES)
            inverse_total = jnp.broadcast_to(1.0 / total, gathered.shape)
            gathered = gathered * inverse_total
            for t in range(CLUSTER):
                mixed.append(gathered[t])
                inverses.append(inverse_total[t])
        for i in range(5):
            second = mixed[2 * i + 1] if 2 * i + 1 < QUERY_HEADS else 0.0
            part = jnp.where(low, mixed[2 * i], second)
            o_ref[rows, i * LANES : (i + 1) * LANES] = part.astype(bf16)
            second = inverses[2 * i + 1] if 2 * i + 1 < QUERY_HEADS else 0.0
            inv_ref[rows, i * LANES : (i + 1) * LANES] = jnp.where(low, inverses[2 * i], second)


def project_kernel(
    where_ref, tokens_ref, o_ref, gains_ref, out0, out1, out2, out3,
    h_ref, a2_ref, a2_turned_ref, out_weight_ref,
):
    me = where_ref[0]
    tokens = tokens_ref.shape[0]
    shard_rows = out0.shape[0]
    for j, out in enumerate((out0, out1, out2, out3)):
        start = pl.multiple_of((me ^ j) * shard_rows, 16)
        out_weight_ref[pl.ds(start, shard_rows), :] = out[...]
    x = tokens_ref[...].astype(f32)
    h = x + dot_plain(o_ref[:, :MODEL_WIDTH], out_weight_ref[...])
    h_ref[...] = h
    inverse = lax.rsqrt(jnp.mean(h * h, axis=1, keepdims=True) + norm_eps)
    a2 = h * inverse * gains_ref[1:2, :MODEL_WIDTH]
    for i, block in enumerate(lane_blocks(a2)):
        a2_ref[:, i * LANES : (i + 1) * LANES] = block.astype(bf16)
    a2_turned_ref[...] = a2.T.astype(bf16)


def head_stack(ref, rows, g):
    parts = []
    for t in range(CLUSTER):
        head = g * CLUSTER + t
        block = ref[rows, (head // 2) * LANES : (head // 2 + 1) * LANES]
        low = lower_half(block.shape)
        keep = low if head % 2 == 0 else jnp.logical_not(low)
        parts.append(jnp.where(keep, block, jnp.zeros_like(block)))
    return jnp.concatenate(parts, axis=0)


def feed_kernel(groups, first, halved, parts, *refs):
    refs = list(refs)

    def take(count):
        taken = refs[:count]
        del refs[:count]
        return taken

    where_ref, a2_ref, a2_turned_ref, e_ref, e_turned_ref, base_ref = take(6)
    acc_in = None if first else take(1)[0]
    gate_ups = take(2 if halved else 1)
    (down,) = take(1)
    total_ref, acc_ref = take(2)
    outs = take(parts)
    (stack,) = refs
    mine = where_ref[1]
    hidden_rows = down.shape[1]
    whole = MODEL_WIDTH // LANES * LANES
    for half, gate_up in enumerate(gate_ups):
        rows = gate_up.shape[0]
        start = pl.multiple_of(((mine & 1) ^ half) * rows, 16) if halved else 0
        rest = gate_up[:, 2 * whole :]
        turned = pltpu.roll(rest.astype(f32), HEAD_SIZE, 1).astype(bf16)
        stack[pl.ds(start, rows), :whole] = gate_up[:, :whole]
        stack[pl.ds(start, rows), whole:] = rest
        start = start + hidden_rows
        stack[pl.ds(start, rows), :whole] = gate_up[:, whole : 2 * whole]
        stack[pl.ds(start, rows), whole:] = turned
    both = dot_last(a2_ref[...], stack[...])
    gate, up = both[:, :hidden_rows], both[:, hidden_rows:]
    sigma = 1.0 / (1.0 + jnp.exp(-gate))
    active = gate * sigma
    hidden = (active * up).astype(bf16)
    grad_hidden = dot_plain(e_ref[...], down[...])
    grad_gate = (grad_hidden * up * (sigma * (1.0 + gate * (1.0 - sigma)))).astype(bf16)
    grad_up = (grad_hidden * active).astype(bf16)
    grads = jnp.concatenate([grad_gate, grad_up], axis=1)
    half = groups // 2
    each = groups // parts
    width = OUT_ROW
    block_rows = OUT_ROW + DOWN_ROWS
    turned = dot_plain(a2_turned_ref[...], grads)
    for b in range(groups):
        at, inner = divmod(b, each)
        row, lane = (b % half) * width, (b // half) * hidden_rows
        to = inner * block_rows
        block = turned[row : row + width, lane : lane + hidden_rows]
        outs[at][to : to + width, :] = block.astype(bf16)
    turned = dot_plain(e_turned_ref[...], hidden)
    thin = MODEL_WIDTH // groups
    fill = jnp.zeros((DOWN_ROWS - thin, turned.shape[1]), f32)
    for b in range(groups):
        at, inner = divmod(b, each)
        block = jnp.concatenate([turned[b * thin : (b + 1) * thin], fill], axis=0)
        to = inner * block_rows + width
        outs[at][to : to + DOWN_ROWS, :] = block.astype(bf16)
    part = dot_plain(grads, stack[...])
    acc_ref[...] = part if first else acc_in[...] + part
    total = base_ref[...] + dot_last(hidden, down[...])
    total_ref[...] = total


def core_sum_kernel(groups, parts, where_ref, *refs):
    mine = where_ref[1]
    own, came = refs[:parts], refs[parts : 2 * parts]
    gate_kept, gate_sent, down_total, held_ref = refs[2 * parts :]
    each = groups // parts
    block_rows = OUT_ROW + DOWN_ROWS
    for b in range(groups):
        at, inner = divmod(b, each)
        place = block_place(b, mine, groups)
        rows = slice(inner * block_rows, inner * block_rows + OUT_ROW)
        total = own[at][rows, :].astype(f32) + came[at][rows, :].astype(f32)
        held_ref[place] = total.astype(bf16)
        rows = slice(inner * block_rows + OUT_ROW, (inner + 1) * block_rows)
        total = own[at][rows, :].astype(f32) + came[at][rows, :].astype(f32)
        down_total[pl.ds(pl.multiple_of(place * DOWN_ROWS, 16), DOWN_ROWS), :] = total.astype(bf16)
    half = groups // 2
    gate_kept[...] = held_ref[:half]
    gate_sent[...] = held_ref[half:]


def write_message(held_ref, sent_refs, kept_ref, me, groups):
    rows = held_ref.shape[0] // 4
    each = 2 * groups // len(sent_refs)
    for j in range(4):
        start = pl.multiple_of((me ^ j) * rows, 16)
        for b in range(groups):
            block = held_ref[pl.ds(start, rows), b * LANES : (b + 1) * LANES]
            to = (j // 2) * groups + b
            if j % 2:
                at, to = divmod(to, each)
                sent_refs[at][to * rows : (to + 1) * rows, :] = block
            else:
                kept_ref[to * rows : (to + 1) * rows, :] = block


def middle_kernel(
    groups, where_ref, acc_ref, h_ref, e_ref, gains_ref, o_ref, inv_ref, out_weight_ref,
    dh_ref, dol_ref, small_ref, sent0, sent1, kept_ref, held_ref,
):
    me = where_ref[0]
    tokens = h_ref.shape[0]
    gain = gains_ref[1:2, :MODEL_WIDTH]
    h = h_ref[...]
    da2 = acc_ref[:, :MODEL_WIDTH]
    inverse = lax.rsqrt(jnp.mean(h * h, axis=1, keepdims=True) + norm_eps)
    weighted = da2 * gain
    inner = jnp.mean(weighted * h, axis=1, keepdims=True)
    dh = e_ref[...].astype(f32) + inverse * weighted - h * (inverse * inverse * inverse) * inner
    dh_ref[...] = dh
    small_ref[...] = jnp.sum(da2 * h * inverse, axis=0, keepdims=True)
    dhl = dh.astype(bf16)
    spread = dhl.astype(f32)
    blocks = lane_blocks(spread)
    width = MODEL_WIDTH // groups
    chosen = jnp.concatenate(
        [cut_lanes(blocks, b * width, width).astype(bf16) for b in range(groups)], axis=1
    )
    held_ref[...] = dot_first(o_ref[:, :MODEL_WIDTH], chosen).astype(bf16)
    write_message(held_ref, (sent0, sent1), kept_ref, me, groups)
    dol = dot_last(dhl, out_weight_ref[...])
    dol_blocks = lane_blocks(dol.astype(bf16).astype(f32))
    for i in range(5):
        lanes = slice(i * LANES, (i + 1) * LANES)
        dol_ref[:, lanes] = (dol_blocks[i] * inv_ref[:, lanes]).astype(bf16)


def attention_back_kernel(g, where_ref, q_ref, k_ref, v_ref, lifted_ref, o_ref, dol_ref, dq_ref, dk_ref, dv_ref):
    tokens = q_ref.shape[0]
    step = ROW_BLOCK
    lanes = slice(g * LANES, (g + 1) * LANES)
    dk = None
    dv = None
    for at in reversed(range(tokens // step)):
        rows = slice(at * step, (at + 1) * step)
        seen = (at + 1) * step
        q_stack = head_stack(q_ref, rows, g)
        o_stack = head_stack(o_ref, rows, g)
        dol_stack = head_stack(dol_ref, rows, g)
        lifted = lifted_ref[:, rows, :seen].reshape(CLUSTER * step, seen)
        inner = jnp.sum(o_stack.astype(f32) * dol_stack.astype(f32), axis=1, keepdims=True)
        grad = dot_last(dol_stack, v_ref[:seen, lanes])
        dsl = (lifted.astype(f32) * (grad - inner)).astype(bf16)
        dq = dot_plain(dsl, k_ref[:seen, lanes]) * HEAD_SIZE ** (-0.5)
        dq_ref[:, rows, :] = dq.reshape(CLUSTER, step, LANES)
        dk_part = dot_first(q_stack, dsl)
        dv_part = dot_first(dol_stack, lifted)
        if dk is None:
            dk, dv = dk_part, dv_part
        else:
            dk = jnp.concatenate([dk[:, :seen] + dk_part, dk[:, seen:]], axis=1)
            dv = jnp.concatenate([dv[:, :seen] + dv_part, dv[:, seen:]], axis=1)
    dk = dk.T
    dv = dv.T
    dk_ref[...] = dk + pltpu.roll(dk, HEAD_SIZE, 1)
    dv_ref[...] = dv + pltpu.roll(dv, HEAD_SIZE, 1)


def last_kernel(
    groups, where_ref, dq0, dq1, dq2, dk0, dk1, dk2, dv0, dv1, dv2, cos_ref, sin_ref,
    a_ref, sent0, sent1, kept_ref, dpl_ref, bias_ref, held_ref,
):
    me = where_ref[0]
    tokens = a_ref.shape[0]
    low = lower_half((tokens, LANES))
    heads = [ref[t] for ref in (dq0, dq1, dq2) for t in range(CLUSTER)]
    blocks = [jnp.where(low, heads[2 * i], heads[2 * i + 1]) for i in range(4)]
    blocks.append(jnp.where(low, heads[8], dk0[...]))
    blocks.append(jnp.where(low, dk1[...], dk2[...]))
    cosine, sine = cos_ref[...], sin_ref[...]
    blocks = [block * cosine - swap_pairs(block) * sine for block in blocks]
    blocks.append(jnp.where(low, dv0[...], dv1[...]))
    blocks.append(jnp.where(low, dv2[...], 0.0))
    low_blocks = [block.astype(bf16) for block in blocks]
    blocks = [block.astype(f32) for block in low_blocks]
    dpl_ref[...] = jnp.concatenate(low_blocks, axis=1)
    width = QKV_WIDTH // groups
    chosen = jnp.concatenate(
        [cut_lanes(blocks, b * width, width).astype(bf16) for b in range(groups)], axis=1
    )
    held_ref[...] = dot_first(a_ref[...], chosen).astype(bf16)
    write_message(held_ref, (sent0, sent1), kept_ref, me, groups)
    bias_ref[...] = jnp.concatenate([jnp.sum(block, axis=0, keepdims=True) for block in blocks], axis=1)


def input_kernel(where_ref, dpl_ref, bias_ref, tokens_ref, weight_ref, gain_two_ref, da_ref, small_ref):
    bias_blocks = lane_blocks(bias_ref[...])
    x = tokens_ref[...].astype(f32)
    inverse = lax.rsqrt(jnp.mean(x * x, axis=1, keepdims=True) + norm_eps)
    da = dot_last(dpl_ref[...], weight_ref[...])
    gain_one_blocks = lane_blocks(jnp.sum(da * x * inverse, axis=0, keepdims=True))
    gain_two_blocks = lane_blocks(gain_two_ref[...])
    da_ref[...] = da

    gain_each = 2 * MODEL_WIDTH // 4
    bias_each = QKV_WIDTH // 4
    lines = []
    for s in range(4):
        source = gain_one_blocks if s < 2 else gain_two_blocks
        count = 0
        for t in range(0, gain_each, LANES):
            lines.append(cut_lanes(source, (s % 2) * gain_each + t, min(LANES, gain_each - t)))
            count += 1
        for t in range(0, bias_each, LANES):
            lines.append(cut_lanes(bias_blocks, s * bias_each + t, min(LANES, bias_each - t)))
            count += 1
        lines += [jnp.zeros((1, LANES), f32)] * (SMALL_ROWS // 4 - count)
    small_ref[...] = jnp.concatenate(lines, axis=0).astype(bf16)


def tokens_kernel(where_ref, da_ref, tokens_ref, dh_ref, gains_ref, total_ref, tokens_grad_ref, output_ref, sign_ref):
    output_ref[...] = total_ref[...].T.astype(bf16)
    sign_ref[...] = jnp.zeros(sign_ref.shape, f32)
    da = da_ref[...]
    x = tokens_ref[...].astype(f32)
    inverse = lax.rsqrt(jnp.mean(x * x, axis=1, keepdims=True) + norm_eps)
    weighted = da * gains_ref[0:1, :MODEL_WIDTH]
    inner = jnp.mean(weighted * x, axis=1, keepdims=True)
    tokens_grad = dh_ref[...] + inverse * weighted - x * (inverse * inverse * inverse) * inner
    tokens_grad_ref[...] = tokens_grad.T.astype(bf16)


def place_sum(held_ref, kept_ref, came_refs, mine, groups, rows):
    half = groups // 2
    each = 2 * groups // len(came_refs)
    for j in range(2):
        for b in range(groups):
            at = j * groups + b
            part, inner = divmod(at, each)
            total = kept_ref[at * rows : (at + 1) * rows, :].astype(f32)
            total = total + came_refs[part][inner * rows : (inner + 1) * rows, :].astype(f32)
            place = block_place(b, mine, groups)
            beyond = jnp.where((place & half) == 0, 0, half)
            to = pl.multiple_of((place + beyond + j * half) * rows, 16)
            held_ref[pl.ds(to, rows), :] = total.astype(bf16)


def halve_first_kernel(
    groups, where_ref, kept_ref, came0, came1, small_ref, small_came, sent_ref, left_ref, held_ref
):
    rows = OUT_ROW
    part = groups * rows
    place_sum(held_ref, kept_ref, (came0, came1), where_ref[1], groups, rows)
    small = small_ref[...].astype(f32) + small_came[...].astype(f32)
    for ref, start in ((left_ref, 0), (sent_ref, part)):
        ref[:part, :] = held_ref[start : start + part, :]
        ref[part:, :] = small.astype(bf16)


def down_out_kernel(groups, where_ref, down_zero, down_came, kept_ref, came0, came1, sent_ref, left_ref, held_ref):
    rows = OUT_ROW
    part = groups * rows
    place_sum(held_ref, kept_ref, (came0, came1), where_ref[1], groups, rows)
    lanes = down_zero.shape[1] // LANES
    for ref, start, first in ((left_ref, 0, 0), (sent_ref, part, groups // 2)):
        ref[:part, :] = held_ref[start : start + part, :]
        for b in range(groups // 2):
            rows = slice((first + b) * DOWN_ROWS, (first + b + 1) * DOWN_ROWS)
            total = down_zero[rows, :].astype(f32) + down_came[rows, :].astype(f32)
            for i in range(lanes):
                to = part + (b * lanes + i) * DOWN_ROWS
                ref[to : to + DOWN_ROWS, :] = total[:, i * LANES : (i + 1) * LANES].astype(bf16)


def halve_kernel(small_rows, where_ref, kept_ref, came_ref, sent_ref, left_ref):
    part = left_ref.shape[0] - small_rows
    rows = 2 * part + small_rows
    total = kept_ref[:rows, :].astype(f32) + came_ref[:rows, :].astype(f32)
    total = total.astype(bf16)
    left_ref[:part, :] = total[:part]
    sent_ref[:part, :] = total[part : 2 * part]
    if small_rows:
        left_ref[part:, :] = total[2 * part :]
        sent_ref[part:, :] = total[2 * part :]


def fold_feed_kernel(where_ref, gate_kept, gate_came, gate_across, low_kept, low_came, left_ref, sent_ref):
    blocks, rows = gate_kept.shape[:2]
    half = blocks // 2
    lanes = gate_kept.shape[2] // LANES
    first = low_kept.shape[0] - blocks * lanes * DOWN_ROWS
    for b in range(blocks):
        ref, at = (left_ref, b) if b < half else (sent_ref, b - half)
        gate_up = gate_kept[b].astype(f32) + gate_came[b].astype(f32) + gate_across[b].astype(f32)
        ref[at, :rows, :] = gate_up.astype(bf16)
        for i in range(lanes):
            start = first + (b * lanes + i) * DOWN_ROWS
            down = low_kept[start : start + DOWN_ROWS, :].astype(f32)
            down = down + low_came[start : start + DOWN_ROWS, :].astype(f32)
            ref[at, rows:, i * LANES : (i + 1) * LANES] = down.astype(bf16)


def fold_attention_kernel(where_ref, out_kept, out_came, qkv_kept, qkv_came, left_ref, sent_ref):
    rows = OUT_ROW
    blocks = out_kept.shape[0] // rows
    half = blocks // 2
    out = (out_kept[...].astype(f32) + out_came[...].astype(f32)).astype(bf16)
    qkv = (qkv_kept[...].astype(f32) + qkv_came[...].astype(f32)).astype(bf16)
    small = qkv[blocks * rows :].astype(f32)
    each = SMALL_ROWS // 4
    mine = small[:each]
    for s in range(1, 4):
        mine = jnp.where(where_ref[0] == s, small[s * each : (s + 1) * each], mine)
    mine = jnp.concatenate([mine, jnp.zeros_like(mine)], axis=0).astype(bf16)
    for b in range(blocks):
        ref, at = (left_ref, b) if b < half else (sent_ref, b - half)
        ref[at, :rows, :LANES] = out[b * rows : (b + 1) * rows]
        ref[at, :rows, LANES:] = qkv[b * rows : (b + 1) * rows]
        ref[at, rows:, :LANES] = mine
        ref[at, rows:, LANES:] = jnp.zeros_like(mine)


def fold_kernel(where_ref, kept_ref, came_ref, left_ref, sent_ref):
    half = left_ref.shape[0]
    for b in range(half):
        left_ref[b] = (kept_ref[b].astype(f32) + came_ref[b].astype(f32)).astype(bf16)
        at = b + half
        sent_ref[b] = (kept_ref[at].astype(f32) + came_ref[at].astype(f32)).astype(bf16)


def read_total(refs, parts):
    total = refs[0][0].astype(f32)
    for ref in refs[1:parts]:
        total = total + ref[0].astype(f32)
    return total


def step_with(refs):
    count = len(refs) // 2
    ins, outs = refs[:count], refs[count:]

    def step(at, gradient, rate):
        new = adam_update(ins[at][...], ins[at + 1][...], ins[at + 2][...], gradient, rate)
        for i in range(3):
            outs[at + i][...] = new[i]

    return ins, step


def feed_step_kernel(step_rates, parts, where_ref, *refs):
    total = read_total(refs, parts)
    ins, step = step_with(refs[parts:])
    step(0, total[: ins[0].shape[0]], step_rates[2])
    step(3, total[OUT_ROW : OUT_ROW + ins[3].shape[0]], step_rates[3])


def attention_step_kernel(step_rates, parts, where_ref, *refs):
    total = read_total(refs, parts)
    ins, step = step_with(refs[parts:])
    step(0, total[:OUT_ROW, LANES : LANES + ins[0].shape[1]], step_rates[0])
    step(3, total[:OUT_ROW, : ins[3].shape[1]], step_rates[1])
    mine = total[OUT_ROW:, :LANES]
    line = 0
    for at in (6, 9):
        width = ins[at].shape[0]
        lines = -(-width // LANES)
        wide = jnp.concatenate([mine[line + t : line + t + 1, :] for t in range(lines)], axis=1)
        line += lines
        step(at, wide[:, :width].reshape(width), step_rates[4 if at == 6 else 5])


def swap(values, axis, bit):
    size = lax.axis_size(axis)
    return lax.ppermute(values, axis, [(i, i ^ bit) for i in range(size)])


def add_low(left, right):
    return (left.astype(f32) + right.astype(f32)).astype(bf16)


def halves(values):
    half = values.shape[0] // 2
    return values[:half], values[half:]


def own_term(total, extra, places):
    bit = 1
    while bit < extra:
        total = total + swap(total, "rep", bit)
        bit *= 2
    at = lax.axis_index("rep") % extra
    result = total
    for row, rows, lane, lanes, dim, width in places:
        part = total[row : row + rows, lane : lane + lanes]
        own = lax.dynamic_slice_in_dim(part, at * width, width, dim)
        result = lax.dynamic_update_slice(result, own, (row, lane))
    return result[None]


def finish(left, came, extra, places):
    if extra == 1:
        return [left, came]
    return [own_term((left.astype(f32) + came.astype(f32))[0], extra, places)]


def on_device(
    tokens,
    segments,
    cotangent,
    projection_weight,
    out_weight,
    gate_up_weight,
    down_weight,
    norm_gains,
    projection_bias,
    projection_first_moment,
    out_first,
    gate_up_first,
    down_first,
    gains_first,
    bias_first_moment,
    projection_second_moment,
    out_second,
    gate_up_second,
    down_second,
    gains_second,
    bias_second_moment,
):
    count = tokens.shape[0]
    replicas = lax.axis_size("rep")
    groups = min(replicas, 8)
    extra = replicas // groups
    replica = lax.axis_index("rep")
    where = jnp.stack([lax.axis_index("fsdp"), replica // extra, replica]).astype(jnp.int32)
    rates = learn_rates()
    wide = 1024
    shard_rows, ff_rows = projection_weight.shape[0], gate_up_weight.shape[0]
    q_wide = 5 * LANES
    kv_wide = KEY_VALUE_HEADS * LANES
    tokens_turned, e_turned, down_turned = tokens.T, cotangent.T, down_weight.T

    pack = pack_attention(projection_weight, norm_gains, projection_bias, wide)
    pack2 = swap(pack, "fsdp", 2)
    pack1 = swap(pack, "fsdp", 1)

    (cosine, sine, mask, tokens_low, e, low_out, low_gate_up, half, low_down,
     own_qkv, own_out, own_gate_up, own_down) = kernel_call(
        tables_kernel,
        [
            shaped((count, LANES), f32),
            shaped((count, LANES), f32),
            shaped((count, count), f32),
            shaped((count, MODEL_WIDTH), bf16),
            shaped((count, MODEL_WIDTH), bf16),
            shaped(out_weight.shape, bf16),
            shaped((ff_rows, 2 * MODEL_WIDTH), bf16),
            shaped((ff_rows // 2, 2 * MODEL_WIDTH), bf16),
            shaped((MODEL_WIDTH, ff_rows), bf16),
            shaped(projection_first_moment.shape, f32),
            shaped(out_first.shape, f32),
            shaped(gate_up_first.shape[::-1], f32),
            shaped(down_first.shape[::-1], f32),
        ],
        "tables", 3.0,
        scratch=[pltpu.VMEM((2 * MODEL_WIDTH, ff_rows), f32)], after=(pack,),
    )(
        where, segments, tokens_turned, e_turned,
        projection_weight, out_weight, gate_up_weight, down_turned,
    )

    pack2, low_out, half = gate([pack2, low_out, half], [pack1, cosine], "after_pack")
    pack3 = swap(pack2, "fsdp", 1)
    out2 = swap(low_out, "fsdp", 2)
    half_across = swap(half, "fsdp", 2)
    out1 = swap(low_out, "fsdp", 1)
    gate_up1 = swap(low_gate_up, "fsdp", 1)
    down1 = swap(low_down, "fsdp", 1)

    (a, q, k, v, lifted0, lifted1, lifted2, inv, o, weight_full, gains) = kernel_call(
        forward_kernel,
        [
            shaped((count, MODEL_WIDTH), bf16),
            shaped((count, q_wide), bf16),
            shaped((count, kv_wide), bf16),
            shaped((count, kv_wide), bf16),
        ]
        + [shaped((CLUSTER, count, count), bf16)] * 3
        + [
            shaped((count, q_wide), f32),
            shaped((count, q_wide), bf16),
            shaped((MODEL_WIDTH, wide), bf16),
            shaped((2, q_wide), f32),
        ],
        "attention_forward", 6.0,
    )(where, tokens_low, cosine, sine, mask, pack, pack1, pack2, pack3)

    (out2,) = gate([out2], [o], "after_attention")
    out3 = swap(out2, "fsdp", 1)

    h, a2, a2_turned, out_full = kernel_call(
        project_kernel,
        [
            shaped((count, MODEL_WIDTH), f32),
            shaped((count, q_wide), bf16),
            shaped((MODEL_WIDTH, count), bf16),
            shaped((MODEL_WIDTH, MODEL_WIDTH), bf16),
        ],
        "project", 2.0,
    )(where, tokens_low, o, gains, low_out, out1, out2, out3)

    half_across, low_down_late = gate([half_across, low_down], [h, down1], "after_project")
    down2 = swap(low_down_late, "fsdp", 2)
    half_beside = swap(half_across, "rep", extra)
    half_across3 = swap(half_across, "fsdp", 1)
    gate_ups = {0: [low_gate_up], 1: [gate_up1]}
    downs = {0: low_down_late, 1: down1}

    gate_up_block = (2 * MODEL_WIDTH // groups, ff_rows)
    half_block = (groups // 2,) + gate_up_block

    def grad_parts(count):
        return [shaped((groups // count * (OUT_ROW + DOWN_ROWS), ff_rows), bf16)] * count

    def core_sum(own, sent, name, after=()):
        came = [swap(part, "fsdp", 1) for part in sent]
        return kernel_call(
            functools.partial(core_sum_kernel, groups, len(own)),
            [shaped(half_block, bf16), shaped(half_block, bf16), shaped((groups * DOWN_ROWS, ff_rows), bf16)],
            name, 0.2, scratch=[pltpu.VMEM((groups,) + gate_up_block, bf16)], after=after,
        )(where, *own, *came)

    grads = {}
    total, accumulated = h, []
    for j in (1, 0, 3, 2):
        first = j == 1
        waits = (half_across,) if first else (zero_sent,) if j == 3 else ()
        parts = 4 if j > 1 else 2
        total, *results = kernel_call(
            functools.partial(feed_kernel, groups, first, j > 1, parts),
            [
                shaped((count, MODEL_WIDTH), f32),
                shaped((count, q_wide), f32),
            ] + grad_parts(parts),
            "feed_" + str(j), 0.5,
            scratch=[pltpu.VMEM((2 * ff_rows, q_wide), bf16)],
            after=waits,
        )(
            where, a2, a2_turned, e, e_turned, total, *accumulated, *gate_ups[j], downs[j],
        )
        accumulated, grads[j] = results[:1], results[1:]
        if j == 0:
            half_beside, down2 = gate([half_beside, down2], [total], "after_feed_0")
            gate_ups[2] = [half_across, half_beside]
            gate_ups[3] = [half_across3, swap(half_beside, "fsdp", 1)]
            downs[2], downs[3] = down2, swap(down2, "fsdp", 1)
            zero_kept, zero_sent, down_zero = core_sum(grads[0], grads[1], "core_sum_0")
            zero_came = swap(zero_sent, "rep", extra)
    two_kept, two_sent, down_two = core_sum(grads[2], grads[3], "core_sum_2", (zero_came,))
    two_came = swap(two_sent, "rep", extra)
    down_came = swap(down_two, "fsdp", 2)

    message = 2 * groups * shard_rows
    dh, dol, gain_two, *out_parts = kernel_call(
        functools.partial(middle_kernel, groups),
        [
            shaped((count, MODEL_WIDTH), f32),
            shaped((count, q_wide), bf16),
            shaped((1, MODEL_WIDTH), f32),
            shaped((message // 2, LANES), bf16),
            shaped((message // 2, LANES), bf16),
            shaped((message, LANES), bf16),
        ],
        "middle", 0.5, after=(two_sent, down_two),
        scratch=[pltpu.VMEM((MODEL_WIDTH, groups * LANES), bf16)],
    )(where, *accumulated, h, e, gains, o, inv, out_full)

    def halve(kept, came, small_rows, name, after=()):
        part = (kept.shape[0] - small_rows) // 2 + small_rows
        return kernel_call(
            functools.partial(halve_kernel, small_rows),
            [shaped((part, LANES), bf16)] * 2, name, 0.3, after=after,
        )(where, kept, came)

    *out_sent, out_kept = out_parts
    out_came = [swap(part, "fsdp", 1) for part in out_sent]

    dqs, dks, dvs = [], [], []
    waits = ()
    for g, lifted in enumerate((lifted0, lifted1, lifted2)):
        if g == 2:
            two_kept, down_zero = gate([two_kept, down_zero], [dqs[1]], "after_back")
            two = add_low(two_kept, two_came)
            gate_up_across = swap(two, "fsdp", 2)
            low_rows = message // 2 + groups // 2 * (ff_rows // LANES) * DOWN_ROWS
            low_sent, low_kept = kernel_call(
                functools.partial(down_out_kernel, groups),
                [shaped((low_rows, LANES), bf16)] * 2, "down_out", 0.2,
                scratch=[pltpu.VMEM((message, LANES), bf16)],
            )(where, down_zero, down_came, out_kept, *out_came)
            low_came = swap(low_sent, "rep", extra)
            waits = (two, low_sent)
        dq, dk, dv = kernel_call(
            functools.partial(attention_back_kernel, g),
            [shaped((CLUSTER, count, LANES), f32), shaped((count, LANES), f32), shaped((count, LANES), f32)],
            "attention_back_" + str(g), 0.2, after=waits + tuple(dqs),
        )(where, q, k, v, lifted, o, dol)
        dqs.append(dq)
        dks.append(dk)
        dvs.append(dv)

    *sent, kept, dpl, bias_grad = kernel_call(
        functools.partial(last_kernel, groups),
        [
            shaped((message // 2, LANES), bf16),
            shaped((message // 2, LANES), bf16),
            shaped((message, LANES), bf16),
            shaped((count, wide), bf16),
            shaped((1, wide), f32),
        ],
        "last", 0.2,
        scratch=[pltpu.VMEM((MODEL_WIDTH, groups * LANES), bf16)],
    )(where, *dqs, *dks, *dvs, cosine, sine, a)
    came = [swap(part, "fsdp", 1) for part in sent]
    da, small = kernel_call(
        input_kernel,
        [shaped((count, MODEL_WIDTH), f32), shaped((SMALL_ROWS, LANES), bf16)], "input_gradient", 0.2,
    )(where, dpl, bias_grad, tokens_low, weight_full, gain_two)
    small_came = swap(small, "fsdp", 1)
    sent, kept = kernel_call(
        functools.partial(halve_first_kernel, groups),
        [shaped((message // 2 + SMALL_ROWS, LANES), bf16)] * 2, "halve_first", 0.3, after=(gate_up_across,),
        scratch=[pltpu.VMEM((message, LANES), bf16)],
    )(where, kept, *came, small, small_came)
    came = swap(sent, "rep", extra)

    quarter = groups // 4
    rows = OUT_ROW + DOWN_ROWS
    feed_left, feed_sent = kernel_call(
        fold_feed_kernel, [shaped((quarter, rows, ff_rows), bf16)] * 2, "fold_feed", 0.5, after=(sent,)
    )(where, zero_kept, zero_came, gate_up_across, low_kept, low_came)
    feed_came = swap(feed_sent, "rep", 2 * extra)
    out_sent, out_kept = kernel_call(
        functools.partial(halve_kernel, 0),
        [shaped((message // 4, LANES), bf16)] * 2, "out_halve", 0.3, after=(feed_sent,),
    )(where, low_kept, low_came)
    out_came = swap(out_sent, "fsdp", 2)
    sent, kept = halve(kept, came, SMALL_ROWS, "halve_2")
    came = swap(sent, "fsdp", 2)

    def fold(left, came, name, after=()):
        half = left.shape[0] // 2
        return kernel_call(
            fold_kernel, [shaped((half,) + left.shape[1:], bf16)] * 2, name, 0.3, after=after
        )(where, left, came)

    bits = [1 << i for i in range(2, groups.bit_length() - 1)]
    for bit in bits:
        feed_left, feed_sent = fold(feed_left, feed_came, "fold_feed_" + str(bit), (sent, out_came))
        feed_came = swap(feed_sent, "rep", bit * extra)
    left, sent = kernel_call(
        fold_attention_kernel,
        [shaped((quarter, OUT_ROW + SMALL_ROWS // 2, 2 * LANES), bf16)] * 2, "fold_attention", 0.5, after=(feed_sent,),
    )(where, out_kept, out_came, kept, came)
    came = swap(sent, "rep", 2 * extra)
    tokens_grad, output, sign = kernel_call(
        tokens_kernel,
        [shaped((MODEL_WIDTH, count), bf16), shaped((MODEL_WIDTH, count), bf16), shaped((8, LANES), f32)],
        "tokens_gradient", 0.5, after=(sent,),
    )(where, da, tokens_low, dh, gains, total)
    for bit in bits:
        left, sent = fold(left, came, "fold_attention_" + str(bit), (feed_came, sign))
        came = swap(sent, "rep", bit * extra)

    feed_states = (
        own_gate_up, gate_up_first.T, gate_up_second.T, own_down, down_first.T, down_second.T,
    )
    wide_gate, wide_down = own_gate_up.shape[0] * extra, own_down.shape[0] * extra
    feed_parts = finish(feed_left, feed_came, extra, (
        (0, wide_gate, 0, ff_rows, 0, own_gate_up.shape[0]),
        (OUT_ROW, wide_down, 0, ff_rows, 0, own_down.shape[0]),
    ))
    feed_news = kernel_call(
        functools.partial(feed_step_kernel, rates, len(feed_parts)),
        [shaped(state.shape, f32) for state in feed_states], "feed_step", 0.5, after=(sent,),
    )(where, *feed_parts, *feed_states)
    states = (
        own_qkv, projection_first_moment, projection_second_moment,
        own_out, out_first, out_second,
        norm_gains, gains_first, gains_second,
        projection_bias, bias_first_moment, bias_second_moment,
    )
    parts = finish(left, came, extra, (
        (0, OUT_ROW, LANES, own_qkv.shape[1] * extra, 1, own_qkv.shape[1]),
        (0, OUT_ROW, 0, own_out.shape[1] * extra, 1, own_out.shape[1]),
    ))
    news = kernel_call(
        functools.partial(attention_step_kernel, rates, len(parts)),
        [shaped(state.shape, f32) for state in states], "attention_step", 1.0,
    )(where, *parts, *states)
    return (
        output.T,
        tokens_grad.T,
        *news[:6],
        *[new.T for new in feed_news],
        *news[6:],
    )


def solution(mesh):
    rows = P(("rep", "fsdp"), None)
    weight = P("fsdp", None)
    state = P("fsdp", "rep")
    vector = P("fsdp")
    states = (state,) * 4 + (vector,) * 2
    in_specs = (rows, P(("rep", "fsdp")), rows) + (weight,) * 4 + (vector,) * 2 + states + states
    out_specs = (rows, rows) + (state,) * 12 + (vector,) * 6
    return jax.shard_map(
        on_device, mesh=mesh, in_specs=in_specs, out_specs=out_specs, check_vma=False
    )
```

```python
import functools
import math

import jax
import jax.numpy as jnp
from jax import lax
from jax.experimental import pallas as pl
from jax.experimental.pallas import tpu as pltpu
from jax.sharding import PartitionSpec as P

MODEL_WIDTH = 576
QUERY_HEADS = 9
KEY_VALUE_HEADS = 3
HEAD_SIZE = 64
FF = 1536
STEP = 10

norm_eps = 1e-05
rope_base = 100000.0
beta_one = 0.9
beta_two = 0.95
adam_eps = 1e-08
decay_rate = 0.1

LANES = 128
QKV_WIDTH = (QUERY_HEADS + 2 * KEY_VALUE_HEADS) * HEAD_SIZE
CLUSTER = QUERY_HEADS // KEY_VALUE_HEADS
SMALL_ROWS = 32
ROW_BLOCK = 128
OUT_ROW = MODEL_WIDTH // 4
DOWN_ROWS = 80
bf16 = jnp.bfloat16
f32 = jnp.float32


def learn_rates():
    out_fan = max(QUERY_HEADS * HEAD_SIZE // 16, 1)
    return (MODEL_WIDTH ** (-0.5), out_fan ** (-0.5), MODEL_WIDTH ** (-0.5), FF ** (-0.5), 0.5, 0.5)


def adam_update(weight, first_moment, second_moment, gradient, step_rate):
    first_new = beta_one * first_moment + (1.0 - beta_one) * gradient
    second_new = beta_two * second_moment + (1.0 - beta_two) * gradient * gradient
    first_fix = 1.0 - beta_one**STEP
    second_fix = 1.0 - beta_two**STEP
    direction = first_new / first_fix / (jnp.sqrt(second_new / second_fix) + adam_eps)
    return (first_new, second_new, weight - step_rate * (direction + decay_rate * weight))


def dot_plain(left, right):
    return lax.dot_general(left, right, (((1,), (0,)), ((), ())), preferred_element_type=f32)


def dot_last(left, right):
    return lax.dot_general(left, right, (((1,), (1,)), ((), ())), preferred_element_type=f32)


def dot_first(left, right):
    return lax.dot_general(left, right, (((0,), (0,)), ((), ())), preferred_element_type=f32)


def kernel_call(body, outs, name, time, scratch=(), vmem=12, after=()):
    def call(scalars, *arrays):
        count = len(after)

        def run(*refs):
            body(refs[0], *refs[1 + count :])

        return pl.pallas_call(
            run,
            out_shape=tuple(outs),
            in_specs=[pl.BlockSpec(memory_space=pltpu.SMEM)]
            + [pl.BlockSpec(memory_space=pl.ANY)] * count
            + [pl.BlockSpec(memory_space=pltpu.VMEM)] * len(arrays),
            out_specs=tuple(pl.BlockSpec(memory_space=pltpu.VMEM) for _ in outs),
            scratch_shapes=list(scratch),
            name=name,
            compiler_params=pltpu.CompilerParams(vmem_limit_bytes=vmem * 2**20),
            cost_estimate=pl.CostEstimate(
                flops=int(time * 1.15e9), bytes_accessed=0, transcendentals=0
            ),
        )(scalars, *after, *arrays)

    return call


def gate(values, after, name):
    def nothing(*refs):
        pass

    result = pl.pallas_call(
        nothing,
        out_shape=tuple(shaped(v.shape, v.dtype) for v in values),
        in_specs=[pl.BlockSpec(memory_space=pl.ANY)] * (len(values) + len(after)),
        out_specs=tuple(pl.BlockSpec(memory_space=pl.ANY) for _ in values),
        input_output_aliases={i: i for i in range(len(values))},
        name=name,
        compiler_params=pltpu.CompilerParams(vmem_limit_bytes=2**20),
        cost_estimate=pl.CostEstimate(flops=0, bytes_accessed=0, transcendentals=0),
    )(*values, *after)
    return list(result)


def shaped(shape, dtype):
    return jax.ShapeDtypeStruct(tuple(shape), dtype)


def lane_index(shape):
    return lax.broadcasted_iota(jnp.int32, shape, len(shape) - 1)


def lower_half(shape):
    return lane_index(shape) < HEAD_SIZE


def swap_pairs(block):
    first = (lane_index(block.shape) & (HEAD_SIZE // 2)) == 0
    ahead = pltpu.roll(block, LANES - HEAD_SIZE // 2, 1)
    behind = pltpu.roll(block, HEAD_SIZE // 2, 1)
    return jnp.where(first, ahead, behind)


def both_halves(block, upper):
    other = pltpu.roll(block, HEAD_SIZE, 1)
    low = lower_half(block.shape)
    return jnp.where(low, other, block) if upper else jnp.where(low, block, other)


def cut_lanes(blocks, start, width):
    at, offset = divmod(start, LANES)
    lane = lane_index(blocks[0].shape)
    part = blocks[at]
    if offset:
        part = pltpu.roll(part, LANES - offset, 1)
        if offset + width > LANES:
            after = pltpu.roll(blocks[at + 1], LANES - offset, 1)
            part = jnp.where(lane < LANES - offset, part, after)
    if width < LANES:
        part = jnp.where(lane < width, part, 0.0)
    return part


def lane_blocks(values):
    width = values.shape[1]
    full = width // LANES
    blocks = [values[:, i * LANES : (i + 1) * LANES] for i in range(full)]
    if width % LANES:
        rest = values[:, full * LANES :]
        fill = jnp.zeros((values.shape[0], LANES - width % LANES), values.dtype)
        blocks.append(jnp.concatenate([rest, fill], axis=1))
    return blocks


def block_place(block, mine, groups):
    away = mine ^ block
    place = 0
    bit = 1
    while bit < groups:
        place = place * 2 + jnp.where((away & bit) == 0, 0, 1)
        bit *= 2
    return place


def own_rows(ref, replica, width):
    if width % 8 == 0:
        return ref[pl.ds(pl.multiple_of(replica * width, 8), width), :]
    rows = ref.shape[0]
    return pltpu.roll(ref[...], rows - replica * width, 0)[:width]


def pack_kernel(
    qkv_hbm, out_hbm, gains_hbm, bias_hbm, pack_ref, qkv_ref, out_ref, gains_ref, bias_ref, sems
):
    pairs = ((qkv_hbm, qkv_ref), (out_hbm, out_ref), (gains_hbm, gains_ref), (bias_hbm, bias_ref))
    copies = [
        pltpu.make_async_copy(source, target, sems.at[i]) for i, (source, target) in enumerate(pairs)
    ]
    for copy in copies:
        copy.start()
    for copy in copies:
        copy.wait()
    blocks = lane_blocks(qkv_ref[...])
    bias, gains = (ref[...].reshape(1, ref.shape[0]) for ref in (bias_ref, gains_ref))
    lines = []
    for block in lane_blocks(bias) + lane_blocks(gains):
        lines += [pltpu.roll(block, HEAD_SIZE, 1), block]
    lines.append(jnp.zeros((pack_ref.shape[0] - len(lines), LANES), f32))
    low = lower_half(blocks[-1].shape)
    blocks[-1] = jnp.where(low, blocks[-1], jnp.concatenate(lines, axis=0))
    for i, block in enumerate(blocks + lane_blocks(out_ref[...])):
        pack_ref[:, i * LANES : (i + 1) * LANES] = block.astype(bf16)


def pack_attention(weight, out, gains, bias):
    sources = (weight, out, gains, bias)
    lanes = sum(-(-w.shape[1] // LANES) * LANES for w in (weight, out))
    return pl.pallas_call(
        pack_kernel,
        out_shape=shaped((weight.shape[0], lanes), bf16),
        in_specs=[pl.BlockSpec(memory_space=pl.ANY)] * 4,
        out_specs=pl.BlockSpec(memory_space=pltpu.VMEM),
        scratch_shapes=[pltpu.VMEM(source.shape, f32) for source in sources]
        + [pltpu.SemaphoreType.DMA((4,))],
        name="pack_attention",
        compiler_params=pltpu.CompilerParams(vmem_limit_bytes=60 * 2**20),
        cost_estimate=pl.CostEstimate(flops=10**9, bytes_accessed=0, transcendentals=0),
    )(*sources)


def tables_kernel(
    where_ref, segments_ref, tokens_turned_ref, e_turned_ref, qkv_ref, out_ref, gate_up_ref, down_ref,
    cos_ref, sin_ref, mask_ref, tokens_ref, e_ref, low_gate_up_ref, half_ref, low_down_ref,
    own_qkv_ref, own_out_ref, own_gate_up_ref, own_down_ref, turned_ref,
):
    tokens = segments_ref.shape[0]
    row = segments_ref[...].reshape(1, tokens).astype(f32)
    column = jnp.broadcast_to(row, (LANES, tokens)).T[:, :1]
    query = lax.broadcasted_iota(jnp.int32, (tokens, tokens), 0)
    key = lax.broadcasted_iota(jnp.int32, (tokens, tokens), 1)
    same = column == row
    earlier = jnp.sum(jnp.where(same & (key < query), 1.0, 0.0), axis=1, keepdims=True)
    mask_ref[...] = jnp.where(same & (key <= query), 0.0, -1e30)
    lane = lane_index((tokens, LANES))
    exponent = (lane & (HEAD_SIZE // 2 - 1)).astype(f32) * (2.0 / HEAD_SIZE)
    frequency = jnp.exp(exponent * (-math.log(rope_base)))
    angles = earlier * frequency
    cos_ref[...] = jnp.cos(angles)
    sine = jnp.sin(angles)
    sin_ref[...] = jnp.where((lane & (HEAD_SIZE // 2)) == 0, -sine, sine)
    tokens_ref[...] = tokens_turned_ref[...].astype(f32).T.astype(bf16)
    e_ref[...] = e_turned_ref[...].astype(f32).T.astype(bf16)

    gate_up = gate_up_ref[...]
    whole = MODEL_WIDTH // LANES * LANES
    blocks = [gate_up[:, i * LANES : (i + 1) * LANES] for i in range(gate_up.shape[1] // LANES)]
    low = lower_half(blocks[0].shape)
    low_gate_up_ref[:, :whole] = gate_up[:, :whole].astype(bf16)
    first = MODEL_WIDTH // LANES
    turned = [pltpu.roll(block, HEAD_SIZE, 1) for block in blocks[first:]]
    for i in range(first):
        block = jnp.where(low, turned[i], turned[i + 1])
        low_gate_up_ref[:, whole + i * LANES : whole + (i + 1) * LANES] = block.astype(bf16)
    low_gate_up_ref[:, 2 * whole :] = jnp.where(low, blocks[first], blocks[-1]).astype(bf16)
    rows = half_ref.shape[0]
    start = pl.multiple_of((where_ref[1] & 1) * rows, 16)
    half_ref[...] = low_gate_up_ref[pl.ds(start, rows), :]
    low_down_ref[...] = down_ref[...].astype(bf16)
    replica = where_ref[2]
    turned_ref[...] = gate_up.T
    width = own_gate_up_ref.shape[0]
    own_gate_up_ref[...] = own_rows(turned_ref, replica, width)
    width = own_down_ref.shape[0]
    own_down_ref[...] = own_rows(down_ref, replica, width)
    for ref, own in ((qkv_ref, own_qkv_ref), (out_ref, own_out_ref)):
        width = own.shape[1]
        wide = jnp.concatenate(lane_blocks(ref[...]), axis=1)
        own[...] = pltpu.roll(wide, wide.shape[1] - replica * width, 1)[:, :width]


def forward_kernel(
    where_ref, tokens_ref, cos_ref, sin_ref, mask_ref, pack0, pack1, pack2, pack3,
    a_ref, q_ref, k_ref, v_ref, e0_ref, e1_ref, e2_ref, inv_ref, o_ref, weight_ref, gains_ref,
):
    me = where_ref[0]
    tokens = tokens_ref.shape[0]
    shard_rows = MODEL_WIDTH // 4
    packs = (pack0, pack1, pack2, pack3)
    lines = []
    for j in range(4):
        start = pl.multiple_of((me ^ j) * shard_rows, 16)
        weight_ref[pl.ds(start, shard_rows), :] = packs[j][:, : weight_ref.shape[1]]
        extra = packs[j][:16, weight_ref.shape[1] - LANES : weight_ref.shape[1]].astype(f32)
        half = lower_half((1, LANES))
        turned = pltpu.roll(extra, HEAD_SIZE, 1)
        lines.append(
            jnp.concatenate(
                [jnp.where(half, turned[2 * i : 2 * i + 1], extra[2 * i + 1 : 2 * i + 2]) for i in range(5)],
                axis=1,
            )
        )
    bias_wide = lane_index((1, LANES)) * 0.0
    ordered = []
    for s in range(4):
        line = jnp.where((me ^ s) == 0, lines[0], 0.0)
        for j in range(1, 4):
            line = jnp.where((me ^ s) == j, lines[j], line)
        ordered.append(line)
    bias_blocks = [bias_wide for _ in range(weight_ref.shape[1] // LANES)]
    gain_blocks = [[bias_wide for _ in range(5)] for _ in range(2)]
    lane = lane_index((1, LANES))

    def put(blocks, source, width, start):
        done = 0
        while done < width:
            at, offset = divmod(start + done, LANES)
            count = min(LANES - offset, width - done)
            from_at, from_offset = divmod(done, LANES)
            count = min(count, LANES - from_offset)
            turn = (offset - from_offset) % LANES
            part = source[from_at]
            if turn:
                part = pltpu.roll(part, turn, 1)
            blocks[at] = jnp.where((lane >= offset) & (lane < offset + count), part, blocks[at])
            done += count

    bias_each = QKV_WIDTH // 4
    gain_each = 2 * MODEL_WIDTH // 4
    bias_lanes = -(-bias_each // LANES) * LANES
    for s in range(4):
        pieces = [ordered[s][:, i * LANES : (i + 1) * LANES] for i in range(5)]
        put(bias_blocks, pieces, bias_each, s * bias_each)
        put(gain_blocks[s // 2], pieces[bias_lanes // LANES :], gain_each, (s % 2) * gain_each)
    gains = [jnp.concatenate(blocks, axis=1) for blocks in gain_blocks]
    for i in range(2):
        gains_ref[i : i + 1, :] = gains[i]
    bias = jnp.concatenate(bias_blocks, axis=1)

    x = tokens_ref[...].astype(f32)
    inverse = lax.rsqrt(jnp.mean(x * x, axis=1, keepdims=True) + norm_eps)
    a = (x * inverse * gains[0][:, :MODEL_WIDTH]).astype(bf16)
    a_ref[...] = a
    p = dot_plain(a, weight_ref[...]) + bias
    cosine, sine = cos_ref[...], sin_ref[...]
    blocks = [p[:, i * LANES : (i + 1) * LANES] for i in range(8)]
    for i in range(6):
        blocks[i] = blocks[i] * cosine + swap_pairs(blocks[i]) * sine
    low = lower_half((tokens, LANES))
    for i in range(5):
        scaled = blocks[i] * HEAD_SIZE ** (-0.5)
        if i == 4:
            scaled = jnp.where(low, scaled, 0.0)
        q_ref[:, i * LANES : (i + 1) * LANES] = scaled.astype(bf16)
    keys = [both_halves(blocks[4], True), both_halves(blocks[5], False), both_halves(blocks[5], True)]
    values = [both_halves(blocks[6], False), both_halves(blocks[6], True), both_halves(blocks[7], False)]
    for g in range(KEY_VALUE_HEADS):
        k_ref[:, g * LANES : (g + 1) * LANES] = keys[g].astype(bf16)
        v_ref[:, g * LANES : (g + 1) * LANES] = values[g].astype(bf16)

    e_refs = (e0_ref, e1_ref, e2_ref)
    step = ROW_BLOCK
    low = lower_half((step, LANES))
    for at in range(tokens // step):
        rows = slice(at * step, (at + 1) * step)
        seen = (at + 1) * step
        mixed = []
        inverses = []
        for g in range(KEY_VALUE_HEADS):
            stack = head_stack(q_ref, rows, g)
            scores = dot_last(stack, k_ref[:seen, g * LANES : (g + 1) * LANES])
            scores = scores.reshape(CLUSTER, step, seen) + mask_ref[rows, :seen][None]
            lifted = jnp.exp(scores - jnp.max(scores, axis=2, keepdims=True))
            total = jnp.sum(lifted, axis=2, keepdims=True)
            kept = lifted.astype(bf16)
            e_refs[g][:, rows, :seen] = kept
            gathered = dot_plain(
                kept.reshape(CLUSTER * step, seen), v_ref[:seen, g * LANES : (g + 1) * LANES]
            ).reshape(CLUSTER, step, LANES)
            inverse_total = jnp.broadcast_to(1.0 / total, gathered.shape)
            gathered = gathered * inverse_total
            for t in range(CLUSTER):
                mixed.append(gathered[t])
                inverses.append(inverse_total[t])
        for i in range(5):
            second = mixed[2 * i + 1] if 2 * i + 1 < QUERY_HEADS else 0.0
            part = jnp.where(low, mixed[2 * i], second)
            o_ref[rows, i * LANES : (i + 1) * LANES] = part.astype(bf16)
            second = inverses[2 * i + 1] if 2 * i + 1 < QUERY_HEADS else 0.0
            inv_ref[rows, i * LANES : (i + 1) * LANES] = jnp.where(low, inverses[2 * i], second)


def project_kernel(
    where_ref, tokens_ref, o_ref, gains_ref, pack0, pack1, pack2, pack3,
    h_ref, a2_ref, a2_turned_ref, out_weight_ref,
):
    me = where_ref[0]
    tokens = tokens_ref.shape[0]
    shard_rows = pack0.shape[0]
    lanes = pack0.shape[1] - 5 * LANES
    for j, pack in enumerate((pack0, pack1, pack2, pack3)):
        start = pl.multiple_of((me ^ j) * shard_rows, 16)
        out_weight_ref[pl.ds(start, shard_rows), :] = pack[:, lanes : lanes + MODEL_WIDTH]
    x = tokens_ref[...].astype(f32)
    h = x + dot_plain(o_ref[:, :MODEL_WIDTH], out_weight_ref[...])
    h_ref[...] = h
    inverse = lax.rsqrt(jnp.mean(h * h, axis=1, keepdims=True) + norm_eps)
    a2 = h * inverse * gains_ref[1:2, :MODEL_WIDTH]
    for i, block in enumerate(lane_blocks(a2)):
        a2_ref[:, i * LANES : (i + 1) * LANES] = block.astype(bf16)
    a2_turned_ref[...] = a2.T.astype(bf16)


def head_stack(ref, rows, g):
    parts = []
    for t in range(CLUSTER):
        head = g * CLUSTER + t
        block = ref[rows, (head // 2) * LANES : (head // 2 + 1) * LANES]
        low = lower_half(block.shape)
        keep = low if head % 2 == 0 else jnp.logical_not(low)
        parts.append(jnp.where(keep, block, jnp.zeros_like(block)))
    return jnp.concatenate(parts, axis=0)


def feed_kernel(groups, first, halved, parts, *refs):
    refs = list(refs)

    def take(count):
        taken = refs[:count]
        del refs[:count]
        return taken

    where_ref, a2_ref, a2_turned_ref, e_ref, e_turned_ref, base_ref = take(6)
    acc_in = None if first else take(1)[0]
    gate_ups = take(2 if halved else 1)
    (down,) = take(1)
    total_ref, acc_ref = take(2)
    outs = take(parts)
    (stack,) = refs
    mine = where_ref[1]
    hidden_rows = down.shape[1]
    whole = MODEL_WIDTH // LANES * LANES
    for half, gate_up in enumerate(gate_ups):
        rows = gate_up.shape[0]
        start = pl.multiple_of(((mine & 1) ^ half) * rows, 16) if halved else 0
        rest = gate_up[:, 2 * whole :]
        turned = pltpu.roll(rest.astype(f32), HEAD_SIZE, 1).astype(bf16)
        stack[pl.ds(start, rows), :whole] = gate_up[:, :whole]
        stack[pl.ds(start, rows), whole:] = rest
        start = start + hidden_rows
        stack[pl.ds(start, rows), :whole] = gate_up[:, whole : 2 * whole]
        stack[pl.ds(start, rows), whole:] = turned
    both = dot_last(a2_ref[...], stack[...])
    gate, up = both[:, :hidden_rows], both[:, hidden_rows:]
    sigma = 1.0 / (1.0 + jnp.exp(-gate))
    active = gate * sigma
    hidden = (active * up).astype(bf16)
    grad_hidden = dot_plain(e_ref[...], down[...])
    grad_gate = (grad_hidden * up * (sigma * (1.0 + gate * (1.0 - sigma)))).astype(bf16)
    grad_up = (grad_hidden * active).astype(bf16)
    grads = jnp.concatenate([grad_gate, grad_up], axis=1)
    half = groups // 2
    each = groups // parts
    width = OUT_ROW
    block_rows = OUT_ROW + DOWN_ROWS
    turned = dot_plain(a2_turned_ref[...], grads)
    for b in range(groups):
        at, inner = divmod(b, each)
        row, lane = (b % half) * width, (b // half) * hidden_rows
        to = inner * block_rows
        block = turned[row : row + width, lane : lane + hidden_rows]
        outs[at][to : to + width, :] = block.astype(bf16)
    turned = dot_plain(e_turned_ref[...], hidden)
    thin = MODEL_WIDTH // groups
    fill = jnp.zeros((DOWN_ROWS - thin, turned.shape[1]), f32)
    for b in range(groups):
        at, inner = divmod(b, each)
        block = jnp.concatenate([turned[b * thin : (b + 1) * thin], fill], axis=0)
        to = inner * block_rows + width
        outs[at][to : to + DOWN_ROWS, :] = block.astype(bf16)
    part = dot_plain(grads, stack[...])
    acc_ref[...] = part if first else acc_in[...] + part
    total = base_ref[...] + dot_last(hidden, down[...])
    total_ref[...] = total


def core_sum_kernel(groups, parts, where_ref, *refs):
    mine = where_ref[1]
    own, came = refs[:parts], refs[parts : 2 * parts]
    gate_kept, gate_sent, down_total, held_ref = refs[2 * parts :]
    each = groups // parts
    block_rows = OUT_ROW + DOWN_ROWS
    for b in range(groups):
        at, inner = divmod(b, each)
        place = block_place(b, mine, groups)
        rows = slice(inner * block_rows, inner * block_rows + OUT_ROW)
        total = own[at][rows, :].astype(f32) + came[at][rows, :].astype(f32)
        held_ref[place] = total.astype(bf16)
        rows = slice(inner * block_rows + OUT_ROW, (inner + 1) * block_rows)
        total = own[at][rows, :].astype(f32) + came[at][rows, :].astype(f32)
        down_total[pl.ds(pl.multiple_of(place * DOWN_ROWS, 16), DOWN_ROWS), :] = total.astype(bf16)
    half = groups // 2
    gate_kept[...] = held_ref[:half]
    gate_sent[...] = held_ref[half:]


def write_message(held_ref, sent_refs, kept_ref, me, groups):
    rows = held_ref.shape[0] // 4
    each = 2 * groups // len(sent_refs)
    for j in range(4):
        start = pl.multiple_of((me ^ j) * rows, 16)
        for b in range(groups):
            block = held_ref[pl.ds(start, rows), b * LANES : (b + 1) * LANES]
            to = (j // 2) * groups + b
            if j % 2:
                at, to = divmod(to, each)
                sent_refs[at][to * rows : (to + 1) * rows, :] = block
            else:
                kept_ref[to * rows : (to + 1) * rows, :] = block


def middle_kernel(
    groups, where_ref, acc_ref, h_ref, e_ref, gains_ref, o_ref, inv_ref, out_weight_ref,
    dh_ref, dol_ref, small_ref, sent0, sent1, kept_ref, held_ref,
):
    me = where_ref[0]
    tokens = h_ref.shape[0]
    gain = gains_ref[1:2, :MODEL_WIDTH]
    h = h_ref[...]
    da2 = acc_ref[:, :MODEL_WIDTH]
    inverse = lax.rsqrt(jnp.mean(h * h, axis=1, keepdims=True) + norm_eps)
    weighted = da2 * gain
    inner = jnp.mean(weighted * h, axis=1, keepdims=True)
    dh = e_ref[...].astype(f32) + inverse * weighted - h * (inverse * inverse * inverse) * inner
    dh_ref[...] = dh
    small_ref[...] = jnp.sum(da2 * h * inverse, axis=0, keepdims=True)
    dhl = dh.astype(bf16)
    spread = dhl.astype(f32)
    blocks = lane_blocks(spread)
    width = MODEL_WIDTH // groups
    chosen = jnp.concatenate(
        [cut_lanes(blocks, b * width, width).astype(bf16) for b in range(groups)], axis=1
    )
    held_ref[...] = dot_first(o_ref[:, :MODEL_WIDTH], chosen).astype(bf16)
    write_message(held_ref, (sent0, sent1), kept_ref, me, groups)
    dol = dot_last(dhl, out_weight_ref[...])
    dol_blocks = lane_blocks(dol.astype(bf16).astype(f32))
    for i in range(5):
        lanes = slice(i * LANES, (i + 1) * LANES)
        dol_ref[:, lanes] = (dol_blocks[i] * inv_ref[:, lanes]).astype(bf16)


def attention_back_kernel(g, where_ref, q_ref, k_ref, v_ref, lifted_ref, o_ref, dol_ref, dq_ref, dk_ref, dv_ref):
    tokens = q_ref.shape[0]
    step = ROW_BLOCK
    lanes = slice(g * LANES, (g + 1) * LANES)
    dk = None
    dv = None
    for at in reversed(range(tokens // step)):
        rows = slice(at * step, (at + 1) * step)
        seen = (at + 1) * step
        q_stack = head_stack(q_ref, rows, g)
        o_stack = head_stack(o_ref, rows, g)
        dol_stack = head_stack(dol_ref, rows, g)
        lifted = lifted_ref[:, rows, :seen].reshape(CLUSTER * step, seen)
        inner = jnp.sum(o_stack.astype(f32) * dol_stack.astype(f32), axis=1, keepdims=True)
        grad = dot_last(dol_stack, v_ref[:seen, lanes])
        dsl = (lifted.astype(f32) * (grad - inner)).astype(bf16)
        dq = dot_plain(dsl, k_ref[:seen, lanes]) * HEAD_SIZE ** (-0.5)
        dq_ref[:, rows, :] = dq.reshape(CLUSTER, step, LANES)
        dk_part = dot_first(q_stack, dsl)
        dv_part = dot_first(dol_stack, lifted)
        if dk is None:
            dk, dv = dk_part, dv_part
        else:
            dk = jnp.concatenate([dk[:, :seen] + dk_part, dk[:, seen:]], axis=1)
            dv = jnp.concatenate([dv[:, :seen] + dv_part, dv[:, seen:]], axis=1)
    dk = dk.T
    dv = dv.T
    dk_ref[...] = dk + pltpu.roll(dk, HEAD_SIZE, 1)
    dv_ref[...] = dv + pltpu.roll(dv, HEAD_SIZE, 1)


def last_kernel(
    groups, where_ref, dq0, dq1, dq2, dk0, dk1, dk2, dv0, dv1, dv2, cos_ref, sin_ref,
    a_ref, sent0, sent1, kept_ref, dpl_ref, bias_ref, held_ref,
):
    me = where_ref[0]
    tokens = a_ref.shape[0]
    low = lower_half((tokens, LANES))
    heads = [ref[t] for ref in (dq0, dq1, dq2) for t in range(CLUSTER)]
    blocks = [jnp.where(low, heads[2 * i], heads[2 * i + 1]) for i in range(4)]
    blocks.append(jnp.where(low, heads[8], dk0[...]))
    blocks.append(jnp.where(low, dk1[...], dk2[...]))
    cosine, sine = cos_ref[...], sin_ref[...]
    blocks = [block * cosine - swap_pairs(block) * sine for block in blocks]
    blocks.append(jnp.where(low, dv0[...], dv1[...]))
    blocks.append(jnp.where(low, dv2[...], 0.0))
    low_blocks = [block.astype(bf16) for block in blocks]
    blocks = [block.astype(f32) for block in low_blocks]
    dpl_ref[...] = jnp.concatenate(low_blocks, axis=1)
    width = QKV_WIDTH // groups
    chosen = jnp.concatenate(
        [cut_lanes(blocks, b * width, width).astype(bf16) for b in range(groups)], axis=1
    )
    held_ref[...] = dot_first(a_ref[...], chosen).astype(bf16)
    write_message(held_ref, (sent0, sent1), kept_ref, me, groups)
    bias_ref[...] = jnp.concatenate([jnp.sum(block, axis=0, keepdims=True) for block in blocks], axis=1)


def input_kernel(where_ref, dpl_ref, bias_ref, tokens_ref, weight_ref, gain_two_ref, da_ref, small_ref):
    bias_blocks = lane_blocks(bias_ref[...])
    x = tokens_ref[...].astype(f32)
    inverse = lax.rsqrt(jnp.mean(x * x, axis=1, keepdims=True) + norm_eps)
    da = dot_last(dpl_ref[...], weight_ref[...])
    gain_one_blocks = lane_blocks(jnp.sum(da * x * inverse, axis=0, keepdims=True))
    gain_two_blocks = lane_blocks(gain_two_ref[...])
    da_ref[...] = da

    gain_each = 2 * MODEL_WIDTH // 4
    bias_each = QKV_WIDTH // 4
    lines = []
    for s in range(4):
        source = gain_one_blocks if s < 2 else gain_two_blocks
        count = 0
        for t in range(0, gain_each, LANES):
            lines.append(cut_lanes(source, (s % 2) * gain_each + t, min(LANES, gain_each - t)))
            count += 1
        for t in range(0, bias_each, LANES):
            lines.append(cut_lanes(bias_blocks, s * bias_each + t, min(LANES, bias_each - t)))
            count += 1
        lines += [jnp.zeros((1, LANES), f32)] * (SMALL_ROWS // 4 - count)
    small_ref[...] = jnp.concatenate(lines, axis=0).astype(bf16)


def tokens_kernel(where_ref, da_ref, tokens_ref, dh_ref, gains_ref, total_ref, tokens_grad_ref, output_ref, sign_ref):
    output_ref[...] = total_ref[...].T.astype(bf16)
    sign_ref[...] = jnp.zeros(sign_ref.shape, f32)
    da = da_ref[...]
    x = tokens_ref[...].astype(f32)
    inverse = lax.rsqrt(jnp.mean(x * x, axis=1, keepdims=True) + norm_eps)
    weighted = da * gains_ref[0:1, :MODEL_WIDTH]
    inner = jnp.mean(weighted * x, axis=1, keepdims=True)
    tokens_grad = dh_ref[...] + inverse * weighted - x * (inverse * inverse * inverse) * inner
    tokens_grad_ref[...] = tokens_grad.T.astype(bf16)


def place_sum(held_ref, kept_ref, came_refs, mine, groups, rows):
    half = groups // 2
    each = 2 * groups // len(came_refs)
    for j in range(2):
        for b in range(groups):
            at = j * groups + b
            part, inner = divmod(at, each)
            total = kept_ref[at * rows : (at + 1) * rows, :].astype(f32)
            total = total + came_refs[part][inner * rows : (inner + 1) * rows, :].astype(f32)
            place = block_place(b, mine, groups)
            beyond = jnp.where((place & half) == 0, 0, half)
            to = pl.multiple_of((place + beyond + j * half) * rows, 16)
            held_ref[pl.ds(to, rows), :] = total.astype(bf16)


def halve_first_kernel(
    groups, where_ref, kept_ref, came0, came1, small_ref, small_came, sent_ref, left_ref, held_ref
):
    rows = OUT_ROW
    part = groups * rows
    place_sum(held_ref, kept_ref, (came0, came1), where_ref[1], groups, rows)
    small = small_ref[...].astype(f32) + small_came[...].astype(f32)
    for ref, start in ((left_ref, 0), (sent_ref, part)):
        ref[:part, :] = held_ref[start : start + part, :]
        ref[part:, :] = small.astype(bf16)


def down_out_kernel(groups, where_ref, down_zero, down_came, kept_ref, came0, came1, sent_ref, left_ref, held_ref):
    rows = OUT_ROW
    part = groups * rows
    place_sum(held_ref, kept_ref, (came0, came1), where_ref[1], groups, rows)
    lanes = down_zero.shape[1] // LANES
    for ref, start, first in ((left_ref, 0, 0), (sent_ref, part, groups // 2)):
        ref[:part, :] = held_ref[start : start + part, :]
        for b in range(groups // 2):
            rows = slice((first + b) * DOWN_ROWS, (first + b + 1) * DOWN_ROWS)
            total = down_zero[rows, :].astype(f32) + down_came[rows, :].astype(f32)
            for i in range(lanes):
                to = part + (b * lanes + i) * DOWN_ROWS
                ref[to : to + DOWN_ROWS, :] = total[:, i * LANES : (i + 1) * LANES].astype(bf16)


def halve_kernel(small_rows, where_ref, kept_ref, came_ref, sent_ref, left_ref):
    part = left_ref.shape[0] - small_rows
    rows = 2 * part + small_rows
    total = kept_ref[:rows, :].astype(f32) + came_ref[:rows, :].astype(f32)
    total = total.astype(bf16)
    left_ref[:part, :] = total[:part]
    sent_ref[:part, :] = total[part : 2 * part]
    if small_rows:
        left_ref[part:, :] = total[2 * part :]
        sent_ref[part:, :] = total[2 * part :]


def fold_feed_kernel(where_ref, gate_kept, gate_came, gate_across, low_kept, low_came, left_ref, sent_ref):
    blocks, rows = gate_kept.shape[:2]
    half = blocks // 2
    lanes = gate_kept.shape[2] // LANES
    first = low_kept.shape[0] - blocks * lanes * DOWN_ROWS
    for b in range(blocks):
        ref, at = (left_ref, b) if b < half else (sent_ref, b - half)
        gate_up = gate_kept[b].astype(f32) + gate_came[b].astype(f32) + gate_across[b].astype(f32)
        ref[at, :rows, :] = gate_up.astype(bf16)
        for i in range(lanes):
            start = first + (b * lanes + i) * DOWN_ROWS
            down = low_kept[start : start + DOWN_ROWS, :].astype(f32)
            down = down + low_came[start : start + DOWN_ROWS, :].astype(f32)
            ref[at, rows:, i * LANES : (i + 1) * LANES] = down.astype(bf16)


def fold_attention_kernel(where_ref, out_kept, out_came, qkv_kept, qkv_came, left_ref, sent_ref):
    rows = OUT_ROW
    blocks = out_kept.shape[0] // rows
    half = blocks // 2
    out = (out_kept[...].astype(f32) + out_came[...].astype(f32)).astype(bf16)
    qkv = (qkv_kept[...].astype(f32) + qkv_came[...].astype(f32)).astype(bf16)
    small = qkv[blocks * rows :].astype(f32)
    each = SMALL_ROWS // 4
    mine = small[:each]
    for s in range(1, 4):
        mine = jnp.where(where_ref[0] == s, small[s * each : (s + 1) * each], mine)
    mine = jnp.concatenate([mine, jnp.zeros_like(mine)], axis=0).astype(bf16)
    for b in range(blocks):
        ref, at = (left_ref, b) if b < half else (sent_ref, b - half)
        ref[at, :rows, :LANES] = out[b * rows : (b + 1) * rows]
        ref[at, :rows, LANES:] = qkv[b * rows : (b + 1) * rows]
        ref[at, rows:, :LANES] = mine
        ref[at, rows:, LANES:] = jnp.zeros_like(mine)


def fold_kernel(where_ref, kept_ref, came_ref, left_ref, sent_ref):
    half = left_ref.shape[0]
    for b in range(half):
        left_ref[b] = (kept_ref[b].astype(f32) + came_ref[b].astype(f32)).astype(bf16)
        at = b + half
        sent_ref[b] = (kept_ref[at].astype(f32) + came_ref[at].astype(f32)).astype(bf16)


def read_total(refs, parts):
    total = refs[0][0].astype(f32)
    for ref in refs[1:parts]:
        total = total + ref[0].astype(f32)
    return total


def step_with(refs):
    count = len(refs) // 2
    ins, outs = refs[:count], refs[count:]

    def step(at, gradient, rate):
        new = adam_update(ins[at][...], ins[at + 1][...], ins[at + 2][...], gradient, rate)
        for i in range(3):
            outs[at + i][...] = new[i]

    return ins, step


def feed_step_kernel(step_rates, parts, where_ref, *refs):
    total = read_total(refs, parts)
    ins, step = step_with(refs[parts:])
    step(0, total[: ins[0].shape[0]], step_rates[2])
    step(3, total[OUT_ROW : OUT_ROW + ins[3].shape[0]], step_rates[3])


def attention_step_kernel(step_rates, parts, where_ref, *refs):
    total = read_total(refs, parts)
    ins, step = step_with(refs[parts:])
    step(0, total[:OUT_ROW, LANES : LANES + ins[0].shape[1]], step_rates[0])
    step(3, total[:OUT_ROW, : ins[3].shape[1]], step_rates[1])
    mine = total[OUT_ROW:, :LANES]
    line = 0
    for at in (6, 9):
        width = ins[at].shape[0]
        lines = -(-width // LANES)
        wide = jnp.concatenate([mine[line + t : line + t + 1, :] for t in range(lines)], axis=1)
        line += lines
        step(at, wide[:, :width].reshape(width), step_rates[4 if at == 6 else 5])


def swap(values, axis, bit):
    size = lax.axis_size(axis)
    return lax.ppermute(values, axis, [(i, i ^ bit) for i in range(size)])


def add_low(left, right):
    return (left.astype(f32) + right.astype(f32)).astype(bf16)


def halves(values):
    half = values.shape[0] // 2
    return values[:half], values[half:]


def own_term(total, extra, places):
    bit = 1
    while bit < extra:
        total = total + swap(total, "rep", bit)
        bit *= 2
    at = lax.axis_index("rep") % extra
    result = total
    for row, rows, lane, lanes, dim, width in places:
        part = total[row : row + rows, lane : lane + lanes]
        own = lax.dynamic_slice_in_dim(part, at * width, width, dim)
        result = lax.dynamic_update_slice(result, own, (row, lane))
    return result[None]


def finish(left, came, extra, places):
    if extra == 1:
        return [left, came]
    return [own_term((left.astype(f32) + came.astype(f32))[0], extra, places)]


def on_device(
    tokens,
    segments,
    cotangent,
    projection_weight,
    out_weight,
    gate_up_weight,
    down_weight,
    norm_gains,
    projection_bias,
    projection_first_moment,
    out_first,
    gate_up_first,
    down_first,
    gains_first,
    bias_first_moment,
    projection_second_moment,
    out_second,
    gate_up_second,
    down_second,
    gains_second,
    bias_second_moment,
):
    count = tokens.shape[0]
    replicas = lax.axis_size("rep")
    groups = min(replicas, 8)
    extra = replicas // groups
    replica = lax.axis_index("rep")
    where = jnp.stack([lax.axis_index("fsdp"), replica // extra, replica]).astype(jnp.int32)
    rates = learn_rates()
    wide = 1024
    shard_rows, ff_rows = projection_weight.shape[0], gate_up_weight.shape[0]
    q_wide = 5 * LANES
    kv_wide = KEY_VALUE_HEADS * LANES
    tokens_turned, e_turned, down_turned = tokens.T, cotangent.T, down_weight.T

    pack = pack_attention(projection_weight, out_weight, norm_gains, projection_bias)
    pack2 = swap(pack, "fsdp", 2)
    pack1 = swap(pack, "fsdp", 1)

    (cosine, sine, mask, tokens_low, e, low_gate_up, half, low_down,
     own_qkv, own_out, own_gate_up, own_down) = kernel_call(
        tables_kernel,
        [
            shaped((count, LANES), f32),
            shaped((count, LANES), f32),
            shaped((count, count), f32),
            shaped((count, MODEL_WIDTH), bf16),
            shaped((count, MODEL_WIDTH), bf16),
            shaped((ff_rows, 2 * MODEL_WIDTH), bf16),
            shaped((ff_rows // 2, 2 * MODEL_WIDTH), bf16),
            shaped((MODEL_WIDTH, ff_rows), bf16),
            shaped(projection_first_moment.shape, f32),
            shaped(out_first.shape, f32),
            shaped(gate_up_first.shape[::-1], f32),
            shaped(down_first.shape[::-1], f32),
        ],
        "tables", 3.0,
        scratch=[pltpu.VMEM((2 * MODEL_WIDTH, ff_rows), f32)], after=(pack,),
    )(
        where, segments, tokens_turned, e_turned,
        projection_weight, out_weight, gate_up_weight, down_turned,
    )

    pack2, half = gate([pack2, half], [pack1, cosine], "after_pack")
    pack3 = swap(pack2, "fsdp", 1)
    half_across = swap(half, "fsdp", 2)
    gate_up1 = swap(low_gate_up, "fsdp", 1)
    down1 = swap(low_down, "fsdp", 1)

    (a, q, k, v, lifted0, lifted1, lifted2, inv, o, weight_full, gains) = kernel_call(
        forward_kernel,
        [
            shaped((count, MODEL_WIDTH), bf16),
            shaped((count, q_wide), bf16),
            shaped((count, kv_wide), bf16),
            shaped((count, kv_wide), bf16),
        ]
        + [shaped((CLUSTER, count, count), bf16)] * 3
        + [
            shaped((count, q_wide), f32),
            shaped((count, q_wide), bf16),
            shaped((MODEL_WIDTH, wide), bf16),
            shaped((2, q_wide), f32),
        ],
        "attention_forward", 6.0,
    )(where, tokens_low, cosine, sine, mask, pack, pack1, pack2, pack3)

    h, a2, a2_turned, out_full = kernel_call(
        project_kernel,
        [
            shaped((count, MODEL_WIDTH), f32),
            shaped((count, q_wide), bf16),
            shaped((MODEL_WIDTH, count), bf16),
            shaped((MODEL_WIDTH, MODEL_WIDTH), bf16),
        ],
        "project", 2.0,
    )(where, tokens_low, o, gains, pack, pack1, pack2, pack3)

    half_across, low_down_late = gate([half_across, low_down], [h, down1], "after_project")
    down2 = swap(low_down_late, "fsdp", 2)
    half_beside = swap(half_across, "rep", extra)
    half_across3 = swap(half_across, "fsdp", 1)
    gate_ups = {0: [low_gate_up], 1: [gate_up1]}
    downs = {0: low_down_late, 1: down1}

    gate_up_block = (2 * MODEL_WIDTH // groups, ff_rows)
    half_block = (groups // 2,) + gate_up_block

    def grad_parts(count):
        return [shaped((groups // count * (OUT_ROW + DOWN_ROWS), ff_rows), bf16)] * count

    def core_sum(own, sent, name, after=()):
        came = [swap(part, "fsdp", 1) for part in sent]
        return kernel_call(
            functools.partial(core_sum_kernel, groups, len(own)),
            [shaped(half_block, bf16), shaped(half_block, bf16), shaped((groups * DOWN_ROWS, ff_rows), bf16)],
            name, 0.2, scratch=[pltpu.VMEM((groups,) + gate_up_block, bf16)], after=after,
        )(where, *own, *came)

    grads = {}
    total, accumulated = h, []
    for j in (1, 0, 3, 2):
        first = j == 1
        waits = (half_across,) if first else (zero_sent,) if j == 3 else ()
        parts = 4 if j > 1 else 2
        total, *results = kernel_call(
            functools.partial(feed_kernel, groups, first, j > 1, parts),
            [
                shaped((count, MODEL_WIDTH), f32),
                shaped((count, q_wide), f32),
            ] + grad_parts(parts),
            "feed_" + str(j), 0.5,
            scratch=[pltpu.VMEM((2 * ff_rows, q_wide), bf16)],
            after=waits,
        )(
            where, a2, a2_turned, e, e_turned, total, *accumulated, *gate_ups[j], downs[j],
        )
        accumulated, grads[j] = results[:1], results[1:]
        if j == 0:
            half_beside, down2 = gate([half_beside, down2], [total], "after_feed_0")
            gate_ups[2] = [half_across, half_beside]
            gate_ups[3] = [half_across3, swap(half_beside, "fsdp", 1)]
            downs[2], downs[3] = down2, swap(down2, "fsdp", 1)
            zero_kept, zero_sent, down_zero = core_sum(grads[0], grads[1], "core_sum_0")
            zero_came = swap(zero_sent, "rep", extra)
    two_kept, two_sent, down_two = core_sum(grads[2], grads[3], "core_sum_2", (zero_came,))
    two_came = swap(two_sent, "rep", extra)
    down_came = swap(down_two, "fsdp", 2)

    message = 2 * groups * shard_rows
    dh, dol, gain_two, *out_parts = kernel_call(
        functools.partial(middle_kernel, groups),
        [
            shaped((count, MODEL_WIDTH), f32),
            shaped((count, q_wide), bf16),
            shaped((1, MODEL_WIDTH), f32),
            shaped((message // 2, LANES), bf16),
            shaped((message // 2, LANES), bf16),
            shaped((message, LANES), bf16),
        ],
        "middle", 0.5, after=(two_sent, down_two),
        scratch=[pltpu.VMEM((MODEL_WIDTH, groups * LANES), bf16)],
    )(where, *accumulated, h, e, gains, o, inv, out_full)

    def halve(kept, came, small_rows, name, after=()):
        part = (kept.shape[0] - small_rows) // 2 + small_rows
        return kernel_call(
            functools.partial(halve_kernel, small_rows),
            [shaped((part, LANES), bf16)] * 2, name, 0.3, after=after,
        )(where, kept, came)

    *out_sent, out_kept = out_parts
    out_came = [swap(part, "fsdp", 1) for part in out_sent]

    dqs, dks, dvs = [], [], []
    waits = ()
    for g, lifted in enumerate((lifted0, lifted1, lifted2)):
        if g == 2:
            two_kept, down_zero = gate([two_kept, down_zero], [dqs[1]], "after_back")
            two = add_low(two_kept, two_came)
            gate_up_across = swap(two, "fsdp", 2)
            low_rows = message // 2 + groups // 2 * (ff_rows // LANES) * DOWN_ROWS
            low_sent, low_kept = kernel_call(
                functools.partial(down_out_kernel, groups),
                [shaped((low_rows, LANES), bf16)] * 2, "down_out", 0.2,
                scratch=[pltpu.VMEM((message, LANES), bf16)],
            )(where, down_zero, down_came, out_kept, *out_came)
            low_came = swap(low_sent, "rep", extra)
            waits = (two, low_sent)
        dq, dk, dv = kernel_call(
            functools.partial(attention_back_kernel, g),
            [shaped((CLUSTER, count, LANES), f32), shaped((count, LANES), f32), shaped((count, LANES), f32)],
            "attention_back_" + str(g), 0.2, after=waits + tuple(dqs),
        )(where, q, k, v, lifted, o, dol)
        dqs.append(dq)
        dks.append(dk)
        dvs.append(dv)

    *sent, kept, dpl, bias_grad = kernel_call(
        functools.partial(last_kernel, groups),
        [
            shaped((message // 2, LANES), bf16),
            shaped((message // 2, LANES), bf16),
            shaped((message, LANES), bf16),
            shaped((count, wide), bf16),
            shaped((1, wide), f32),
        ],
        "last", 0.2,
        scratch=[pltpu.VMEM((MODEL_WIDTH, groups * LANES), bf16)],
    )(where, *dqs, *dks, *dvs, cosine, sine, a)
    came = [swap(part, "fsdp", 1) for part in sent]
    da, small = kernel_call(
        input_kernel,
        [shaped((count, MODEL_WIDTH), f32), shaped((SMALL_ROWS, LANES), bf16)], "input_gradient", 0.2,
    )(where, dpl, bias_grad, tokens_low, weight_full, gain_two)
    small_came = swap(small, "fsdp", 1)
    sent, kept = kernel_call(
        functools.partial(halve_first_kernel, groups),
        [shaped((message // 2 + SMALL_ROWS, LANES), bf16)] * 2, "halve_first", 0.3, after=(gate_up_across,),
        scratch=[pltpu.VMEM((message, LANES), bf16)],
    )(where, kept, *came, small, small_came)
    came = swap(sent, "rep", extra)

    quarter = groups // 4
    rows = OUT_ROW + DOWN_ROWS
    feed_left, feed_sent = kernel_call(
        fold_feed_kernel, [shaped((quarter, rows, ff_rows), bf16)] * 2, "fold_feed", 0.5, after=(sent,)
    )(where, zero_kept, zero_came, gate_up_across, low_kept, low_came)
    feed_came = swap(feed_sent, "rep", 2 * extra)
    out_sent, out_kept = kernel_call(
        functools.partial(halve_kernel, 0),
        [shaped((message // 4, LANES), bf16)] * 2, "out_halve", 0.3, after=(feed_sent,),
    )(where, low_kept, low_came)
    out_came = swap(out_sent, "fsdp", 2)
    sent, kept = halve(kept, came, SMALL_ROWS, "halve_2")
    came = swap(sent, "fsdp", 2)

    def fold(left, came, name, after=()):
        half = left.shape[0] // 2
        return kernel_call(
            fold_kernel, [shaped((half,) + left.shape[1:], bf16)] * 2, name, 0.3, after=after
        )(where, left, came)

    bits = [1 << i for i in range(2, groups.bit_length() - 1)]
    for bit in bits:
        feed_left, feed_sent = fold(feed_left, feed_came, "fold_feed_" + str(bit), (sent, out_came))
        feed_came = swap(feed_sent, "rep", bit * extra)
    left, sent = kernel_call(
        fold_attention_kernel,
        [shaped((quarter, OUT_ROW + SMALL_ROWS // 2, 2 * LANES), bf16)] * 2, "fold_attention", 0.5, after=(feed_sent,),
    )(where, out_kept, out_came, kept, came)
    came = swap(sent, "rep", 2 * extra)
    tokens_grad, output, sign = kernel_call(
        tokens_kernel,
        [shaped((MODEL_WIDTH, count), bf16), shaped((MODEL_WIDTH, count), bf16), shaped((8, LANES), f32)],
        "tokens_gradient", 0.5, after=(sent,),
    )(where, da, tokens_low, dh, gains, total)
    for bit in bits:
        left, sent = fold(left, came, "fold_attention_" + str(bit), (feed_came, sign))
        came = swap(sent, "rep", bit * extra)

    feed_states = (
        own_gate_up, gate_up_first.T, gate_up_second.T, own_down, down_first.T, down_second.T,
    )
    wide_gate, wide_down = own_gate_up.shape[0] * extra, own_down.shape[0] * extra
    feed_parts = finish(feed_left, feed_came, extra, (
        (0, wide_gate, 0, ff_rows, 0, own_gate_up.shape[0]),
        (OUT_ROW, wide_down, 0, ff_rows, 0, own_down.shape[0]),
    ))
    feed_news = kernel_call(
        functools.partial(feed_step_kernel, rates, len(feed_parts)),
        [shaped(state.shape, f32) for state in feed_states], "feed_step", 0.5, after=(sent,),
    )(where, *feed_parts, *feed_states)
    states = (
        own_qkv, projection_first_moment, projection_second_moment,
        own_out, out_first, out_second,
        norm_gains, gains_first, gains_second,
        projection_bias, bias_first_moment, bias_second_moment,
    )
    parts = finish(left, came, extra, (
        (0, OUT_ROW, LANES, own_qkv.shape[1] * extra, 1, own_qkv.shape[1]),
        (0, OUT_ROW, 0, own_out.shape[1] * extra, 1, own_out.shape[1]),
    ))
    news = kernel_call(
        functools.partial(attention_step_kernel, rates, len(parts)),
        [shaped(state.shape, f32) for state in states], "attention_step", 1.0,
    )(where, *parts, *states)
    return (
        output.T,
        tokens_grad.T,
        *news[:6],
        *[new.T for new in feed_news],
        *news[6:],
    )


def solution(mesh):
    rows = P(("rep", "fsdp"), None)
    weight = P("fsdp", None)
    state = P("fsdp", "rep")
    vector = P("fsdp")
    states = (state,) * 4 + (vector,) * 2
    in_specs = (rows, P(("rep", "fsdp")), rows) + (weight,) * 4 + (vector,) * 2 + states + states
    out_specs = (rows, rows) + (state,) * 12 + (vector,) * 6
    return jax.shard_map(
        on_device, mesh=mesh, in_specs=in_specs, out_specs=out_specs, check_vma=False
    )
```

```python
import functools
import math

import jax
import jax.numpy as jnp
from jax import lax
from jax.experimental import pallas as pl
from jax.experimental.pallas import tpu as pltpu
from jax.sharding import PartitionSpec as P

MODEL_WIDTH = 576
QUERY_HEADS = 9
KEY_VALUE_HEADS = 3
HEAD_SIZE = 64
FF = 1536
STEP = 10

norm_eps = 1e-05
rope_base = 100000.0
beta_one = 0.9
beta_two = 0.95
adam_eps = 1e-08
decay_rate = 0.1

LANES = 128
QKV_WIDTH = (QUERY_HEADS + 2 * KEY_VALUE_HEADS) * HEAD_SIZE
CLUSTER = QUERY_HEADS // KEY_VALUE_HEADS
SMALL_ROWS = 32
ROW_BLOCK = 128
OUT_ROW = MODEL_WIDTH // 4
DOWN_ROWS = 80
bf16 = jnp.bfloat16
f32 = jnp.float32


def learn_rates():
    out_fan = max(QUERY_HEADS * HEAD_SIZE // 16, 1)
    return (MODEL_WIDTH ** (-0.5), out_fan ** (-0.5), MODEL_WIDTH ** (-0.5), FF ** (-0.5), 0.5, 0.5)


def adam_update(weight, first_moment, second_moment, gradient, step_rate):
    first_new = beta_one * first_moment + (1.0 - beta_one) * gradient
    second_new = beta_two * second_moment + (1.0 - beta_two) * gradient * gradient
    first_fix = 1.0 - beta_one**STEP
    second_fix = 1.0 - beta_two**STEP
    direction = first_new / first_fix / (jnp.sqrt(second_new / second_fix) + adam_eps)
    return (first_new, second_new, weight - step_rate * (direction + decay_rate * weight))


def dot_plain(left, right):
    return lax.dot_general(left, right, (((1,), (0,)), ((), ())), preferred_element_type=f32)


def dot_last(left, right):
    return lax.dot_general(left, right, (((1,), (1,)), ((), ())), preferred_element_type=f32)


def dot_first(left, right):
    return lax.dot_general(left, right, (((0,), (0,)), ((), ())), preferred_element_type=f32)


def kernel_call(body, outs, name, time, scratch=(), vmem=12, after=()):
    def call(scalars, *arrays):
        count = len(after)

        def run(*refs):
            body(refs[0], *refs[1 + count :])

        return pl.pallas_call(
            run,
            out_shape=tuple(outs),
            in_specs=[pl.BlockSpec(memory_space=pltpu.SMEM)]
            + [pl.BlockSpec(memory_space=pl.ANY)] * count
            + [pl.BlockSpec(memory_space=pltpu.VMEM)] * len(arrays),
            out_specs=tuple(pl.BlockSpec(memory_space=pltpu.VMEM) for _ in outs),
            scratch_shapes=list(scratch),
            name=name,
            compiler_params=pltpu.CompilerParams(vmem_limit_bytes=vmem * 2**20),
            cost_estimate=pl.CostEstimate(
                flops=int(time * 1.15e9), bytes_accessed=0, transcendentals=0
            ),
        )(scalars, *after, *arrays)

    return call


def gate(values, after, name):
    def nothing(*refs):
        pass

    result = pl.pallas_call(
        nothing,
        out_shape=tuple(shaped(v.shape, v.dtype) for v in values),
        in_specs=[pl.BlockSpec(memory_space=pl.ANY)] * (len(values) + len(after)),
        out_specs=tuple(pl.BlockSpec(memory_space=pl.ANY) for _ in values),
        input_output_aliases={i: i for i in range(len(values))},
        name=name,
        compiler_params=pltpu.CompilerParams(vmem_limit_bytes=2**20),
        cost_estimate=pl.CostEstimate(flops=0, bytes_accessed=0, transcendentals=0),
    )(*values, *after)
    return list(result)


def shaped(shape, dtype):
    return jax.ShapeDtypeStruct(tuple(shape), dtype)


def lane_index(shape):
    return lax.broadcasted_iota(jnp.int32, shape, len(shape) - 1)


def lower_half(shape):
    return lane_index(shape) < HEAD_SIZE


def swap_pairs(block):
    first = (lane_index(block.shape) & (HEAD_SIZE // 2)) == 0
    ahead = pltpu.roll(block, LANES - HEAD_SIZE // 2, 1)
    behind = pltpu.roll(block, HEAD_SIZE // 2, 1)
    return jnp.where(first, ahead, behind)


def both_halves(block, upper):
    other = pltpu.roll(block, HEAD_SIZE, 1)
    low = lower_half(block.shape)
    return jnp.where(low, other, block) if upper else jnp.where(low, block, other)


def cut_lanes(blocks, start, width):
    at, offset = divmod(start, LANES)
    lane = lane_index(blocks[0].shape)
    part = blocks[at]
    if offset:
        part = pltpu.roll(part, LANES - offset, 1)
        if offset + width > LANES:
            after = pltpu.roll(blocks[at + 1], LANES - offset, 1)
            part = jnp.where(lane < LANES - offset, part, after)
    if width < LANES:
        part = jnp.where(lane < width, part, 0.0)
    return part


def lane_blocks(values):
    width = values.shape[1]
    full = width // LANES
    blocks = [values[:, i * LANES : (i + 1) * LANES] for i in range(full)]
    if width % LANES:
        rest = values[:, full * LANES :]
        fill = jnp.zeros((values.shape[0], LANES - width % LANES), values.dtype)
        blocks.append(jnp.concatenate([rest, fill], axis=1))
    return blocks


def block_place(block, mine, groups):
    away = mine ^ block
    place = 0
    bit = 1
    while bit < groups:
        place = place * 2 + jnp.where((away & bit) == 0, 0, 1)
        bit *= 2
    return place


def own_rows(ref, replica, width):
    if width % 8 == 0:
        return ref[pl.ds(pl.multiple_of(replica * width, 8), width), :]
    rows = ref.shape[0]
    return pltpu.roll(ref[...], rows - replica * width, 0)[:width]


def pack_kernel(
    qkv_hbm, out_hbm, gains_hbm, bias_hbm, pack_ref, qkv_ref, out_ref, gains_ref, bias_ref, sems
):
    pairs = ((qkv_hbm, qkv_ref), (out_hbm, out_ref), (gains_hbm, gains_ref), (bias_hbm, bias_ref))
    copies = [
        pltpu.make_async_copy(source, target, sems.at[i]) for i, (source, target) in enumerate(pairs)
    ]
    for copy in copies:
        copy.start()
    for copy in copies:
        copy.wait()
    blocks = lane_blocks(qkv_ref[...])
    bias, gains = (ref[...].reshape(1, ref.shape[0]) for ref in (bias_ref, gains_ref))
    lines = []
    for block in lane_blocks(bias) + lane_blocks(gains):
        lines += [pltpu.roll(block, HEAD_SIZE, 1), block]
    lines.append(jnp.zeros((pack_ref.shape[0] - len(lines), LANES), f32))
    low = lower_half(blocks[-1].shape)
    blocks[-1] = jnp.where(low, blocks[-1], jnp.concatenate(lines, axis=0))
    for i, block in enumerate(blocks + lane_blocks(out_ref[...])):
        pack_ref[:, i * LANES : (i + 1) * LANES] = block.astype(bf16)


def pack_attention(weight, out, gains, bias):
    sources = (weight, out, gains, bias)
    lanes = sum(-(-w.shape[1] // LANES) * LANES for w in (weight, out))
    return pl.pallas_call(
        pack_kernel,
        out_shape=shaped((weight.shape[0], lanes), bf16),
        in_specs=[pl.BlockSpec(memory_space=pl.ANY)] * 4,
        out_specs=pl.BlockSpec(memory_space=pltpu.VMEM),
        scratch_shapes=[pltpu.VMEM(source.shape, f32) for source in sources]
        + [pltpu.SemaphoreType.DMA((4,))],
        name="pack_attention",
        compiler_params=pltpu.CompilerParams(vmem_limit_bytes=60 * 2**20),
        cost_estimate=pl.CostEstimate(flops=10**9, bytes_accessed=0, transcendentals=0),
    )(*sources)


def tables_kernel(
    where_ref, segments_ref, tokens_turned_ref, e_turned_ref, qkv_ref, out_ref, gate_up_ref, down_ref,
    cos_ref, sin_ref, mask_ref, tokens_ref, e_ref, low_gate_up_ref, half_ref, low_down_ref,
    own_qkv_ref, own_out_ref, own_gate_up_ref, own_down_ref, turned_ref,
):
    tokens = segments_ref.shape[0]
    row = segments_ref[...].reshape(1, tokens).astype(f32)
    column = jnp.broadcast_to(row, (LANES, tokens)).T[:, :1]
    query = lax.broadcasted_iota(jnp.int32, (tokens, tokens), 0)
    key = lax.broadcasted_iota(jnp.int32, (tokens, tokens), 1)
    same = column == row
    earlier = jnp.sum(jnp.where(same & (key < query), 1.0, 0.0), axis=1, keepdims=True)
    mask_ref[...] = jnp.where(same & (key <= query), 0.0, -1e30)
    lane = lane_index((tokens, LANES))
    exponent = (lane & (HEAD_SIZE // 2 - 1)).astype(f32) * (2.0 / HEAD_SIZE)
    frequency = jnp.exp(exponent * (-math.log(rope_base)))
    angles = earlier * frequency
    cos_ref[...] = jnp.cos(angles)
    sine = jnp.sin(angles)
    sin_ref[...] = jnp.where((lane & (HEAD_SIZE // 2)) == 0, -sine, sine)
    tokens_ref[...] = tokens_turned_ref[...].astype(f32).T.astype(bf16)
    e_ref[...] = e_turned_ref[...].astype(f32).T.astype(bf16)

    gate_up = gate_up_ref[...]
    whole = MODEL_WIDTH // LANES * LANES
    blocks = [gate_up[:, i * LANES : (i + 1) * LANES] for i in range(gate_up.shape[1] // LANES)]
    low = lower_half(blocks[0].shape)
    low_gate_up_ref[:, :whole] = gate_up[:, :whole].astype(bf16)
    first = MODEL_WIDTH // LANES
    turned = [pltpu.roll(block, HEAD_SIZE, 1) for block in blocks[first:]]
    for i in range(first):
        block = jnp.where(low, turned[i], turned[i + 1])
        low_gate_up_ref[:, whole + i * LANES : whole + (i + 1) * LANES] = block.astype(bf16)
    low_gate_up_ref[:, 2 * whole :] = jnp.where(low, blocks[first], blocks[-1]).astype(bf16)
    rows = half_ref.shape[0]
    start = pl.multiple_of((where_ref[1] & 1) * rows, 16)
    half_ref[...] = low_gate_up_ref[pl.ds(start, rows), :]
    low_down_ref[...] = down_ref[...].astype(bf16)
    replica = where_ref[2]
    turned_ref[...] = gate_up.T
    width = own_gate_up_ref.shape[0]
    own_gate_up_ref[...] = own_rows(turned_ref, replica, width)
    width = own_down_ref.shape[0]
    own_down_ref[...] = own_rows(down_ref, replica, width)
    for ref, own in ((qkv_ref, own_qkv_ref), (out_ref, own_out_ref)):
        width = own.shape[1]
        wide = jnp.concatenate(lane_blocks(ref[...]), axis=1)
        own[...] = pltpu.roll(wide, wide.shape[1] - replica * width, 1)[:, :width]


def forward_kernel(
    where_ref, tokens_ref, cos_ref, sin_ref, mask_ref, pack0, pack1, pack2, pack3,
    a_ref, q_ref, k_ref, v_ref, e0_ref, e1_ref, e2_ref, inv_ref, o_ref, weight_ref, gains_ref,
):
    me = where_ref[0]
    tokens = tokens_ref.shape[0]
    shard_rows = MODEL_WIDTH // 4
    packs = (pack0, pack1, pack2, pack3)
    lines = []
    for j in range(4):
        start = pl.multiple_of((me ^ j) * shard_rows, 16)
        weight_ref[pl.ds(start, shard_rows), :] = packs[j][:, : weight_ref.shape[1]]
        extra = packs[j][:16, weight_ref.shape[1] - LANES : weight_ref.shape[1]].astype(f32)
        half = lower_half((1, LANES))
        turned = pltpu.roll(extra, HEAD_SIZE, 1)
        lines.append(
            jnp.concatenate(
                [jnp.where(half, turned[2 * i : 2 * i + 1], extra[2 * i + 1 : 2 * i + 2]) for i in range(5)],
                axis=1,
            )
        )
    bias_wide = lane_index((1, LANES)) * 0.0
    ordered = []
    for s in range(4):
        line = jnp.where((me ^ s) == 0, lines[0], 0.0)
        for j in range(1, 4):
            line = jnp.where((me ^ s) == j, lines[j], line)
        ordered.append(line)
    bias_blocks = [bias_wide for _ in range(weight_ref.shape[1] // LANES)]
    gain_blocks = [[bias_wide for _ in range(5)] for _ in range(2)]
    lane = lane_index((1, LANES))

    def put(blocks, source, width, start):
        done = 0
        while done < width:
            at, offset = divmod(start + done, LANES)
            count = min(LANES - offset, width - done)
            from_at, from_offset = divmod(done, LANES)
            count = min(count, LANES - from_offset)
            turn = (offset - from_offset) % LANES
            part = source[from_at]
            if turn:
                part = pltpu.roll(part, turn, 1)
            blocks[at] = jnp.where((lane >= offset) & (lane < offset + count), part, blocks[at])
            done += count

    bias_each = QKV_WIDTH // 4
    gain_each = 2 * MODEL_WIDTH // 4
    bias_lanes = -(-bias_each // LANES) * LANES
    for s in range(4):
        pieces = [ordered[s][:, i * LANES : (i + 1) * LANES] for i in range(5)]
        put(bias_blocks, pieces, bias_each, s * bias_each)
        put(gain_blocks[s // 2], pieces[bias_lanes // LANES :], gain_each, (s % 2) * gain_each)
    gains = [jnp.concatenate(blocks, axis=1) for blocks in gain_blocks]
    for i in range(2):
        gains_ref[i : i + 1, :] = gains[i]
    bias = jnp.concatenate(bias_blocks, axis=1)

    x = tokens_ref[...].astype(f32)
    inverse = lax.rsqrt(jnp.mean(x * x, axis=1, keepdims=True) + norm_eps)
    a = (x * inverse * gains[0][:, :MODEL_WIDTH]).astype(bf16)
    a_ref[...] = a
    p = dot_plain(a, weight_ref[...]) + bias
    cosine, sine = cos_ref[...], sin_ref[...]
    blocks = [p[:, i * LANES : (i + 1) * LANES] for i in range(8)]
    for i in range(6):
        blocks[i] = blocks[i] * cosine + swap_pairs(blocks[i]) * sine
    low = lower_half((tokens, LANES))
    for i in range(5):
        scaled = blocks[i] * HEAD_SIZE ** (-0.5)
        if i == 4:
            scaled = jnp.where(low, scaled, 0.0)
        q_ref[:, i * LANES : (i + 1) * LANES] = scaled.astype(bf16)
    keys = [both_halves(blocks[4], True), both_halves(blocks[5], False), both_halves(blocks[5], True)]
    values = [both_halves(blocks[6], False), both_halves(blocks[6], True), both_halves(blocks[7], False)]
    for g in range(KEY_VALUE_HEADS):
        k_ref[:, g * LANES : (g + 1) * LANES] = keys[g].astype(bf16)
        v_ref[:, g * LANES : (g + 1) * LANES] = values[g].astype(bf16)

    e_refs = (e0_ref, e1_ref, e2_ref)
    step = ROW_BLOCK
    low = lower_half((step, LANES))
    for at in range(tokens // step):
        rows = slice(at * step, (at + 1) * step)
        seen = (at + 1) * step
        mixed = []
        inverses = []
        for g in range(KEY_VALUE_HEADS):
            stack = head_stack(q_ref, rows, g)
            scores = dot_last(stack, k_ref[:seen, g * LANES : (g + 1) * LANES])
            scores = scores.reshape(CLUSTER, step, seen) + mask_ref[rows, :seen][None]
            lifted = jnp.exp(scores - jnp.max(scores, axis=2, keepdims=True))
            total = jnp.sum(lifted, axis=2, keepdims=True)
            kept = lifted.astype(bf16)
            e_refs[g][:, rows, :seen] = kept
            gathered = dot_plain(
                kept.reshape(CLUSTER * step, seen), v_ref[:seen, g * LANES : (g + 1) * LANES]
            ).reshape(CLUSTER, step, LANES)
            inverse_total = jnp.broadcast_to(1.0 / total, gathered.shape)
            gathered = gathered * inverse_total
            for t in range(CLUSTER):
                mixed.append(gathered[t])
                inverses.append(inverse_total[t])
        for i in range(5):
            second = mixed[2 * i + 1] if 2 * i + 1 < QUERY_HEADS else 0.0
            part = jnp.where(low, mixed[2 * i], second)
            o_ref[rows, i * LANES : (i + 1) * LANES] = part.astype(bf16)
            second = inverses[2 * i + 1] if 2 * i + 1 < QUERY_HEADS else 0.0
            inv_ref[rows, i * LANES : (i + 1) * LANES] = jnp.where(low, inverses[2 * i], second)


def project_kernel(
    where_ref, tokens_ref, o_ref, gains_ref, pack0, pack1, pack2, pack3,
    h_ref, a2_ref, a2_turned_ref, out_weight_ref,
):
    me = where_ref[0]
    tokens = tokens_ref.shape[0]
    shard_rows = pack0.shape[0]
    lanes = pack0.shape[1] - 5 * LANES
    for j, pack in enumerate((pack0, pack1, pack2, pack3)):
        start = pl.multiple_of((me ^ j) * shard_rows, 16)
        out_weight_ref[pl.ds(start, shard_rows), :] = pack[:, lanes : lanes + MODEL_WIDTH]
    x = tokens_ref[...].astype(f32)
    h = x + dot_plain(o_ref[:, :MODEL_WIDTH], out_weight_ref[...])
    h_ref[...] = h
    inverse = lax.rsqrt(jnp.mean(h * h, axis=1, keepdims=True) + norm_eps)
    a2 = h * inverse * gains_ref[1:2, :MODEL_WIDTH]
    for i, block in enumerate(lane_blocks(a2)):
        a2_ref[:, i * LANES : (i + 1) * LANES] = block.astype(bf16)
    a2_turned_ref[...] = a2.T.astype(bf16)


def head_stack(ref, rows, g):
    parts = []
    for t in range(CLUSTER):
        head = g * CLUSTER + t
        block = ref[rows, (head // 2) * LANES : (head // 2 + 1) * LANES]
        low = lower_half(block.shape)
        keep = low if head % 2 == 0 else jnp.logical_not(low)
        parts.append(jnp.where(keep, block, jnp.zeros_like(block)))
    return jnp.concatenate(parts, axis=0)


def feed_kernel(groups, first, halved, parts, *refs):
    refs = list(refs)

    def take(count):
        taken = refs[:count]
        del refs[:count]
        return taken

    where_ref, a2_ref, a2_turned_ref, e_ref, e_turned_ref, base_ref = take(6)
    acc_in = None if first else take(1)[0]
    gate_ups = take(2 if halved else 1)
    (down,) = take(1)
    total_ref, acc_ref = take(2)
    outs = take(parts)
    (stack,) = refs
    mine = where_ref[1]
    hidden_rows = down.shape[1]
    whole = MODEL_WIDTH // LANES * LANES
    for half, gate_up in enumerate(gate_ups):
        rows = gate_up.shape[0]
        start = pl.multiple_of(((mine & 1) ^ half) * rows, 16) if halved else 0
        rest = gate_up[:, 2 * whole :]
        turned = pltpu.roll(rest.astype(f32), HEAD_SIZE, 1).astype(bf16)
        stack[pl.ds(start, rows), :whole] = gate_up[:, :whole]
        stack[pl.ds(start, rows), whole:] = rest
        start = start + hidden_rows
        stack[pl.ds(start, rows), :whole] = gate_up[:, whole : 2 * whole]
        stack[pl.ds(start, rows), whole:] = turned
    both = dot_last(a2_ref[...], stack[...])
    gate, up = both[:, :hidden_rows], both[:, hidden_rows:]
    sigma = 1.0 / (1.0 + jnp.exp(-gate))
    active = gate * sigma
    hidden = (active * up).astype(bf16)
    grad_hidden = dot_plain(e_ref[...], down[...])
    grad_gate = (grad_hidden * up * (sigma * (1.0 + gate * (1.0 - sigma)))).astype(bf16)
    grad_up = (grad_hidden * active).astype(bf16)
    grads = jnp.concatenate([grad_gate, grad_up], axis=1)
    half = groups // 2
    each = groups // parts
    width = OUT_ROW
    block_rows = OUT_ROW + DOWN_ROWS
    turned = dot_plain(a2_turned_ref[...], grads)
    for b in range(groups):
        at, inner = divmod(b, each)
        row, lane = (b % half) * width, (b // half) * hidden_rows
        to = inner * block_rows
        block = turned[row : row + width, lane : lane + hidden_rows]
        outs[at][to : to + width, :] = block.astype(bf16)
    turned = dot_plain(e_turned_ref[...], hidden)
    thin = MODEL_WIDTH // groups
    fill = jnp.zeros((DOWN_ROWS - thin, turned.shape[1]), f32)
    for b in range(groups):
        at, inner = divmod(b, each)
        block = jnp.concatenate([turned[b * thin : (b + 1) * thin], fill], axis=0)
        to = inner * block_rows + width
        outs[at][to : to + DOWN_ROWS, :] = block.astype(bf16)
    part = dot_plain(grads, stack[...])
    acc_ref[...] = part if first else acc_in[...] + part
    total = base_ref[...] + dot_last(hidden, down[...])
    total_ref[...] = total


def core_sum_kernel(groups, parts, where_ref, *refs):
    mine = where_ref[1]
    own, came = refs[:parts], refs[parts : 2 * parts]
    gate_kept, gate_sent, down_total, held_ref = refs[2 * parts :]
    each = groups // parts
    block_rows = OUT_ROW + DOWN_ROWS
    for b in range(groups):
        at, inner = divmod(b, each)
        place = block_place(b, mine, groups)
        rows = slice(inner * block_rows, inner * block_rows + OUT_ROW)
        total = own[at][rows, :].astype(f32) + came[at][rows, :].astype(f32)
        held_ref[place] = total.astype(bf16)
        rows = slice(inner * block_rows + OUT_ROW, (inner + 1) * block_rows)
        total = own[at][rows, :].astype(f32) + came[at][rows, :].astype(f32)
        down_total[pl.ds(pl.multiple_of(place * DOWN_ROWS, 16), DOWN_ROWS), :] = total.astype(bf16)
    half = groups // 2
    gate_kept[...] = held_ref[:half]
    gate_sent[...] = held_ref[half:]


def write_message(held_ref, sent_refs, kept_ref, me, groups):
    rows = held_ref.shape[0] // 4
    each = 2 * groups // len(sent_refs)
    for j in range(4):
        start = pl.multiple_of((me ^ j) * rows, 16)
        for b in range(groups):
            block = held_ref[pl.ds(start, rows), b * LANES : (b + 1) * LANES]
            to = (j // 2) * groups + b
            if j % 2:
                at, to = divmod(to, each)
                sent_refs[at][to * rows : (to + 1) * rows, :] = block
            else:
                kept_ref[to * rows : (to + 1) * rows, :] = block


def middle_kernel(
    groups, where_ref, acc_ref, h_ref, e_ref, gains_ref, o_ref, inv_ref, out_weight_ref,
    dh_ref, dol_ref, small_ref, sent0, sent1, kept_ref, held_ref,
):
    me = where_ref[0]
    tokens = h_ref.shape[0]
    gain = gains_ref[1:2, :MODEL_WIDTH]
    h = h_ref[...]
    da2 = acc_ref[:, :MODEL_WIDTH]
    inverse = lax.rsqrt(jnp.mean(h * h, axis=1, keepdims=True) + norm_eps)
    weighted = da2 * gain
    inner = jnp.mean(weighted * h, axis=1, keepdims=True)
    dh = e_ref[...].astype(f32) + inverse * weighted - h * (inverse * inverse * inverse) * inner
    dh_ref[...] = dh
    small_ref[...] = jnp.sum(da2 * h * inverse, axis=0, keepdims=True)
    dhl = dh.astype(bf16)
    spread = dhl.astype(f32)
    blocks = lane_blocks(spread)
    width = MODEL_WIDTH // groups
    chosen = jnp.concatenate(
        [cut_lanes(blocks, b * width, width).astype(bf16) for b in range(groups)], axis=1
    )
    held_ref[...] = dot_first(o_ref[:, :MODEL_WIDTH], chosen).astype(bf16)
    write_message(held_ref, (sent0, sent1), kept_ref, me, groups)
    dol = dot_last(dhl, out_weight_ref[...])
    dol_blocks = lane_blocks(dol.astype(bf16).astype(f32))
    for i in range(5):
        lanes = slice(i * LANES, (i + 1) * LANES)
        dol_ref[:, lanes] = (dol_blocks[i] * inv_ref[:, lanes]).astype(bf16)


def attention_back_kernel(g, where_ref, q_ref, k_ref, v_ref, lifted_ref, o_ref, dol_ref, dq_ref, dk_ref, dv_ref):
    tokens = q_ref.shape[0]
    step = ROW_BLOCK
    lanes = slice(g * LANES, (g + 1) * LANES)
    dk = None
    dv = None
    for at in reversed(range(tokens // step)):
        rows = slice(at * step, (at + 1) * step)
        seen = (at + 1) * step
        q_stack = head_stack(q_ref, rows, g)
        o_stack = head_stack(o_ref, rows, g)
        dol_stack = head_stack(dol_ref, rows, g)
        lifted = lifted_ref[:, rows, :seen].reshape(CLUSTER * step, seen)
        inner = jnp.sum(o_stack.astype(f32) * dol_stack.astype(f32), axis=1, keepdims=True)
        grad = dot_last(dol_stack, v_ref[:seen, lanes])
        dsl = (lifted.astype(f32) * (grad - inner)).astype(bf16)
        dq = dot_plain(dsl, k_ref[:seen, lanes]) * HEAD_SIZE ** (-0.5)
        dq_ref[:, rows, :] = dq.reshape(CLUSTER, step, LANES)
        dk_part = dot_first(q_stack, dsl)
        dv_part = dot_first(dol_stack, lifted)
        if dk is None:
            dk, dv = dk_part, dv_part
        else:
            dk = jnp.concatenate([dk[:, :seen] + dk_part, dk[:, seen:]], axis=1)
            dv = jnp.concatenate([dv[:, :seen] + dv_part, dv[:, seen:]], axis=1)
    dk = dk.T
    dv = dv.T
    dk_ref[...] = dk + pltpu.roll(dk, HEAD_SIZE, 1)
    dv_ref[...] = dv + pltpu.roll(dv, HEAD_SIZE, 1)


def last_kernel(
    groups, where_ref, dq0, dq1, dq2, dk0, dk1, dk2, dv0, dv1, dv2, cos_ref, sin_ref,
    a_ref, sent0, sent1, kept_ref, dpl_ref, bias_ref, held_ref,
):
    me = where_ref[0]
    tokens = a_ref.shape[0]
    low = lower_half((tokens, LANES))
    heads = [ref[t] for ref in (dq0, dq1, dq2) for t in range(CLUSTER)]
    blocks = [jnp.where(low, heads[2 * i], heads[2 * i + 1]) for i in range(4)]
    blocks.append(jnp.where(low, heads[8], dk0[...]))
    blocks.append(jnp.where(low, dk1[...], dk2[...]))
    cosine, sine = cos_ref[...], sin_ref[...]
    blocks = [block * cosine - swap_pairs(block) * sine for block in blocks]
    blocks.append(jnp.where(low, dv0[...], dv1[...]))
    blocks.append(jnp.where(low, dv2[...], 0.0))
    low_blocks = [block.astype(bf16) for block in blocks]
    blocks = [block.astype(f32) for block in low_blocks]
    dpl_ref[...] = jnp.concatenate(low_blocks, axis=1)
    width = QKV_WIDTH // groups
    chosen = jnp.concatenate(
        [cut_lanes(blocks, b * width, width).astype(bf16) for b in range(groups)], axis=1
    )
    held_ref[...] = dot_first(a_ref[...], chosen).astype(bf16)
    write_message(held_ref, (sent0, sent1), kept_ref, me, groups)
    bias_ref[...] = jnp.concatenate([jnp.sum(block, axis=0, keepdims=True) for block in blocks], axis=1)


def input_kernel(where_ref, dpl_ref, bias_ref, tokens_ref, weight_ref, gain_two_ref, da_ref, small_ref):
    bias_blocks = lane_blocks(bias_ref[...])
    x = tokens_ref[...].astype(f32)
    inverse = lax.rsqrt(jnp.mean(x * x, axis=1, keepdims=True) + norm_eps)
    da = dot_last(dpl_ref[...], weight_ref[...])
    gain_one_blocks = lane_blocks(jnp.sum(da * x * inverse, axis=0, keepdims=True))
    gain_two_blocks = lane_blocks(gain_two_ref[...])
    da_ref[...] = da

    gain_each = 2 * MODEL_WIDTH // 4
    bias_each = QKV_WIDTH // 4
    lines = []
    for s in range(4):
        source = gain_one_blocks if s < 2 else gain_two_blocks
        count = 0
        for t in range(0, gain_each, LANES):
            lines.append(cut_lanes(source, (s % 2) * gain_each + t, min(LANES, gain_each - t)))
            count += 1
        for t in range(0, bias_each, LANES):
            lines.append(cut_lanes(bias_blocks, s * bias_each + t, min(LANES, bias_each - t)))
            count += 1
        lines += [jnp.zeros((1, LANES), f32)] * (SMALL_ROWS // 4 - count)
    small_ref[...] = jnp.concatenate(lines, axis=0).astype(bf16)


def tokens_kernel(where_ref, da_ref, tokens_ref, dh_ref, gains_ref, total_ref, tokens_grad_ref, output_ref, sign_ref):
    output_ref[...] = total_ref[...].T.astype(bf16)
    sign_ref[...] = jnp.zeros(sign_ref.shape, f32)
    da = da_ref[...]
    x = tokens_ref[...].astype(f32)
    inverse = lax.rsqrt(jnp.mean(x * x, axis=1, keepdims=True) + norm_eps)
    weighted = da * gains_ref[0:1, :MODEL_WIDTH]
    inner = jnp.mean(weighted * x, axis=1, keepdims=True)
    tokens_grad = dh_ref[...] + inverse * weighted - x * (inverse * inverse * inverse) * inner
    tokens_grad_ref[...] = tokens_grad.T.astype(bf16)


def place_sum(held_ref, kept_ref, came_refs, mine, groups, rows):
    half = groups // 2
    each = 2 * groups // len(came_refs)
    for j in range(2):
        for b in range(groups):
            at = j * groups + b
            part, inner = divmod(at, each)
            total = kept_ref[at * rows : (at + 1) * rows, :].astype(f32)
            total = total + came_refs[part][inner * rows : (inner + 1) * rows, :].astype(f32)
            place = block_place(b, mine, groups)
            beyond = jnp.where((place & half) == 0, 0, half)
            to = pl.multiple_of((place + beyond + j * half) * rows, 16)
            held_ref[pl.ds(to, rows), :] = total.astype(bf16)


def halve_first_kernel(
    groups, where_ref, kept_ref, came0, came1, small_ref, small_came, sent_ref, left_ref, held_ref
):
    rows = OUT_ROW
    part = groups * rows
    place_sum(held_ref, kept_ref, (came0, came1), where_ref[1], groups, rows)
    small = small_ref[...].astype(f32) + small_came[...].astype(f32)
    for ref, start in ((left_ref, 0), (sent_ref, part)):
        ref[:part, :] = held_ref[start : start + part, :]
        ref[part:, :] = small.astype(bf16)


def down_out_kernel(groups, where_ref, down_zero, down_came, kept_ref, came0, came1, sent_ref, left_ref, held_ref):
    rows = OUT_ROW
    part = groups * rows
    place_sum(held_ref, kept_ref, (came0, came1), where_ref[1], groups, rows)
    lanes = down_zero.shape[1] // LANES
    for ref, start, first in ((left_ref, 0, 0), (sent_ref, part, groups // 2)):
        ref[:part, :] = held_ref[start : start + part, :]
        for b in range(groups // 2):
            rows = slice((first + b) * DOWN_ROWS, (first + b + 1) * DOWN_ROWS)
            total = down_zero[rows, :].astype(f32) + down_came[rows, :].astype(f32)
            for i in range(lanes):
                to = part + (b * lanes + i) * DOWN_ROWS
                ref[to : to + DOWN_ROWS, :] = total[:, i * LANES : (i + 1) * LANES].astype(bf16)


def halve_kernel(small_rows, where_ref, kept_ref, came_ref, sent_ref, left_ref):
    part = left_ref.shape[0] - small_rows
    rows = 2 * part + small_rows
    total = kept_ref[:rows, :].astype(f32) + came_ref[:rows, :].astype(f32)
    total = total.astype(bf16)
    left_ref[:part, :] = total[:part]
    sent_ref[:part, :] = total[part : 2 * part]
    if small_rows:
        left_ref[part:, :] = total[2 * part :]
        sent_ref[part:, :] = total[2 * part :]


def fold_feed_kernel(where_ref, gate_kept, gate_came, gate_across, low_kept, low_came, left_ref, sent_ref):
    blocks, rows = gate_kept.shape[:2]
    half = blocks // 2
    lanes = gate_kept.shape[2] // LANES
    first = low_kept.shape[0] - blocks * lanes * DOWN_ROWS
    for b in range(blocks):
        ref, at = (left_ref, b) if b < half else (sent_ref, b - half)
        gate_up = gate_kept[b].astype(f32) + gate_came[b].astype(f32) + gate_across[b].astype(f32)
        ref[at, :rows, :] = gate_up.astype(bf16)
        for i in range(lanes):
            start = first + (b * lanes + i) * DOWN_ROWS
            down = low_kept[start : start + DOWN_ROWS, :].astype(f32)
            down = down + low_came[start : start + DOWN_ROWS, :].astype(f32)
            ref[at, rows:, i * LANES : (i + 1) * LANES] = down.astype(bf16)


def fold_attention_kernel(where_ref, out_kept, out_came, qkv_kept, qkv_came, left_ref, sent_ref):
    rows = OUT_ROW
    blocks = out_kept.shape[0] // rows
    half = blocks // 2
    out = (out_kept[...].astype(f32) + out_came[...].astype(f32)).astype(bf16)
    qkv = (qkv_kept[...].astype(f32) + qkv_came[...].astype(f32)).astype(bf16)
    small = qkv[blocks * rows :].astype(f32)
    each = SMALL_ROWS // 4
    mine = small[:each]
    for s in range(1, 4):
        mine = jnp.where(where_ref[0] == s, small[s * each : (s + 1) * each], mine)
    mine = jnp.concatenate([mine, jnp.zeros_like(mine)], axis=0).astype(bf16)
    for b in range(blocks):
        ref, at = (left_ref, b) if b < half else (sent_ref, b - half)
        ref[at, :rows, :LANES] = out[b * rows : (b + 1) * rows]
        ref[at, :rows, LANES:] = qkv[b * rows : (b + 1) * rows]
        ref[at, rows:, :LANES] = mine
        ref[at, rows:, LANES:] = jnp.zeros_like(mine)


def fold_kernel(where_ref, kept_ref, came_ref, left_ref, sent_ref):
    half = left_ref.shape[0]
    for b in range(half):
        left_ref[b] = (kept_ref[b].astype(f32) + came_ref[b].astype(f32)).astype(bf16)
        at = b + half
        sent_ref[b] = (kept_ref[at].astype(f32) + came_ref[at].astype(f32)).astype(bf16)


def read_total(refs, parts):
    total = refs[0][0].astype(f32)
    for ref in refs[1:parts]:
        total = total + ref[0].astype(f32)
    return total


def step_with(refs):
    count = len(refs) // 2
    ins, outs = refs[:count], refs[count:]

    def step(at, gradient, rate):
        new = adam_update(ins[at][...], ins[at + 1][...], ins[at + 2][...], gradient, rate)
        for i in range(3):
            outs[at + i][...] = new[i]

    return ins, step


def feed_step_kernel(step_rates, parts, where_ref, *refs):
    total = read_total(refs, parts)
    ins, step = step_with(refs[parts:])
    step(0, total[: ins[0].shape[0]], step_rates[2])
    step(3, total[OUT_ROW : OUT_ROW + ins[3].shape[0]], step_rates[3])


def attention_step_kernel(step_rates, parts, where_ref, *refs):
    total = read_total(refs, parts)
    ins, step = step_with(refs[parts:])
    step(0, total[:OUT_ROW, LANES : LANES + ins[0].shape[1]], step_rates[0])
    step(3, total[:OUT_ROW, : ins[3].shape[1]], step_rates[1])
    mine = total[OUT_ROW:, :LANES]
    line = 0
    for at in (6, 9):
        width = ins[at].shape[0]
        lines = -(-width // LANES)
        wide = jnp.concatenate([mine[line + t : line + t + 1, :] for t in range(lines)], axis=1)
        line += lines
        step(at, wide[:, :width].reshape(width), step_rates[4 if at == 6 else 5])


def swap(values, axis, bit):
    size = lax.axis_size(axis)
    return lax.ppermute(values, axis, [(i, i ^ bit) for i in range(size)])


def add_low(left, right):
    return (left.astype(f32) + right.astype(f32)).astype(bf16)


def halves(values):
    half = values.shape[0] // 2
    return values[:half], values[half:]


def own_term(total, extra, places):
    bit = 1
    while bit < extra:
        total = total + swap(total, "rep", bit)
        bit *= 2
    at = lax.axis_index("rep") % extra
    result = total
    for row, rows, lane, lanes, dim, width in places:
        part = total[row : row + rows, lane : lane + lanes]
        own = lax.dynamic_slice_in_dim(part, at * width, width, dim)
        result = lax.dynamic_update_slice(result, own, (row, lane))
    return result[None]


def finish(left, came, extra, places):
    if extra == 1:
        return [left, came]
    return [own_term((left.astype(f32) + came.astype(f32))[0], extra, places)]


def on_device(
    tokens,
    segments,
    cotangent,
    projection_weight,
    out_weight,
    gate_up_weight,
    down_weight,
    norm_gains,
    projection_bias,
    projection_first_moment,
    out_first,
    gate_up_first,
    down_first,
    gains_first,
    bias_first_moment,
    projection_second_moment,
    out_second,
    gate_up_second,
    down_second,
    gains_second,
    bias_second_moment,
):
    count = tokens.shape[0]
    replicas = lax.axis_size("rep")
    groups = min(replicas, 8)
    extra = replicas // groups
    replica = lax.axis_index("rep")
    where = jnp.stack([lax.axis_index("fsdp"), replica // extra, replica]).astype(jnp.int32)
    rates = learn_rates()
    wide = 1024
    shard_rows, ff_rows = projection_weight.shape[0], gate_up_weight.shape[0]
    q_wide = 5 * LANES
    kv_wide = KEY_VALUE_HEADS * LANES
    tokens_turned, e_turned, down_turned = tokens.T, cotangent.T, down_weight.T

    pack = pack_attention(projection_weight, out_weight, norm_gains, projection_bias)
    pack2 = swap(pack, "fsdp", 2)
    pack1 = swap(pack, "fsdp", 1)

    (cosine, sine, mask, tokens_low, e, low_gate_up, half, low_down,
     own_qkv, own_out, own_gate_up, own_down) = kernel_call(
        tables_kernel,
        [
            shaped((count, LANES), f32),
            shaped((count, LANES), f32),
            shaped((count, count), f32),
            shaped((count, MODEL_WIDTH), bf16),
            shaped((count, MODEL_WIDTH), bf16),
            shaped((ff_rows, 2 * MODEL_WIDTH), bf16),
            shaped((ff_rows // 2, 2 * MODEL_WIDTH), bf16),
            shaped((MODEL_WIDTH, ff_rows), bf16),
            shaped(projection_first_moment.shape, f32),
            shaped(out_first.shape, f32),
            shaped(gate_up_first.shape[::-1], f32),
            shaped(down_first.shape[::-1], f32),
        ],
        "tables", 3.0,
        scratch=[pltpu.VMEM((2 * MODEL_WIDTH, ff_rows), f32)], after=(pack,),
    )(
        where, segments, tokens_turned, e_turned,
        projection_weight, out_weight, gate_up_weight, down_turned,
    )

    pack2, half = gate([pack2, half], [pack1, cosine], "after_pack")
    pack3 = swap(pack2, "fsdp", 1)
    half_across = swap(half, "fsdp", 2)
    gate_up1 = swap(low_gate_up, "fsdp", 1)
    down1 = swap(low_down, "fsdp", 1)

    (a, q, k, v, lifted0, lifted1, lifted2, inv, o, weight_full, gains) = kernel_call(
        forward_kernel,
        [
            shaped((count, MODEL_WIDTH), bf16),
            shaped((count, q_wide), bf16),
            shaped((count, kv_wide), bf16),
            shaped((count, kv_wide), bf16),
        ]
        + [shaped((CLUSTER, count, count), bf16)] * 3
        + [
            shaped((count, q_wide), f32),
            shaped((count, q_wide), bf16),
            shaped((MODEL_WIDTH, wide), bf16),
            shaped((2, q_wide), f32),
        ],
        "attention_forward", 6.0,
    )(where, tokens_low, cosine, sine, mask, pack, pack1, pack2, pack3)

    h, a2, a2_turned, out_full = kernel_call(
        project_kernel,
        [
            shaped((count, MODEL_WIDTH), f32),
            shaped((count, q_wide), bf16),
            shaped((MODEL_WIDTH, count), bf16),
            shaped((MODEL_WIDTH, MODEL_WIDTH), bf16),
        ],
        "project", 2.0,
    )(where, tokens_low, o, gains, pack, pack1, pack2, pack3)

    half_across, low_down_late = gate([half_across, low_down], [h, down1], "after_project")
    down2 = swap(low_down_late, "fsdp", 2)
    half_beside = swap(half_across, "rep", extra)
    half_across3 = swap(half_across, "fsdp", 1)
    gate_ups = {0: [low_gate_up], 1: [gate_up1]}
    downs = {0: low_down_late, 1: down1}

    gate_up_block = (2 * MODEL_WIDTH // groups, ff_rows)
    half_block = (groups // 2,) + gate_up_block

    def grad_parts(count):
        return [shaped((groups // count * (OUT_ROW + DOWN_ROWS), ff_rows), bf16)] * count

    def core_sum(own, sent, name, after=()):
        came = [swap(part, "fsdp", 1) for part in sent]
        return kernel_call(
            functools.partial(core_sum_kernel, groups, len(own)),
            [shaped(half_block, bf16), shaped(half_block, bf16), shaped((groups * DOWN_ROWS, ff_rows), bf16)],
            name, 0.02, scratch=[pltpu.VMEM((groups,) + gate_up_block, bf16)], after=after,
        )(where, *own, *came)

    grads = {}
    total, accumulated = h, []
    for j in (1, 0, 3, 2):
        first = j == 1
        waits = (half_across,) if first else (zero_sent,) if j == 3 else ()
        parts = 4 if j > 1 else 2
        total, *results = kernel_call(
            functools.partial(feed_kernel, groups, first, j > 1, parts),
            [
                shaped((count, MODEL_WIDTH), f32),
                shaped((count, q_wide), f32),
            ] + grad_parts(parts),
            "feed_" + str(j), 0.5,
            scratch=[pltpu.VMEM((2 * ff_rows, q_wide), bf16)],
            after=waits,
        )(
            where, a2, a2_turned, e, e_turned, total, *accumulated, *gate_ups[j], downs[j],
        )
        accumulated, grads[j] = results[:1], results[1:]
        if j == 0:
            half_beside, down2 = gate([half_beside, down2], [total], "after_feed_0")
            gate_ups[2] = [half_across, half_beside]
            gate_ups[3] = [half_across3, swap(half_beside, "fsdp", 1)]
            downs[2], downs[3] = down2, swap(down2, "fsdp", 1)
            zero_kept, zero_sent, down_zero = core_sum(grads[0], grads[1], "core_sum_0")
            zero_came = swap(zero_sent, "rep", extra)
    two_kept, two_sent, down_two = core_sum(grads[2], grads[3], "core_sum_2")
    (two_sent,) = gate([two_sent], [zero_came], "after_zero")
    two_came = swap(two_sent, "rep", extra)
    down_came = swap(down_two, "fsdp", 2)

    message = 2 * groups * shard_rows
    dh, dol, gain_two, *out_parts = kernel_call(
        functools.partial(middle_kernel, groups),
        [
            shaped((count, MODEL_WIDTH), f32),
            shaped((count, q_wide), bf16),
            shaped((1, MODEL_WIDTH), f32),
            shaped((message // 2, LANES), bf16),
            shaped((message // 2, LANES), bf16),
            shaped((message, LANES), bf16),
        ],
        "middle", 0.5, after=(two_sent, down_two),
        scratch=[pltpu.VMEM((MODEL_WIDTH, groups * LANES), bf16)],
    )(where, *accumulated, h, e, gains, o, inv, out_full)

    def halve(kept, came, small_rows, name, after=()):
        part = (kept.shape[0] - small_rows) // 2 + small_rows
        return kernel_call(
            functools.partial(halve_kernel, small_rows),
            [shaped((part, LANES), bf16)] * 2, name, 0.3, after=after,
        )(where, kept, came)

    *out_sent, out_kept = out_parts
    out_came = [swap(part, "fsdp", 1) for part in out_sent]

    dqs, dks, dvs = [], [], []
    waits = ()
    for g, lifted in enumerate((lifted0, lifted1, lifted2)):
        if g == 2:
            two_kept, down_zero = gate([two_kept, down_zero], [dqs[1]], "after_back")
            two = add_low(two_kept, two_came)
            gate_up_across = swap(two, "fsdp", 2)
            low_rows = message // 2 + groups // 2 * (ff_rows // LANES) * DOWN_ROWS
            low_sent, low_kept = kernel_call(
                functools.partial(down_out_kernel, groups),
                [shaped((low_rows, LANES), bf16)] * 2, "down_out", 0.2,
                scratch=[pltpu.VMEM((message, LANES), bf16)],
            )(where, down_zero, down_came, out_kept, *out_came)
            low_came = swap(low_sent, "rep", extra)
            waits = (two, low_sent)
        dq, dk, dv = kernel_call(
            functools.partial(attention_back_kernel, g),
            [shaped((CLUSTER, count, LANES), f32), shaped((count, LANES), f32), shaped((count, LANES), f32)],
            "attention_back_" + str(g), 0.2, after=waits + tuple(dqs),
        )(where, q, k, v, lifted, o, dol)
        dqs.append(dq)
        dks.append(dk)
        dvs.append(dv)

    *sent, kept, dpl, bias_grad = kernel_call(
        functools.partial(last_kernel, groups),
        [
            shaped((message // 2, LANES), bf16),
            shaped((message // 2, LANES), bf16),
            shaped((message, LANES), bf16),
            shaped((count, wide), bf16),
            shaped((1, wide), f32),
        ],
        "last", 0.2,
        scratch=[pltpu.VMEM((MODEL_WIDTH, groups * LANES), bf16)],
    )(where, *dqs, *dks, *dvs, cosine, sine, a)
    came = [swap(part, "fsdp", 1) for part in sent]
    da, small = kernel_call(
        input_kernel,
        [shaped((count, MODEL_WIDTH), f32), shaped((SMALL_ROWS, LANES), bf16)], "input_gradient", 0.2,
    )(where, dpl, bias_grad, tokens_low, weight_full, gain_two)
    small_came = swap(small, "fsdp", 1)
    sent, kept = kernel_call(
        functools.partial(halve_first_kernel, groups),
        [shaped((message // 2 + SMALL_ROWS, LANES), bf16)] * 2, "halve_first", 0.3, after=(gate_up_across,),
        scratch=[pltpu.VMEM((message, LANES), bf16)],
    )(where, kept, *came, small, small_came)
    came = swap(sent, "rep", extra)

    quarter = groups // 4
    rows = OUT_ROW + DOWN_ROWS
    feed_left, feed_sent = kernel_call(
        fold_feed_kernel, [shaped((quarter, rows, ff_rows), bf16)] * 2, "fold_feed", 0.5, after=(sent,)
    )(where, zero_kept, zero_came, gate_up_across, low_kept, low_came)
    feed_came = swap(feed_sent, "rep", 2 * extra)
    out_sent, out_kept = kernel_call(
        functools.partial(halve_kernel, 0),
        [shaped((message // 4, LANES), bf16)] * 2, "out_halve", 0.3, after=(feed_sent,),
    )(where, low_kept, low_came)
    out_came = swap(out_sent, "fsdp", 2)
    sent, kept = halve(kept, came, SMALL_ROWS, "halve_2")
    came = swap(sent, "fsdp", 2)

    def fold(left, came, name, after=()):
        half = left.shape[0] // 2
        return kernel_call(
            fold_kernel, [shaped((half,) + left.shape[1:], bf16)] * 2, name, 0.3, after=after
        )(where, left, came)

    bits = [1 << i for i in range(2, groups.bit_length() - 1)]
    for bit in bits:
        feed_left, feed_sent = fold(feed_left, feed_came, "fold_feed_" + str(bit), (sent, out_came))
        feed_came = swap(feed_sent, "rep", bit * extra)
    left, sent = kernel_call(
        fold_attention_kernel,
        [shaped((quarter, OUT_ROW + SMALL_ROWS // 2, 2 * LANES), bf16)] * 2, "fold_attention", 0.5, after=(feed_sent,),
    )(where, out_kept, out_came, kept, came)
    came = swap(sent, "rep", 2 * extra)
    tokens_grad, output, sign = kernel_call(
        tokens_kernel,
        [shaped((MODEL_WIDTH, count), bf16), shaped((MODEL_WIDTH, count), bf16), shaped((8, LANES), f32)],
        "tokens_gradient", 0.5, after=(sent,),
    )(where, da, tokens_low, dh, gains, total)
    for bit in bits:
        left, sent = fold(left, came, "fold_attention_" + str(bit), (feed_came, sign))
        came = swap(sent, "rep", bit * extra)

    feed_states = (
        own_gate_up, gate_up_first.T, gate_up_second.T, own_down, down_first.T, down_second.T,
    )
    wide_gate, wide_down = own_gate_up.shape[0] * extra, own_down.shape[0] * extra
    feed_parts = finish(feed_left, feed_came, extra, (
        (0, wide_gate, 0, ff_rows, 0, own_gate_up.shape[0]),
        (OUT_ROW, wide_down, 0, ff_rows, 0, own_down.shape[0]),
    ))
    feed_news = kernel_call(
        functools.partial(feed_step_kernel, rates, len(feed_parts)),
        [shaped(state.shape, f32) for state in feed_states], "feed_step", 0.5, after=(sent,),
    )(where, *feed_parts, *feed_states)
    states = (
        own_qkv, projection_first_moment, projection_second_moment,
        own_out, out_first, out_second,
        norm_gains, gains_first, gains_second,
        projection_bias, bias_first_moment, bias_second_moment,
    )
    parts = finish(left, came, extra, (
        (0, OUT_ROW, LANES, own_qkv.shape[1] * extra, 1, own_qkv.shape[1]),
        (0, OUT_ROW, 0, own_out.shape[1] * extra, 1, own_out.shape[1]),
    ))
    news = kernel_call(
        functools.partial(attention_step_kernel, rates, len(parts)),
        [shaped(state.shape, f32) for state in states], "attention_step", 1.0,
    )(where, *parts, *states)
    return (
        output.T,
        tokens_grad.T,
        *news[:6],
        *[new.T for new in feed_news],
        *news[6:],
    )


def solution(mesh):
    rows = P(("rep", "fsdp"), None)
    weight = P("fsdp", None)
    state = P("fsdp", "rep")
    vector = P("fsdp")
    states = (state,) * 4 + (vector,) * 2
    in_specs = (rows, P(("rep", "fsdp")), rows) + (weight,) * 4 + (vector,) * 2 + states + states
    out_specs = (rows, rows) + (state,) * 12 + (vector,) * 6
    return jax.shard_map(
        on_device, mesh=mesh, in_specs=in_specs, out_specs=out_specs, check_vma=False
    )
```
